32 devices in a mesh: dp: 8 (over z, core), shard: 4 (over y, x).
Axes of the slice: x: 2, y: 2, z: 4, core: 2. Of those that a mesh axis runs over, the one named last changes fastest.
Arguments:
- tokens: bfloat16 [32768, 1024], P(('dp', 'shard')), may hold values from -6 to 6
- cotangent: bfloat16 [32768, 1024], P(('dp', 'shard')), may hold values from -6 to 6
- lengths: int32 [32, 4], P(('dp', 'shard')), may hold values from 0 to 1024, as said below
- attn_w: float32 [1024, 4096], P('shard')
- attn_m: float32 [1024, 4096], P('shard')
- attn_v: float32 [1024, 4096], P('shard'), as said below
- mlp_w: float32 [1024, 8192], P('shard'), may hold values from -0.1875 to 0.1875
- mlp_m: float32 [1024, 8192], P('shard')
- mlp_v: float32 [1024, 8192], P('shard'), as said below
- small: float32 [12288], P('shard')
- small_m: float32 [12288], P('shard')
- small_v: float32 [12288], P('shard'), as said below
Outputs:
- output: bfloat16 [32768, 1024], P(('dp', 'shard'))
- grad_input: float32 [32768, 1024], P(('dp', 'shard'))
- attn_w_new: float32 [1024, 4096], P('shard')
- attn_m_new: float32 [1024, 4096], P('shard')
- attn_v_new: float32 [1024, 4096], P('shard')
- mlp_w_new: float32 [1024, 8192], P('shard')
- mlp_m_new: float32 [1024, 8192], P('shard')
- mlp_v_new: float32 [1024, 8192], P('shard')
- small_new: float32 [12288], P('shard')
- small_m_new: float32 [12288], P('shard')
- small_v_new: float32 [12288], P('shard')
The draws below stay inside these ranges and needn't reach their ends.
Inputs may be any that keep to these rules, and one draw needn't show every extreme that they name: Row b lists the document lengths of block b; zero entries are empty slots; a row sums to 512 or more and to 1024 at most; in every draw some row holds a single document of 1024. `attn_v`: Positive. `mlp_v`: Positive. `small_v`: Positive.
All inputs are finite; a program needn't handle non-finite values.
Results may differ from the reference program's by a relative error of at most 0.012.
The reference program's roundings to bfloat16 on the way count: a program that leaves them out, or rounds other values in their place, can miss the bound.
Values may be sent and summed in bfloat16 or wider, within the bound.
No kernel may reach another device: no remote copies, remote signals or barrier semaphores. Data moves between devices by JAX's collectives and lax.ppermute only.
A program may use at most 384 MiB of HBM per device.

```python
import jax
import jax.numpy as jnp
from jax import lax

H = 16
HD = 64
D = 1024
FF = 4096
BLOCK = 1024
DOCS = 4
STEP = 10
DEVS = 32
TOKENS = 32768


def draw_lengths(key, part):
    key = jax.random.fold_in(key, 11)
    key_total, key_cuts, key_pick = jax.random.split(key, 3)
    totals = jax.random.randint(key_total, (DEVS,), BLOCK // 2, BLOCK + 1)
    cuts = jnp.sort(jax.random.randint(key_cuts, (DEVS, DOCS - 1), 0, BLOCK + 1), axis=1)
    cuts = jnp.minimum(cuts, totals[:, None])
    bounds = jnp.concatenate([jnp.zeros((DEVS, 1), jnp.int32), cuts, totals[:, None]], axis=1)
    pieces = bounds[:, 1:] - bounds[:, :-1]
    chosen = jax.random.randint(key_pick, (), 0, DEVS)
    single = jnp.zeros((DOCS,), jnp.int32).at[0].set(BLOCK)
    rows_all = jnp.arange(DEVS, dtype=jnp.int32)
    pieces = jnp.where((rows_all == chosen)[:, None], single[None, :], pieces)
    return pieces.astype(jnp.int32)


def draw_attn_w(key, part):
    key = jax.random.fold_in(key, 3)
    base = jax.random.normal(key, (D, 4 * D), jnp.float32)
    columns = jnp.arange(4 * D)
    scale = jnp.where(columns < 3 * D, D ** (-0.5), 8.0 * D ** (-0.5))
    return (base * scale[None, :]).astype(jnp.float32)


def draw_small(key, part):
    key = jax.random.fold_in(key, 5)
    base = jnp.clip(jax.random.normal(key, (8 * D + FF,), jnp.float32), -3.0, 3.0)
    places = jnp.arange(8 * D + FF)
    first_gain = (places >= 4 * D + FF) & (places < 5 * D + FF)
    second_gain = (places >= 6 * D + FF) & (places < 7 * D + FF)
    return jnp.where(first_gain | second_gain, 1.0 + 0.2 * base, 0.2 * base).astype(jnp.float32)


def attn_sizes():
    columns = jnp.arange(4 * D)
    return jnp.where(columns < 3 * D, 1.0, 0.25) * TOKENS ** 0.5


def mlp_sizes():
    columns = jnp.arange(2 * FF)
    return jnp.where(columns < FF, 0.5, 0.57) * TOKENS ** 0.5


def small_sizes():
    places = jnp.arange(8 * D + FF)
    size = jnp.where(places < 3 * D, 1.0, 1.0)
    size = jnp.where((places >= 3 * D) & (places < 3 * D + FF), 0.5, size)
    size = jnp.where((places >= 3 * D + FF) & (places < 4 * D + FF), 0.87, size)
    size = jnp.where((places >= 4 * D + FF) & (places < 6 * D + FF), 1.7, size)
    return size * TOKENS ** 0.5


def first_moment(key, shape, size):
    base = jnp.clip(jax.random.normal(key, shape, jnp.float32), -3.0, 3.0)
    return (base * size / 9.0).astype(jnp.float32)


def second_moment(key, shape, size):
    factor = jnp.exp(jax.random.uniform(key, shape, jnp.float32, 0.0, 1.3862944))
    return (factor * size * size / 19.0).astype(jnp.float32)


def draw_attn_m(key, part):
    key = jax.random.fold_in(key, 21)
    return first_moment(key, (D, 4 * D), attn_sizes()[None, :])


def draw_attn_v(key, part):
    key = jax.random.fold_in(key, 22)
    return second_moment(key, (D, 4 * D), attn_sizes()[None, :])


def draw_mlp_m(key, part):
    key = jax.random.fold_in(key, 23)
    return first_moment(key, (D, 2 * FF), mlp_sizes()[None, :])


def draw_mlp_v(key, part):
    key = jax.random.fold_in(key, 24)
    return second_moment(key, (D, 2 * FF), mlp_sizes()[None, :])


def draw_small_m(key, part):
    key = jax.random.fold_in(key, 25)
    return first_moment(key, (8 * D + FF,), small_sizes())


def draw_small_v(key, part):
    key = jax.random.fold_in(key, 26)
    return second_moment(key, (8 * D + FF,), small_sizes())


def levels(stream_key, shape, cuts, least, largest):
    level, own = 1.0, jax.random.fold_in(stream_key, 6)
    for axis_at, parts in cuts:
        heights = jnp.exp(jax.random.uniform(jax.random.fold_in(own, axis_at), (parts,), jnp.float32, least / len(cuts), largest / len(cuts)))
        level = level * jnp.repeat(heights, shape[axis_at] // parts).reshape([-1 if axis == axis_at else 1 for axis in range(len(shape))])
    return level


def bell_draw(key, extent, width, bound, cuts=(), kind=jnp.bfloat16):
    array = jax.random.normal(key, extent, jnp.float32) * width
    if len(cuts) > 0:
        array = levels(key, extent, cuts, -0.22, 0.18) * array
    return jnp.clip(array, min=-bound, max=bound).astype(kind)


def setup_inputs(seed: int = 0) -> dict:
    arg_keys = jax.random.split(jax.random.key(seed), 13)
    return {
        "tokens": bell_draw(arg_keys[0], (TOKENS, D), 1.0, 6.0, ((0, 32),)),
        "cotangent": bell_draw(arg_keys[1], (TOKENS, D), 1.0, 6.0, ((0, 32),)),
        "lengths": draw_lengths(jax.random.fold_in(arg_keys[12], 71), 0),
        "attn_w": draw_attn_w(jax.random.fold_in(arg_keys[12], 71), 0),
        "attn_m": draw_attn_m(jax.random.fold_in(arg_keys[12], 71), 0),
        "attn_v": draw_attn_v(jax.random.fold_in(arg_keys[12], 71), 0),
        "mlp_w": bell_draw(arg_keys[6], (D, 2 * FF), D ** -0.5, 0.1875, ((0, 4),), jnp.float32),
        "mlp_m": draw_mlp_m(jax.random.fold_in(arg_keys[12], 71), 0),
        "mlp_v": draw_mlp_v(jax.random.fold_in(arg_keys[12], 71), 0),
        "small": draw_small(jax.random.fold_in(arg_keys[12], 71), 0),
        "small_m": draw_small_m(jax.random.fold_in(arg_keys[12], 71), 0),
        "small_v": draw_small_v(jax.random.fold_in(arg_keys[12], 71), 0),
    }


highest = lax.Precision.HIGHEST
beta_one = 0.9
beta_two = 0.95
adam_eps = 1e-08
norm_eps = 1e-05

@jax.custom_vjp
def low(v):
    return lax.optimization_barrier(v.astype(jnp.bfloat16)).astype(jnp.float32)

@jax.custom_vjp
def low_back(v):
    return v

def low_keep(v):
    return (low(v), None)

def low_pass(kept, grad):
    return (grad,)

def back_keep(v):
    return (v, None)

def back_low(kept, grad):
    return (low(grad),)
low.defvjp(low_keep, low_pass)
low_back.defvjp(back_keep, back_low)

def matmul(left, right):
    return jnp.dot(left, right, precision=highest)

def layer_norm(values, gain, shift):
    center = values - lax.optimization_barrier(jnp.mean(values, axis=-1, keepdims=True))
    spread = lax.optimization_barrier(jnp.mean(center * center, axis=-1, keepdims=True))
    return center * lax.rsqrt(spread + norm_eps) * gain + shift

def block_layout(lengths_row, rows):
    ends = jnp.cumsum(lengths_row, dtype=jnp.int32)
    places = jnp.arange(rows, dtype=jnp.int32)
    seg = lax.optimization_barrier(jnp.sum((places[:, None] >= ends[None, :]).astype(jnp.int32), axis=1))
    live = (places < ends[-1]).astype(jnp.float32)
    return (seg, live)

def attend(query, keys, values, seg):
    rows = query.shape[0]
    qh = query.reshape(rows, H, HD)
    kh = keys.reshape(rows, H, HD)
    vh = values.reshape(rows, H, HD)
    scores = jnp.einsum('qhd,khd->hqk', qh, kh, precision=highest) * HD ** (-0.5)
    scores = low_back(scores)
    places = jnp.arange(rows, dtype=jnp.int32)
    allowed = (places[:, None] >= places[None, :]) & (seg[:, None] == seg[None, :])
    scores = jnp.where(allowed[None], scores, -1e+30)
    top = lax.optimization_barrier(jnp.max(scores, axis=-1, keepdims=True))
    expo = jnp.exp(scores - top)
    probs = low(expo / lax.optimization_barrier(jnp.sum(expo, axis=-1, keepdims=True)))
    mixed = jnp.einsum('hqk,khd->qhd', probs, vh, precision=highest)
    return mixed.reshape(rows, H * HD)

def forward(values, attn_w, mlp_w, small, seg):
    bias_q = small[0:D]
    bias_v = small[D:2 * D]
    bias_o = small[2 * D:3 * D]
    bias_up = small[3 * D:3 * D + FF]
    bias_dn = small[3 * D + FF:4 * D + FF]
    gain_one = small[4 * D + FF:5 * D + FF]
    shift_one = small[5 * D + FF:6 * D + FF]
    gain_two = small[6 * D + FF:7 * D + FF]
    shift_two = small[7 * D + FF:8 * D + FF]
    hidden_one = low(layer_norm(values, gain_one, shift_one))
    joint = matmul(hidden_one, attn_w[:, :3 * D])
    query = low(low_back(joint[:, :D] + bias_q))
    keys = low(low_back(joint[:, D:2 * D]))
    vals = low(low_back(joint[:, 2 * D:] + bias_v))
    mixed = low(low_back(jax.checkpoint(attend)(query, keys, vals, seg)))
    branch = low_back(matmul(mixed, attn_w[:, 3 * D:]) + bias_o)
    after = values + branch
    hidden_two = low(layer_norm(after, gain_two, shift_two))
    upper = low_back(matmul(hidden_two, mlp_w[:, :FF]) + bias_up)
    active = low(jax.nn.gelu(upper, approximate=True))
    return after + matmul(active, mlp_w[:, FF:].T) + bias_dn

def adamw(weight, first, second, grad, rate, decay):
    first_new = beta_one * first + (1.0 - beta_one) * grad
    second_new = beta_two * second + (1.0 - beta_two) * grad * grad
    first_hat = first_new / (1.0 - beta_one ** STEP)
    second_hat = second_new / (1.0 - beta_two ** STEP)
    weight_new = weight - rate * (first_hat / (jnp.sqrt(second_hat) + adam_eps) + decay * weight)
    return (weight_new, first_new, second_new)

def reference(tokens, cotangent, lengths, attn_w, attn_m, attn_v, mlp_w, mlp_m, mlp_v, small, small_m, small_v):
    attn_low = low(attn_w)
    mlp_low = low(mlp_w)
    small_low = low(small)
    blocks = tokens.reshape(DEVS, BLOCK, D)
    cot_blocks = cotangent.reshape(DEVS, BLOCK, D)

    def one_block(totals, item):
        token_block, cot_block, length_row = item
        seg, live = block_layout(length_row, BLOCK)
        start = token_block.astype(jnp.float32)
        back = cot_block.astype(jnp.float32) * live[:, None]

        def local_forward(values, first_w, second_w, third_w):
            return forward(values, first_w, second_w, third_w, seg)
        result, pull = jax.vjp(local_forward, start, attn_low, mlp_low, small_low)
        grad_in, grad_a, grad_m, grad_s = pull(back)
        totals = (totals[0] + grad_a, totals[1] + grad_m, totals[2] + grad_s)
        return (totals, (result.astype(jnp.bfloat16), grad_in))
    zeros = (jnp.zeros(attn_w.shape, jnp.float32), jnp.zeros(mlp_w.shape, jnp.float32), jnp.zeros(small.shape, jnp.float32))
    totals, (results, grads_in) = lax.scan(one_block, zeros, (blocks, cot_blocks, lengths))
    attn_new = adamw(attn_w, attn_m, attn_v, totals[0], 0.05, 0.1)
    mlp_new = adamw(mlp_w, mlp_m, mlp_v, totals[1], 0.05, 0.1)
    small_new = adamw(small, small_m, small_v, totals[2], 0.4, 0.0)
    return (results.reshape(TOKENS, D), grads_in.reshape(TOKENS, D), attn_new[0], attn_new[1], attn_new[2], mlp_new[0], mlp_new[1], mlp_new[2], small_new[0], small_new[1], small_new[2])
```

```python
import functools

import jax
import jax.numpy as jnp
from jax import lax
from jax.experimental import pallas as pl
from jax.experimental.pallas import tpu as pltpu
from jax.sharding import PartitionSpec as P

HD = 64
STEP = 10
LANES = 128
MASKED = -1e30
SAFE = 60.0
GELU_IN = 0.7978845608028654
GELU_CUBE = 0.044715

beta_one = 0.9
beta_two = 0.95
adam_eps = 1e-08
norm_eps = 1e-05

F32 = jnp.float32
BF16 = jnp.bfloat16
MIB = 1024 * 1024
VMEM_MIB = 64

ANY = pl.BlockSpec(memory_space=pl.ANY)
SMEM = pl.BlockSpec(memory_space=pltpu.SMEM)


def dot_nn(left, right):
    return lax.dot_general(left, right, (((1,), (0,)), ((), ())), preferred_element_type=F32)


def dot_nt(left, right):
    return lax.dot_general(left, right, (((1,), (1,)), ((), ())), preferred_element_type=F32)


def dot_tn(left, right):
    return lax.dot_general(left, right, (((0,), (0,)), ((), ())), preferred_element_type=F32)


def whole(shape):
    return pl.BlockSpec(shape, lambda *_: (0,) * len(shape))


def call(kernel, grid, ins, outs, after=(), reuse=(), prefetch=(), scratch=(), cost=None, name=None):
    known = len(prefetch) + len(ins)
    idle = [*after, *(array for array, _ in reuse)]

    def run(*refs):
        kernel(*refs[:known], *refs[known + len(idle) :])

    def placed(array, spec):
        if spec is SMEM:
            return array
        return pltpu.with_memory_space_constraint(array, pltpu.HBM)

    return pl.pallas_call(
        run,
        grid_spec=pltpu.PrefetchScalarGridSpec(
            num_scalar_prefetch=len(prefetch),
            grid=grid,
            in_specs=[spec for _, spec in ins] + [ANY] * len(idle),
            out_specs=[spec for _, _, spec in outs],
            scratch_shapes=list(scratch),
        ),
        out_shape=[pltpu.HBM(shape, dtype) for shape, dtype, _ in outs],
        input_output_aliases={
            known + len(after) + number: output for number, (_, output) in enumerate(reuse)
        },
        compiler_params=pltpu.CompilerParams(vmem_limit_bytes=VMEM_MIB * MIB),
        cost_estimate=pl.CostEstimate(flops=0, bytes_accessed=0, transcendentals=0),
        name=name,
    )(*prefetch, *(placed(*item) for item in ins), *(placed(array, ANY) for array in idle))


def param(small, number, width):
    return (small, pl.BlockSpec((1, width), lambda *_: (0, number)))


def cost(flops, moved, exps=0):
    return pl.CostEstimate(flops=int(flops), bytes_accessed=int(moved), transcendentals=int(exps))


def store_turned(turned_ref, toff, block, half, value, columns):
    turned = value.astype(BF16).T
    for part in range(LANES // half):
        offset = pl.multiple_of(toff[block * (LANES // half) + part], half)
        turned_ref[pl.ds(offset, half), columns] = turned[part * half : (part + 1) * half]


def norm_stats(values):
    center = values - jnp.mean(values, axis=-1, keepdims=True)
    spread = jnp.mean(center * center, axis=-1, keepdims=True)
    scale = lax.rsqrt(spread + norm_eps)
    return center * scale, scale


def norm_back(hat, scale, grad_hat):
    mean = jnp.mean(grad_hat, axis=-1, keepdims=True)
    along = jnp.mean(grad_hat * hat, axis=-1, keepdims=True)
    return scale * (grad_hat - mean - hat * along)


def accumulate(ref, value, first):
    @pl.when(first)
    def _():
        ref[...] = value

    @pl.when(jnp.logical_not(first))
    def _():
        ref[...] += value


class Weights:
    def __init__(self, pieces, plan, offs, first=0):
        self.pieces, self.plan, self.offs, self.first = pieces, plan, offs, first

    def at(self, first):
        return Weights(self.pieces, self.plan, self.offs, self.first + first)

    def inputs(self):
        return [(self.offs, SMEM)] + [(piece, ANY) for piece in self.pieces]

    def sems(self):
        return pltpu.SemaphoreType.DMA((len(self.plan),))

    def rest(self, refs):
        return refs[1 + len(self.pieces) :]

    def copies(self, refs, size, target, sems, start=None):
        offs, refs = refs[0], refs[1:]
        columns = slice(self.first, self.first + size)
        if start is not None:
            columns = pl.ds(pl.multiple_of(self.first + start, LANES), size)
        made = []
        for number, (piece, first, rows, index) in enumerate(self.plan):
            offset = pl.multiple_of(offs[index], rows)
            made.append(
                pltpu.make_async_copy(
                    refs[piece].at[pl.ds(first, rows), columns],
                    target(offset, rows),
                    sems.at[number],
                )
            )
        return made, refs[len(self.pieces) :]


def start_all(copies):
    @pl.when(pl.program_id(0) == 0)
    def _():
        for copy in copies:
            copy.start()


def wait_all(copies):
    @pl.when(pl.program_id(0) == 0)
    def _():
        for copy in copies:
            copy.wait()


def cot_kernel(half, toff, ends, cot_ref, dy_ref, turned_ref, bias_ref):
    rows = cot_ref.shape[0]
    place = lax.broadcasted_iota(jnp.int32, (rows, LANES), 0)
    live = (place < ends[ends.shape[0] - 1]).astype(F32)
    for block in range(cot_ref.shape[1] // LANES):
        columns = slice(block * LANES, (block + 1) * LANES)
        value = cot_ref[:, columns].astype(F32) * live
        dy_ref[:, columns] = value.astype(BF16)
        bias_ref[:, columns] = jnp.sum(value, axis=0, keepdims=True)
        store_turned(turned_ref, toff, block, half, value, slice(None))


def run_cot(half, toff, ends, cot, after=()):
    rows, width = cot.shape
    return call(
        functools.partial(cot_kernel, half),
        (1,),
        [(toff, SMEM), (ends, SMEM), (cot, whole(cot.shape))],
        [
            ((rows, width), BF16, whole((rows, width))),
            ((width, rows), BF16, whole((width, rows))),
            ((1, width), F32, whole((1, width))),
        ],
        after=after,
        cost=cost(0, 6 * rows * width),
        name="cotangent",
    )


def run_qkv(half, weights, toff, x, small, numbers, after=()):
    rows, width = x.shape
    span = 256

    def kernel(*refs):
        weight, sems = refs[-2:]
        copies, refs = weights.copies(
            refs, 3 * width, lambda at, size: weight.at[pl.ds(at, size), :], sems
        )
        toff_ref, x_ref, bias_q, bias_v, gain_ref, shift_ref, qkv_ref, turned_ref = refs[:8]
        start_all(copies)
        hat, _ = norm_stats(x_ref[...].astype(F32))
        normed = hat * gain_ref[...] + shift_ref[...]
        for block in range(width // LANES):
            columns = slice(block * LANES, (block + 1) * LANES)
            store_turned(turned_ref, toff_ref, block, half, normed[:, columns], slice(None))
        wait_all(copies)
        low = normed.astype(BF16)
        for part in range(3):
            columns = slice(part * width, (part + 1) * width)
            value = dot_nn(low, weight[:, columns])
            if part == 2:
                value += bias_v[...]
            if part == 0:
                value = (value + bias_q[...]).astype(BF16).astype(F32) * HD ** (-0.5)
            qkv_ref[:, columns] = value.astype(BF16)

    return call(
        kernel,
        (rows // span,),
        weights.inputs()
        + [
            (toff, SMEM),
            (x, pl.BlockSpec((span, width), lambda i: (i, 0))),
        ]
        + [param(small, number, width) for number in numbers],
        [
            ((rows, 3 * width), BF16, pl.BlockSpec((span, 3 * width), lambda i: (i, 0))),
            ((width, rows), BF16, pl.BlockSpec((width, span), lambda i: (0, i))),
        ],
        after=after,
        scratch=[pltpu.VMEM((width, 3 * width), BF16), weights.sems()],
        cost=cost(6 * rows * width * width, 16 * rows * width),
        name="qkv",
    )


def first_of_row(ends, place):
    first = jnp.zeros_like(place)
    for number in range(ends.shape[0]):
        first = jnp.where(place >= ends[number], ends[number], first)
    return first


def attend_kernel(ends, q_ref, k_ref, v_ref, o_ref, lse_ref, allow):
    rows = q_ref.shape[0]
    span = min(256, rows)

    @pl.when(pl.program_id(0) == 0)
    def _():
        for start in range(0, rows, span):
            keys = start + span
            place = lax.broadcasted_iota(jnp.int32, (span, 1), 0) + start
            first = first_of_row(ends, place)
            key = lax.broadcasted_iota(jnp.int32, (span, keys), 1)
            allow[start:keys, :keys] = jnp.where((key <= place) & (key >= first), 0.0, MASKED)

    lane = lax.broadcasted_iota(jnp.int32, (1, LANES), 1)
    low_lane = lane < HD
    one = low_lane.astype(BF16)
    masks = (one, 1 - one)

    same = (lax.broadcasted_iota(jnp.int32, (LANES, LANES), 0) < HD) == (
        lax.broadcasted_iota(jnp.int32, (LANES, LANES), 1) < HD
    )
    same = same.astype(F32).astype(BF16)
    longest = [
        jnp.max(dot_nn(ref[...] * ref[...], same), axis=0, keepdims=True) for ref in (q_ref, k_ref)
    ]
    bounded = jnp.max(longest[0] * longest[1]) < SAFE * SAFE

    def attend(shift):
        mixed = [v_ref[...] * mask + (1 - mask) for mask in masks]
        for start in range(0, rows, span):
            keys = start + span
            sums = []
            tops = []
            for head in range(2):
                query = q_ref[start:keys, :] * masks[head]
                scores = dot_nt(query, k_ref[:keys, :]) + allow[start:keys, :keys]
                if shift:
                    top = jnp.max(scores, axis=1, keepdims=True)
                    tops.append(top)
                    scores = scores - top
                probs = jnp.exp(scores).astype(BF16)
                sums.append(dot_nn(probs, mixed[head][:keys]))
            total = pltpu.roll(jnp.where(low_lane, sums[1], sums[0]), HD, 1)
            out = jnp.where(low_lane, sums[0], sums[1]) / total
            o_ref[start:keys, :] = out.astype(BF16)
            lse = jnp.log(total)
            if shift:
                lse += jnp.where(low_lane, tops[0], tops[1])
            lse = lse.T
            lse_ref[0, 0:1, start:keys] = lse[0:1]
            lse_ref[0, 1:2, start:keys] = lse[HD : HD + 1]

    @pl.when(bounded)
    def _():
        attend(False)

    @pl.when(jnp.logical_not(bounded))
    def _():
        attend(True)


def run_attend(ends, qkv, first, count, earlier=None, after=()):
    rows = qkv.shape[0]
    width = qkv.shape[1] // 3
    pairs = width // LANES
    column = lambda shift: pl.BlockSpec((rows, LANES), lambda i: (0, i + shift))
    return call(
        attend_kernel,
        (count,),
        [(ends, SMEM)] + [(qkv, column(first + part * pairs)) for part in range(3)],
        [
            ((rows, width), BF16, column(first)),
            ((pairs, 2, rows), F32, pl.BlockSpec((1, 2, rows), lambda i: (i + first, 0, 0))),
        ],
        after=after,
        reuse=[] if earlier is None else [(earlier[0], 0), (earlier[1], 1)],
        scratch=[pltpu.VMEM((rows, rows), F32)],
        cost=cost(8 * rows * rows * LANES * count, 8 * rows * LANES * count, 2 * rows * rows * count),
        name="attend",
    )


def run_after(half, weights, toffs, mixed, x, small, numbers, after=()):
    rows, width = x.shape
    span = 256

    def kernel(*refs):
        weight, sems = refs[-2:]
        copies, refs = weights.copies(
            refs, width, lambda at, size: weight.at[pl.ds(at, size), :], sems
        )
        mixed_toff, low_toff, mixed_ref, x_ref, bias_ref, gain_ref, shift_ref = refs[:7]
        after_ref, low_ref, turned_ref, mixed_turned_ref = refs[7:11]
        start_all(copies)
        for block in range(width // LANES):
            columns = slice(block * LANES, (block + 1) * LANES)
            store_turned(mixed_turned_ref, mixed_toff, block, half, mixed_ref[:, columns], slice(None))
        wait_all(copies)
        value = x_ref[...].astype(F32) + dot_nn(mixed_ref[...], weight[...]) + bias_ref[...]
        after_ref[...] = value
        hat, _ = norm_stats(value)
        normed = hat * gain_ref[...] + shift_ref[...]
        low_ref[...] = normed.astype(BF16)
        for block in range(width // LANES):
            columns = slice(block * LANES, (block + 1) * LANES)
            store_turned(turned_ref, low_toff, block, half, normed[:, columns], slice(None))

    by_row = pl.BlockSpec((span, width), lambda i: (i, 0))
    by_column = pl.BlockSpec((width, span), lambda i: (0, i))
    return call(
        kernel,
        (rows // span,),
        weights.inputs()
        + [(toff, SMEM) for toff in toffs]
        + [(mixed, by_row), (x, by_row)]
        + [param(small, number, width) for number in numbers],
        [
            ((rows, width), F32, by_row),
            ((rows, width), BF16, by_row),
            ((width, rows), BF16, by_column),
            ((width, rows), BF16, by_column),
        ],
        after=after,
        scratch=[pltpu.VMEM((width, width), BF16), weights.sems()],
        cost=cost(2 * rows * width * width, 14 * rows * width),
        name="after",
    )


def run_feed(up_weights, down_weights, low, turned, dy, dyt, small, first, begin, block, earlier, after=()):
    rows, width = low.shape
    hidden = earlier[0].shape[1] if earlier is not None else block_total(small, width)
    span = 256
    mid = width // 2
    count = block // span
    by_column = lambda size: pl.BlockSpec((size, span), lambda i: (0, i))
    shifted = pl.BlockSpec((rows, span), lambda i: (0, begin // span + i))
    grad = ((2, mid, block), BF16, pl.BlockSpec((2, mid, span), lambda i: (0, 0, i)))

    def kernel(*refs):
        up, down, up_sems, down_sems = refs[-4:]
        step = pl.program_id(0)

        def copies(number):
            columns = pl.ds(pl.multiple_of(number * span, span), span)
            made, rest = up_weights.copies(
                refs,
                span,
                lambda at, size: up.at[pl.ds(at, size), columns],
                up_sems.at[number],
                number * span,
            )
            more, _ = down_weights.copies(
                rest,
                span,
                lambda at, size: down.at[pl.ds(at, size), columns],
                down_sems.at[number],
                number * span,
            )
            return made + more

        @pl.when(step == 0)
        def _():
            for copy in copies(0):
                copy.start()

        @pl.when(step + 1 < count)
        def _():
            for copy in copies(step + 1):
                copy.start()

        for copy in copies(step):
            copy.wait()
        low_ref, turned_ref, dy_ref, dyt_ref, bias_ref, act_ref, du_ref, own_ref, sib_ref, gbias_ref = (
            down_weights.rest(up_weights.rest(refs))[:10]
        )
        columns = pl.ds(pl.multiple_of(step * span, span), span)
        upper = dot_nn(low_ref[...], up[:, columns]) + bias_ref[...]
        grad_act = dot_nn(dy_ref[...], down[:, columns])
        square = (GELU_IN * GELU_CUBE) * (upper * upper)
        tanh = jnp.tanh(upper * (GELU_IN + square))
        share = 0.5 + 0.5 * tanh
        act = upper * share
        slope = share + act * (1.0 - tanh) * (GELU_IN + 3.0 * square)
        act = act.astype(BF16)
        du = (grad_act * slope).astype(BF16)
        act_ref[...] = act
        du_ref[...] = du
        gbias_ref[...] = jnp.sum(du.astype(F32), axis=0, keepdims=True)
        grad_up = dot_nn(turned_ref[...], du).astype(BF16)
        own_ref[0] = grad_up[:mid]
        sib_ref[0] = grad_up[mid:]
        grad_dn = dot_nn(dyt_ref[...], act).astype(BF16)
        own_ref[1] = grad_dn[:mid]
        sib_ref[1] = grad_dn[mid:]

    return call(
        kernel,
        (count,),
        up_weights.inputs()
        + down_weights.inputs()
        + [
            (low, whole((rows, width))),
            (turned, whole((width, rows))),
            (dy, whole((rows, width))),
            (dyt, whole((width, rows))),
            (small, pl.BlockSpec((1, span), lambda i: (0, first // span + i))),
        ],
        [
            ((rows, hidden), BF16, shifted),
            ((rows, hidden), BF16, shifted),
            grad,
            grad,
            ((1, block), F32, by_column(1)),
        ],
        after=after,
        reuse=[] if earlier is None else [(earlier[0], 0), (earlier[1], 1)],
        scratch=[
            pltpu.VMEM((width, block), BF16),
            pltpu.VMEM((width, block), BF16),
            pltpu.SemaphoreType.DMA((count, len(up_weights.plan))),
            pltpu.SemaphoreType.DMA((count, len(down_weights.plan))),
        ],
        cost=cost(8 * rows * width * block, 24 * width * block, rows * block),
        name="feed",
    )


def block_total(small, width):
    return small.shape[1] - 8 * width


class Stream:
    def __init__(self):
        self.parts = []

    def add(self, copies):
        self.parts.append(copies)

    def start(self):
        for copies in self.parts:
            for copy in copies:
                copy.start()

    def wait(self, number):
        for copy in self.parts[number]:
            copy.wait()


def run_output(weights, acts, after_value, small, number, after=()):
    rows, width = after_value.shape
    hidden = acts.shape[1]
    part = width
    parts = hidden // part
    places = [
        (item.at(start)) for size, item in weights for start in range(0, size, part)
    ]
    most = max(len(item.plan) for item in places)

    def kernel(*refs):
        act, down, start_value, sems, own_sems = refs[-5:]
        stream = Stream()
        for index, item in enumerate(places):
            columns = slice(index * part, (index + 1) * part)
            copies, refs = item.copies(
                refs,
                part,
                lambda at, size, columns=columns: down.at[pl.ds(at, size), columns],
                sems.at[index],
            )
            stream.add(copies)
        act_ref, after_ref, bias_ref, out_ref = refs[:4]
        for index in range(parts):
            columns = slice(index * part, (index + 1) * part)
            stream.parts[index].append(
                pltpu.make_async_copy(
                    act_ref.at[:, columns], act.at[:, columns], own_sems.at[index]
                )
            )
        stream.add([pltpu.make_async_copy(after_ref, start_value, own_sems.at[parts])])
        stream.start()
        total = None
        for index in range(parts):
            columns = slice(index * part, (index + 1) * part)
            stream.wait(index)
            value = dot_nt(act[:, columns], down[:, columns])
            total = value if total is None else total + value
        stream.wait(parts)
        out_ref[...] = (total + start_value[...] + bias_ref[...]).astype(BF16)

    (out,) = call(
        kernel,
        (1,),
        [item for place in places for item in place.inputs()]
        + [(acts, ANY), (after_value, ANY), param(small, number, width)],
        [((rows, width), BF16, whole((rows, width)))],
        after=after,
        scratch=[
            pltpu.VMEM((rows, hidden), BF16),
            pltpu.VMEM((width, hidden), BF16),
            pltpu.VMEM((rows, width), F32),
            pltpu.SemaphoreType.DMA((parts, most)),
            pltpu.SemaphoreType.DMA((parts + 1,)),
        ],
        cost=cost(2 * rows * width * hidden, 22 * rows * width),
        name="output",
    )
    return out


def run_middle(weights, out_weights, dus, after_value, dy, small, number, turned, after=()):
    rows, width = after_value.shape
    hidden = dus.shape[1]
    part = width
    parts = hidden // part
    span = 256
    mid = width // 2
    places = [
        (item.at(start)) for size, item in weights for start in range(0, size, part)
    ]
    most = max(len(item.plan) for item in places)

    def kernel(*refs):
        du, up, value_in, dy_in, turned_in, out_weight, branch, sems, out_sems, own_sems = refs[-10:]
        stream = Stream()
        for index, item in enumerate(places):
            columns = slice(index * part, (index + 1) * part)
            copies, refs = item.copies(
                refs,
                part,
                lambda at, size, columns=columns: up.at[pl.ds(at, size), columns],
                sems.at[index],
            )
            stream.add(copies)
        more, refs = out_weights.copies(
            refs, width, lambda at, size: out_weight.at[pl.ds(at, size), :], out_sems
        )
        du_ref, after_ref, dy_ref, gain_ref, turned_ref = refs[:5]
        grad_ref, dmix_ref, own_ref, sib_ref, gbias_ref, ggain_ref, gshift_ref = refs[5:12]
        for index in range(parts):
            columns = slice(index * part, (index + 1) * part)
            stream.parts[index].append(
                pltpu.make_async_copy(du_ref.at[:, columns], du.at[:, columns], own_sems.at[index])
            )
        stream.add(
            [
                pltpu.make_async_copy(after_ref, value_in, own_sems.at[parts]),
                pltpu.make_async_copy(dy_ref, dy_in, own_sems.at[parts + 1]),
            ]
        )
        stream.add([pltpu.make_async_copy(turned_ref, turned_in, own_sems.at[parts + 2]), *more])
        stream.start()
        total = None
        for index in range(parts):
            columns = slice(index * part, (index + 1) * part)
            stream.wait(index)
            value = dot_nt(du[:, columns], up[:, columns])
            total = value if total is None else total + value
        stream.wait(parts)
        gain = gain_ref[...]
        sums = [jnp.zeros((1, width), F32)] * 3
        for start in range(0, rows, span):
            lines = slice(start, start + span)
            grad = total[lines]
            hat, scale = norm_stats(value_in[lines, :])
            full = dy_in[lines, :].astype(F32) + norm_back(hat, scale, grad * gain)
            grad_ref[lines, :] = full
            low = full.astype(BF16)
            branch[lines, :] = low
            for index, value in enumerate((low.astype(F32), grad * hat, grad)):
                sums[index] = sums[index] + jnp.sum(value, axis=0, keepdims=True)
        gbias_ref[...], ggain_ref[...], gshift_ref[...] = sums
        stream.wait(parts + 1)
        dmix_ref[...] = dot_nt(branch[...], out_weight[...]).astype(BF16)
        for side in range(2):
            columns = slice(side * (width // 2), (side + 1) * (width // 2))
            value = dot_nn(turned_in[...], branch[:, columns]).astype(BF16)
            own_ref[side] = value[:mid]
            sib_ref[side] = value[mid:]

    grads = ((2, mid, width // 2), BF16, whole((2, mid, width // 2)))
    vector = ((1, width), F32, whole((1, width)))
    full = whole((rows, width))
    return call(
        kernel,
        (1,),
        [item for place in places for item in place.inputs()]
        + out_weights.inputs()
        + [(dus, ANY), (after_value, ANY), (dy, ANY), param(small, number, width), (turned, ANY)],
        [((rows, width), F32, full), ((rows, width), BF16, full), grads, grads] + [vector] * 3,
        after=after,
        scratch=[
            pltpu.VMEM((rows, hidden), BF16),
            pltpu.VMEM((width, hidden), BF16),
            pltpu.VMEM((rows, width), F32),
            pltpu.VMEM((rows, width), BF16),
            pltpu.VMEM((width, rows), BF16),
            pltpu.VMEM((width, width), BF16),
            pltpu.VMEM((rows, width), BF16),
            pltpu.SemaphoreType.DMA((parts, most)),
            out_weights.sems(),
            pltpu.SemaphoreType.DMA((parts + 3,)),
        ],
        cost=cost(2 * rows * width * (hidden + 2 * width), 30 * rows * width),
        name="middle",
    )


def attend_back_kernel(
    ends,
    q_ref,
    k_ref,
    v_ref,
    o_ref,
    do_ref,
    lse_ref,
    dq_ref,
    dk_ref,
    dv_ref,
    gq_ref,
    gv_ref,
    allow,
    total,
):
    rows = q_ref.shape[0]
    span = min(256, rows)

    @pl.when(pl.program_id(0) == 0)
    def _():
        for start in range(0, rows, span):
            query = lax.broadcasted_iota(jnp.int32, (1, rows - start), 1) + start
            first = first_of_row(ends, query)
            key = lax.broadcasted_iota(jnp.int32, (span, rows - start), 0) + start
            allow[start : start + span, start:] = jnp.where(
                (key <= query) & (key >= first), 0.0, MASKED
            )

    lane = lax.broadcasted_iota(jnp.int32, (1, LANES), 1)
    low_lane = lane < HD
    one = low_lane.astype(BF16)
    masks = (one, 1 - one)
    product = (o_ref[...].astype(F32) * do_ref[...].astype(F32)).T
    inner = (
        jnp.sum(product[:HD], axis=0, keepdims=True),
        jnp.sum(product[HD:], axis=0, keepdims=True),
    )
    for start in range(0, rows, span):
        stop = start + span
        grads = []
        for head in range(2):
            keys = k_ref[start:stop, :] * masks[head]
            vals = v_ref[start:stop, :] * masks[head]
            scores = dot_nt(keys, q_ref[start:, :]) + allow[start:stop, start:]
            probs = jnp.exp(scores - lse_ref[0, head : head + 1, start:])
            grad_probs = dot_nt(vals, do_ref[start:, :])
            grad_scores = (probs * (grad_probs - inner[head][:, start:])).astype(BF16)
            grad_vals = dot_nn(probs.astype(BF16), do_ref[start:, :])
            grad_keys = dot_nn(grad_scores, q_ref[start:, :])
            grads.append((grad_keys, grad_vals))
            update = dot_tn(grad_scores, keys)
            if start == 0 and head == 0:
                total[...] = update
            else:
                total[start:, :] += update
        dk_ref[start:stop, :] = jnp.where(low_lane, grads[0][0], grads[1][0]).astype(BF16)
        dv_ref[start:stop, :] = jnp.where(low_lane, grads[0][1], grads[1][1]).astype(BF16)
    grad_query = (total[...] * HD ** (-0.5)).astype(BF16)
    dq_ref[...] = grad_query
    gq_ref[...] = jnp.sum(grad_query.astype(F32), axis=0, keepdims=True)
    gv_ref[...] = jnp.sum(dv_ref[...].astype(F32), axis=0, keepdims=True)


def run_attend_back(ends, qkv, mixed, dmix, lse, first, count, after=()):
    rows, width = mixed.shape
    pairs = width // LANES
    column = lambda shift: pl.BlockSpec((rows, LANES), lambda i: (0, i + shift))
    return call(
        attend_back_kernel,
        (count,),
        [(ends, SMEM)]
        + [(qkv, column(first + part * pairs)) for part in range(3)]
        + [
            (mixed, column(first)),
            (dmix, column(first)),
            (lse, pl.BlockSpec((1, 2, rows), lambda i: (i + first, 0, 0))),
        ],
        [((rows, LANES * count), BF16, column(0))] * 3
        + [((1, LANES * count), F32, pl.BlockSpec((1, LANES), lambda i: (0, i)))] * 2,
        after=after,
        scratch=[pltpu.VMEM((rows, rows), F32), pltpu.VMEM((rows, LANES), F32)],
        cost=cost(
            20 * rows * rows * LANES * count, 16 * rows * LANES * count, 2 * rows * rows * count
        ),
        name="attend_back",
    )


def project_kernel(turned_ref, dq_ref, dk_ref, dv_ref, own_ref, sib_ref):
    mid = own_ref.shape[1]
    size = dq_ref.shape[1]
    left = jnp.concatenate([dq_ref[...], dk_ref[:, : size // 2]], axis=1)
    right = jnp.concatenate([dk_ref[:, size // 2 :], dv_ref[...]], axis=1)
    for side, columns in enumerate((left, right)):
        own_ref[side] = dot_nn(turned_ref[:mid], columns).astype(BF16)
        sib_ref[side] = dot_nn(turned_ref[mid:], columns).astype(BF16)


def run_project(turned, dq, dk, dv, after=()):
    width, rows = turned.shape
    size = dq.shape[1]
    mid = width // 2
    grad = ((2, mid, 3 * size // 2), BF16, whole((2, mid, 3 * size // 2)))
    return call(
        project_kernel,
        (1,),
        [(turned, whole((width, rows)))] + [(value, whole((rows, size))) for value in (dq, dk, dv)],
        [grad, grad],
        after=after,
        cost=cost(6 * rows * width * size, 14 * rows * size),
        name="project",
    )


def run_input(weights, grads, x, grad_after, small, number, after=()):
    rows, width = x.shape
    span = 256
    size = grads[0][0].shape[1]
    flat = [value for group in grads for value in group]
    count = len(flat)

    def kernel(*refs):
        held, weight, x_in, grad_in, sems, own_sems = refs[-6:]
        pieces = refs
        refs = weights.rest(refs)
        grad_refs = refs[:count]
        x_ref, grad_ref, gain_ref, out_ref, ggain_ref, gshift_ref = refs[count : count + 6]
        stream = Stream()
        begins = []
        for index in range(count):
            group, part = divmod(index, 3)
            begin = part * width + group * size
            begins.append(begin)
            columns = slice(begin, begin + size)
            copies, _ = weights.at(begin).copies(
                pieces,
                size,
                lambda at, lines, columns=columns: weight.at[pl.ds(at, lines), columns],
                sems.at[index],
            )
            copies.append(
                pltpu.make_async_copy(grad_refs[index], held.at[index], own_sems.at[index])
            )
            stream.add(copies)
        stream.add(
            [
                pltpu.make_async_copy(x_ref, x_in, own_sems.at[count]),
                pltpu.make_async_copy(grad_ref, grad_in, own_sems.at[count + 1]),
            ]
        )
        stream.start()
        total = None
        for index in range(count):
            stream.wait(index)
            columns = slice(begins[index], begins[index] + size)
            value = dot_nt(held[index], weight[:, columns])
            total = value if total is None else total + value
        stream.wait(count)
        gain = gain_ref[...]
        sums = [jnp.zeros((1, width), F32)] * 2
        for start in range(0, rows, span):
            lines = slice(start, start + span)
            grad = total[lines]
            hat, scale = norm_stats(x_in[lines, :].astype(F32))
            out_ref[lines, :] = grad_in[lines, :] + norm_back(hat, scale, grad * gain)
            for index, value in enumerate((grad * hat, grad)):
                sums[index] = sums[index] + jnp.sum(value, axis=0, keepdims=True)
        ggain_ref[...], gshift_ref[...] = sums

    vector = ((1, width), F32, whole((1, width)))
    return call(
        kernel,
        (1,),
        weights.inputs()
        + [(value, ANY) for value in flat]
        + [(x, ANY), (grad_after, ANY), param(small, number, width)],
        [((rows, width), F32, whole((rows, width))), vector, vector],
        after=after,
        scratch=[
            pltpu.VMEM((count, rows, size), BF16),
            pltpu.VMEM((width, 3 * width), BF16),
            pltpu.VMEM((rows, width), BF16),
            pltpu.VMEM((rows, width), F32),
            pltpu.SemaphoreType.DMA((count, len(weights.plan))),
            pltpu.SemaphoreType.DMA((count + 2,)),
        ],
        cost=cost(6 * rows * width * width, 22 * rows * width),
        name="grad_input",
    )


def adamw(weight, first, second, grad, rate, decay):
    first_new = beta_one * first + (1.0 - beta_one) * grad
    second_new = beta_two * second + (1.0 - beta_two) * grad * grad
    first_hat = first_new / (1.0 - beta_one**STEP)
    second_hat = second_new / (1.0 - beta_two**STEP)
    weight_new = weight - rate * (first_hat / (jnp.sqrt(second_hat) + adam_eps) + decay * weight)
    return (weight_new, first_new, second_new)


def run_adam(core, state, groups, span, places, pick, earlier, after=()):
    half = groups[0][0].shape[1]
    count = len(places)
    table = jnp.array(places, jnp.int32)
    place = pl.BlockSpec((half, span), lambda p, h, c, t: (jnp.bitwise_xor(h, c[0]), t[p]))
    flat = [value for group in groups for value in group]

    def kernel(core_ref, table_ref, w_ref, m_ref, v_ref, *refs):
        w_out, m_out, v_out, grad_ref = refs[-4:]
        for side in range(2):
            mine = refs[side : 2 * len(groups) : 2]
            for block in range(count):

                @pl.when((pl.program_id(1) == side) & (pl.program_id(0) == block))
                def _(mine=mine, block=block):
                    start = 0
                    for value in pick(block, mine):
                        grad_ref[:, start : start + value.shape[1]] = value
                        start += value.shape[1]

        w_out[...], m_out[...], v_out[...] = adamw(
            w_ref[...], m_ref[...], v_ref[...], grad_ref[...].astype(F32), 0.05, 0.1
        )

    moved = 2 * half * count * span
    return call(
        kernel,
        (count, 2),
        [(value, place) for value in state] + [(value, whole(value.shape)) for value in flat],
        [(state[0].shape, F32, place)] * 3,
        after=after,
        reuse=[] if earlier is None else [(value, n) for n, value in enumerate(earlier)],
        prefetch=(core, table),
        scratch=[pltpu.VMEM((half, span), BF16)],
        cost=cost(20 * moved, 26 * moved),
        name="adam",
    )


def run_side(core, jobs, after=(), steps=4):
    counts = [(len(job[0]), len(job[1])) for job in jobs]
    total_in = sum(count[0] for count in counts)

    def kernel(core_ref, *refs):
        ins = refs[:total_in]
        outs = refs[total_in:]
        for job, (have, give) in zip(jobs, counts):
            more = (core_ref,) if "places" in job[2].__code__.co_varnames else ()
            job[2](ins[:have], outs[:give], *more)
            ins = ins[have:]
            outs = outs[give:]

    def spec(block, index):
        return pl.BlockSpec(block, lambda i, c: index(i, c))

    moved = sum(array.size * 2 for job in jobs for array, _, _ in job[0])
    results = call(
        kernel,
        (steps,),
        [(array, spec(block, index)) for job in jobs for array, block, index in job[0]],
        [(shape, dtype, spec(block, index)) for job in jobs for shape, dtype, block, index in job[1]],
        after=after,
        prefetch=(core,),
        cost=cost(0, 2 * moved),
        name="side",
    )
    split = []
    for _, give in counts:
        split.append(results[:give])
        results = results[give:]
    return split


def job_cast(rows, columns, by_core, steps):
    span = rows // steps
    total = sum(size for _, _, size in columns)
    ins = []
    for state, number, size in columns:
        index = lambda i, c, number=number: (c[0] * steps * by_core + i, number)
        ins.append((state, (span, size), index))
    outs = [((rows, total), BF16, (span, total), lambda i, c: (i, 0))]

    def run(have, give):
        start = 0
        for ref, (_, _, size) in zip(have, columns):
            give[0][:, start : start + size] = ref[...].astype(BF16)
            start += size

    return ins, outs, run


def job_join(pairs, steps):
    blocks, rows, size = pairs[0][0].shape[1:]
    span = rows // steps
    four = lambda i, c: (0, 0, i, 0)
    count = 2 * len(pairs)
    ins = [(value, (2, blocks, span, size), four) for pair in pairs for value in pair]
    outs = [((blocks, count, rows, size), BF16, (blocks, count, span, size), four)]

    def run(have, give):
        for number in range(len(pairs)):
            left, right = have[2 * number : 2 * number + 2]
            for side in range(2):
                for block in range(blocks):
                    give[0][block, 2 * number + side] = left[side, block] + right[side, block]

    return ins, outs, run


def job_copy(value, first, rows):
    size = value.shape[1]
    ins = [(value, value.shape, lambda i, c: (0, 0))]
    outs = [((rows, size), value.dtype, (rows, size), lambda i, c: (0, 0))]

    def run(have, give):
        give[0][...] = have[0][first : first + rows, :]

    return ins, outs, run


def job_add(left, right, steps):
    at = left.ndim - 2
    if left.shape[at] == 1:
        same = lambda i, c: (0,) * left.ndim

        def run_whole(have, give):
            give[0][...] = have[0][...] + have[1][...]

        return (
            [(left, left.shape, same), (right, right.shape, same)],
            [(left.shape, left.dtype, left.shape, same)],
            run_whole,
        )
    block = tuple(size // steps if axis == at else size for axis, size in enumerate(left.shape))
    index = lambda i, c: (0,) * at + (i, 0)

    def run(have, give):
        give[0][...] = have[0][...] + have[1][...]

    return [(left, block, index), (right, block, index)], [(left.shape, left.dtype, block, index)], run


def job_pick(own, received, steps):
    count, rows, size = own.shape
    block = (count, rows // steps, size)
    index = lambda i, c: (0, i, 0)

    def run(have, give, places):
        give[0][...] = jnp.where(places[2] == 1, have[0][...], have[1][...])

    return [(own, block, index), (received, block, index)], [(own.shape, own.dtype, block, index)], run


def job_sum(groups, keep, send, steps):
    _, blocks, rows, _ = groups[0][0].shape
    span = rows // steps
    total = sum(own.shape[3] for own, _ in groups)
    four = lambda i, c: (0, 0, i, 0)
    three = lambda i, c: (0, i, 0)
    ins = []
    for own, received in groups:
        size = own.shape[3]
        ins.append((own, (2, blocks, span, size), four))
        if len(received) == 1:
            ins.append((received[0], (2, blocks, span, size), four))
        else:
            ins += [(value, (blocks, span, size), three) for value in received]
    kept = len(keep[0])
    outs = [((2, kept, rows, total), BF16, (2, kept, span, total), four)]
    if len(send) == 1:
        gone = len(send[0])
        outs.append(((2, gone, rows, total), BF16, (2, gone, span, total), four))
    else:
        for side in range(2):
            if send[side]:
                gone = len(send[side])
                outs.append(((gone, rows, total), BF16, (gone, span, total), three))

    def run(have, give):
        start = 0
        for own, received in groups:
            size = own.shape[3]
            columns = slice(start, start + size)
            start += size
            for side in range(2):
                for block in range(blocks):
                    other = have[1][side, block] if len(received) == 1 else have[1 + side][block]
                    value = have[0][side, block] + other
                    if block in keep[side]:
                        give[0][side, keep[side].index(block), :, columns] = value
                    elif len(send) == 1:
                        give[1][side, send[0].index(block), :, columns] = value
                    else:
                        give[1 + side][send[side].index(block), :, columns] = value
            have = have[1 + len(received) :]

    return ins, outs, run


def job_params(rows, shards, small_size):
    ins = []
    for array, row in rows:
        if array.shape[0] == 1:
            ins.append((array, array.shape, lambda i, c: (0, 0)))
        else:
            size = array.shape[1]
            ins.append((array, (16, size), lambda i, c, row=row: (row // 16, 0)))
    shape = (1, shards * small_size)
    outs = [(shape, F32, shape, lambda i, c: (0, 0))]

    def run(have, give, places):
        for number, ref in enumerate(have):
            owner = jnp.bitwise_xor(places[1], number)
            start = pl.multiple_of(owner * small_size, LANES)
            value = ref[0:1, :small_size].astype(BF16).astype(F32)
            give[0][:, pl.ds(start, small_size)] = value

    return ins, outs, run


def job_lay(values):
    total = sum(value.shape[1] for value in values)
    same = lambda i, c: (0, 0)
    ins = [(value, value.shape, same) for value in values]

    def run(have, give):
        start = 0
        for ref in have:
            give[0][:, start : start + ref.shape[1]] = ref[...]
            start += ref.shape[1]

    return ins, [((1, total), F32, (1, total), same)], run


class Links:
    def __init__(self, sizes, shard_rows):
        self.replicas, self.shards = sizes
        dp = lax.axis_index("dp")
        self.shard = lax.axis_index("shard")
        self.core = lax.rem(dp, 2)
        place = dp // 2
        self.inner = (place > 0) & (place < sizes[0] // 2 - 1)
        self.core_arr = jnp.stack([self.core, self.shard, self.inner]).astype(jnp.int32)
        self.rows = shard_rows
        self.half = shard_rows // 2
        self.fast = sizes == (8, 4)

    def swap(self, value):
        return self.across_dp(value, 1)

    def across_dp(self, value, bit):
        return lax.ppermute(value, "dp", [(d, d ^ bit) for d in range(self.replicas)])

    def along_dp(self, value, step):
        hops = ([(0, 1), (3, 2)], [(1, 2), (2, 1)], [(1, 0), (2, 3)])[step]
        pairs = [(2 * a + core, 2 * b + core) for a, b in hops for core in range(2)]
        return lax.ppermute(value, "dp", pairs)

    def across_shard(self, value, bit):
        return lax.ppermute(value, "shard", [(s, s ^ bit) for s in range(self.shards)])

    def turned_offsets(self, around):
        blocks = jnp.arange(2 * self.shards, dtype=jnp.int32)
        owner = blocks // 2
        if around:
            owner = jnp.bitwise_xor(owner, self.shard)
        away = jnp.bitwise_xor(lax.rem(blocks, 2), self.core)
        return away * (self.shards * self.half) + owner * self.half

    def gather(self, half_rows):
        return lax.all_gather(half_rows, "shard", axis=0, tiled=True)

    def gathered(self, mine, behind=None):
        if behind is not None:
            mine, _ = lax.optimization_barrier((mine, behind))
        first = jnp.arange(self.shards, dtype=jnp.int32) * self.rows
        offs = jnp.concatenate([first + self.core * self.half, first + (1 - self.core) * self.half])
        stride = mine.shape[0] // self.shards
        plan = tuple((0, t * stride, self.half, t) for t in range(self.shards)) + tuple(
            (1, t * stride, self.half, self.shards + t) for t in range(self.shards)
        )
        return Weights((mine, self.swap(mine)), plan, offs.astype(jnp.int32))

    def over_dp(self, values):
        groups = [[d for d in range(self.replicas) if d % 2 == c] for c in range(2)]
        return lax.psum(values, "dp", axis_index_groups=groups)


class Gather:
    def __init__(self, links, half_rows, own):
        self.links = links
        self.own = own
        self.by_x = links.across_shard(half_rows, 1)
        self.by_y = links.across_shard(half_rows, 2)

    def jobs(self):
        part = self.links.half // 2
        rest = self.by_x.shape[0] - part
        return [job_copy(self.by_y, 0, part), job_copy(self.by_x, part, rest)]

    def forward(self, results):
        links = self.links
        self.far = (
            links.across_shard(results[0], 1),
            links.across_shard(results[1], 2),
        )
        self.near = (links.swap(self.by_x), links.swap(self.by_y))

    def weights(self):
        links = self.links
        half, rows = links.half, links.rows
        part = half // 2
        far = tuple(links.swap(value) for value in self.far)
        pieces = (self.own, self.by_x, self.by_y, *self.near, *self.far, *far)
        plan = ((0, 0, rows, 0),)
        plan += tuple((n, 0, half, n) for n in range(1, 5))
        plan += tuple((n, 0, part, n) for n in range(5, 9))
        at = lambda bits: jnp.bitwise_xor(links.shard, bits) * rows
        mine = links.core * half
        other = (1 - links.core) * half
        offs = [at(0), at(1) + mine, at(2) + mine, at(1) + other, at(2) + other]
        offs += [at(3) + mine, at(3) + mine + part, at(3) + other, at(3) + other + part]
        return Weights(pieces, plan, jnp.stack(offs).astype(jnp.int32))


class Reduce:
    def __init__(self, links, line):
        self.links = links
        self.line = line
        self.stage = 0
        self.groups = []

    def add(self, own, sib):
        shape = (2, self.links.shards, self.links.half, own.shape[2])
        self.groups.append((own.reshape(shape), (self.links.swap(sib).reshape(shape),)))
        return self

    def job(self, steps):
        if self.stage > 2:
            own, received = self.groups[0]
            if self.line and self.stage == 5:
                return job_pick(own, received, steps)
            return job_add(own, received, steps)
        blocks = self.groups[0][0].shape[1]
        odd = lambda block: block % 2 == 1
        late = lambda block: block >= blocks // 2
        goes = [odd, late]
        if blocks == 2:
            goes = [odd, odd]
        if blocks == 1:
            goes = [lambda block: False] * 2
        keep = [[block for block in range(blocks) if not go(block)] for go in goes]
        send = [[block for block in range(blocks) if go(block)] for go in goes]
        return job_sum(self.groups, keep, send, steps)

    def advance(self, results):
        links = self.links
        own = results[0]
        stage = self.stage
        self.stage += 1
        if stage < 2:
            bits = (1, 2) if stage == 0 else (2, 1)
            received = tuple(
                links.across_shard(value, bit) for value, bit in zip(results[1:], bits)
            )
            self.groups = [(own, received)]
            return
        if stage == 2:
            own = own.reshape(2, own.shape[2], own.shape[3])
        if self.line and stage < 5:
            self.groups = [(own, links.along_dp(own, stage - 2))]
        elif not self.line and stage < 4:
            self.groups = [(own, links.across_dp(own, 2 * (stage - 1)))]
        else:
            self.grads = (own, links.swap(own))


class Wide:
    def __init__(self, links, joined):
        self.links = links
        self.stage = 0
        count, half, size = joined.shape[1:]
        flat = joined.reshape(links.shards * count * half, size)
        mine = lax.psum_scatter(flat, "shard", scatter_dimension=0, tiled=True)
        self.own = mine.reshape(count, half, size)

    def send(self):
        before = self.own
        self.received = self.links.along_dp(before, 0)
        return before

    def job(self, steps):
        if self.stage == 2:
            return job_pick(self.own, self.received, steps)
        return job_add(self.own, self.received, steps)

    def advance(self, results):
        self.own = results[0]
        self.stage += 1
        if self.stage < 3:
            self.received = self.links.along_dp(self.own, self.stage)
        else:
            self.grads = (self.own, self.links.swap(self.own))


class Side:
    def __init__(self, links):
        self.links = links
        self.order = ()

    def jobs(self, jobs, steps=1, after=()):
        results = run_side(self.links.core_arr, jobs, after=(*self.order, *after), steps=steps)
        self.order = (results[0][0],)
        return [result[0] for result in results]

    def reduce(self, reduces, jobs=(), steps=2):
        work = [item.job(steps) for item in reduces] + list(jobs)
        results = run_side(self.links.core_arr, work, after=self.order, steps=steps)
        for item, result in zip(reduces, results):
            item.advance(result)
        self.order = (results[0][0],)
        return [result[0] for result in results[len(reduces) :]]

    def then(self, results):
        self.order = (results[0],)
        return results


def small_parts(small, width, hidden):
    bounds = [width] * 3 + [hidden] + [width] * 5
    parts = []
    start = 0
    for size in bounds:
        parts.append(small[:, start : start + size])
        start += size
    return parts


def body(sizes, *args):
    tokens, cotangent, lengths = args[:3]
    attn_state, mlp_state, small_state = args[3:6], args[6:9], args[9:12]
    rows, width = tokens.shape
    links = Links(sizes, attn_state[0].shape[0])
    half = links.half
    hidden = mlp_state[0].shape[1] // 2
    pairs = width // LANES
    pad = 16
    core_arr = links.core_arr
    by_owner = links.turned_offsets(False)
    around = links.turned_offsets(True) if links.fast else by_owner
    side = Side(links)

    ends = jnp.cumsum(lengths[0], dtype=jnp.int32)
    small_own = small_state[0][None]
    small_size = small_own.shape[1]
    (
        BIAS_Q,
        BIAS_V,
        BIAS_O,
        BIAS_UP,
    ) = range(4)
    BIAS_DN, GAIN_ONE, SHIFT_ONE, GAIN_TWO, SHIFT_TWO = range(
        BIAS_UP + hidden // width, BIAS_UP + hidden // width + 5
    )

    def first_job():
        ins = [
            (attn_state[0], (half, 3 * width), lambda i, c: (c[0], 0)),
            (small_own, (1, small_size), lambda i, c: (0, 0)),
        ]
        outs = [((half + pad, 3 * width), BF16, (half + pad, 3 * width), lambda i, c: (0, 0))]

        def job(have, give):
            give[0][:half] = have[0][...].astype(BF16)
            row = have[1][...].astype(BF16)
            give[0][half:, :small_size] = jnp.broadcast_to(row, (pad, small_size))

        return ins, outs, job

    blocks = 4
    block = hidden // blocks
    columns = [(attn_state[0], 3, width)]
    columns += [(mlp_state[0], number, block) for number in (0, 1, blocks, blocks + 1)]
    more_columns = [
        (mlp_state[0], number, block) for number in (2, 3, blocks + 2, blocks + 3)
    ]
    (first_half,) = side.jobs([first_job()])
    if links.fast:
        qkv_gather = Gather(links, first_half, None)
    else:
        qkv_weights = links.gathered(links.gather(first_half))
    dy, dyt, grad_bias_dn = side.then(run_cot(half, by_owner, ends, cotangent, after=side.order))
    if links.fast:
        (qkv_gather.own,) = side.jobs(
            [job_cast(links.rows, [(attn_state[0], 0, 3 * width)], 0, 4)], steps=4
        )
        qkv_gather.forward(side.jobs(qkv_gather.jobs()))
    (out_half,) = side.jobs([job_cast(half, columns, 1, 4)], steps=4)
    wide = links.gather(out_half)
    (feed_half,) = side.jobs([job_cast(half, more_columns, 1, 4)], steps=4)
    more_wide = links.gather(feed_half)
    if links.fast:
        qkv_weights = qkv_gather.weights()
        rows_of = [
            (small_own, 0),
            (qkv_gather.by_x, half),
            (qkv_gather.by_y, half),
            (qkv_gather.far[1], half // 2),
        ]
        (small,) = side.jobs([job_params(rows_of, links.shards, small_size)])
    else:
        small = qkv_weights.pieces[0].reshape(links.shards, half + pad, 3 * width)
        small = small[:, half, :small_size].astype(F32).reshape(1, -1)

    qkv, turned_one = side.then(
        run_qkv(
            half,
            qkv_weights,
            around,
            tokens,
            small,
            (BIAS_Q, BIAS_V, GAIN_ONE, SHIFT_ONE),
            after=side.order,
        )
    )
    attended = side.then(run_attend(ends, qkv, 0, pairs // 2, after=side.order))
    wide = links.gathered(wide, attended[1])
    mixed, lse = side.then(
        run_attend(ends, qkv, pairs // 2, pairs // 2, attended, after=(wide.pieces[0],))
    )
    after, low_two, turned_two, turned_mixed = side.then(
        run_after(
            half,
            wide,
            (around, by_owner),
            mixed,
            tokens,
            small,
            (BIAS_O, GAIN_TWO, SHIFT_TWO),
            after=side.order,
        )
    )

    passed, grad_bias_up, mlp_grads = [None], [], []
    feeds = [(0, 2 * block, wide.at(width), wide.at(width + 2 * block))]

    def feed(number):
        start, size, up_weights, down_weights = feeds[number]
        act, du, own, sib, gbias = side.then(
            run_feed(
                up_weights,
                down_weights,
                low_two,
                turned_two,
                dy,
                dyt,
                small,
                BIAS_UP * width + start,
                start,
                size,
                passed[-1],
                after=side.order,
            )
        )
        side.order = (own,)
        passed.append((act, du))
        grad_bias_up.append(gbias)
        shape = (2, links.shards, half, size)
        mlp_grads.append((own.reshape(shape), links.swap(sib).reshape(shape)))

    def join(pairs):
        return side.jobs([job_join(pairs, half // 16)], steps=half // 16)[0]

    feed(0)
    more_wide = links.gathered(more_wide, grad_bias_up[0])
    feeds += [
        (2 * block, block, more_wide, more_wide.at(2 * block)),
        (3 * block, block, more_wide.at(block), more_wide.at(3 * block)),
    ]
    feed(1)
    reduces = [Wide(links, join([mlp_grads[0]]))]
    feed(2)
    (
        grad_after,
        dmix,
        own_out,
        sib_out,
        grad_bias_o,
        grad_gain_two,
        grad_shift_two,
    ) = side.then(
        run_middle(
            [(item[1], item[2]) for item in feeds],
            wide,
            passed[-1][1],
            after,
            dy,
            small,
            GAIN_TWO,
            turned_mixed,
            after=side.order,
        )
    )
    reduces.append(Wide(links, join([mlp_grads[1], mlp_grads[2]])))
    if links.fast:
        reduces.append(Reduce(links, True).add(own_out, sib_out))
    else:
        reduces.append((own_out, sib_out))
    grads, biases = [], []

    def attend_back(first):
        dq, dk, dv, gq, gv = side.then(
            run_attend_back(ends, qkv, mixed, dmix, lse, first, pairs // 2, after=side.order)
        )
        grads.append((dq, dk, dv))
        biases.append((gq, gv))

    def project(group):
        own, sib = side.then(run_project(turned_one, *grads[group], after=side.order))
        if not links.fast:
            reduces.append((own, sib))
        elif group == 0:
            reduces[2].add(own, sib)
        else:
            reduces.append(Reduce(links, False).add(own, sib))

    def reduce(numbers, jobs=()):
        if links.fast:
            return side.reduce([reduces[number] for number in numbers], jobs)
        return side.jobs(jobs) if jobs else None

    attend_back(0)
    if links.fast:
        side.order += (reduces[0].send(),)
    project(0)
    attend_back(pairs // 2)
    reduce([0, 2])
    if links.fast:
        side.order += (reduces[1].send(),)
    project(1)
    reduce([2])
    grad_input, grad_gain_one, grad_shift_one = side.then(
        run_input(
            qkv_weights, grads, tokens, grad_after, small, GAIN_ONE, after=side.order
        )
    )
    small_grads = [biases[0][0], biases[1][0], biases[0][1], biases[1][1], grad_bias_o]
    small_grads += grad_bias_up
    small_grads += [grad_bias_dn, grad_gain_one, grad_shift_one, grad_gain_two, grad_shift_two]
    (grad_small,) = reduce([0, 1, 2, 3], [job_lay(small_grads)])
    output = run_output(
        [(item[1], item[3]) for item in feeds],
        passed[-1][0],
        after,
        small,
        BIAS_DN,
        after=side.order,
    )
    side.then([output])

    out_block = width // 2
    pick_mlp = (
        lambda number, arrays: [arrays[0][number]],
        lambda number, arrays: [arrays[0][number], arrays[0][2 + number]],
    )

    def pick_heads(number, arrays):
        skip = arrays[0].shape[2] - 3 * out_block // 2
        left, right = arrays[0][0], arrays[0][1]
        split = skip + out_block // 2
        return (
            [left[:, skip : skip + out_block]],
            [left[:, skip + out_block :], right[:, skip:split]],
            [right[:, split:]],
            [left[:, :skip]],
            [right[:, :skip]],
        )[number]

    def adam_attn(group, earlier):
        places = [0, 2, 4, 6, 7] if group == 0 else [1, 3, 5]
        return side.then(
            run_adam(
                core_arr,
                attn_state,
                [reduces[2 + group].grads],
                out_block,
                places,
                pick_heads,
                earlier,
                after=side.order,
            )
        )

    def adam_mlp(group, earlier):
        return side.then(
            run_adam(
                core_arr,
                mlp_state,
                [reduces[group].grads],
                2 * block,
                [group, blocks // 2 + group],
                pick_mlp[group],
                earlier,
                after=side.order,
            )
        )

    if links.fast:

        def step(numbers, move):
            (total,) = reduce(numbers, [job_add(grad_small, moved, 2)])
            return total, move(total) if move else None

        across = lambda bit: functools.partial(links.across_dp, bit=bit)
        reduce([0, 1, 2, 3])
        moved = links.across_shard(grad_small, 1)
        mlp_new = adam_mlp(0, None)
        grad_small, moved = step([1, 2, 3], functools.partial(links.across_shard, bit=2))
        mlp_new = adam_mlp(1, mlp_new)
        grad_small, moved = step([2, 3], links.swap)
        attn_new = adam_attn(0, None)
        grad_small, moved = step([3], across(2))
        grad_small, moved = step([], across(4))
        attn_new = adam_attn(1, attn_new)
        grad_small, _ = step([], None)
    else:
        blocked = lambda value: value.reshape(2, links.shards, half, value.shape[2])
        for number in range(2, len(reduces)):
            own, sib = reduces[number]
            pair = (blocked(own), blocked(links.swap(sib)))
            reduces[number] = Wide(links, join([pair]))
        for item in reduces:
            item.own = links.over_dp(item.own)
            item.grads = (item.own, links.swap(item.own))
        mine = jnp.concatenate([reduces[2].own, reduces[3].own], axis=2)
        reduces[2].grads = (mine, links.swap(mine))
        reduces[3] = reduces.pop()
        grad_small = lax.psum(grad_small, ("dp", "shard"))
        mlp_new = adam_mlp(1, adam_mlp(0, None))
        attn_new = adam_attn(1, adam_attn(0, None))
    grad_small = lax.dynamic_slice_in_dim(grad_small, links.shard * small_size, small_size, 1)[0]
    small_new = adamw(*small_state, grad_small, 0.4, 0.0)
    return (output, grad_input, *attn_new, *mlp_new, *small_new)


def solution(mesh):
    tokens = P(("dp", "shard"), None)
    state = P("shard", None)
    vector = P("shard")
    return jax.shard_map(
        functools.partial(body, (mesh.shape["dp"], mesh.shape["shard"])),
        mesh=mesh,
        in_specs=(tokens,) * 3 + (state,) * 6 + (vector,) * 3,
        out_specs=(tokens,) * 2 + (state,) * 6 + (vector,) * 3,
        check_vma=False,
    )
```

```python
import functools

import jax
import jax.numpy as jnp
from jax import lax
from jax.experimental import pallas as pl
from jax.experimental.pallas import tpu as pltpu
from jax.sharding import PartitionSpec as P

HD = 64
STEP = 10
LANES = 128
MASKED = -1e30
SAFE = 60.0
GELU_IN = 0.7978845608028654
GELU_CUBE = 0.044715

beta_one = 0.9
beta_two = 0.95
adam_eps = 1e-08
norm_eps = 1e-05

F32 = jnp.float32
BF16 = jnp.bfloat16
MIB = 1024 * 1024
VMEM_MIB = 64

ANY = pl.BlockSpec(memory_space=pl.ANY)
SMEM = pl.BlockSpec(memory_space=pltpu.SMEM)


def dot_nn(left, right):
    return lax.dot_general(left, right, (((1,), (0,)), ((), ())), preferred_element_type=F32)


def dot_nt(left, right):
    return lax.dot_general(left, right, (((1,), (1,)), ((), ())), preferred_element_type=F32)


def dot_tn(left, right):
    return lax.dot_general(left, right, (((0,), (0,)), ((), ())), preferred_element_type=F32)


def whole(shape):
    return pl.BlockSpec(shape, lambda *_: (0,) * len(shape))


def call(kernel, grid, ins, outs, after=(), reuse=(), prefetch=(), scratch=(), cost=None, name=None):
    known = len(prefetch) + len(ins)
    idle = [*after, *(array for array, _ in reuse)]

    def run(*refs):
        kernel(*refs[:known], *refs[known + len(idle) :])

    def placed(array, spec):
        if spec is SMEM:
            return array
        return pltpu.with_memory_space_constraint(array, pltpu.HBM)

    return pl.pallas_call(
        run,
        grid_spec=pltpu.PrefetchScalarGridSpec(
            num_scalar_prefetch=len(prefetch),
            grid=grid,
            in_specs=[spec for _, spec in ins] + [ANY] * len(idle),
            out_specs=[spec for _, _, spec in outs],
            scratch_shapes=list(scratch),
        ),
        out_shape=[pltpu.HBM(shape, dtype) for shape, dtype, _ in outs],
        input_output_aliases={
            known + len(after) + number: output for number, (_, output) in enumerate(reuse)
        },
        compiler_params=pltpu.CompilerParams(vmem_limit_bytes=VMEM_MIB * MIB),
        cost_estimate=cost,
        name=name,
    )(*prefetch, *(placed(*item) for item in ins), *(placed(array, ANY) for array in idle))


def param(small, number, width):
    return (small, pl.BlockSpec((1, width), lambda *_: (0, number)))


def cost(flops, moved, exps=0):
    return pl.CostEstimate(flops=int(flops), bytes_accessed=int(moved), transcendentals=int(exps))


def store_turned(turned_ref, toff, block, half, value, columns):
    turned = value.astype(BF16).T
    for part in range(LANES // half):
        offset = pl.multiple_of(toff[block * (LANES // half) + part], half)
        turned_ref[pl.ds(offset, half), columns] = turned[part * half : (part + 1) * half]


def norm_stats(values):
    center = values - jnp.mean(values, axis=-1, keepdims=True)
    spread = jnp.mean(center * center, axis=-1, keepdims=True)
    scale = lax.rsqrt(spread + norm_eps)
    return center * scale, scale


def norm_back(hat, scale, grad_hat):
    mean = jnp.mean(grad_hat, axis=-1, keepdims=True)
    along = jnp.mean(grad_hat * hat, axis=-1, keepdims=True)
    return scale * (grad_hat - mean - hat * along)


def accumulate(ref, value, first):
    @pl.when(first)
    def _():
        ref[...] = value

    @pl.when(jnp.logical_not(first))
    def _():
        ref[...] += value


class Weights:
    def __init__(self, pieces, plan, offs, first=0):
        self.pieces, self.plan, self.offs, self.first = pieces, plan, offs, first

    def at(self, first):
        return Weights(self.pieces, self.plan, self.offs, self.first + first)

    def inputs(self):
        return [(self.offs, SMEM)] + [(piece, ANY) for piece in self.pieces]

    def sems(self):
        return pltpu.SemaphoreType.DMA((len(self.plan),))

    def rest(self, refs):
        return refs[1 + len(self.pieces) :]

    def copies(self, refs, size, target, sems, start=None):
        offs, refs = refs[0], refs[1:]
        columns = slice(self.first, self.first + size)
        if start is not None:
            columns = pl.ds(pl.multiple_of(self.first + start, LANES), size)
        made = []
        for number, (piece, first, rows, index) in enumerate(self.plan):
            offset = pl.multiple_of(offs[index], rows)
            made.append(
                pltpu.make_async_copy(
                    refs[piece].at[pl.ds(first, rows), columns],
                    target(offset, rows),
                    sems.at[number],
                )
            )
        return made, refs[len(self.pieces) :]


def start_all(copies):
    @pl.when(pl.program_id(0) == 0)
    def _():
        for copy in copies:
            copy.start()


def wait_all(copies):
    @pl.when(pl.program_id(0) == 0)
    def _():
        for copy in copies:
            copy.wait()


def cot_kernel(half, toff, ends, cot_ref, dy_ref, turned_ref, bias_ref):
    rows = cot_ref.shape[0]
    place = lax.broadcasted_iota(jnp.int32, (rows, LANES), 0)
    live = (place < ends[ends.shape[0] - 1]).astype(F32)
    for block in range(cot_ref.shape[1] // LANES):
        columns = slice(block * LANES, (block + 1) * LANES)
        value = cot_ref[:, columns].astype(F32) * live
        dy_ref[:, columns] = value.astype(BF16)
        bias_ref[:, columns] = jnp.sum(value, axis=0, keepdims=True)
        store_turned(turned_ref, toff, block, half, value, slice(None))


def run_cot(half, toff, ends, cot, after=()):
    rows, width = cot.shape
    return call(
        functools.partial(cot_kernel, half),
        (1,),
        [(toff, SMEM), (ends, SMEM), (cot, whole(cot.shape))],
        [
            ((rows, width), BF16, whole((rows, width))),
            ((width, rows), BF16, whole((width, rows))),
            ((1, width), F32, whole((1, width))),
        ],
        after=after,
        cost=cost(0, 6 * rows * width),
        name="cotangent",
    )


def run_qkv(half, weights, toff, x, small, numbers, after=()):
    rows, width = x.shape
    span = 256

    def kernel(*refs):
        weight, sems = refs[-2:]
        copies, refs = weights.copies(
            refs, 3 * width, lambda at, size: weight.at[pl.ds(at, size), :], sems
        )
        toff_ref, x_ref, bias_q, bias_v, gain_ref, shift_ref, qkv_ref, turned_ref = refs[:8]
        start_all(copies)
        hat, _ = norm_stats(x_ref[...].astype(F32))
        normed = hat * gain_ref[...] + shift_ref[...]
        for block in range(width // LANES):
            columns = slice(block * LANES, (block + 1) * LANES)
            store_turned(turned_ref, toff_ref, block, half, normed[:, columns], slice(None))
        wait_all(copies)
        low = normed.astype(BF16)
        for part in range(3):
            columns = slice(part * width, (part + 1) * width)
            value = dot_nn(low, weight[:, columns])
            if part == 2:
                value += bias_v[...]
            if part == 0:
                value = (value + bias_q[...]).astype(BF16).astype(F32) * HD ** (-0.5)
            qkv_ref[:, columns] = value.astype(BF16)

    return call(
        kernel,
        (rows // span,),
        weights.inputs()
        + [
            (toff, SMEM),
            (x, pl.BlockSpec((span, width), lambda i: (i, 0))),
        ]
        + [param(small, number, width) for number in numbers],
        [
            ((rows, 3 * width), BF16, pl.BlockSpec((span, 3 * width), lambda i: (i, 0))),
            ((width, rows), BF16, pl.BlockSpec((width, span), lambda i: (0, i))),
        ],
        after=after,
        scratch=[pltpu.VMEM((width, 3 * width), BF16), weights.sems()],
        cost=cost(6 * rows * width * width, 16 * rows * width),
        name="qkv",
    )


def first_of_row(ends, place):
    first = jnp.zeros_like(place)
    for number in range(ends.shape[0]):
        first = jnp.where(place >= ends[number], ends[number], first)
    return first


def attend_kernel(ends, q_ref, k_ref, v_ref, o_ref, lse_ref, allow):
    rows = q_ref.shape[0]
    span = min(256, rows)

    @pl.when(pl.program_id(0) == 0)
    def _():
        for start in range(0, rows, span):
            keys = start + span
            place = lax.broadcasted_iota(jnp.int32, (span, 1), 0) + start
            first = first_of_row(ends, place)
            key = lax.broadcasted_iota(jnp.int32, (span, keys), 1)
            allow[start:keys, :keys] = jnp.where((key <= place) & (key >= first), 0.0, MASKED)

    lane = lax.broadcasted_iota(jnp.int32, (1, LANES), 1)
    low_lane = lane < HD
    one = low_lane.astype(BF16)
    masks = (one, 1 - one)

    same = (lax.broadcasted_iota(jnp.int32, (LANES, LANES), 0) < HD) == (
        lax.broadcasted_iota(jnp.int32, (LANES, LANES), 1) < HD
    )
    same = same.astype(F32).astype(BF16)
    longest = [
        jnp.max(dot_nn(ref[...] * ref[...], same), axis=0, keepdims=True) for ref in (q_ref, k_ref)
    ]
    bounded = jnp.max(longest[0] * longest[1]) < SAFE * SAFE

    def attend(shift):
        mixed = [v_ref[...] * mask + (1 - mask) for mask in masks]
        for start in range(0, rows, span):
            keys = start + span
            sums = []
            tops = []
            for head in range(2):
                query = q_ref[start:keys, :] * masks[head]
                scores = dot_nt(query, k_ref[:keys, :]) + allow[start:keys, :keys]
                if shift:
                    top = jnp.max(scores, axis=1, keepdims=True)
                    tops.append(top)
                    scores = scores - top
                probs = jnp.exp(scores).astype(BF16)
                sums.append(dot_nn(probs, mixed[head][:keys]))
            total = pltpu.roll(jnp.where(low_lane, sums[1], sums[0]), HD, 1)
            out = jnp.where(low_lane, sums[0], sums[1]) / total
            o_ref[start:keys, :] = out.astype(BF16)
            lse = jnp.log(total)
            if shift:
                lse += jnp.where(low_lane, tops[0], tops[1])
            lse = lse.T
            lse_ref[0, 0:1, start:keys] = lse[0:1]
            lse_ref[0, 1:2, start:keys] = lse[HD : HD + 1]

    @pl.when(bounded)
    def _():
        attend(False)

    @pl.when(jnp.logical_not(bounded))
    def _():
        attend(True)


def run_attend(ends, qkv, first, count, earlier=None, after=()):
    rows = qkv.shape[0]
    width = qkv.shape[1] // 3
    pairs = width // LANES
    column = lambda shift: pl.BlockSpec((rows, LANES), lambda i: (0, i + shift))
    return call(
        attend_kernel,
        (count,),
        [(ends, SMEM)] + [(qkv, column(first + part * pairs)) for part in range(3)],
        [
            ((rows, width), BF16, column(first)),
            ((pairs, 2, rows), F32, pl.BlockSpec((1, 2, rows), lambda i: (i + first, 0, 0))),
        ],
        after=after,
        reuse=[] if earlier is None else [(earlier[0], 0), (earlier[1], 1)],
        scratch=[pltpu.VMEM((rows, rows), F32)],
        cost=cost(8 * rows * rows * LANES * count, 8 * rows * LANES * count, 2 * rows * rows * count),
        name="attend",
    )


def run_after(half, weights, toffs, mixed, x, small, numbers, after=()):
    rows, width = x.shape
    span = 256

    def kernel(*refs):
        weight, sems = refs[-2:]
        copies, refs = weights.copies(
            refs, width, lambda at, size: weight.at[pl.ds(at, size), :], sems
        )
        mixed_toff, low_toff, mixed_ref, x_ref, bias_ref, gain_ref, shift_ref = refs[:7]
        after_ref, low_ref, turned_ref, mixed_turned_ref = refs[7:11]
        start_all(copies)
        for block in range(width // LANES):
            columns = slice(block * LANES, (block + 1) * LANES)
            store_turned(mixed_turned_ref, mixed_toff, block, half, mixed_ref[:, columns], slice(None))
        wait_all(copies)
        value = x_ref[...].astype(F32) + dot_nn(mixed_ref[...], weight[...]) + bias_ref[...]
        after_ref[...] = value
        hat, _ = norm_stats(value)
        normed = hat * gain_ref[...] + shift_ref[...]
        low_ref[...] = normed.astype(BF16)
        for block in range(width // LANES):
            columns = slice(block * LANES, (block + 1) * LANES)
            store_turned(turned_ref, low_toff, block, half, normed[:, columns], slice(None))

    by_row = pl.BlockSpec((span, width), lambda i: (i, 0))
    by_column = pl.BlockSpec((width, span), lambda i: (0, i))
    return call(
        kernel,
        (rows // span,),
        weights.inputs()
        + [(toff, SMEM) for toff in toffs]
        + [(mixed, by_row), (x, by_row)]
        + [param(small, number, width) for number in numbers],
        [
            ((rows, width), F32, by_row),
            ((rows, width), BF16, by_row),
            ((width, rows), BF16, by_column),
            ((width, rows), BF16, by_column),
        ],
        after=after,
        scratch=[pltpu.VMEM((width, width), BF16), weights.sems()],
        cost=cost(2 * rows * width * width, 14 * rows * width),
        name="after",
    )


def run_feed(up_weights, down_weights, low, turned, dy, dyt, small, first, begin, block, earlier, after=()):
    rows, width = low.shape
    hidden = earlier[0].shape[1] if earlier is not None else block_total(small, width)
    span = 256
    mid = width // 2
    count = block // span
    by_column = lambda size: pl.BlockSpec((size, span), lambda i: (0, i))
    shifted = pl.BlockSpec((rows, span), lambda i: (0, begin // span + i))
    grad = ((2, mid, block), BF16, pl.BlockSpec((2, mid, span), lambda i: (0, 0, i)))

    def kernel(*refs):
        up, down, up_sems, down_sems = refs[-4:]
        step = pl.program_id(0)

        def copies(number):
            columns = pl.ds(pl.multiple_of(number * span, span), span)
            made, rest = up_weights.copies(
                refs,
                span,
                lambda at, size: up.at[pl.ds(at, size), columns],
                up_sems.at[number],
                number * span,
            )
            more, _ = down_weights.copies(
                rest,
                span,
                lambda at, size: down.at[pl.ds(at, size), columns],
                down_sems.at[number],
                number * span,
            )
            return made + more

        @pl.when(step == 0)
        def _():
            for copy in copies(0):
                copy.start()

        @pl.when(step + 1 < count)
        def _():
            for copy in copies(step + 1):
                copy.start()

        for copy in copies(step):
            copy.wait()
        low_ref, turned_ref, dy_ref, dyt_ref, bias_ref, act_ref, du_ref, own_ref, sib_ref, gbias_ref = (
            down_weights.rest(up_weights.rest(refs))[:10]
        )
        columns = pl.ds(pl.multiple_of(step * span, span), span)
        upper = dot_nn(low_ref[...], up[:, columns]) + bias_ref[...]
        grad_act = dot_nn(dy_ref[...], down[:, columns])
        square = (GELU_IN * GELU_CUBE) * (upper * upper)
        tanh = jnp.tanh(upper * (GELU_IN + square))
        share = 0.5 + 0.5 * tanh
        act = upper * share
        slope = share + act * (1.0 - tanh) * (GELU_IN + 3.0 * square)
        act = act.astype(BF16)
        du = (grad_act * slope).astype(BF16)
        act_ref[...] = act
        du_ref[...] = du
        gbias_ref[...] = jnp.sum(du.astype(F32), axis=0, keepdims=True)
        grad_up = dot_nn(turned_ref[...], du).astype(BF16)
        own_ref[0] = grad_up[:mid]
        sib_ref[0] = grad_up[mid:]
        grad_dn = dot_nn(dyt_ref[...], act).astype(BF16)
        own_ref[1] = grad_dn[:mid]
        sib_ref[1] = grad_dn[mid:]

    return call(
        kernel,
        (count,),
        up_weights.inputs()
        + down_weights.inputs()
        + [
            (low, whole((rows, width))),
            (turned, whole((width, rows))),
            (dy, whole((rows, width))),
            (dyt, whole((width, rows))),
            (small, pl.BlockSpec((1, span), lambda i: (0, first // span + i))),
        ],
        [
            ((rows, hidden), BF16, shifted),
            ((rows, hidden), BF16, shifted),
            grad,
            grad,
            ((1, block), F32, by_column(1)),
        ],
        after=after,
        reuse=[] if earlier is None else [(earlier[0], 0), (earlier[1], 1)],
        scratch=[
            pltpu.VMEM((width, block), BF16),
            pltpu.VMEM((width, block), BF16),
            pltpu.SemaphoreType.DMA((count, len(up_weights.plan))),
            pltpu.SemaphoreType.DMA((count, len(down_weights.plan))),
        ],
        cost=cost(8 * rows * width * block, 24 * width * block, rows * block),
        name="feed",
    )


def block_total(small, width):
    return small.shape[1] - 8 * width


class Stream:
    def __init__(self):
        self.parts = []

    def add(self, copies):
        self.parts.append(copies)

    def start(self):
        for copies in self.parts:
            for copy in copies:
                copy.start()

    def wait(self, number):
        for copy in self.parts[number]:
            copy.wait()


def run_output(weights, acts, after_value, small, number, after=()):
    rows, width = after_value.shape
    hidden = acts.shape[1]
    span = 256
    bounds = [0]
    for size, _ in weights:
        bounds.append(bounds[-1] + size)
    by_row = lambda size: pl.BlockSpec((span, size), lambda i: (i, 0))

    def kernel(*refs):
        down = refs[-1 - len(weights)]
        sems = refs[-len(weights) :]
        stream = []
        for index, (size, item) in enumerate(weights):
            columns = slice(bounds[index], bounds[index + 1])
            copies, refs = item.copies(
                refs,
                size,
                lambda at, lines, columns=columns: down.at[pl.ds(at, lines), columns],
                sems[index],
            )
            stream.append(copies)
        act_ref, after_ref, bias_ref, out_ref = refs[:4]
        for copies in stream:
            start_all(copies)
        total = after_ref[...] + bias_ref[...]
        for index, copies in enumerate(stream):
            wait_all(copies)
            columns = slice(bounds[index], bounds[index + 1])
            total += dot_nt(act_ref[:, columns], down[:, columns])
        out_ref[...] = total.astype(BF16)

    (out,) = call(
        kernel,
        (rows // span,),
        [item for _, weight in weights for item in weight.inputs()]
        + [(acts, by_row(hidden)), (after_value, by_row(width)), param(small, number, width)],
        [((rows, width), BF16, by_row(width))],
        after=after,
        scratch=[pltpu.VMEM((width, hidden), BF16)] + [weight.sems() for _, weight in weights],
        cost=cost(2 * rows * width * hidden, 22 * rows * width),
        name="output",
    )
    return out


def run_middle(weights, out_weights, dus, after_value, dy, small, number, turned, after=()):
    rows, width = after_value.shape
    hidden = dus.shape[1]
    part = width
    parts = hidden // part
    span = 256
    mid = width // 2
    places = [
        (item.at(start)) for size, item in weights for start in range(0, size, part)
    ]
    most = max(len(item.plan) for item in places)

    def kernel(*refs):
        du, up, value_in, dy_in, turned_in, out_weight, branch, sems, out_sems, own_sems = refs[-10:]
        stream = Stream()
        for index, item in enumerate(places):
            columns = slice(index * part, (index + 1) * part)
            copies, refs = item.copies(
                refs,
                part,
                lambda at, size, columns=columns: up.at[pl.ds(at, size), columns],
                sems.at[index],
            )
            stream.add(copies)
        more, refs = out_weights.copies(
            refs, width, lambda at, size: out_weight.at[pl.ds(at, size), :], out_sems
        )
        du_ref, after_ref, dy_ref, gain_ref, turned_ref = refs[:5]
        grad_ref, dmix_ref, own_ref, sib_ref, gbias_ref, ggain_ref, gshift_ref = refs[5:12]
        for index in range(parts):
            columns = slice(index * part, (index + 1) * part)
            stream.parts[index].append(
                pltpu.make_async_copy(du_ref.at[:, columns], du.at[:, columns], own_sems.at[index])
            )
        stream.add(
            [
                pltpu.make_async_copy(after_ref, value_in, own_sems.at[parts]),
                pltpu.make_async_copy(dy_ref, dy_in, own_sems.at[parts + 1]),
            ]
        )
        stream.add([pltpu.make_async_copy(turned_ref, turned_in, own_sems.at[parts + 2]), *more])
        stream.start()
        total = None
        for index in range(parts):
            columns = slice(index * part, (index + 1) * part)
            stream.wait(index)
            value = dot_nt(du[:, columns], up[:, columns])
            total = value if total is None else total + value
        stream.wait(parts)
        gain = gain_ref[...]
        sums = [jnp.zeros((1, width), F32)] * 3
        for start in range(0, rows, span):
            lines = slice(start, start + span)
            grad = total[lines]
            hat, scale = norm_stats(value_in[lines, :])
            full = dy_in[lines, :].astype(F32) + norm_back(hat, scale, grad * gain)
            grad_ref[lines, :] = full
            low = full.astype(BF16)
            branch[lines, :] = low
            for index, value in enumerate((low.astype(F32), grad * hat, grad)):
                sums[index] = sums[index] + jnp.sum(value, axis=0, keepdims=True)
        gbias_ref[...], ggain_ref[...], gshift_ref[...] = sums
        stream.wait(parts + 1)
        dmix_ref[...] = dot_nt(branch[...], out_weight[...]).astype(BF16)
        for side in range(2):
            columns = slice(side * (width // 2), (side + 1) * (width // 2))
            value = dot_nn(turned_in[...], branch[:, columns]).astype(BF16)
            own_ref[side] = value[:mid]
            sib_ref[side] = value[mid:]

    grads = ((2, mid, width // 2), BF16, whole((2, mid, width // 2)))
    vector = ((1, width), F32, whole((1, width)))
    full = whole((rows, width))
    return call(
        kernel,
        (1,),
        [item for place in places for item in place.inputs()]
        + out_weights.inputs()
        + [(dus, ANY), (after_value, ANY), (dy, ANY), param(small, number, width), (turned, ANY)],
        [((rows, width), F32, full), ((rows, width), BF16, full), grads, grads] + [vector] * 3,
        after=after,
        scratch=[
            pltpu.VMEM((rows, hidden), BF16),
            pltpu.VMEM((width, hidden), BF16),
            pltpu.VMEM((rows, width), F32),
            pltpu.VMEM((rows, width), BF16),
            pltpu.VMEM((width, rows), BF16),
            pltpu.VMEM((width, width), BF16),
            pltpu.VMEM((rows, width), BF16),
            pltpu.SemaphoreType.DMA((parts, most)),
            out_weights.sems(),
            pltpu.SemaphoreType.DMA((parts + 3,)),
        ],
        cost=cost(8 * rows * width * (hidden + 2 * width), 120 * rows * width),
        name="middle",
    )


def attend_back_kernel(
    ends,
    q_ref,
    k_ref,
    v_ref,
    o_ref,
    do_ref,
    lse_ref,
    dq_ref,
    dk_ref,
    dv_ref,
    gq_ref,
    gv_ref,
    allow,
    total,
):
    rows = q_ref.shape[0]
    span = min(256, rows)

    @pl.when(pl.program_id(0) == 0)
    def _():
        for start in range(0, rows, span):
            query = lax.broadcasted_iota(jnp.int32, (1, rows - start), 1) + start
            first = first_of_row(ends, query)
            key = lax.broadcasted_iota(jnp.int32, (span, rows - start), 0) + start
            allow[start : start + span, start:] = jnp.where(
                (key <= query) & (key >= first), 0.0, MASKED
            )

    lane = lax.broadcasted_iota(jnp.int32, (1, LANES), 1)
    low_lane = lane < HD
    one = low_lane.astype(BF16)
    masks = (one, 1 - one)
    product = (o_ref[...].astype(F32) * do_ref[...].astype(F32)).T
    inner = (
        jnp.sum(product[:HD], axis=0, keepdims=True),
        jnp.sum(product[HD:], axis=0, keepdims=True),
    )
    for start in range(0, rows, span):
        stop = start + span
        grads = []
        for head in range(2):
            keys = k_ref[start:stop, :] * masks[head]
            vals = v_ref[start:stop, :] * masks[head]
            scores = dot_nt(keys, q_ref[start:, :]) + allow[start:stop, start:]
            probs = jnp.exp(scores - lse_ref[0, head : head + 1, start:])
            grad_probs = dot_nt(vals, do_ref[start:, :])
            grad_scores = (probs * (grad_probs - inner[head][:, start:])).astype(BF16)
            grad_vals = dot_nn(probs.astype(BF16), do_ref[start:, :])
            grad_keys = dot_nn(grad_scores, q_ref[start:, :])
            grads.append((grad_keys, grad_vals))
            update = dot_tn(grad_scores, keys)
            if start == 0 and head == 0:
                total[...] = update
            else:
                total[start:, :] += update
        dk_ref[start:stop, :] = jnp.where(low_lane, grads[0][0], grads[1][0]).astype(BF16)
        dv_ref[start:stop, :] = jnp.where(low_lane, grads[0][1], grads[1][1]).astype(BF16)
    grad_query = (total[...] * HD ** (-0.5)).astype(BF16)
    dq_ref[...] = grad_query
    gq_ref[...] = jnp.sum(grad_query.astype(F32), axis=0, keepdims=True)
    gv_ref[...] = jnp.sum(dv_ref[...].astype(F32), axis=0, keepdims=True)


def run_attend_back(ends, qkv, mixed, dmix, lse, first, count, after=()):
    rows, width = mixed.shape
    pairs = width // LANES
    column = lambda shift: pl.BlockSpec((rows, LANES), lambda i: (0, i + shift))
    return call(
        attend_back_kernel,
        (count,),
        [(ends, SMEM)]
        + [(qkv, column(first + part * pairs)) for part in range(3)]
        + [
            (mixed, column(first)),
            (dmix, column(first)),
            (lse, pl.BlockSpec((1, 2, rows), lambda i: (i + first, 0, 0))),
        ],
        [((rows, LANES * count), BF16, column(0))] * 3
        + [((1, LANES * count), F32, pl.BlockSpec((1, LANES), lambda i: (0, i)))] * 2,
        after=after,
        scratch=[pltpu.VMEM((rows, rows), F32), pltpu.VMEM((rows, LANES), F32)],
        cost=cost(
            (80 if first == 0 else 20) * rows * rows * LANES * count,
            16 * rows * LANES * count,
            2 * rows * rows * count,
        ),
        name="attend_back",
    )


def project_kernel(turned_ref, dq_ref, dk_ref, dv_ref, own_ref, sib_ref):
    mid = own_ref.shape[1]
    size = dq_ref.shape[1]
    left = jnp.concatenate([dq_ref[...], dk_ref[:, : size // 2]], axis=1)
    right = jnp.concatenate([dk_ref[:, size // 2 :], dv_ref[...]], axis=1)
    for side, columns in enumerate((left, right)):
        own_ref[side] = dot_nn(turned_ref[:mid], columns).astype(BF16)
        sib_ref[side] = dot_nn(turned_ref[mid:], columns).astype(BF16)


def run_project(turned, dq, dk, dv, after=()):
    width, rows = turned.shape
    size = dq.shape[1]
    mid = width // 2
    grad = ((2, mid, 3 * size // 2), BF16, whole((2, mid, 3 * size // 2)))
    return call(
        project_kernel,
        (1,),
        [(turned, whole((width, rows)))] + [(value, whole((rows, size))) for value in (dq, dk, dv)],
        [grad, grad],
        after=after,
        cost=cost(6 * rows * width * size, 14 * rows * size),
        name="project",
    )


def run_input(weights, grads, x, grad_after, small, number, after=()):
    rows, width = x.shape
    span = 256
    size = grads[0][0].shape[1]
    flat = [value for group in grads for value in group]
    count = len(flat)
    by_row = lambda size: pl.BlockSpec((span, size), lambda i: (i, 0))

    def kernel(*refs):
        weight, sems = refs[-2:]
        stream = []
        for part in range(3):
            columns = slice(part * width, (part + 1) * width)
            copies, rest = weights.at(part * width).copies(
                refs,
                width,
                lambda at, lines, columns=columns: weight.at[pl.ds(at, lines), columns],
                sems.at[part],
            )
            stream.append(copies)
        refs = rest
        for copies in stream:
            start_all(copies)
        x_ref, grad_ref, gain_ref, out_ref, ggain_ref, gshift_ref = refs[count : count + 6]
        step = pl.program_id(0)
        total = None
        for part in range(3):
            wait_all(stream[part])
            for group in range(len(grads)):
                begin = part * width + group * size
                value = dot_nt(refs[3 * group + part][...], weight[:, begin : begin + size])
                total = value if total is None else total + value
        hat, scale = norm_stats(x_ref[...].astype(F32))
        accumulate(gshift_ref, jnp.sum(total, axis=0, keepdims=True), step == 0)
        accumulate(ggain_ref, jnp.sum(total * hat, axis=0, keepdims=True), step == 0)
        out_ref[...] = grad_ref[...] + norm_back(hat, scale, total * gain_ref[...])

    vector = ((1, width), F32, whole((1, width)))
    return call(
        kernel,
        (rows // span,),
        weights.inputs()
        + [(value, by_row(size)) for value in flat]
        + [(x, by_row(width)), (grad_after, by_row(width)), param(small, number, width)],
        [((rows, width), F32, by_row(width)), vector, vector],
        after=after,
        scratch=[
            pltpu.VMEM((width, 3 * width), BF16),
            pltpu.SemaphoreType.DMA((3, len(weights.plan))),
        ],
        cost=cost(6 * rows * width * width, 22 * rows * width),
        name="grad_input",
    )


def adamw(weight, first, second, grad, rate, decay):
    first_new = beta_one * first + (1.0 - beta_one) * grad
    second_new = beta_two * second + (1.0 - beta_two) * grad * grad
    first_hat = first_new / (1.0 - beta_one**STEP)
    second_hat = second_new / (1.0 - beta_two**STEP)
    weight_new = weight - rate * (first_hat / (jnp.sqrt(second_hat) + adam_eps) + decay * weight)
    return (weight_new, first_new, second_new)


def run_adam(core, state, groups, span, places, pick, earlier, after=()):
    half = groups[0][0].shape[-2]
    count = len(places)
    table = jnp.array(places, jnp.int32)
    place = pl.BlockSpec((half, span), lambda p, h, c, t: (jnp.bitwise_xor(h, c[0]), t[p]))
    flat = [value for group in groups for value in group]

    def kernel(core_ref, table_ref, w_ref, m_ref, v_ref, *refs):
        w_out, m_out, v_out, grad_ref = refs[-4:]
        for side in range(2):
            mine = refs[side : 2 * len(groups) : 2]
            for block in range(count):

                @pl.when((pl.program_id(1) == side) & (pl.program_id(0) == block))
                def _(mine=mine, block=block):
                    start = 0
                    for value in pick(block, mine):
                        grad_ref[:, start : start + value.shape[1]] = value
                        start += value.shape[1]

        w_out[...], m_out[...], v_out[...] = adamw(
            w_ref[...], m_ref[...], v_ref[...], grad_ref[...].astype(F32), 0.05, 0.1
        )

    moved = 2 * half * count * span
    return call(
        kernel,
        (count, 2),
        [(value, place) for value in state] + [(value, whole(value.shape)) for value in flat],
        [(state[0].shape, F32, place)] * 3,
        after=after,
        reuse=[] if earlier is None else [(value, n) for n, value in enumerate(earlier)],
        prefetch=(core, table),
        scratch=[pltpu.VMEM((half, span), BF16)],
        cost=cost(20 * moved, 26 * moved),
        name="adam",
    )


def run_side(core, jobs, after=(), steps=4):
    counts = [(len(job[0]), len(job[1])) for job in jobs]
    total_in = sum(count[0] for count in counts)

    def kernel(core_ref, *refs):
        ins = refs[:total_in]
        outs = refs[total_in:]
        for job, (have, give) in zip(jobs, counts):
            more = (core_ref,) if "places" in job[2].__code__.co_varnames else ()
            job[2](ins[:have], outs[:give], *more)
            ins = ins[have:]
            outs = outs[give:]

    def spec(block, index):
        return pl.BlockSpec(block, lambda i, c: index(i, c))

    moved = sum(array.size * 2 for job in jobs for array, _, _ in job[0])
    results = call(
        kernel,
        (steps,),
        [(array, spec(block, index)) for job in jobs for array, block, index in job[0]],
        [(shape, dtype, spec(block, index)) for job in jobs for shape, dtype, block, index in job[1]],
        after=after,
        prefetch=(core,),
        cost=cost(0, 2 * moved),
        name="side",
    )
    split = []
    for _, give in counts:
        split.append(results[:give])
        results = results[give:]
    return split


def job_cast(rows, columns, by_core, steps):
    span = rows // steps
    total = sum(size for _, _, size in columns)
    ins = []
    for state, number, size in columns:
        index = lambda i, c, number=number: (c[0] * steps * by_core + i, number)
        ins.append((state, (span, size), index))
    outs = [((rows, total), BF16, (span, total), lambda i, c: (i, 0))]

    def run(have, give):
        start = 0
        for ref, (_, _, size) in zip(have, columns):
            give[0][:, start : start + size] = ref[...].astype(BF16)
            start += size

    return ins, outs, run


def job_join(left, right, steps):
    _, blocks, rows, size = left.shape
    span = rows // steps
    four = lambda i, c: (0, 0, i, 0)
    ins = [(value, (2, blocks, span, size), four) for value in (left, right)]
    outs = [((blocks, 2, rows, size), BF16, (blocks, 2, span, size), four)]

    def run(have, give):
        for side in range(2):
            for block in range(blocks):
                give[0][block, side] = have[0][side, block] + have[1][side, block]

    return ins, outs, run


def job_copy(value, first, rows):
    size = value.shape[1]
    ins = [(value, value.shape, lambda i, c: (0, 0))]
    outs = [((rows, size), value.dtype, (rows, size), lambda i, c: (0, 0))]

    def run(have, give):
        give[0][...] = have[0][first : first + rows, :]

    return ins, outs, run


def job_add(left, right, steps):
    at = left.ndim - 2
    if left.shape[at] == 1:
        same = lambda i, c: (0,) * left.ndim

        def run_whole(have, give):
            give[0][...] = have[0][...] + have[1][...]

        return (
            [(left, left.shape, same), (right, right.shape, same)],
            [(left.shape, left.dtype, left.shape, same)],
            run_whole,
        )
    block = tuple(size // steps if axis == at else size for axis, size in enumerate(left.shape))
    index = lambda i, c: (0,) * at + (i, 0)

    def run(have, give):
        give[0][...] = have[0][...] + have[1][...]

    return [(left, block, index), (right, block, index)], [(left.shape, left.dtype, block, index)], run


def job_pick(own, received, steps):
    at = own.ndim - 2
    block = tuple(size // steps if axis == at else size for axis, size in enumerate(own.shape))
    index = lambda i, c: (0,) * at + (i, 0)

    def run(have, give, places):
        give[0][...] = jnp.where(places[2] == 1, have[0][...], have[1][...])

    return [(own, block, index), (received, block, index)], [(own.shape, own.dtype, block, index)], run


def job_sum(groups, keep, send, steps):
    _, blocks, rows, _ = groups[0][0].shape
    span = rows // steps
    total = sum(own.shape[3] for own, _ in groups)
    four = lambda i, c: (0, 0, i, 0)
    three = lambda i, c: (0, i, 0)
    ins = []
    for own, received in groups:
        size = own.shape[3]
        ins.append((own, (2, blocks, span, size), four))
        if len(received) == 1:
            ins.append((received[0], (2, blocks, span, size), four))
        else:
            ins += [(value, (blocks, span, size), three) for value in received]
    kept = len(keep[0])
    outs = [((2, kept, rows, total), BF16, (2, kept, span, total), four)]
    if len(send) == 1:
        gone = len(send[0])
        outs.append(((2, gone, rows, total), BF16, (2, gone, span, total), four))
    else:
        for side in range(2):
            if send[side]:
                gone = len(send[side])
                outs.append(((gone, rows, total), BF16, (gone, span, total), three))

    def run(have, give):
        start = 0
        for own, received in groups:
            size = own.shape[3]
            columns = slice(start, start + size)
            start += size
            for side in range(2):
                for block in range(blocks):
                    other = have[1][side, block] if len(received) == 1 else have[1 + side][block]
                    value = have[0][side, block] + other
                    if block in keep[side]:
                        give[0][side, keep[side].index(block), :, columns] = value
                    elif len(send) == 1:
                        give[1][side, send[0].index(block), :, columns] = value
                    else:
                        give[1 + side][send[side].index(block), :, columns] = value
            have = have[1 + len(received) :]

    return ins, outs, run


def job_params(rows, shards, small_size):
    ins = []
    for array, row in rows:
        if array.shape[0] == 1:
            ins.append((array, array.shape, lambda i, c: (0, 0)))
        else:
            size = array.shape[1]
            ins.append((array, (16, size), lambda i, c, row=row: (row // 16, 0)))
    shape = (1, shards * small_size)
    outs = [(shape, F32, shape, lambda i, c: (0, 0))]

    def run(have, give, places):
        for number, ref in enumerate(have):
            owner = jnp.bitwise_xor(places[1], number)
            start = pl.multiple_of(owner * small_size, LANES)
            value = ref[0:1, :small_size].astype(BF16).astype(F32)
            give[0][:, pl.ds(start, small_size)] = value

    return ins, outs, run


def job_lay(values):
    total = sum(value.shape[1] for value in values)
    same = lambda i, c: (0, 0)
    ins = [(value, value.shape, same) for value in values]

    def run(have, give):
        start = 0
        for ref in have:
            give[0][:, start : start + ref.shape[1]] = ref[...]
            start += ref.shape[1]

    return ins, [((1, total), F32, (1, total), same)], run


class Links:
    def __init__(self, sizes, shard_rows):
        self.replicas, self.shards = sizes
        dp = lax.axis_index("dp")
        self.shard = lax.axis_index("shard")
        self.core = lax.rem(dp, 2)
        place = dp // 2
        self.inner = (place > 0) & (place < sizes[0] // 2 - 1)
        self.core_arr = jnp.stack([self.core, self.shard, self.inner]).astype(jnp.int32)
        self.rows = shard_rows
        self.half = shard_rows // 2
        self.fast = sizes == (8, 4)

    def swap(self, value):
        return self.across_dp(value, 1)

    def across_dp(self, value, bit):
        return lax.ppermute(value, "dp", [(d, d ^ bit) for d in range(self.replicas)])

    def along_dp(self, value, step):
        hops = ([(0, 1), (3, 2)], [(1, 2), (2, 1)], [(1, 0), (2, 3)])[step]
        pairs = [(2 * a + core, 2 * b + core) for a, b in hops for core in range(2)]
        return lax.ppermute(value, "dp", pairs)

    def across_shard(self, value, bit):
        return lax.ppermute(value, "shard", [(s, s ^ bit) for s in range(self.shards)])

    def turned_offsets(self, around):
        blocks = jnp.arange(2 * self.shards, dtype=jnp.int32)
        owner = blocks // 2
        if around:
            owner = jnp.bitwise_xor(owner, self.shard)
        away = jnp.bitwise_xor(lax.rem(blocks, 2), self.core)
        return away * (self.shards * self.half) + owner * self.half

    def gather(self, half_rows):
        return lax.all_gather(half_rows, "shard", axis=0, tiled=True)

    def gathered(self, mine, behind=None):
        if behind is not None:
            mine, _ = lax.optimization_barrier((mine, behind))
        first = jnp.arange(self.shards, dtype=jnp.int32) * self.rows
        offs = jnp.concatenate([first + self.core * self.half, first + (1 - self.core) * self.half])
        stride = mine.shape[0] // self.shards
        plan = tuple((0, t * stride, self.half, t) for t in range(self.shards)) + tuple(
            (1, t * stride, self.half, self.shards + t) for t in range(self.shards)
        )
        return Weights((mine, self.swap(mine)), plan, offs.astype(jnp.int32))

    def over_dp(self, values):
        groups = [[d for d in range(self.replicas) if d % 2 == c] for c in range(2)]
        return lax.psum(values, "dp", axis_index_groups=groups)


class Gather:
    def __init__(self, links, half_rows, own):
        self.links = links
        self.own = own
        self.by_x = links.across_shard(half_rows, 1)
        self.by_y = links.across_shard(half_rows, 2)

    def jobs(self):
        part = self.links.half // 2
        rest = self.by_x.shape[0] - part
        return [job_copy(self.by_y, 0, part), job_copy(self.by_x, part, rest)]

    def forward(self, results):
        links = self.links
        self.far = (
            links.across_shard(results[0], 1),
            links.across_shard(results[1], 2),
        )
        self.near = (links.swap(self.by_x), links.swap(self.by_y))

    def weights(self):
        links = self.links
        half, rows = links.half, links.rows
        part = half // 2
        far = tuple(links.swap(value) for value in self.far)
        pieces = (self.own, self.by_x, self.by_y, *self.near, *self.far, *far)
        plan = ((0, 0, rows, 0),)
        plan += tuple((n, 0, half, n) for n in range(1, 5))
        plan += tuple((n, 0, part, n) for n in range(5, 9))
        at = lambda bits: jnp.bitwise_xor(links.shard, bits) * rows
        mine = links.core * half
        other = (1 - links.core) * half
        offs = [at(0), at(1) + mine, at(2) + mine, at(1) + other, at(2) + other]
        offs += [at(3) + mine, at(3) + mine + part, at(3) + other, at(3) + other + part]
        return Weights(pieces, plan, jnp.stack(offs).astype(jnp.int32))


class Reduce:
    def __init__(self, links, line):
        self.links = links
        self.line = line
        self.stage = 0
        self.groups = []

    def add(self, own, sib):
        shape = (2, self.links.shards, self.links.half, own.shape[2])
        self.groups.append((own.reshape(shape), (self.links.swap(sib).reshape(shape),)))
        return self

    def job(self, steps):
        if self.stage > 2:
            own, received = self.groups[0]
            if self.line and self.stage == 5:
                return job_pick(own, received, steps)
            return job_add(own, received, steps)
        blocks = self.groups[0][0].shape[1]
        odd = lambda block: block % 2 == 1
        late = lambda block: block >= blocks // 2
        goes = [odd, late]
        if blocks == 2:
            goes = [odd, odd]
        if blocks == 1:
            goes = [lambda block: False] * 2
        keep = [[block for block in range(blocks) if not go(block)] for go in goes]
        send = [[block for block in range(blocks) if go(block)] for go in goes]
        return job_sum(self.groups, keep, send, steps)

    def advance(self, results):
        links = self.links
        own = results[0]
        stage = self.stage
        self.stage += 1
        if stage < 2:
            bits = (1, 2) if stage == 0 else (2, 1)
            received = tuple(
                links.across_shard(value, bit) for value, bit in zip(results[1:], bits)
            )
            self.groups = [(own, received)]
            return
        if stage == 2:
            own = own.reshape(2, own.shape[2], own.shape[3])
        if self.line and stage < 5:
            self.groups = [(own, links.along_dp(own, stage - 2))]
        elif not self.line and stage < 4:
            self.groups = [(own, links.across_dp(own, 2 * (stage - 1)))]
        else:
            self.grads = (own, links.swap(own))


class Wide:
    def __init__(self, links, joined):
        self.links = links
        self.shape = joined.shape[1:]
        flat = joined.reshape(-1, joined.shape[3])
        self.own = lax.psum_scatter(flat, "shard", scatter_dimension=0, tiled=True)

    def finish(self):
        self.own = self.links.over_dp(self.own).reshape(self.shape)


class Side:
    def __init__(self, links):
        self.links = links
        self.order = ()

    def jobs(self, jobs, steps=1, after=()):
        results = run_side(self.links.core_arr, jobs, after=(*self.order, *after), steps=steps)
        self.order = (results[0][0],)
        return [result[0] for result in results]

    def reduce(self, reduces, jobs=(), steps=2):
        work = [item.job(steps) for item in reduces] + list(jobs)
        results = run_side(self.links.core_arr, work, after=self.order, steps=steps)
        for item, result in zip(reduces, results):
            item.advance(result)
        self.order = (results[0][0],)
        return [result[0] for result in results[len(reduces) :]]

    def then(self, results):
        self.order = (results[0],)
        return results


def small_parts(small, width, hidden):
    bounds = [width] * 3 + [hidden] + [width] * 5
    parts = []
    start = 0
    for size in bounds:
        parts.append(small[:, start : start + size])
        start += size
    return parts


def body(sizes, *args):
    tokens, cotangent, lengths = args[:3]
    attn_state, mlp_state, small_state = args[3:6], args[6:9], args[9:12]
    rows, width = tokens.shape
    links = Links(sizes, attn_state[0].shape[0])
    half = links.half
    hidden = mlp_state[0].shape[1] // 2
    pairs = width // LANES
    pad = 16
    core_arr = links.core_arr
    around = links.turned_offsets(links.fast)
    side = Side(links)

    ends = jnp.cumsum(lengths[0], dtype=jnp.int32)
    small_own = small_state[0][None]
    small_size = small_own.shape[1]
    (
        BIAS_Q,
        BIAS_V,
        BIAS_O,
        BIAS_UP,
    ) = range(4)
    BIAS_DN, GAIN_ONE, SHIFT_ONE, GAIN_TWO, SHIFT_TWO = range(
        BIAS_UP + hidden // width, BIAS_UP + hidden // width + 5
    )

    def first_job():
        ins = [
            (attn_state[0], (half, 4 * width), lambda i, c: (c[0], 0)),
            (small_own, (1, small_size), lambda i, c: (0, 0)),
        ]
        outs = [((half + pad, 4 * width), BF16, (half + pad, 4 * width), lambda i, c: (0, 0))]

        def job(have, give):
            give[0][:half] = have[0][...].astype(BF16)
            row = have[1][...].astype(BF16)
            give[0][half:, :small_size] = jnp.broadcast_to(row, (pad, small_size))

        return ins, outs, job

    block = hidden // 2
    groups = [[(mlp_state[0], number, block) for number in pair] for pair in ((0, 2), (1, 3))]
    (first_half,) = side.jobs([first_job()])
    if links.fast:
        attn_gather = Gather(links, first_half, None)
    else:
        attn_weights = links.gathered(links.gather(first_half))
    dy, dyt, grad_bias_dn = side.then(run_cot(half, around, ends, cotangent, after=side.order))
    (more_half,) = side.jobs([job_cast(half, groups[1], 1, 4)], steps=4)
    if links.fast:
        (attn_gather.own,) = side.jobs(
            [job_cast(links.rows, [(attn_state[0], 0, 4 * width)], 0, 4)], steps=4
        )
        *copied, feed_half = side.jobs([*attn_gather.jobs(), job_cast(half, groups[0], 1, 1)])
        attn_gather.forward(copied)
    else:
        (feed_half,) = side.jobs([job_cast(half, groups[0], 1, 1)])
    wide = links.gather(feed_half)
    more_wide = links.gather(more_half)
    if links.fast:
        attn_weights = attn_gather.weights()
        rows_of = [
            (small_own, 0),
            (attn_gather.by_x, half),
            (attn_gather.by_y, half),
            (attn_gather.far[1], half // 2),
        ]
        (small,) = side.jobs([job_params(rows_of, links.shards, small_size)])
    else:
        small = attn_weights.pieces[0].reshape(links.shards, half + pad, 4 * width)
        small = small[:, half, :small_size].astype(F32).reshape(1, -1)

    qkv, turned_one = side.then(
        run_qkv(
            half,
            attn_weights,
            around,
            tokens,
            small,
            (BIAS_Q, BIAS_V, GAIN_ONE, SHIFT_ONE),
            after=side.order,
        )
    )
    mixed, lse = side.then(run_attend(ends, qkv, 0, pairs, after=side.order))
    wide = links.gathered(wide, lse)
    side.order += (wide.pieces[0],)
    after, low_two, turned_two, turned_mixed = side.then(
        run_after(
            half,
            attn_weights.at(3 * width),
            (around, around),
            mixed,
            tokens,
            small,
            (BIAS_O, GAIN_TWO, SHIFT_TWO),
            after=side.order,
        )
    )

    passed, grad_bias_up = [None], []
    blocked = lambda value: value.reshape(2, links.shards, half, value.shape[2])

    def feed(start, up_weights, down_weights):
        act, du, own, sib, gbias = run_feed(
            up_weights,
            down_weights,
            low_two,
            turned_two,
            dy,
            dyt,
            small,
            BIAS_UP * width + start,
            start,
            block,
            passed[-1],
            after=side.order,
        )
        side.order = (own,)
        passed.append((act, du))
        grad_bias_up.append(gbias)
        return own, sib

    def unit(line, *grads):
        if links.fast:
            return Reduce(links, line).add(*grads)
        return Wide(links, side.jobs([job_join(blocked(grads[0]), blocked(links.swap(grads[1])), 4)], steps=4)[0])

    def reduce(units, jobs=(), steps=2):
        if links.fast:
            return side.reduce(units, jobs, steps)
        return side.jobs(jobs) if jobs else None

    group_a = feed(0, wide, wide.at(block))
    more_wide = links.gathered(more_wide, grad_bias_up[0])
    unit_a = unit(True, *group_a)
    reduce([unit_a], steps=4)
    unit_b = unit(True, *feed(block, more_wide, more_wide.at(block)))
    reduce([unit_a], steps=4)
    (
        grad_after,
        dmix,
        own_out,
        sib_out,
        grad_bias_o,
        grad_gain_two,
        grad_shift_two,
    ) = side.then(
        run_middle(
            [(block, wide), (block, more_wide)],
            attn_weights.at(3 * width),
            passed[-1][1],
            after,
            dy,
            small,
            GAIN_TWO,
            turned_mixed,
            after=side.order,
        )
    )
    unit_c = unit(False, own_out, sib_out)
    reduce([unit_a, unit_b], steps=4)
    grads, biases = [], []

    def attend_back(first):
        dq, dk, dv, gq, gv = side.then(
            run_attend_back(ends, qkv, mixed, dmix, lse, first, pairs // 2, after=side.order)
        )
        grads.append((dq, dk, dv))
        biases.append((gq, gv))

    def project(group):
        return side.then(run_project(turned_one, *grads[group], after=side.order))

    attend_back(0)
    reduce([unit_a, unit_b], steps=4)
    if links.fast:
        unit_c.add(*project(0))
    else:
        unit_e = unit(False, *project(0))
    attend_back(pairs // 2)
    reduce([unit_a, unit_b, unit_c], steps=4)
    unit_d = unit(False, *project(1))
    grad_input, grad_gain_one, grad_shift_one = side.then(
        run_input(attn_weights, grads, tokens, grad_after, small, GAIN_ONE, after=side.order)
    )
    small_grads = [biases[0][0], biases[1][0], biases[0][1], biases[1][1], grad_bias_o]
    small_grads += grad_bias_up
    small_grads += [grad_bias_dn, grad_gain_one, grad_shift_one, grad_gain_two, grad_shift_two]
    (grad_small,) = reduce([unit_a, unit_b, unit_c, unit_d], [job_lay(small_grads)])

    def pick_feed(number, arrays):
        return [arrays[0][number]]

    def adam_mlp(number, item, earlier):
        return side.then(
            run_adam(
                core_arr,
                mlp_state,
                [item.grads],
                block,
                [number, 2 + number],
                pick_feed,
                earlier,
                after=side.order,
            )
        )

    out_block = width // 2

    def pick_heads(number, arrays):
        left, right = arrays[0][0], arrays[0][1]
        skip = arrays[0].shape[2] - 3 * out_block // 2
        split = skip + out_block // 2
        return (
            [left[:, skip : skip + out_block]],
            [left[:, skip + out_block :], right[:, skip:split]],
            [right[:, split:]],
            [left[:, :skip]],
            [right[:, :skip]],
        )[number]

    def adam_attn(item, places, earlier):
        return side.then(
            run_adam(
                core_arr,
                attn_state,
                [item.grads],
                out_block,
                places,
                pick_heads,
                earlier,
                after=side.order,
            )
        )

    def output_now():
        out = run_output(
            [(block, wide.at(block)), (block, more_wide.at(block))],
            passed[-1][0],
            after,
            small,
            BIAS_DN,
            after=side.order,
        )
        side.then([out])
        return out

    if links.fast:
        shard_move = lambda bit: functools.partial(links.across_shard, bit=bit)
        dp_move = lambda bit: functools.partial(links.across_dp, bit=bit)
        moved = links.across_shard(grad_small, 1)

        def step(units, move):
            (total,) = reduce(units, [job_add(grad_small, moved, 2)])
            return total, move(total) if move else None

        mlp_new = adam_mlp(0, unit_a, None)
        grad_small, moved = step([unit_b, unit_c, unit_d], shard_move(2))
        output = output_now()
        grad_small, moved = step([unit_b, unit_c, unit_d], links.swap)
        mlp_new = adam_mlp(1, unit_b, mlp_new)
        grad_small, moved = step([unit_c, unit_d], dp_move(2))
        attn_new = adam_attn(unit_c, [0, 2, 4, 6, 7], None)
        grad_small, moved = step([unit_d], dp_move(4))
        attn_new = adam_attn(unit_d, [1, 3, 5], attn_new)
        grad_small, _ = step([], None)
    else:
        for item in (unit_a, unit_b, unit_c, unit_d, unit_e):
            item.finish()
        unit_c.own = jnp.concatenate([unit_c.own, unit_e.own], axis=2)
        for item in (unit_a, unit_b, unit_c, unit_d):
            item.grads = (item.own, links.swap(item.own))
        grad_small = lax.psum(grad_small, ("dp", "shard"))
        output = output_now()
        mlp_new = adam_mlp(1, unit_b, adam_mlp(0, unit_a, None))
        attn_new = adam_attn(unit_c, [0, 2, 4, 6, 7], None)
        attn_new = adam_attn(unit_d, [1, 3, 5], attn_new)
    grad_small = lax.dynamic_slice_in_dim(grad_small, links.shard * small_size, small_size, 1)[0]
    small_new = adamw(*small_state, grad_small, 0.4, 0.0)
    return (output, grad_input, *attn_new, *mlp_new, *small_new)


def solution(mesh):
    tokens = P(("dp", "shard"), None)
    state = P("shard", None)
    vector = P("shard")
    return jax.shard_map(
        functools.partial(body, (mesh.shape["dp"], mesh.shape["shard"])),
        mesh=mesh,
        in_specs=(tokens,) * 3 + (state,) * 6 + (vector,) * 3,
        out_specs=(tokens,) * 2 + (state,) * 6 + (vector,) * 3,
        check_vma=False,
    )
```

```python
import functools

import jax
import jax.numpy as jnp
from jax import lax
from jax.experimental import pallas as pl
from jax.experimental.pallas import tpu as pltpu
from jax.sharding import PartitionSpec as P

HD = 64
STEP = 10
LANES = 128
MASKED = -1e30
SAFE = 60.0
GELU_IN = 0.7978845608028654
GELU_CUBE = 0.044715

beta_one = 0.9
beta_two = 0.95
adam_eps = 1e-08
norm_eps = 1e-05

F32 = jnp.float32
BF16 = jnp.bfloat16
MIB = 1024 * 1024
VMEM_MIB = 64

ANY = pl.BlockSpec(memory_space=pl.ANY)
SMEM = pl.BlockSpec(memory_space=pltpu.SMEM)


def dot_nn(left, right):
    return lax.dot_general(left, right, (((1,), (0,)), ((), ())), preferred_element_type=F32)


def dot_nt(left, right):
    return lax.dot_general(left, right, (((1,), (1,)), ((), ())), preferred_element_type=F32)


def dot_tn(left, right):
    return lax.dot_general(left, right, (((0,), (0,)), ((), ())), preferred_element_type=F32)


def whole(shape):
    return pl.BlockSpec(shape, lambda *_: (0,) * len(shape))


def call(kernel, grid, ins, outs, after=(), reuse=(), prefetch=(), scratch=(), cost=None, name=None):
    known = len(prefetch) + len(ins)
    idle = [*after, *(array for array, _ in reuse)]

    def run(*refs):
        kernel(*refs[:known], *refs[known + len(idle) :])

    def placed(array, spec):
        if spec is SMEM:
            return array
        return pltpu.with_memory_space_constraint(array, pltpu.HBM)

    return pl.pallas_call(
        run,
        grid_spec=pltpu.PrefetchScalarGridSpec(
            num_scalar_prefetch=len(prefetch),
            grid=grid,
            in_specs=[spec for _, spec in ins] + [ANY] * len(idle),
            out_specs=[spec for _, _, spec in outs],
            scratch_shapes=list(scratch),
        ),
        out_shape=[pltpu.HBM(shape, dtype) for shape, dtype, _ in outs],
        input_output_aliases={
            known + len(after) + number: output for number, (_, output) in enumerate(reuse)
        },
        compiler_params=pltpu.CompilerParams(vmem_limit_bytes=VMEM_MIB * MIB),
        cost_estimate=cost,
        name=name,
    )(*prefetch, *(placed(*item) for item in ins), *(placed(array, ANY) for array in idle))


def param(small, number, width):
    return (small, pl.BlockSpec((1, width), lambda *_: (0, number)))


def cost(flops, moved, exps=0):
    return pl.CostEstimate(flops=int(flops), bytes_accessed=int(moved), transcendentals=int(exps))


def store_turned(turned_ref, toff, block, half, value, columns):
    turned = value.astype(BF16).T
    for part in range(LANES // half):
        offset = pl.multiple_of(toff[block * (LANES // half) + part], half)
        turned_ref[pl.ds(offset, half), columns] = turned[part * half : (part + 1) * half]


def norm_stats(values):
    center = values - jnp.mean(values, axis=-1, keepdims=True)
    spread = jnp.mean(center * center, axis=-1, keepdims=True)
    scale = lax.rsqrt(spread + norm_eps)
    return center * scale, scale


def norm_back(hat, scale, grad_hat):
    mean = jnp.mean(grad_hat, axis=-1, keepdims=True)
    along = jnp.mean(grad_hat * hat, axis=-1, keepdims=True)
    return scale * (grad_hat - mean - hat * along)


def accumulate(ref, value, first):
    @pl.when(first)
    def _():
        ref[...] = value

    @pl.when(jnp.logical_not(first))
    def _():
        ref[...] += value


class Weights:
    def __init__(self, pieces, plan, offs, first=0):
        self.pieces, self.plan, self.offs, self.first = pieces, plan, offs, first

    def at(self, first):
        return Weights(self.pieces, self.plan, self.offs, self.first + first)

    def inputs(self):
        return [(self.offs, SMEM)] + [(piece, ANY) for piece in self.pieces]

    def sems(self):
        return pltpu.SemaphoreType.DMA((len(self.plan),))

    def rest(self, refs):
        return refs[1 + len(self.pieces) :]

    def copies(self, refs, size, target, sems, start=None):
        offs, refs = refs[0], refs[1:]
        columns = slice(self.first, self.first + size)
        if start is not None:
            columns = pl.ds(pl.multiple_of(self.first + start, LANES), size)
        made = []
        for number, (piece, first, rows, index) in enumerate(self.plan):
            offset = pl.multiple_of(offs[index], rows)
            made.append(
                pltpu.make_async_copy(
                    refs[piece].at[pl.ds(first, rows), columns],
                    target(offset, rows),
                    sems.at[number],
                )
            )
        return made, refs[len(self.pieces) :]


def start_all(copies):
    @pl.when(pl.program_id(0) == 0)
    def _():
        for copy in copies:
            copy.start()


def wait_all(copies):
    @pl.when(pl.program_id(0) == 0)
    def _():
        for copy in copies:
            copy.wait()


def cot_kernel(half, toff, ends, cot_ref, dy_ref, turned_ref, bias_ref):
    rows = cot_ref.shape[0]
    place = lax.broadcasted_iota(jnp.int32, (rows, LANES), 0)
    live = (place < ends[ends.shape[0] - 1]).astype(F32)
    for block in range(cot_ref.shape[1] // LANES):
        columns = slice(block * LANES, (block + 1) * LANES)
        value = cot_ref[:, columns].astype(F32) * live
        dy_ref[:, columns] = value.astype(BF16)
        bias_ref[:, columns] = jnp.sum(value, axis=0, keepdims=True)
        store_turned(turned_ref, toff, block, half, value, slice(None))


def run_cot(half, toff, ends, cot, after=()):
    rows, width = cot.shape
    return call(
        functools.partial(cot_kernel, half),
        (1,),
        [(toff, SMEM), (ends, SMEM), (cot, whole(cot.shape))],
        [
            ((rows, width), BF16, whole((rows, width))),
            ((width, rows), BF16, whole((width, rows))),
            ((1, width), F32, whole((1, width))),
        ],
        after=after,
        cost=cost(0, 6 * rows * width),
        name="cotangent",
    )


def run_qkv(half, weights, toff, x, small, numbers, after=()):
    rows, width = x.shape
    span = 256

    def kernel(*refs):
        weight, sems = refs[-2:]
        copies, refs = weights.copies(
            refs, 3 * width, lambda at, size: weight.at[pl.ds(at, size), :], sems
        )
        toff_ref, x_ref, bias_q, bias_v, gain_ref, shift_ref, qkv_ref, turned_ref = refs[:8]
        start_all(copies)
        hat, _ = norm_stats(x_ref[...].astype(F32))
        normed = hat * gain_ref[...] + shift_ref[...]
        for block in range(width // LANES):
            columns = slice(block * LANES, (block + 1) * LANES)
            store_turned(turned_ref, toff_ref, block, half, normed[:, columns], slice(None))
        wait_all(copies)
        low = normed.astype(BF16)
        for part in range(3):
            columns = slice(part * width, (part + 1) * width)
            value = dot_nn(low, weight[:, columns])
            if part == 2:
                value += bias_v[...]
            if part == 0:
                value = (value + bias_q[...]).astype(BF16).astype(F32) * HD ** (-0.5)
            qkv_ref[:, columns] = value.astype(BF16)

    return call(
        kernel,
        (rows // span,),
        weights.inputs()
        + [
            (toff, SMEM),
            (x, pl.BlockSpec((span, width), lambda i: (i, 0))),
        ]
        + [param(small, number, width) for number in numbers],
        [
            ((rows, 3 * width), BF16, pl.BlockSpec((span, 3 * width), lambda i: (i, 0))),
            ((width, rows), BF16, pl.BlockSpec((width, span), lambda i: (0, i))),
        ],
        after=after,
        scratch=[pltpu.VMEM((width, 3 * width), BF16), weights.sems()],
        cost=cost(6 * rows * width * width, 16 * rows * width),
        name="qkv",
    )


def first_of_row(ends, place):
    first = jnp.zeros_like(place)
    for number in range(ends.shape[0]):
        first = jnp.where(place >= ends[number], ends[number], first)
    return first


def attend_kernel(ends, q_ref, k_ref, v_ref, o_ref, lse_ref, allow):
    rows = q_ref.shape[0]
    span = min(256, rows)

    @pl.when(pl.program_id(0) == 0)
    def _():
        for start in range(0, rows, span):
            keys = start + span
            place = lax.broadcasted_iota(jnp.int32, (span, 1), 0) + start
            first = first_of_row(ends, place)
            key = lax.broadcasted_iota(jnp.int32, (span, keys), 1)
            allow[start:keys, :keys] = jnp.where((key <= place) & (key >= first), 0.0, MASKED)

    lane = lax.broadcasted_iota(jnp.int32, (1, LANES), 1)
    low_lane = lane < HD
    one = low_lane.astype(BF16)
    masks = (one, 1 - one)

    same = (lax.broadcasted_iota(jnp.int32, (LANES, LANES), 0) < HD) == (
        lax.broadcasted_iota(jnp.int32, (LANES, LANES), 1) < HD
    )
    same = same.astype(F32).astype(BF16)
    longest = [
        jnp.max(dot_nn(ref[...] * ref[...], same), axis=0, keepdims=True) for ref in (q_ref, k_ref)
    ]
    bounded = jnp.max(longest[0] * longest[1]) < SAFE * SAFE

    def attend(shift):
        mixed = [v_ref[...] * mask + (1 - mask) for mask in masks]
        for start in range(0, rows, span):
            keys = start + span
            sums = []
            tops = []
            for head in range(2):
                query = q_ref[start:keys, :] * masks[head]
                scores = dot_nt(query, k_ref[:keys, :]) + allow[start:keys, :keys]
                if shift:
                    top = jnp.max(scores, axis=1, keepdims=True)
                    tops.append(top)
                    scores = scores - top
                probs = jnp.exp(scores).astype(BF16)
                sums.append(dot_nn(probs, mixed[head][:keys]))
            total = pltpu.roll(jnp.where(low_lane, sums[1], sums[0]), HD, 1)
            out = jnp.where(low_lane, sums[0], sums[1]) / total
            o_ref[start:keys, :] = out.astype(BF16)
            lse = jnp.log(total)
            if shift:
                lse += jnp.where(low_lane, tops[0], tops[1])
            lse = lse.T
            lse_ref[0, 0:1, start:keys] = lse[0:1]
            lse_ref[0, 1:2, start:keys] = lse[HD : HD + 1]

    @pl.when(bounded)
    def _():
        attend(False)

    @pl.when(jnp.logical_not(bounded))
    def _():
        attend(True)


def run_attend(ends, qkv, first, count, earlier=None, after=()):
    rows = qkv.shape[0]
    width = qkv.shape[1] // 3
    pairs = width // LANES
    column = lambda shift: pl.BlockSpec((rows, LANES), lambda i: (0, i + shift))
    return call(
        attend_kernel,
        (count,),
        [(ends, SMEM)] + [(qkv, column(first + part * pairs)) for part in range(3)],
        [
            ((rows, width), BF16, column(first)),
            ((pairs, 2, rows), F32, pl.BlockSpec((1, 2, rows), lambda i: (i + first, 0, 0))),
        ],
        after=after,
        reuse=[] if earlier is None else [(earlier[0], 0), (earlier[1], 1)],
        scratch=[pltpu.VMEM((rows, rows), F32)],
        cost=cost(8 * rows * rows * LANES * count, 8 * rows * LANES * count, 2 * rows * rows * count),
        name="attend",
    )


def run_after(half, weights, toffs, mixed, x, small, numbers, after=()):
    rows, width = x.shape
    span = 256

    def kernel(*refs):
        weight, sems = refs[-2:]
        copies, refs = weights.copies(
            refs, width, lambda at, size: weight.at[pl.ds(at, size), :], sems
        )
        mixed_toff, low_toff, mixed_ref, x_ref, bias_ref, gain_ref, shift_ref = refs[:7]
        after_ref, low_ref, turned_ref, mixed_turned_ref = refs[7:11]
        start_all(copies)
        for block in range(width // LANES):
            columns = slice(block * LANES, (block + 1) * LANES)
            store_turned(mixed_turned_ref, mixed_toff, block, half, mixed_ref[:, columns], slice(None))
        wait_all(copies)
        value = x_ref[...].astype(F32) + dot_nn(mixed_ref[...], weight[...]) + bias_ref[...]
        after_ref[...] = value
        hat, _ = norm_stats(value)
        normed = hat * gain_ref[...] + shift_ref[...]
        low_ref[...] = normed.astype(BF16)
        for block in range(width // LANES):
            columns = slice(block * LANES, (block + 1) * LANES)
            store_turned(turned_ref, low_toff, block, half, normed[:, columns], slice(None))

    by_row = pl.BlockSpec((span, width), lambda i: (i, 0))
    by_column = pl.BlockSpec((width, span), lambda i: (0, i))
    return call(
        kernel,
        (rows // span,),
        weights.inputs()
        + [(toff, SMEM) for toff in toffs]
        + [(mixed, by_row), (x, by_row)]
        + [param(small, number, width) for number in numbers],
        [
            ((rows, width), F32, by_row),
            ((rows, width), BF16, by_row),
            ((width, rows), BF16, by_column),
            ((width, rows), BF16, by_column),
        ],
        after=after,
        scratch=[pltpu.VMEM((width, width), BF16), weights.sems()],
        cost=cost(2 * rows * width * width, 14 * rows * width),
        name="after",
    )


def run_feed(up_weights, down_weights, low, turned, dy, dyt, small, first, begin, block, earlier, after=()):
    rows, width = low.shape
    hidden = earlier[0].shape[1] if earlier is not None else block_total(small, width)
    span = 256
    mid = width // 2
    count = block // span
    by_column = lambda size: pl.BlockSpec((size, span), lambda i: (0, i))
    shifted = pl.BlockSpec((rows, span), lambda i: (0, begin // span + i))
    grad = ((2, mid, block), BF16, pl.BlockSpec((2, mid, span), lambda i: (0, 0, i)))

    def kernel(*refs):
        up, down, up_sems, down_sems = refs[-4:]
        step = pl.program_id(0)

        def copies(number):
            columns = pl.ds(pl.multiple_of(number * span, span), span)
            made, rest = up_weights.copies(
                refs,
                span,
                lambda at, size: up.at[pl.ds(at, size), columns],
                up_sems.at[number],
                number * span,
            )
            more, _ = down_weights.copies(
                rest,
                span,
                lambda at, size: down.at[pl.ds(at, size), columns],
                down_sems.at[number],
                number * span,
            )
            return made + more

        @pl.when(step == 0)
        def _():
            for copy in copies(0):
                copy.start()

        @pl.when(step + 1 < count)
        def _():
            for copy in copies(step + 1):
                copy.start()

        for copy in copies(step):
            copy.wait()
        low_ref, turned_ref, dy_ref, dyt_ref, bias_ref, act_ref, du_ref, own_ref, sib_ref, gbias_ref = (
            down_weights.rest(up_weights.rest(refs))[:10]
        )
        columns = pl.ds(pl.multiple_of(step * span, span), span)
        upper = dot_nn(low_ref[...], up[:, columns]) + bias_ref[...]
        grad_act = dot_nn(dy_ref[...], down[:, columns])
        square = (GELU_IN * GELU_CUBE) * (upper * upper)
        tanh = jnp.tanh(upper * (GELU_IN + square))
        share = 0.5 + 0.5 * tanh
        act = upper * share
        slope = share + act * (1.0 - tanh) * (GELU_IN + 3.0 * square)
        act = act.astype(BF16)
        du = (grad_act * slope).astype(BF16)
        act_ref[...] = act
        du_ref[...] = du
        gbias_ref[...] = jnp.sum(du.astype(F32), axis=0, keepdims=True)
        grad_up = dot_nn(turned_ref[...], du).astype(BF16)
        own_ref[0] = grad_up[:mid]
        sib_ref[0] = grad_up[mid:]
        grad_dn = dot_nn(dyt_ref[...], act).astype(BF16)
        own_ref[1] = grad_dn[:mid]
        sib_ref[1] = grad_dn[mid:]

    return call(
        kernel,
        (count,),
        up_weights.inputs()
        + down_weights.inputs()
        + [
            (low, whole((rows, width))),
            (turned, whole((width, rows))),
            (dy, whole((rows, width))),
            (dyt, whole((width, rows))),
            (small, pl.BlockSpec((1, span), lambda i: (0, first // span + i))),
        ],
        [
            ((rows, hidden), BF16, shifted),
            ((rows, hidden), BF16, shifted),
            grad,
            grad,
            ((1, block), F32, by_column(1)),
        ],
        after=after,
        reuse=[] if earlier is None else [(earlier[0], 0), (earlier[1], 1)],
        scratch=[
            pltpu.VMEM((width, block), BF16),
            pltpu.VMEM((width, block), BF16),
            pltpu.SemaphoreType.DMA((count, len(up_weights.plan))),
            pltpu.SemaphoreType.DMA((count, len(down_weights.plan))),
        ],
        cost=cost(8 * rows * width * block, 24 * width * block, rows * block),
        name="feed",
    )


def block_total(small, width):
    return small.shape[1] - 8 * width


class Stream:
    def __init__(self):
        self.parts = []

    def add(self, copies):
        self.parts.append(copies)

    def start(self):
        for copies in self.parts:
            for copy in copies:
                copy.start()

    def wait(self, number):
        for copy in self.parts[number]:
            copy.wait()


def run_output(weights, acts, after_value, small, number, after=()):
    rows, width = after_value.shape
    hidden = acts.shape[1]
    span = 256
    bounds = [0]
    for size, _ in weights:
        bounds.append(bounds[-1] + size)
    by_row = lambda size: pl.BlockSpec((span, size), lambda i: (i, 0))

    def kernel(*refs):
        down = refs[-1 - len(weights)]
        sems = refs[-len(weights) :]
        stream = []
        for index, (size, item) in enumerate(weights):
            columns = slice(bounds[index], bounds[index + 1])
            copies, refs = item.copies(
                refs,
                size,
                lambda at, lines, columns=columns: down.at[pl.ds(at, lines), columns],
                sems[index],
            )
            stream.append(copies)
        act_ref, after_ref, bias_ref, out_ref = refs[:4]
        for copies in stream:
            start_all(copies)
        total = after_ref[...] + bias_ref[...]
        for index, copies in enumerate(stream):
            wait_all(copies)
            columns = slice(bounds[index], bounds[index + 1])
            total += dot_nt(act_ref[:, columns], down[:, columns])
        out_ref[...] = total.astype(BF16)

    (out,) = call(
        kernel,
        (rows // span,),
        [item for _, weight in weights for item in weight.inputs()]
        + [(acts, by_row(hidden)), (after_value, by_row(width)), param(small, number, width)],
        [((rows, width), BF16, by_row(width))],
        after=after,
        scratch=[pltpu.VMEM((width, hidden), BF16)] + [weight.sems() for _, weight in weights],
        cost=cost(2 * rows * width * hidden, 22 * rows * width),
        name="output",
    )
    return out


def run_middle(weights, out_weights, dus, after_value, dy, small, number, turned, after=()):
    rows, width = after_value.shape
    hidden = dus.shape[1]
    part = width
    parts = hidden // part
    span = 256
    mid = width // 2
    places = [
        (item.at(start)) for size, item in weights for start in range(0, size, part)
    ]
    most = max(len(item.plan) for item in places)

    def kernel(*refs):
        du, up, value_in, dy_in, turned_in, out_weight, branch, sems, out_sems, own_sems = refs[-10:]
        stream = Stream()
        for index, item in enumerate(places):
            columns = slice(index * part, (index + 1) * part)
            copies, refs = item.copies(
                refs,
                part,
                lambda at, size, columns=columns: up.at[pl.ds(at, size), columns],
                sems.at[index],
            )
            stream.add(copies)
        more, refs = out_weights.copies(
            refs, width, lambda at, size: out_weight.at[pl.ds(at, size), :], out_sems
        )
        du_ref, after_ref, dy_ref, gain_ref, turned_ref = refs[:5]
        grad_ref, dmix_ref, own_ref, sib_ref, gbias_ref, ggain_ref, gshift_ref = refs[5:12]
        for index in range(parts):
            columns = slice(index * part, (index + 1) * part)
            stream.parts[index].append(
                pltpu.make_async_copy(du_ref.at[:, columns], du.at[:, columns], own_sems.at[index])
            )
        stream.add(
            [
                pltpu.make_async_copy(after_ref, value_in, own_sems.at[parts]),
                pltpu.make_async_copy(dy_ref, dy_in, own_sems.at[parts + 1]),
            ]
        )
        stream.add([pltpu.make_async_copy(turned_ref, turned_in, own_sems.at[parts + 2]), *more])
        stream.start()
        total = None
        for index in range(parts):
            columns = slice(index * part, (index + 1) * part)
            stream.wait(index)
            value = dot_nt(du[:, columns], up[:, columns])
            total = value if total is None else total + value
        stream.wait(parts)
        gain = gain_ref[...]
        sums = [jnp.zeros((1, width), F32)] * 3
        for start in range(0, rows, span):
            lines = slice(start, start + span)
            grad = total[lines]
            hat, scale = norm_stats(value_in[lines, :])
            full = dy_in[lines, :].astype(F32) + norm_back(hat, scale, grad * gain)
            grad_ref[lines, :] = full
            low = full.astype(BF16)
            branch[lines, :] = low
            for index, value in enumerate((low.astype(F32), grad * hat, grad)):
                sums[index] = sums[index] + jnp.sum(value, axis=0, keepdims=True)
        gbias_ref[...], ggain_ref[...], gshift_ref[...] = sums
        stream.wait(parts + 1)
        dmix_ref[...] = dot_nt(branch[...], out_weight[...]).astype(BF16)
        for side in range(2):
            columns = slice(side * (width // 2), (side + 1) * (width // 2))
            value = dot_nn(turned_in[...], branch[:, columns]).astype(BF16)
            own_ref[side] = value[:mid]
            sib_ref[side] = value[mid:]

    grads = ((2, mid, width // 2), BF16, whole((2, mid, width // 2)))
    vector = ((1, width), F32, whole((1, width)))
    full = whole((rows, width))
    return call(
        kernel,
        (1,),
        [item for place in places for item in place.inputs()]
        + out_weights.inputs()
        + [(dus, ANY), (after_value, ANY), (dy, ANY), param(small, number, width), (turned, ANY)],
        [((rows, width), F32, full), ((rows, width), BF16, full), grads, grads] + [vector] * 3,
        after=after,
        scratch=[
            pltpu.VMEM((rows, hidden), BF16),
            pltpu.VMEM((width, hidden), BF16),
            pltpu.VMEM((rows, width), F32),
            pltpu.VMEM((rows, width), BF16),
            pltpu.VMEM((width, rows), BF16),
            pltpu.VMEM((width, width), BF16),
            pltpu.VMEM((rows, width), BF16),
            pltpu.SemaphoreType.DMA((parts, most)),
            out_weights.sems(),
            pltpu.SemaphoreType.DMA((parts + 3,)),
        ],
        cost=cost(8 * rows * width * (hidden + 2 * width), 120 * rows * width),
        name="middle",
    )


def attend_back_kernel(
    ends,
    q_ref,
    k_ref,
    v_ref,
    o_ref,
    do_ref,
    lse_ref,
    dq_ref,
    dk_ref,
    dv_ref,
    gq_ref,
    gv_ref,
    allow,
    total,
):
    rows = q_ref.shape[0]
    span = min(256, rows)

    @pl.when(pl.program_id(0) == 0)
    def _():
        for start in range(0, rows, span):
            query = lax.broadcasted_iota(jnp.int32, (1, rows - start), 1) + start
            first = first_of_row(ends, query)
            key = lax.broadcasted_iota(jnp.int32, (span, rows - start), 0) + start
            allow[start : start + span, start:] = jnp.where(
                (key <= query) & (key >= first), 0.0, MASKED
            )

    lane = lax.broadcasted_iota(jnp.int32, (1, LANES), 1)
    low_lane = lane < HD
    one = low_lane.astype(BF16)
    masks = (one, 1 - one)
    product = (o_ref[...].astype(F32) * do_ref[...].astype(F32)).T
    inner = (
        jnp.sum(product[:HD], axis=0, keepdims=True),
        jnp.sum(product[HD:], axis=0, keepdims=True),
    )
    for start in range(0, rows, span):
        stop = start + span
        grads = []
        for head in range(2):
            keys = k_ref[start:stop, :] * masks[head]
            vals = v_ref[start:stop, :] * masks[head]
            scores = dot_nt(keys, q_ref[start:, :]) + allow[start:stop, start:]
            probs = jnp.exp(scores - lse_ref[0, head : head + 1, start:])
            grad_probs = dot_nt(vals, do_ref[start:, :])
            grad_scores = (probs * (grad_probs - inner[head][:, start:])).astype(BF16)
            grad_vals = dot_nn(probs.astype(BF16), do_ref[start:, :])
            grad_keys = dot_nn(grad_scores, q_ref[start:, :])
            grads.append((grad_keys, grad_vals))
            update = dot_tn(grad_scores, keys)
            if start == 0 and head == 0:
                total[...] = update
            else:
                total[start:, :] += update
        dk_ref[start:stop, :] = jnp.where(low_lane, grads[0][0], grads[1][0]).astype(BF16)
        dv_ref[start:stop, :] = jnp.where(low_lane, grads[0][1], grads[1][1]).astype(BF16)
    grad_query = (total[...] * HD ** (-0.5)).astype(BF16)
    dq_ref[...] = grad_query
    gq_ref[...] = jnp.sum(grad_query.astype(F32), axis=0, keepdims=True)
    gv_ref[...] = jnp.sum(dv_ref[...].astype(F32), axis=0, keepdims=True)


def run_attend_back(ends, qkv, mixed, dmix, lse, first, count, after=()):
    rows, width = mixed.shape
    pairs = width // LANES
    column = lambda shift: pl.BlockSpec((rows, LANES), lambda i: (0, i + shift))
    return call(
        attend_back_kernel,
        (count,),
        [(ends, SMEM)]
        + [(qkv, column(first + part * pairs)) for part in range(3)]
        + [
            (mixed, column(first)),
            (dmix, column(first)),
            (lse, pl.BlockSpec((1, 2, rows), lambda i: (i + first, 0, 0))),
        ],
        [((rows, LANES * count), BF16, column(0))] * 3
        + [((1, LANES * count), F32, pl.BlockSpec((1, LANES), lambda i: (0, i)))] * 2,
        after=after,
        scratch=[pltpu.VMEM((rows, rows), F32), pltpu.VMEM((rows, LANES), F32)],
        cost=cost(
            (80 if first == 0 else 2) * rows * rows * LANES * count, rows * LANES * count
        ),
        name="attend_back",
    )


def project_kernel(turned_ref, dq_ref, dk_ref, dv_ref, own_ref, sib_ref):
    mid = own_ref.shape[1]
    size = dq_ref.shape[1]
    left = jnp.concatenate([dq_ref[...], dk_ref[:, : size // 2]], axis=1)
    right = jnp.concatenate([dk_ref[:, size // 2 :], dv_ref[...]], axis=1)
    for side, columns in enumerate((left, right)):
        own_ref[side] = dot_nn(turned_ref[:mid], columns).astype(BF16)
        sib_ref[side] = dot_nn(turned_ref[mid:], columns).astype(BF16)


def run_project(turned, dq, dk, dv, after=()):
    width, rows = turned.shape
    size = dq.shape[1]
    mid = width // 2
    grad = ((2, mid, 3 * size // 2), BF16, whole((2, mid, 3 * size // 2)))
    return call(
        project_kernel,
        (1,),
        [(turned, whole((width, rows)))] + [(value, whole((rows, size))) for value in (dq, dk, dv)],
        [grad, grad],
        after=after,
        cost=cost(6 * rows * width * size, 14 * rows * size),
        name="project",
    )


def run_input(weights, grads, x, grad_after, small, number, after=()):
    rows, width = x.shape
    span = 256
    size = grads[0][0].shape[1]
    flat = [value for group in grads for value in group]
    count = len(flat)
    by_row = lambda size: pl.BlockSpec((span, size), lambda i: (i, 0))

    def kernel(*refs):
        weight, sems = refs[-2:]
        stream = []
        for part in range(3):
            columns = slice(part * width, (part + 1) * width)
            copies, rest = weights.at(part * width).copies(
                refs,
                width,
                lambda at, lines, columns=columns: weight.at[pl.ds(at, lines), columns],
                sems.at[part],
            )
            stream.append(copies)
        refs = rest
        for copies in stream:
            start_all(copies)
        x_ref, grad_ref, gain_ref, out_ref, ggain_ref, gshift_ref = refs[count : count + 6]
        step = pl.program_id(0)
        total = None
        for part in range(3):
            wait_all(stream[part])
            for group in range(len(grads)):
                begin = part * width + group * size
                value = dot_nt(refs[3 * group + part][...], weight[:, begin : begin + size])
                total = value if total is None else total + value
        hat, scale = norm_stats(x_ref[...].astype(F32))
        accumulate(gshift_ref, jnp.sum(total, axis=0, keepdims=True), step == 0)
        accumulate(ggain_ref, jnp.sum(total * hat, axis=0, keepdims=True), step == 0)
        out_ref[...] = grad_ref[...] + norm_back(hat, scale, total * gain_ref[...])

    vector = ((1, width), F32, whole((1, width)))
    return call(
        kernel,
        (rows // span,),
        weights.inputs()
        + [(value, by_row(size)) for value in flat]
        + [(x, by_row(width)), (grad_after, by_row(width)), param(small, number, width)],
        [((rows, width), F32, by_row(width)), vector, vector],
        after=after,
        scratch=[
            pltpu.VMEM((width, 3 * width), BF16),
            pltpu.SemaphoreType.DMA((3, len(weights.plan))),
        ],
        cost=cost(6 * rows * width * width, 22 * rows * width),
        name="grad_input",
    )


def adamw(weight, first, second, grad, rate, decay):
    first_new = beta_one * first + (1.0 - beta_one) * grad
    second_new = beta_two * second + (1.0 - beta_two) * grad * grad
    first_hat = first_new / (1.0 - beta_one**STEP)
    second_hat = second_new / (1.0 - beta_two**STEP)
    weight_new = weight - rate * (first_hat / (jnp.sqrt(second_hat) + adam_eps) + decay * weight)
    return (weight_new, first_new, second_new)


def run_adam(core, state, groups, span, places, pick, earlier, after=()):
    half = groups[0][0].shape[-2]
    count = len(places)
    table = jnp.array(places, jnp.int32)
    place = pl.BlockSpec((half, span), lambda p, h, c, t: (jnp.bitwise_xor(h, c[0]), t[p]))
    flat = [value for group in groups for value in group]

    def kernel(core_ref, table_ref, w_ref, m_ref, v_ref, *refs):
        w_out, m_out, v_out, grad_ref = refs[-4:]
        for side in range(2):
            mine = refs[side : 2 * len(groups) : 2]
            for block in range(count):

                @pl.when((pl.program_id(1) == side) & (pl.program_id(0) == block))
                def _(mine=mine, block=block):
                    start = 0
                    for value in pick(block, mine):
                        grad_ref[:, start : start + value.shape[1]] = value
                        start += value.shape[1]

        w_out[...], m_out[...], v_out[...] = adamw(
            w_ref[...], m_ref[...], v_ref[...], grad_ref[...].astype(F32), 0.05, 0.1
        )

    moved = 2 * half * count * span
    return call(
        kernel,
        (count, 2),
        [(value, place) for value in state] + [(value, whole(value.shape)) for value in flat],
        [(state[0].shape, F32, place)] * 3,
        after=after,
        reuse=[] if earlier is None else [(value, n) for n, value in enumerate(earlier)],
        prefetch=(core, table),
        scratch=[pltpu.VMEM((half, span), BF16)],
        cost=cost(20 * moved, 26 * moved),
        name="adam",
    )


def run_side(core, jobs, after=(), steps=4):
    counts = [(len(job[0]), len(job[1])) for job in jobs]
    total_in = sum(count[0] for count in counts)

    def kernel(core_ref, *refs):
        ins = refs[:total_in]
        outs = refs[total_in:]
        for job, (have, give) in zip(jobs, counts):
            more = (core_ref,) if "places" in job[2].__code__.co_varnames else ()
            job[2](ins[:have], outs[:give], *more)
            ins = ins[have:]
            outs = outs[give:]

    def spec(block, index):
        return pl.BlockSpec(block, lambda i, c: index(i, c))

    moved = sum(array.size * 2 for job in jobs for array, _, _ in job[0])
    results = call(
        kernel,
        (steps,),
        [(array, spec(block, index)) for job in jobs for array, block, index in job[0]],
        [(shape, dtype, spec(block, index)) for job in jobs for shape, dtype, block, index in job[1]],
        after=after,
        prefetch=(core,),
        cost=cost(0, 2 * moved),
        name="side",
    )
    split = []
    for _, give in counts:
        split.append(results[:give])
        results = results[give:]
    return split


def job_cast(rows, columns, by_core, steps):
    span = rows // steps
    total = sum(size for _, _, size in columns)
    ins = []
    for state, number, size in columns:
        index = lambda i, c, number=number: (c[0] * steps * by_core + i, number)
        ins.append((state, (span, size), index))
    outs = [((rows, total), BF16, (span, total), lambda i, c: (i, 0))]

    def run(have, give):
        start = 0
        for ref, (_, _, size) in zip(have, columns):
            give[0][:, start : start + size] = ref[...].astype(BF16)
            start += size

    return ins, outs, run


def job_join(left, right, steps):
    _, blocks, rows, size = left.shape
    span = rows // steps
    four = lambda i, c: (0, 0, i, 0)
    ins = [(value, (2, blocks, span, size), four) for value in (left, right)]
    outs = [((blocks, 2, rows, size), BF16, (blocks, 2, span, size), four)]

    def run(have, give):
        for side in range(2):
            for block in range(blocks):
                give[0][block, side] = have[0][side, block] + have[1][side, block]

    return ins, outs, run


def job_copy(value, first, rows):
    size = value.shape[1]
    ins = [(value, value.shape, lambda i, c: (0, 0))]
    outs = [((rows, size), value.dtype, (rows, size), lambda i, c: (0, 0))]

    def run(have, give):
        give[0][...] = have[0][first : first + rows, :]

    return ins, outs, run


def job_add(left, right, steps):
    at = left.ndim - 2
    if left.shape[at] == 1:
        same = lambda i, c: (0,) * left.ndim

        def run_whole(have, give):
            give[0][...] = have[0][...] + have[1][...]

        return (
            [(left, left.shape, same), (right, right.shape, same)],
            [(left.shape, left.dtype, left.shape, same)],
            run_whole,
        )
    block = tuple(size // steps if axis == at else size for axis, size in enumerate(left.shape))
    index = lambda i, c: (0,) * at + (i, 0)

    def run(have, give):
        give[0][...] = have[0][...] + have[1][...]

    return [(left, block, index), (right, block, index)], [(left.shape, left.dtype, block, index)], run


def job_pick(own, received, steps):
    at = own.ndim - 2
    block = tuple(size // steps if axis == at else size for axis, size in enumerate(own.shape))
    index = lambda i, c: (0,) * at + (i, 0)

    def run(have, give, places):
        give[0][...] = jnp.where(places[2] == 1, have[0][...], have[1][...])

    return [(own, block, index), (received, block, index)], [(own.shape, own.dtype, block, index)], run


def job_sum(groups, keep, send, steps):
    _, blocks, rows, _ = groups[0][0].shape
    span = rows // steps
    total = sum(own.shape[3] for own, _ in groups)
    four = lambda i, c: (0, 0, i, 0)
    three = lambda i, c: (0, i, 0)
    ins = []
    for own, received in groups:
        size = own.shape[3]
        ins.append((own, (2, blocks, span, size), four))
        if len(received) == 1:
            ins.append((received[0], (2, blocks, span, size), four))
        else:
            ins += [(value, (blocks, span, size), three) for value in received]
    kept = len(keep[0])
    outs = [((2, kept, rows, total), BF16, (2, kept, span, total), four)]
    if len(send) == 1:
        gone = len(send[0])
        outs.append(((2, gone, rows, total), BF16, (2, gone, span, total), four))
    else:
        for side in range(2):
            if send[side]:
                gone = len(send[side])
                outs.append(((gone, rows, total), BF16, (gone, span, total), three))

    def run(have, give):
        start = 0
        for own, received in groups:
            size = own.shape[3]
            columns = slice(start, start + size)
            start += size
            for side in range(2):
                for block in range(blocks):
                    other = have[1][side, block] if len(received) == 1 else have[1 + side][block]
                    value = have[0][side, block] + other
                    if block in keep[side]:
                        give[0][side, keep[side].index(block), :, columns] = value
                    elif len(send) == 1:
                        give[1][side, send[0].index(block), :, columns] = value
                    else:
                        give[1 + side][send[side].index(block), :, columns] = value
            have = have[1 + len(received) :]

    return ins, outs, run


def job_params(rows, shards, small_size):
    ins = []
    for array, row in rows:
        if array.shape[0] == 1:
            ins.append((array, array.shape, lambda i, c: (0, 0)))
        else:
            size = array.shape[1]
            ins.append((array, (16, size), lambda i, c, row=row: (row // 16, 0)))
    shape = (1, shards * small_size)
    outs = [(shape, F32, shape, lambda i, c: (0, 0))]

    def run(have, give, places):
        for number, ref in enumerate(have):
            owner = jnp.bitwise_xor(places[1], number)
            start = pl.multiple_of(owner * small_size, LANES)
            value = ref[0:1, :small_size].astype(BF16).astype(F32)
            give[0][:, pl.ds(start, small_size)] = value

    return ins, outs, run


def job_lay(values):
    total = sum(value.shape[1] for value in values)
    same = lambda i, c: (0, 0)
    ins = [(value, value.shape, same) for value in values]

    def run(have, give):
        start = 0
        for ref in have:
            give[0][:, start : start + ref.shape[1]] = ref[...]
            start += ref.shape[1]

    return ins, [((1, total), F32, (1, total), same)], run


class Links:
    def __init__(self, sizes, shard_rows):
        self.replicas, self.shards = sizes
        dp = lax.axis_index("dp")
        self.shard = lax.axis_index("shard")
        self.core = lax.rem(dp, 2)
        place = dp // 2
        self.inner = (place > 0) & (place < sizes[0] // 2 - 1)
        self.core_arr = jnp.stack([self.core, self.shard, self.inner]).astype(jnp.int32)
        self.rows = shard_rows
        self.half = shard_rows // 2
        self.fast = sizes == (8, 4)

    def swap(self, value):
        return self.across_dp(value, 1)

    def across_dp(self, value, bit):
        return lax.ppermute(value, "dp", [(d, d ^ bit) for d in range(self.replicas)])

    def along_dp(self, value, step):
        hops = ([(0, 1), (3, 2)], [(1, 2), (2, 1)], [(1, 0), (2, 3)])[step]
        pairs = [(2 * a + core, 2 * b + core) for a, b in hops for core in range(2)]
        return lax.ppermute(value, "dp", pairs)

    def across_shard(self, value, bit):
        return lax.ppermute(value, "shard", [(s, s ^ bit) for s in range(self.shards)])

    def turned_offsets(self, around):
        blocks = jnp.arange(2 * self.shards, dtype=jnp.int32)
        owner = blocks // 2
        if around:
            owner = jnp.bitwise_xor(owner, self.shard)
        away = jnp.bitwise_xor(lax.rem(blocks, 2), self.core)
        return away * (self.shards * self.half) + owner * self.half

    def gather(self, half_rows):
        return lax.all_gather(half_rows, "shard", axis=0, tiled=True)

    def gathered(self, mine, behind=None):
        if behind is not None:
            mine, _ = lax.optimization_barrier((mine, behind))
        first = jnp.arange(self.shards, dtype=jnp.int32) * self.rows
        offs = jnp.concatenate([first + self.core * self.half, first + (1 - self.core) * self.half])
        stride = mine.shape[0] // self.shards
        plan = tuple((0, t * stride, self.half, t) for t in range(self.shards)) + tuple(
            (1, t * stride, self.half, self.shards + t) for t in range(self.shards)
        )
        return Weights((mine, self.swap(mine)), plan, offs.astype(jnp.int32))

    def over_dp(self, values):
        groups = [[d for d in range(self.replicas) if d % 2 == c] for c in range(2)]
        return lax.psum(values, "dp", axis_index_groups=groups)


class Gather:
    def __init__(self, links, half_rows, own):
        self.links = links
        self.own = own
        self.by_x = links.across_shard(half_rows, 1)
        self.by_y = links.across_shard(half_rows, 2)

    def jobs(self):
        part = self.links.half // 2
        rest = self.by_x.shape[0] - part
        return [job_copy(self.by_y, 0, part), job_copy(self.by_x, part, rest)]

    def forward(self, results):
        links = self.links
        self.far = (
            links.across_shard(results[0], 1),
            links.across_shard(results[1], 2),
        )
        self.near = (links.swap(self.by_x), links.swap(self.by_y))

    def weights(self):
        links = self.links
        half, rows = links.half, links.rows
        part = half // 2
        far = tuple(links.swap(value) for value in self.far)
        pieces = (self.own, self.by_x, self.by_y, *self.near, *self.far, *far)
        plan = ((0, 0, rows, 0),)
        plan += tuple((n, 0, half, n) for n in range(1, 5))
        plan += tuple((n, 0, part, n) for n in range(5, 9))
        at = lambda bits: jnp.bitwise_xor(links.shard, bits) * rows
        mine = links.core * half
        other = (1 - links.core) * half
        offs = [at(0), at(1) + mine, at(2) + mine, at(1) + other, at(2) + other]
        offs += [at(3) + mine, at(3) + mine + part, at(3) + other, at(3) + other + part]
        return Weights(pieces, plan, jnp.stack(offs).astype(jnp.int32))


LINE, AT_ONCE, EXCHANGE = range(3)


class Reduce:
    def __init__(self, links, way):
        self.links = links
        self.way = way
        self.stage = 0
        self.groups = []

    def add(self, own, sib):
        shape = (2, self.links.shards, self.links.half, own.shape[2])
        self.groups.append((own.reshape(shape), (self.links.swap(sib).reshape(shape),)))
        return self

    def job(self, steps):
        if self.stage > 2:
            own, received = self.groups[0]
            if self.way == LINE and self.stage == 5:
                return job_pick(own, received, steps)
            return job_add(own, received, steps)
        blocks = self.groups[0][0].shape[1]
        odd = lambda block: block % 2 == 1
        late = lambda block: block >= blocks // 2
        goes = [odd, late]
        if blocks == 2:
            goes = [odd, odd]
        if blocks == 1:
            goes = [lambda block: False] * 2
        keep = [[block for block in range(blocks) if not go(block)] for go in goes]
        send = [[block for block in range(blocks) if go(block)] for go in goes]
        return job_sum(self.groups, keep, send, steps)

    def advance(self, results):
        links = self.links
        own = results[0]
        stage = self.stage
        self.stage += 1
        if stage < 2:
            bits = (1, 2) if stage == 0 else (2, 1)
            received = tuple(
                links.across_shard(value, bit) for value, bit in zip(results[1:], bits)
            )
            self.groups = [(own, received)]
            return
        if stage == 2:
            own = own.reshape(2, own.shape[2], own.shape[3])
        if self.way == AT_ONCE:
            self.own = links.over_dp(own)
        elif self.way == LINE and stage < 5:
            self.groups = [(own, links.along_dp(own, stage - 2))]
        elif self.way == EXCHANGE and stage < 4:
            self.groups = [(own, links.across_dp(own, 2 * (stage - 1)))]
        else:
            self.grads = (own, links.swap(own))

    def close(self, behind):
        mine, _ = lax.optimization_barrier((self.own, behind))
        self.grads = (mine, self.links.swap(mine))


class Wide:
    def __init__(self, links, joined):
        self.links = links
        self.shape = joined.shape[1:]
        flat = joined.reshape(-1, joined.shape[3])
        self.own = lax.psum_scatter(flat, "shard", scatter_dimension=0, tiled=True)

    def finish(self):
        self.own = self.links.over_dp(self.own).reshape(self.shape)


class Side:
    def __init__(self, links):
        self.links = links
        self.order = ()

    def jobs(self, jobs, steps=1, after=()):
        results = run_side(self.links.core_arr, jobs, after=(*self.order, *after), steps=steps)
        self.order = (results[0][0],)
        return [result[0] for result in results]

    def reduce(self, reduces, jobs=(), steps=2):
        work = [item.job(steps) for item in reduces] + list(jobs)
        results = run_side(self.links.core_arr, work, after=self.order, steps=steps)
        for item, result in zip(reduces, results):
            item.advance(result)
        self.order = (results[0][0],)
        return [result[0] for result in results[len(reduces) :]]

    def then(self, results):
        self.order = (results[0],)
        return results


def small_parts(small, width, hidden):
    bounds = [width] * 3 + [hidden] + [width] * 5
    parts = []
    start = 0
    for size in bounds:
        parts.append(small[:, start : start + size])
        start += size
    return parts


def body(sizes, *args):
    tokens, cotangent, lengths = args[:3]
    attn_state, mlp_state, small_state = args[3:6], args[6:9], args[9:12]
    rows, width = tokens.shape
    links = Links(sizes, attn_state[0].shape[0])
    half = links.half
    hidden = mlp_state[0].shape[1] // 2
    pairs = width // LANES
    pad = 16
    core_arr = links.core_arr
    around = links.turned_offsets(links.fast)
    side = Side(links)

    ends = jnp.cumsum(lengths[0], dtype=jnp.int32)
    small_own = small_state[0][None]
    small_size = small_own.shape[1]
    (
        BIAS_Q,
        BIAS_V,
        BIAS_O,
        BIAS_UP,
    ) = range(4)
    BIAS_DN, GAIN_ONE, SHIFT_ONE, GAIN_TWO, SHIFT_TWO = range(
        BIAS_UP + hidden // width, BIAS_UP + hidden // width + 5
    )

    def first_job():
        ins = [
            (attn_state[0], (half, 4 * width), lambda i, c: (c[0], 0)),
            (small_own, (1, small_size), lambda i, c: (0, 0)),
        ]
        outs = [((half + pad, 4 * width), BF16, (half + pad, 4 * width), lambda i, c: (0, 0))]

        def job(have, give):
            give[0][:half] = have[0][...].astype(BF16)
            row = have[1][...].astype(BF16)
            give[0][half:, :small_size] = jnp.broadcast_to(row, (pad, small_size))

        return ins, outs, job

    block = hidden // 2
    groups = [[(mlp_state[0], number, block) for number in pair] for pair in ((0, 2), (1, 3))]
    (first_half,) = side.jobs([first_job()])
    if links.fast:
        attn_gather = Gather(links, first_half, None)
    else:
        attn_weights = links.gathered(links.gather(first_half))
    dy, dyt, grad_bias_dn = side.then(run_cot(half, around, ends, cotangent, after=side.order))
    (more_half,) = side.jobs([job_cast(half, groups[1], 1, 4)], steps=4)
    if links.fast:
        (attn_gather.own,) = side.jobs(
            [job_cast(links.rows, [(attn_state[0], 0, 4 * width)], 0, 4)], steps=4
        )
        *copied, feed_half = side.jobs([*attn_gather.jobs(), job_cast(half, groups[0], 1, 1)])
        attn_gather.forward(copied)
    else:
        (feed_half,) = side.jobs([job_cast(half, groups[0], 1, 1)])
    wide = links.gather(feed_half)
    more_wide = links.gather(more_half)
    if links.fast:
        attn_weights = attn_gather.weights()
        rows_of = [
            (small_own, 0),
            (attn_gather.by_x, half),
            (attn_gather.by_y, half),
            (attn_gather.far[1], half // 2),
        ]
        (small,) = side.jobs([job_params(rows_of, links.shards, small_size)])
    else:
        small = attn_weights.pieces[0].reshape(links.shards, half + pad, 4 * width)
        small = small[:, half, :small_size].astype(F32).reshape(1, -1)

    qkv, turned_one = side.then(
        run_qkv(
            half,
            attn_weights,
            around,
            tokens,
            small,
            (BIAS_Q, BIAS_V, GAIN_ONE, SHIFT_ONE),
            after=side.order,
        )
    )
    mixed, lse = side.then(run_attend(ends, qkv, 0, pairs, after=side.order))
    wide = links.gathered(wide, lse)
    side.order += (wide.pieces[0],)
    after, low_two, turned_two, turned_mixed = side.then(
        run_after(
            half,
            attn_weights.at(3 * width),
            (around, around),
            mixed,
            tokens,
            small,
            (BIAS_O, GAIN_TWO, SHIFT_TWO),
            after=side.order,
        )
    )

    passed, grad_bias_up = [None], []
    blocked = lambda value: value.reshape(2, links.shards, half, value.shape[2])

    def feed(start, up_weights, down_weights):
        act, du, own, sib, gbias = run_feed(
            up_weights,
            down_weights,
            low_two,
            turned_two,
            dy,
            dyt,
            small,
            BIAS_UP * width + start,
            start,
            block,
            passed[-1],
            after=side.order,
        )
        side.order = (own,)
        passed.append((act, du))
        grad_bias_up.append(gbias)
        return own, sib

    def unit(way, *grads):
        if links.fast:
            return Reduce(links, way).add(*grads)
        return Wide(links, side.jobs([job_join(blocked(grads[0]), blocked(links.swap(grads[1])), 4)], steps=4)[0])

    def reduce(units, jobs=(), steps=2):
        if links.fast:
            return side.reduce(units, jobs, steps)
        return side.jobs(jobs) if jobs else None

    group_a = feed(0, wide, wide.at(block))
    more_wide = links.gathered(more_wide, grad_bias_up[0])
    unit_a = unit(LINE, *group_a)
    reduce([unit_a], steps=4)
    unit_b = unit(AT_ONCE, *feed(block, more_wide, more_wide.at(block)))
    reduce([unit_a], steps=4)
    (
        grad_after,
        dmix,
        own_out,
        sib_out,
        grad_bias_o,
        grad_gain_two,
        grad_shift_two,
    ) = side.then(
        run_middle(
            [(block, wide), (block, more_wide)],
            attn_weights.at(3 * width),
            passed[-1][1],
            after,
            dy,
            small,
            GAIN_TWO,
            turned_mixed,
            after=side.order,
        )
    )
    if links.fast:
        unit_b.add(own_out, sib_out)
    else:
        unit_e = unit(AT_ONCE, own_out, sib_out)
    reduce([unit_a])
    grads, biases = [], []

    def attend_back(first):
        dq, dk, dv, gq, gv = side.then(
            run_attend_back(ends, qkv, mixed, dmix, lse, first, pairs // 2, after=side.order)
        )
        grads.append((dq, dk, dv))
        biases.append((gq, gv))

    def project(group):
        return side.then(run_project(turned_one, *grads[group], after=side.order))

    attend_back(0)
    reduce([unit_a, unit_b], steps=4)
    unit_c = unit(EXCHANGE, *project(0))
    attend_back(pairs // 2)
    reduce([unit_a, unit_b, unit_c], steps=4)
    unit_d = unit(EXCHANGE, *project(1))
    reduce([unit_c])
    grad_input, grad_gain_one, grad_shift_one = side.then(
        run_input(attn_weights, grads, tokens, grad_after, small, GAIN_ONE, after=side.order)
    )
    small_grads = [biases[0][0], biases[1][0], biases[0][1], biases[1][1], grad_bias_o]
    small_grads += grad_bias_up
    small_grads += [grad_bias_dn, grad_gain_one, grad_shift_one, grad_gain_two, grad_shift_two]
    (grad_small,) = reduce([unit_a, unit_b, unit_c, unit_d], [job_lay(small_grads)])

    def pick_feed(number, arrays):
        return [arrays[0][number, :, :block]]

    def adam_mlp(number, item, earlier):
        return side.then(
            run_adam(
                core_arr,
                mlp_state,
                [item.grads],
                block,
                [number, 2 + number],
                pick_feed,
                earlier,
                after=side.order,
            )
        )

    out_block = width // 2

    def pick_heads(number, arrays):
        left, right = arrays[0][0], arrays[0][1]
        split = out_block // 2
        if number > 2:
            return [arrays[1][number - 3, :, block:]]
        return (
            [left[:, :out_block]],
            [left[:, out_block:], right[:, :split]],
            [right[:, split:]],
        )[number]

    def adam_attn(items, places, earlier):
        return side.then(
            run_adam(
                core_arr,
                attn_state,
                [item.grads for item in items],
                out_block,
                places,
                pick_heads,
                earlier,
                after=side.order,
            )
        )

    def output_now():
        out = run_output(
            [(block, wide.at(block)), (block, more_wide.at(block))],
            passed[-1][0],
            after,
            small,
            BIAS_DN,
            after=side.order,
        )
        side.then([out])
        return out

    if links.fast:
        shard_move = lambda bit: functools.partial(links.across_shard, bit=bit)
        dp_move = lambda bit: functools.partial(links.across_dp, bit=bit)
        moved = links.across_shard(grad_small, 1)

        def step(units, move):
            (total,) = reduce(units, [job_add(grad_small, moved, 2)])
            return total, move(total) if move else None

        mlp_new = adam_mlp(0, unit_a, None)
        grad_small, moved = step([unit_c, unit_d], shard_move(2))
        output = output_now()
        grad_small, moved = step([unit_c, unit_d], links.swap)
        unit_b.close(grad_small)
        attn_new = adam_attn([unit_c], [0, 2, 4], None)
        grad_small, moved = step([unit_d], dp_move(2))
        mlp_new = adam_mlp(1, unit_b, mlp_new)
        grad_small, moved = step([unit_d], dp_move(4))
        attn_new = adam_attn([unit_d, unit_b], [1, 3, 5, 6, 7], attn_new)
        grad_small, _ = step([], None)
    else:
        for item in (unit_a, unit_b, unit_c, unit_d, unit_e):
            item.finish()
        unit_b.own = jnp.concatenate([unit_b.own, unit_e.own], axis=2)
        for item in (unit_a, unit_b, unit_c, unit_d):
            item.grads = (item.own, links.swap(item.own))
        grad_small = lax.psum(grad_small, ("dp", "shard"))
        output = output_now()
        mlp_new = adam_mlp(1, unit_b, adam_mlp(0, unit_a, None))
        attn_new = adam_attn([unit_c], [0, 2, 4], None)
        attn_new = adam_attn([unit_d, unit_b], [1, 3, 5, 6, 7], attn_new)
    grad_small = lax.dynamic_slice_in_dim(grad_small, links.shard * small_size, small_size, 1)[0]
    small_new = adamw(*small_state, grad_small, 0.4, 0.0)
    return (output, grad_input, *attn_new, *mlp_new, *small_new)


def solution(mesh):
    tokens = P(("dp", "shard"), None)
    state = P("shard", None)
    vector = P("shard")
    return jax.shard_map(
        functools.partial(body, (mesh.shape["dp"], mesh.shape["shard"])),
        mesh=mesh,
        in_specs=(tokens,) * 3 + (state,) * 6 + (vector,) * 3,
        out_specs=(tokens,) * 2 + (state,) * 6 + (vector,) * 3,
        check_vma=False,
    )
```

```python
import functools

import jax
import jax.numpy as jnp
from jax import lax
from jax.experimental import pallas as pl
from jax.experimental.pallas import tpu as pltpu
from jax.sharding import PartitionSpec as P

HD = 64
STEP = 10
LANES = 128
MASKED = -1e30
SAFE = 60.0
GELU_IN = 0.7978845608028654
GELU_CUBE = 0.044715

beta_one = 0.9
beta_two = 0.95
adam_eps = 1e-08
norm_eps = 1e-05

F32 = jnp.float32
BF16 = jnp.bfloat16
MIB = 1024 * 1024
VMEM_MIB = 64

ANY = pl.BlockSpec(memory_space=pl.ANY)
SMEM = pl.BlockSpec(memory_space=pltpu.SMEM)


def dot_nn(left, right):
    return lax.dot_general(left, right, (((1,), (0,)), ((), ())), preferred_element_type=F32)


def dot_nt(left, right):
    return lax.dot_general(left, right, (((1,), (1,)), ((), ())), preferred_element_type=F32)


def dot_tn(left, right):
    return lax.dot_general(left, right, (((0,), (0,)), ((), ())), preferred_element_type=F32)


def whole(shape):
    return pl.BlockSpec(shape, lambda *_: (0,) * len(shape))


def call(kernel, grid, ins, outs, after=(), reuse=(), prefetch=(), scratch=(), cost=None, name=None):
    known = len(prefetch) + len(ins)
    idle = [*after, *(array for array, _ in reuse)]

    def run(*refs):
        kernel(*refs[:known], *refs[known + len(idle) :])

    def placed(array, spec):
        if spec is SMEM:
            return array
        return pltpu.with_memory_space_constraint(array, pltpu.HBM)

    return pl.pallas_call(
        run,
        grid_spec=pltpu.PrefetchScalarGridSpec(
            num_scalar_prefetch=len(prefetch),
            grid=grid,
            in_specs=[spec for _, spec in ins] + [ANY] * len(idle),
            out_specs=[spec for _, _, spec in outs],
            scratch_shapes=list(scratch),
        ),
        out_shape=[pltpu.HBM(shape, dtype) for shape, dtype, _ in outs],
        input_output_aliases={
            known + len(after) + number: output for number, (_, output) in enumerate(reuse)
        },
        compiler_params=pltpu.CompilerParams(vmem_limit_bytes=VMEM_MIB * MIB),
        cost_estimate=cost,
        name=name,
    )(*prefetch, *(placed(*item) for item in ins), *(placed(array, ANY) for array in idle))


def param(small, number, width):
    return (small, pl.BlockSpec((1, width), lambda *_: (0, number)))


def cost(flops, moved, exps=0):
    return pl.CostEstimate(flops=int(flops), bytes_accessed=int(moved), transcendentals=int(exps))


def store_turned(turned_ref, toff, block, half, value, columns):
    turned = value.astype(BF16).T
    for part in range(LANES // half):
        offset = pl.multiple_of(toff[block * (LANES // half) + part], half)
        turned_ref[pl.ds(offset, half), columns] = turned[part * half : (part + 1) * half]


def norm_stats(values):
    center = values - jnp.mean(values, axis=-1, keepdims=True)
    spread = jnp.mean(center * center, axis=-1, keepdims=True)
    scale = lax.rsqrt(spread + norm_eps)
    return center * scale, scale


def norm_back(hat, scale, grad_hat):
    mean = jnp.mean(grad_hat, axis=-1, keepdims=True)
    along = jnp.mean(grad_hat * hat, axis=-1, keepdims=True)
    return scale * (grad_hat - mean - hat * along)


def accumulate(ref, value, first):
    @pl.when(first)
    def _():
        ref[...] = value

    @pl.when(jnp.logical_not(first))
    def _():
        ref[...] += value


class Weights:
    def __init__(self, pieces, plan, offs, first=0):
        self.pieces, self.plan, self.offs, self.first = pieces, plan, offs, first

    def at(self, first):
        return Weights(self.pieces, self.plan, self.offs, self.first + first)

    def inputs(self):
        return [(self.offs, SMEM)] + [(piece, ANY) for piece in self.pieces]

    def sems(self):
        return pltpu.SemaphoreType.DMA((len(self.plan),))

    def rest(self, refs):
        return refs[1 + len(self.pieces) :]

    def copies(self, refs, size, target, sems, start=None):
        offs, refs = refs[0], refs[1:]
        columns = slice(self.first, self.first + size)
        if start is not None:
            columns = pl.ds(pl.multiple_of(self.first + start, LANES), size)
        made = []
        for number, (piece, first, rows, index) in enumerate(self.plan):
            offset = pl.multiple_of(offs[index], rows)
            made.append(
                pltpu.make_async_copy(
                    refs[piece].at[pl.ds(first, rows), columns],
                    target(offset, rows),
                    sems.at[number],
                )
            )
        return made, refs[len(self.pieces) :]


def start_all(copies):
    @pl.when(pl.program_id(0) == 0)
    def _():
        for copy in copies:
            copy.start()


def wait_all(copies):
    @pl.when(pl.program_id(0) == 0)
    def _():
        for copy in copies:
            copy.wait()


def cot_kernel(half, toff, ends, cot_ref, dy_ref, turned_ref, bias_ref):
    rows = cot_ref.shape[0]
    place = lax.broadcasted_iota(jnp.int32, (rows, LANES), 0)
    live = (place < ends[ends.shape[0] - 1]).astype(F32)
    for block in range(cot_ref.shape[1] // LANES):
        columns = slice(block * LANES, (block + 1) * LANES)
        value = cot_ref[:, columns].astype(F32) * live
        dy_ref[:, columns] = value.astype(BF16)
        bias_ref[:, columns] = jnp.sum(value, axis=0, keepdims=True)
        store_turned(turned_ref, toff, block, half, value, slice(None))


def run_cot(half, toff, ends, cot, after=()):
    rows, width = cot.shape
    return call(
        functools.partial(cot_kernel, half),
        (1,),
        [(toff, SMEM), (ends, SMEM), (cot, whole(cot.shape))],
        [
            ((rows, width), BF16, whole((rows, width))),
            ((width, rows), BF16, whole((width, rows))),
            ((1, width), F32, whole((1, width))),
        ],
        after=after,
        cost=cost(0, 6 * rows * width),
        name="cotangent",
    )


def run_qkv(half, weights, toff, x, small, numbers, after=()):
    rows, width = x.shape
    span = 256

    def kernel(*refs):
        weight, sems = refs[-2:]
        copies, refs = weights.copies(
            refs, 3 * width, lambda at, size: weight.at[pl.ds(at, size), :], sems
        )
        toff_ref, x_ref, bias_q, bias_v, gain_ref, shift_ref, qkv_ref, turned_ref = refs[:8]
        start_all(copies)
        hat, _ = norm_stats(x_ref[...].astype(F32))
        normed = hat * gain_ref[...] + shift_ref[...]
        for block in range(width // LANES):
            columns = slice(block * LANES, (block + 1) * LANES)
            store_turned(turned_ref, toff_ref, block, half, normed[:, columns], slice(None))
        wait_all(copies)
        low = normed.astype(BF16)
        for part in range(3):
            columns = slice(part * width, (part + 1) * width)
            value = dot_nn(low, weight[:, columns])
            if part == 2:
                value += bias_v[...]
            if part == 0:
                value = (value + bias_q[...]).astype(BF16).astype(F32) * HD ** (-0.5)
            qkv_ref[:, columns] = value.astype(BF16)

    return call(
        kernel,
        (rows // span,),
        weights.inputs()
        + [
            (toff, SMEM),
            (x, pl.BlockSpec((span, width), lambda i: (i, 0))),
        ]
        + [param(small, number, width) for number in numbers],
        [
            ((rows, 3 * width), BF16, pl.BlockSpec((span, 3 * width), lambda i: (i, 0))),
            ((width, rows), BF16, pl.BlockSpec((width, span), lambda i: (0, i))),
        ],
        after=after,
        scratch=[pltpu.VMEM((width, 3 * width), BF16), weights.sems()],
        cost=cost(6 * rows * width * width, 16 * rows * width),
        name="qkv",
    )


def first_of_row(ends, place):
    first = jnp.zeros_like(place)
    for number in range(ends.shape[0]):
        first = jnp.where(place >= ends[number], ends[number], first)
    return first


def attend_kernel(ends, q_ref, k_ref, v_ref, o_ref, lse_ref, allow):
    rows = q_ref.shape[0]
    span = min(256, rows)

    @pl.when(pl.program_id(0) == 0)
    def _():
        for start in range(0, rows, span):
            keys = start + span
            place = lax.broadcasted_iota(jnp.int32, (span, 1), 0) + start
            first = first_of_row(ends, place)
            key = lax.broadcasted_iota(jnp.int32, (span, keys), 1)
            allow[start:keys, :keys] = jnp.where((key <= place) & (key >= first), 0.0, MASKED)

    lane = lax.broadcasted_iota(jnp.int32, (1, LANES), 1)
    low_lane = lane < HD
    one = low_lane.astype(BF16)
    masks = (one, 1 - one)

    same = (lax.broadcasted_iota(jnp.int32, (LANES, LANES), 0) < HD) == (
        lax.broadcasted_iota(jnp.int32, (LANES, LANES), 1) < HD
    )
    same = same.astype(F32).astype(BF16)
    longest = [
        jnp.max(dot_nn(ref[...] * ref[...], same), axis=0, keepdims=True) for ref in (q_ref, k_ref)
    ]
    bounded = jnp.max(longest[0] * longest[1]) < SAFE * SAFE

    def attend(shift):
        mixed = [v_ref[...] * mask + (1 - mask) for mask in masks]
        for start in range(0, rows, span):
            keys = start + span
            sums = []
            tops = []
            for head in range(2):
                query = q_ref[start:keys, :] * masks[head]
                scores = dot_nt(query, k_ref[:keys, :]) + allow[start:keys, :keys]
                if shift:
                    top = jnp.max(scores, axis=1, keepdims=True)
                    tops.append(top)
                    scores = scores - top
                probs = jnp.exp(scores).astype(BF16)
                sums.append(dot_nn(probs, mixed[head][:keys]))
            total = pltpu.roll(jnp.where(low_lane, sums[1], sums[0]), HD, 1)
            out = jnp.where(low_lane, sums[0], sums[1]) / total
            o_ref[start:keys, :] = out.astype(BF16)
            lse = jnp.log(total)
            if shift:
                lse += jnp.where(low_lane, tops[0], tops[1])
            lse = lse.T
            lse_ref[0, 0:1, start:keys] = lse[0:1]
            lse_ref[0, 1:2, start:keys] = lse[HD : HD + 1]

    @pl.when(bounded)
    def _():
        attend(False)

    @pl.when(jnp.logical_not(bounded))
    def _():
        attend(True)


def run_attend(ends, qkv, first, count, earlier=None, after=()):
    rows = qkv.shape[0]
    width = qkv.shape[1] // 3
    pairs = width // LANES
    column = lambda shift: pl.BlockSpec((rows, LANES), lambda i: (0, i + shift))
    return call(
        attend_kernel,
        (count,),
        [(ends, SMEM)] + [(qkv, column(first + part * pairs)) for part in range(3)],
        [
            ((rows, width), BF16, column(first)),
            ((pairs, 2, rows), F32, pl.BlockSpec((1, 2, rows), lambda i: (i + first, 0, 0))),
        ],
        after=after,
        reuse=[] if earlier is None else [(earlier[0], 0), (earlier[1], 1)],
        scratch=[pltpu.VMEM((rows, rows), F32)],
        cost=cost(8 * rows * rows * LANES * count, 8 * rows * LANES * count, 2 * rows * rows * count),
        name="attend",
    )


def run_after(half, weights, toffs, mixed, x, small, numbers, after=()):
    rows, width = x.shape
    span = 256

    def kernel(*refs):
        weight, sems = refs[-2:]
        copies, refs = weights.copies(
            refs, width, lambda at, size: weight.at[pl.ds(at, size), :], sems
        )
        mixed_toff, low_toff, mixed_ref, x_ref, bias_ref, gain_ref, shift_ref = refs[:7]
        after_ref, low_ref, turned_ref, mixed_turned_ref = refs[7:11]
        start_all(copies)
        for block in range(width // LANES):
            columns = slice(block * LANES, (block + 1) * LANES)
            store_turned(mixed_turned_ref, mixed_toff, block, half, mixed_ref[:, columns], slice(None))
        wait_all(copies)
        value = x_ref[...].astype(F32) + dot_nn(mixed_ref[...], weight[...]) + bias_ref[...]
        after_ref[...] = value
        hat, _ = norm_stats(value)
        normed = hat * gain_ref[...] + shift_ref[...]
        low_ref[...] = normed.astype(BF16)
        for block in range(width // LANES):
            columns = slice(block * LANES, (block + 1) * LANES)
            store_turned(turned_ref, low_toff, block, half, normed[:, columns], slice(None))

    by_row = pl.BlockSpec((span, width), lambda i: (i, 0))
    by_column = pl.BlockSpec((width, span), lambda i: (0, i))
    return call(
        kernel,
        (rows // span,),
        weights.inputs()
        + [(toff, SMEM) for toff in toffs]
        + [(mixed, by_row), (x, by_row)]
        + [param(small, number, width) for number in numbers],
        [
            ((rows, width), F32, by_row),
            ((rows, width), BF16, by_row),
            ((width, rows), BF16, by_column),
            ((width, rows), BF16, by_column),
        ],
        after=after,
        scratch=[pltpu.VMEM((width, width), BF16), weights.sems()],
        cost=cost(2 * rows * width * width, 14 * rows * width),
        name="after",
    )


def run_feed(up_weights, down_weights, low, turned, dy, dyt, small, first, begin, block, earlier, after=()):
    rows, width = low.shape
    hidden = earlier[0].shape[1] if earlier is not None else block_total(small, width)
    span = 256
    mid = width // 2
    count = block // span
    by_column = lambda size: pl.BlockSpec((size, span), lambda i: (0, i))
    shifted = pl.BlockSpec((rows, span), lambda i: (0, begin // span + i))
    grad = ((2, mid, block), BF16, pl.BlockSpec((2, mid, span), lambda i: (0, 0, i)))

    def kernel(*refs):
        up, down, up_sems, down_sems = refs[-4:]
        step = pl.program_id(0)

        def copies(number):
            columns = pl.ds(pl.multiple_of(number * span, span), span)
            made, rest = up_weights.copies(
                refs,
                span,
                lambda at, size: up.at[pl.ds(at, size), columns],
                up_sems.at[number],
                number * span,
            )
            more, _ = down_weights.copies(
                rest,
                span,
                lambda at, size: down.at[pl.ds(at, size), columns],
                down_sems.at[number],
                number * span,
            )
            return made + more

        @pl.when(step == 0)
        def _():
            for copy in copies(0):
                copy.start()

        @pl.when(step + 1 < count)
        def _():
            for copy in copies(step + 1):
                copy.start()

        for copy in copies(step):
            copy.wait()
        low_ref, turned_ref, dy_ref, dyt_ref, bias_ref, act_ref, du_ref, own_ref, sib_ref, gbias_ref = (
            down_weights.rest(up_weights.rest(refs))[:10]
        )
        columns = pl.ds(pl.multiple_of(step * span, span), span)
        upper = dot_nn(low_ref[...], up[:, columns]) + bias_ref[...]
        grad_act = dot_nn(dy_ref[...], down[:, columns])
        square = (GELU_IN * GELU_CUBE) * (upper * upper)
        tanh = jnp.tanh(upper * (GELU_IN + square))
        share = 0.5 + 0.5 * tanh
        act = upper * share
        slope = share + act * (1.0 - tanh) * (GELU_IN + 3.0 * square)
        act = act.astype(BF16)
        du = (grad_act * slope).astype(BF16)
        act_ref[...] = act
        du_ref[...] = du
        gbias_ref[...] = jnp.sum(du.astype(F32), axis=0, keepdims=True)
        grad_up = dot_nn(turned_ref[...], du).astype(BF16)
        own_ref[0] = grad_up[:mid]
        sib_ref[0] = grad_up[mid:]
        grad_dn = dot_nn(dyt_ref[...], act).astype(BF16)
        own_ref[1] = grad_dn[:mid]
        sib_ref[1] = grad_dn[mid:]

    return call(
        kernel,
        (count,),
        up_weights.inputs()
        + down_weights.inputs()
        + [
            (low, whole((rows, width))),
            (turned, whole((width, rows))),
            (dy, whole((rows, width))),
            (dyt, whole((width, rows))),
            (small, pl.BlockSpec((1, span), lambda i: (0, first // span + i))),
        ],
        [
            ((rows, hidden), BF16, shifted),
            ((rows, hidden), BF16, shifted),
            grad,
            grad,
            ((1, block), F32, by_column(1)),
        ],
        after=after,
        reuse=[] if earlier is None else [(earlier[0], 0), (earlier[1], 1)],
        scratch=[
            pltpu.VMEM((width, block), BF16),
            pltpu.VMEM((width, block), BF16),
            pltpu.SemaphoreType.DMA((count, len(up_weights.plan))),
            pltpu.SemaphoreType.DMA((count, len(down_weights.plan))),
        ],
        cost=cost(8 * rows * width * block, 24 * width * block, rows * block),
        name="feed",
    )


def block_total(small, width):
    return small.shape[1] - 8 * width


class Stream:
    def __init__(self):
        self.parts = []

    def add(self, copies):
        self.parts.append(copies)

    def start(self):
        for copies in self.parts:
            for copy in copies:
                copy.start()

    def wait(self, number):
        for copy in self.parts[number]:
            copy.wait()


def run_output(weights, acts, after_value, small, number, after=()):
    rows, width = after_value.shape
    hidden = acts.shape[1]
    span = 256
    bounds = [0]
    for size, _ in weights:
        bounds.append(bounds[-1] + size)
    by_row = lambda size: pl.BlockSpec((span, size), lambda i: (i, 0))

    def kernel(*refs):
        down = refs[-1 - len(weights)]
        sems = refs[-len(weights) :]
        stream = []
        for index, (size, item) in enumerate(weights):
            columns = slice(bounds[index], bounds[index + 1])
            copies, refs = item.copies(
                refs,
                size,
                lambda at, lines, columns=columns: down.at[pl.ds(at, lines), columns],
                sems[index],
            )
            stream.append(copies)
        act_ref, after_ref, bias_ref, out_ref = refs[:4]
        for copies in stream:
            start_all(copies)
        total = after_ref[...] + bias_ref[...]
        for index, copies in enumerate(stream):
            wait_all(copies)
            columns = slice(bounds[index], bounds[index + 1])
            total += dot_nt(act_ref[:, columns], down[:, columns])
        out_ref[...] = total.astype(BF16)

    (out,) = call(
        kernel,
        (rows // span,),
        [item for _, weight in weights for item in weight.inputs()]
        + [(acts, by_row(hidden)), (after_value, by_row(width)), param(small, number, width)],
        [((rows, width), BF16, by_row(width))],
        after=after,
        scratch=[pltpu.VMEM((width, hidden), BF16)] + [weight.sems() for _, weight in weights],
        cost=cost(rows * width * hidden // 5, 2 * rows * width),
        name="output",
    )
    return out


def run_middle(weights, out_weights, dus, after_value, dy, small, number, turned, after=()):
    rows, width = after_value.shape
    hidden = dus.shape[1]
    part = width
    parts = hidden // part
    span = 256
    mid = width // 2
    places = [
        (item.at(start)) for size, item in weights for start in range(0, size, part)
    ]
    most = max(len(item.plan) for item in places)

    def kernel(*refs):
        du, up, value_in, dy_in, turned_in, out_weight, branch, sems, out_sems, own_sems = refs[-10:]
        stream = Stream()
        for index, item in enumerate(places):
            columns = slice(index * part, (index + 1) * part)
            copies, refs = item.copies(
                refs,
                part,
                lambda at, size, columns=columns: up.at[pl.ds(at, size), columns],
                sems.at[index],
            )
            stream.add(copies)
        more, refs = out_weights.copies(
            refs, width, lambda at, size: out_weight.at[pl.ds(at, size), :], out_sems
        )
        du_ref, after_ref, dy_ref, gain_ref, turned_ref = refs[:5]
        grad_ref, dmix_ref, own_ref, sib_ref, gbias_ref, ggain_ref, gshift_ref = refs[5:12]
        for index in range(parts):
            columns = slice(index * part, (index + 1) * part)
            stream.parts[index].append(
                pltpu.make_async_copy(du_ref.at[:, columns], du.at[:, columns], own_sems.at[index])
            )
        stream.add(
            [
                pltpu.make_async_copy(after_ref, value_in, own_sems.at[parts]),
                pltpu.make_async_copy(dy_ref, dy_in, own_sems.at[parts + 1]),
            ]
        )
        stream.add([pltpu.make_async_copy(turned_ref, turned_in, own_sems.at[parts + 2]), *more])
        stream.start()
        total = None
        for index in range(parts):
            columns = slice(index * part, (index + 1) * part)
            stream.wait(index)
            value = dot_nt(du[:, columns], up[:, columns])
            total = value if total is None else total + value
        stream.wait(parts)
        gain = gain_ref[...]
        sums = [jnp.zeros((1, width), F32)] * 3
        for start in range(0, rows, span):
            lines = slice(start, start + span)
            grad = total[lines]
            hat, scale = norm_stats(value_in[lines, :])
            full = dy_in[lines, :].astype(F32) + norm_back(hat, scale, grad * gain)
            grad_ref[lines, :] = full
            low = full.astype(BF16)
            branch[lines, :] = low
            for index, value in enumerate((low.astype(F32), grad * hat, grad)):
                sums[index] = sums[index] + jnp.sum(value, axis=0, keepdims=True)
        gbias_ref[...], ggain_ref[...], gshift_ref[...] = sums
        stream.wait(parts + 1)
        dmix_ref[...] = dot_nt(branch[...], out_weight[...]).astype(BF16)
        for side in range(2):
            columns = slice(side * (width // 2), (side + 1) * (width // 2))
            value = dot_nn(turned_in[...], branch[:, columns]).astype(BF16)
            own_ref[side] = value[:mid]
            sib_ref[side] = value[mid:]

    grads = ((2, mid, width // 2), BF16, whole((2, mid, width // 2)))
    vector = ((1, width), F32, whole((1, width)))
    full = whole((rows, width))
    return call(
        kernel,
        (1,),
        [item for place in places for item in place.inputs()]
        + out_weights.inputs()
        + [(dus, ANY), (after_value, ANY), (dy, ANY), param(small, number, width), (turned, ANY)],
        [((rows, width), F32, full), ((rows, width), BF16, full), grads, grads] + [vector] * 3,
        after=after,
        scratch=[
            pltpu.VMEM((rows, hidden), BF16),
            pltpu.VMEM((width, hidden), BF16),
            pltpu.VMEM((rows, width), F32),
            pltpu.VMEM((rows, width), BF16),
            pltpu.VMEM((width, rows), BF16),
            pltpu.VMEM((width, width), BF16),
            pltpu.VMEM((rows, width), BF16),
            pltpu.SemaphoreType.DMA((parts, most)),
            out_weights.sems(),
            pltpu.SemaphoreType.DMA((parts + 3,)),
        ],
        cost=cost(8 * rows * width * (hidden + 2 * width), 120 * rows * width),
        name="middle",
    )


def attend_back_kernel(
    ends,
    q_ref,
    k_ref,
    v_ref,
    o_ref,
    do_ref,
    lse_ref,
    dq_ref,
    dk_ref,
    dv_ref,
    gq_ref,
    gv_ref,
    allow,
    total,
):
    rows = q_ref.shape[0]
    span = min(256, rows)

    @pl.when(pl.program_id(0) == 0)
    def _():
        for start in range(0, rows, span):
            query = lax.broadcasted_iota(jnp.int32, (1, rows - start), 1) + start
            first = first_of_row(ends, query)
            key = lax.broadcasted_iota(jnp.int32, (span, rows - start), 0) + start
            allow[start : start + span, start:] = jnp.where(
                (key <= query) & (key >= first), 0.0, MASKED
            )

    lane = lax.broadcasted_iota(jnp.int32, (1, LANES), 1)
    low_lane = lane < HD
    one = low_lane.astype(BF16)
    masks = (one, 1 - one)
    product = (o_ref[...].astype(F32) * do_ref[...].astype(F32)).T
    inner = (
        jnp.sum(product[:HD], axis=0, keepdims=True),
        jnp.sum(product[HD:], axis=0, keepdims=True),
    )
    for start in range(0, rows, span):
        stop = start + span
        grads = []
        for head in range(2):
            keys = k_ref[start:stop, :] * masks[head]
            vals = v_ref[start:stop, :] * masks[head]
            scores = dot_nt(keys, q_ref[start:, :]) + allow[start:stop, start:]
            probs = jnp.exp(scores - lse_ref[0, head : head + 1, start:])
            grad_probs = dot_nt(vals, do_ref[start:, :])
            grad_scores = (probs * (grad_probs - inner[head][:, start:])).astype(BF16)
            grad_vals = dot_nn(probs.astype(BF16), do_ref[start:, :])
            grad_keys = dot_nn(grad_scores, q_ref[start:, :])
            grads.append((grad_keys, grad_vals))
            update = dot_tn(grad_scores, keys)
            if start == 0 and head == 0:
                total[...] = update
            else:
                total[start:, :] += update
        dk_ref[start:stop, :] = jnp.where(low_lane, grads[0][0], grads[1][0]).astype(BF16)
        dv_ref[start:stop, :] = jnp.where(low_lane, grads[0][1], grads[1][1]).astype(BF16)
    grad_query = (total[...] * HD ** (-0.5)).astype(BF16)
    dq_ref[...] = grad_query
    gq_ref[...] = jnp.sum(grad_query.astype(F32), axis=0, keepdims=True)
    gv_ref[...] = jnp.sum(dv_ref[...].astype(F32), axis=0, keepdims=True)


def run_attend_back(ends, qkv, mixed, dmix, lse, first, count, after=()):
    rows, width = mixed.shape
    pairs = width // LANES
    column = lambda shift: pl.BlockSpec((rows, LANES), lambda i: (0, i + shift))
    return call(
        attend_back_kernel,
        (count,),
        [(ends, SMEM)]
        + [(qkv, column(first + part * pairs)) for part in range(3)]
        + [
            (mixed, column(first)),
            (dmix, column(first)),
            (lse, pl.BlockSpec((1, 2, rows), lambda i: (i + first, 0, 0))),
        ],
        [((rows, LANES * count), BF16, column(0))] * 3
        + [((1, LANES * count), F32, pl.BlockSpec((1, LANES), lambda i: (0, i)))] * 2,
        after=after,
        scratch=[pltpu.VMEM((rows, rows), F32), pltpu.VMEM((rows, LANES), F32)],
        cost=cost(
            (80 if first == 0 else 2) * rows * rows * LANES * count, rows * LANES * count
        ),
        name="attend_back",
    )


def project_kernel(turned_ref, dq_ref, dk_ref, dv_ref, own_ref, sib_ref):
    mid = own_ref.shape[1]
    size = dq_ref.shape[1]
    left = jnp.concatenate([dq_ref[...], dk_ref[:, : size // 2]], axis=1)
    right = jnp.concatenate([dk_ref[:, size // 2 :], dv_ref[...]], axis=1)
    for side, columns in enumerate((left, right)):
        own_ref[side] = dot_nn(turned_ref[:mid], columns).astype(BF16)
        sib_ref[side] = dot_nn(turned_ref[mid:], columns).astype(BF16)


def run_project(turned, dq, dk, dv, after=()):
    width, rows = turned.shape
    size = dq.shape[1]
    mid = width // 2
    grad = ((2, mid, 3 * size // 2), BF16, whole((2, mid, 3 * size // 2)))
    return call(
        project_kernel,
        (1,),
        [(turned, whole((width, rows)))] + [(value, whole((rows, size))) for value in (dq, dk, dv)],
        [grad, grad],
        after=after,
        cost=cost(6 * rows * width * size, 14 * rows * size),
        name="project",
    )


def run_input(weights, grads, x, grad_after, small, number, after=()):
    rows, width = x.shape
    span = 256
    size = grads[0][0].shape[1]
    flat = [value for group in grads for value in group]
    count = len(flat)
    by_row = lambda size: pl.BlockSpec((span, size), lambda i: (i, 0))

    def kernel(*refs):
        weight, sems = refs[-2:]
        stream = []
        for part in range(3):
            columns = slice(part * width, (part + 1) * width)
            copies, rest = weights.at(part * width).copies(
                refs,
                width,
                lambda at, lines, columns=columns: weight.at[pl.ds(at, lines), columns],
                sems.at[part],
            )
            stream.append(copies)
        refs = rest
        for copies in stream:
            start_all(copies)
        x_ref, grad_ref, gain_ref, out_ref, ggain_ref, gshift_ref = refs[count : count + 6]
        step = pl.program_id(0)
        total = None
        for part in range(3):
            wait_all(stream[part])
            for group in range(len(grads)):
                begin = part * width + group * size
                value = dot_nt(refs[3 * group + part][...], weight[:, begin : begin + size])
                total = value if total is None else total + value
        hat, scale = norm_stats(x_ref[...].astype(F32))
        accumulate(gshift_ref, jnp.sum(total, axis=0, keepdims=True), step == 0)
        accumulate(ggain_ref, jnp.sum(total * hat, axis=0, keepdims=True), step == 0)
        out_ref[...] = grad_ref[...] + norm_back(hat, scale, total * gain_ref[...])

    vector = ((1, width), F32, whole((1, width)))
    return call(
        kernel,
        (rows // span,),
        weights.inputs()
        + [(value, by_row(size)) for value in flat]
        + [(x, by_row(width)), (grad_after, by_row(width)), param(small, number, width)],
        [((rows, width), F32, by_row(width)), vector, vector],
        after=after,
        scratch=[
            pltpu.VMEM((width, 3 * width), BF16),
            pltpu.SemaphoreType.DMA((3, len(weights.plan))),
        ],
        cost=cost(6 * rows * width * width, 22 * rows * width),
        name="grad_input",
    )


def adamw(weight, first, second, grad, rate, decay):
    first_new = beta_one * first + (1.0 - beta_one) * grad
    second_new = beta_two * second + (1.0 - beta_two) * grad * grad
    first_hat = first_new / (1.0 - beta_one**STEP)
    second_hat = second_new / (1.0 - beta_two**STEP)
    weight_new = weight - rate * (first_hat / (jnp.sqrt(second_hat) + adam_eps) + decay * weight)
    return (weight_new, first_new, second_new)


def run_adam(core, state, groups, span, places, pick, earlier, after=()):
    half = groups[0][0].shape[-2]
    count = len(places)
    table = jnp.array(places, jnp.int32)
    place = pl.BlockSpec((half, span), lambda p, h, c, t: (jnp.bitwise_xor(h, c[0]), t[p]))
    flat = [value for group in groups for value in group]

    def kernel(core_ref, table_ref, w_ref, m_ref, v_ref, *refs):
        w_out, m_out, v_out, grad_ref = refs[-4:]
        for side in range(2):
            mine = refs[side : 2 * len(groups) : 2]
            for block in range(count):

                @pl.when((pl.program_id(1) == side) & (pl.program_id(0) == block))
                def _(mine=mine, block=block):
                    start = 0
                    for value in pick(block, mine):
                        grad_ref[:, start : start + value.shape[1]] = value
                        start += value.shape[1]

        w_out[...], m_out[...], v_out[...] = adamw(
            w_ref[...], m_ref[...], v_ref[...], grad_ref[...].astype(F32), 0.05, 0.1
        )

    moved = 2 * half * count * span
    return call(
        kernel,
        (count, 2),
        [(value, place) for value in state] + [(value, whole(value.shape)) for value in flat],
        [(state[0].shape, F32, place)] * 3,
        after=after,
        reuse=[] if earlier is None else [(value, n) for n, value in enumerate(earlier)],
        prefetch=(core, table),
        scratch=[pltpu.VMEM((half, span), BF16)],
        cost=cost(2 * moved, 2 * moved),
        name="adam",
    )


def run_side(core, jobs, after=(), steps=4):
    counts = [(len(job[0]), len(job[1])) for job in jobs]
    total_in = sum(count[0] for count in counts)

    def kernel(core_ref, *refs):
        ins = refs[:total_in]
        outs = refs[total_in:]
        for job, (have, give) in zip(jobs, counts):
            more = (core_ref,) if "places" in job[2].__code__.co_varnames else ()
            job[2](ins[:have], outs[:give], *more)
            ins = ins[have:]
            outs = outs[give:]

    def spec(block, index):
        return pl.BlockSpec(block, lambda i, c: index(i, c))

    moved = sum(array.size * 2 for job in jobs for array, _, _ in job[0])
    results = call(
        kernel,
        (steps,),
        [(array, spec(block, index)) for job in jobs for array, block, index in job[0]],
        [(shape, dtype, spec(block, index)) for job in jobs for shape, dtype, block, index in job[1]],
        after=after,
        prefetch=(core,),
        cost=cost(0, 2 * moved),
        name="side",
    )
    split = []
    for _, give in counts:
        split.append(results[:give])
        results = results[give:]
    return split


def job_cast(rows, columns, by_core, steps):
    span = rows // steps
    total = sum(size for _, _, size in columns)
    ins = []
    for state, number, size in columns:
        index = lambda i, c, number=number: (c[0] * steps * by_core + i, number)
        ins.append((state, (span, size), index))
    outs = [((rows, total), BF16, (span, total), lambda i, c: (i, 0))]

    def run(have, give):
        start = 0
        for ref, (_, _, size) in zip(have, columns):
            give[0][:, start : start + size] = ref[...].astype(BF16)
            start += size

    return ins, outs, run


def job_join(left, right, steps, around):
    _, blocks, rows, size = left.shape
    span = rows // steps
    four = lambda i, c: (0, 0, i, 0)
    ins = [(value, (2, blocks, span, size), four) for value in (left, right)]
    outs = [((blocks, 2, rows, size), BF16, (blocks, 2, span, size), four)]

    def run(have, give, places):
        for side in range(2):
            for block in range(blocks):
                owner = jnp.bitwise_xor(places[1], block) if around else block
                give[0][owner, side] = have[0][side, block] + have[1][side, block]

    return ins, outs, run


def job_copy(value, first, rows):
    size = value.shape[1]
    ins = [(value, value.shape, lambda i, c: (0, 0))]
    outs = [((rows, size), value.dtype, (rows, size), lambda i, c: (0, 0))]

    def run(have, give):
        give[0][...] = have[0][first : first + rows, :]

    return ins, outs, run


def job_add(left, right, steps):
    at = left.ndim - 2
    if left.shape[at] == 1:
        same = lambda i, c: (0,) * left.ndim

        def run_whole(have, give):
            give[0][...] = have[0][...] + have[1][...]

        return (
            [(left, left.shape, same), (right, right.shape, same)],
            [(left.shape, left.dtype, left.shape, same)],
            run_whole,
        )
    block = tuple(size // steps if axis == at else size for axis, size in enumerate(left.shape))
    index = lambda i, c: (0,) * at + (i, 0)

    def run(have, give):
        give[0][...] = have[0][...] + have[1][...]

    return [(left, block, index), (right, block, index)], [(left.shape, left.dtype, block, index)], run


def job_pick(own, received, steps):
    at = own.ndim - 2
    block = tuple(size // steps if axis == at else size for axis, size in enumerate(own.shape))
    index = lambda i, c: (0,) * at + (i, 0)

    def run(have, give, places):
        give[0][...] = jnp.where(places[2] == 1, have[0][...], have[1][...])

    return [(own, block, index), (received, block, index)], [(own.shape, own.dtype, block, index)], run


def job_sum(groups, keep, send, steps):
    _, blocks, rows, _ = groups[0][0].shape
    span = rows // steps
    total = sum(own.shape[3] for own, _ in groups)
    four = lambda i, c: (0, 0, i, 0)
    three = lambda i, c: (0, i, 0)
    ins = []
    for own, received in groups:
        size = own.shape[3]
        ins.append((own, (2, blocks, span, size), four))
        if len(received) == 1:
            ins.append((received[0], (2, blocks, span, size), four))
        else:
            ins += [(value, (blocks, span, size), three) for value in received]
    kept = len(keep[0])
    outs = [((2, kept, rows, total), BF16, (2, kept, span, total), four)]
    if len(send) == 1:
        gone = len(send[0])
        outs.append(((2, gone, rows, total), BF16, (2, gone, span, total), four))
    else:
        for side in range(2):
            if send[side]:
                gone = len(send[side])
                outs.append(((gone, rows, total), BF16, (gone, span, total), three))

    def run(have, give):
        start = 0
        for own, received in groups:
            size = own.shape[3]
            columns = slice(start, start + size)
            start += size
            for side in range(2):
                for block in range(blocks):
                    other = have[1][side, block] if len(received) == 1 else have[1 + side][block]
                    value = have[0][side, block] + other
                    if block in keep[side]:
                        give[0][side, keep[side].index(block), :, columns] = value
                    elif len(send) == 1:
                        give[1][side, send[0].index(block), :, columns] = value
                    else:
                        give[1 + side][send[side].index(block), :, columns] = value
            have = have[1 + len(received) :]

    return ins, outs, run


def job_params(rows, shards, small_size):
    ins = []
    for array, row in rows:
        if array.shape[0] == 1:
            ins.append((array, array.shape, lambda i, c: (0, 0)))
        else:
            size = array.shape[1]
            ins.append((array, (16, size), lambda i, c, row=row: (row // 16, 0)))
    shape = (1, shards * small_size)
    outs = [(shape, F32, shape, lambda i, c: (0, 0))]

    def run(have, give, places):
        for number, ref in enumerate(have):
            owner = jnp.bitwise_xor(places[1], number)
            start = pl.multiple_of(owner * small_size, LANES)
            value = ref[0:1, :small_size].astype(BF16).astype(F32)
            give[0][:, pl.ds(start, small_size)] = value

    return ins, outs, run


def job_lay(values):
    total = sum(value.shape[1] for value in values)
    same = lambda i, c: (0, 0)
    ins = [(value, value.shape, same) for value in values]

    def run(have, give):
        start = 0
        for ref in have:
            give[0][:, start : start + ref.shape[1]] = ref[...]
            start += ref.shape[1]

    return ins, [((1, total), F32, (1, total), same)], run


class Links:
    def __init__(self, sizes, shard_rows):
        self.replicas, self.shards = sizes
        dp = lax.axis_index("dp")
        self.shard = lax.axis_index("shard")
        self.core = lax.rem(dp, 2)
        place = dp // 2
        self.inner = (place > 0) & (place < sizes[0] // 2 - 1)
        self.core_arr = jnp.stack([self.core, self.shard, self.inner]).astype(jnp.int32)
        self.rows = shard_rows
        self.half = shard_rows // 2
        self.fast = sizes == (8, 4)

    def swap(self, value):
        return self.across_dp(value, 1)

    def across_dp(self, value, bit):
        return lax.ppermute(value, "dp", [(d, d ^ bit) for d in range(self.replicas)])

    def along_dp(self, value, step):
        hops = ([(0, 1), (3, 2)], [(1, 2), (2, 1)], [(1, 0), (2, 3)])[step]
        pairs = [(2 * a + core, 2 * b + core) for a, b in hops for core in range(2)]
        return lax.ppermute(value, "dp", pairs)

    def across_shard(self, value, bit):
        return lax.ppermute(value, "shard", [(s, s ^ bit) for s in range(self.shards)])

    def turned_offsets(self, around):
        blocks = jnp.arange(2 * self.shards, dtype=jnp.int32)
        owner = blocks // 2
        if around:
            owner = jnp.bitwise_xor(owner, self.shard)
        away = jnp.bitwise_xor(lax.rem(blocks, 2), self.core)
        return away * (self.shards * self.half) + owner * self.half

    def gather(self, half_rows):
        return lax.all_gather(half_rows, "shard", axis=0, tiled=True)

    def gathered(self, mine, behind=None):
        if behind is not None:
            mine, _ = lax.optimization_barrier((mine, behind))
        first = jnp.arange(self.shards, dtype=jnp.int32) * self.rows
        offs = jnp.concatenate([first + self.core * self.half, first + (1 - self.core) * self.half])
        stride = mine.shape[0] // self.shards
        plan = tuple((0, t * stride, self.half, t) for t in range(self.shards)) + tuple(
            (1, t * stride, self.half, self.shards + t) for t in range(self.shards)
        )
        return Weights((mine, self.swap(mine)), plan, offs.astype(jnp.int32))

    def over_dp(self, values):
        groups = [[d for d in range(self.replicas) if d % 2 == c] for c in range(2)]
        return lax.psum(values, "dp", axis_index_groups=groups)


class Gather:
    def __init__(self, links, half_rows, own):
        self.links = links
        self.own = own
        self.by_x = links.across_shard(half_rows, 1)
        self.by_y = links.across_shard(half_rows, 2)

    def jobs(self):
        part = self.links.half // 2
        rest = self.by_x.shape[0] - part
        return [job_copy(self.by_y, 0, part), job_copy(self.by_x, part, rest)]

    def forward(self, results):
        links = self.links
        self.far = (
            links.across_shard(results[0], 1),
            links.across_shard(results[1], 2),
        )
        self.near = (links.swap(self.by_x), links.swap(self.by_y))

    def weights(self):
        links = self.links
        half, rows = links.half, links.rows
        part = half // 2
        far = tuple(links.swap(value) for value in self.far)
        pieces = (self.own, self.by_x, self.by_y, *self.near, *self.far, *far)
        plan = ((0, 0, rows, 0),)
        plan += tuple((n, 0, half, n) for n in range(1, 5))
        plan += tuple((n, 0, part, n) for n in range(5, 9))
        at = lambda bits: jnp.bitwise_xor(links.shard, bits) * rows
        mine = links.core * half
        other = (1 - links.core) * half
        offs = [at(0), at(1) + mine, at(2) + mine, at(1) + other, at(2) + other]
        offs += [at(3) + mine, at(3) + mine + part, at(3) + other, at(3) + other + part]
        return Weights(pieces, plan, jnp.stack(offs).astype(jnp.int32))


LINE, AT_ONCE, EXCHANGE = range(3)


class Reduce:
    def __init__(self, links, way, bits=((1, 2), (2, 1))):
        self.links = links
        self.way = way
        self.bits = bits
        self.stage = 0
        self.groups = []

    def add(self, own, sib):
        shape = (2, self.links.shards, self.links.half, own.shape[2])
        self.groups.append((own.reshape(shape), (self.links.swap(sib).reshape(shape),)))
        return self

    def job(self, steps):
        if self.stage > 2:
            own, received = self.groups[0]
            if self.way == LINE and self.stage == 5:
                return job_pick(own, received, steps)
            return job_add(own, received, steps)
        blocks = self.groups[0][0].shape[1]
        sides = []
        for number in range(2):
            order = self.bits[number % len(self.bits)]
            if blocks == 1:
                sides.append(())
            elif blocks == 2:
                sides.append((1,))
            else:
                sides.append(tuple(block for block in range(blocks) if block & order[0]))
        keep = [[block for block in range(blocks) if block not in gone] for gone in sides]
        send = [list(gone) for gone in sides]
        if len(self.bits) == 1 and blocks > 1:
            send = send[:1]
        return job_sum(self.groups, keep, send, steps)

    def advance(self, results):
        links = self.links
        own = results[0]
        stage = self.stage
        self.stage += 1
        if stage < 2:
            received = tuple(
                links.across_shard(value, order[stage])
                for value, order in zip(results[1:], self.bits)
            )
            self.groups = [(own, received)]
            return
        if stage == 2:
            own = own.reshape(2, own.shape[2], own.shape[3])
        if self.way == AT_ONCE:
            self.own = own
        elif self.way == LINE and stage < 5:
            self.groups = [(own, links.along_dp(own, stage - 2))]
        elif self.way == EXCHANGE and stage < 4:
            self.groups = [(own, links.across_dp(own, 2 * (stage - 1)))]
        else:
            self.grads = (own, links.swap(own))

    def close(self, behind):
        mine, _ = lax.optimization_barrier((self.own, behind))
        self.grads = (mine, self.links.swap(mine))


class Wide:
    def __init__(self, links, joined):
        self.links = links
        self.shape = joined.shape[1:]
        flat = joined.reshape(-1, joined.shape[3])
        self.own = lax.psum_scatter(flat, "shard", scatter_dimension=0, tiled=True)

    def finish(self):
        self.own = self.links.over_dp(self.own).reshape(self.shape)

    def close(self, behind):
        mine, _ = lax.optimization_barrier((self.own, behind))
        self.grads = (mine, self.links.swap(mine))


class Side:
    def __init__(self, links):
        self.links = links
        self.order = ()

    def jobs(self, jobs, steps=1, after=()):
        results = run_side(self.links.core_arr, jobs, after=(*self.order, *after), steps=steps)
        self.order = (results[0][0],)
        return [result[0] for result in results]

    def reduce(self, reduces, jobs=(), steps=2):
        work = [item.job(steps) for item in reduces] + list(jobs)
        results = run_side(self.links.core_arr, work, after=self.order, steps=steps)
        for item, result in zip(reduces, results):
            item.advance(result)
        self.order = (results[0][0],)
        return [result[0] for result in results[len(reduces) :]]

    def then(self, results):
        self.order = (results[0],)
        return results


def small_parts(small, width, hidden):
    bounds = [width] * 3 + [hidden] + [width] * 5
    parts = []
    start = 0
    for size in bounds:
        parts.append(small[:, start : start + size])
        start += size
    return parts


def body(sizes, *args):
    tokens, cotangent, lengths = args[:3]
    attn_state, mlp_state, small_state = args[3:6], args[6:9], args[9:12]
    rows, width = tokens.shape
    links = Links(sizes, attn_state[0].shape[0])
    half = links.half
    hidden = mlp_state[0].shape[1] // 2
    pairs = width // LANES
    pad = 16
    core_arr = links.core_arr
    around = links.turned_offsets(links.fast)
    side = Side(links)

    ends = jnp.cumsum(lengths[0], dtype=jnp.int32)
    small_own = small_state[0][None]
    small_size = small_own.shape[1]
    (
        BIAS_Q,
        BIAS_V,
        BIAS_O,
        BIAS_UP,
    ) = range(4)
    BIAS_DN, GAIN_ONE, SHIFT_ONE, GAIN_TWO, SHIFT_TWO = range(
        BIAS_UP + hidden // width, BIAS_UP + hidden // width + 5
    )

    def first_job():
        ins = [
            (attn_state[0], (half, 4 * width), lambda i, c: (c[0], 0)),
            (small_own, (1, small_size), lambda i, c: (0, 0)),
        ]
        outs = [((half + pad, 4 * width), BF16, (half + pad, 4 * width), lambda i, c: (0, 0))]

        def job(have, give):
            give[0][:half] = have[0][...].astype(BF16)
            row = have[1][...].astype(BF16)
            give[0][half:, :small_size] = jnp.broadcast_to(row, (pad, small_size))

        return ins, outs, job

    block = hidden // 2
    groups = [[(mlp_state[0], number, block) for number in pair] for pair in ((0, 2), (1, 3))]
    (first_half,) = side.jobs([first_job()])
    if links.fast:
        attn_gather = Gather(links, first_half, None)
    else:
        attn_weights = links.gathered(links.gather(first_half))
    dy, dyt, grad_bias_dn = side.then(run_cot(half, around, ends, cotangent, after=side.order))
    (more_half,) = side.jobs([job_cast(half, groups[1], 1, 4)], steps=4)
    if links.fast:
        (attn_gather.own,) = side.jobs(
            [job_cast(links.rows, [(attn_state[0], 0, 4 * width)], 0, 4)], steps=4
        )
        *copied, feed_half = side.jobs([*attn_gather.jobs(), job_cast(half, groups[0], 1, 1)])
        attn_gather.forward(copied)
    else:
        (feed_half,) = side.jobs([job_cast(half, groups[0], 1, 1)])
    wide = links.gather(feed_half)
    more_wide = links.gather(more_half)
    if links.fast:
        attn_weights = attn_gather.weights()
        rows_of = [
            (small_own, 0),
            (attn_gather.by_x, half),
            (attn_gather.by_y, half),
            (attn_gather.far[1], half // 2),
        ]
        (small,) = side.jobs([job_params(rows_of, links.shards, small_size)])
    else:
        small = attn_weights.pieces[0].reshape(links.shards, half + pad, 4 * width)
        small = small[:, half, :small_size].astype(F32).reshape(1, -1)

    qkv, turned_one = side.then(
        run_qkv(
            half,
            attn_weights,
            around,
            tokens,
            small,
            (BIAS_Q, BIAS_V, GAIN_ONE, SHIFT_ONE),
            after=side.order,
        )
    )
    mixed, lse = side.then(run_attend(ends, qkv, 0, pairs, after=side.order))
    wide = links.gathered(wide, lse)
    side.order += (wide.pieces[0],)
    after, low_two, turned_two, turned_mixed = side.then(
        run_after(
            half,
            attn_weights.at(3 * width),
            (around, around),
            mixed,
            tokens,
            small,
            (BIAS_O, GAIN_TWO, SHIFT_TWO),
            after=side.order,
        )
    )

    passed, grad_bias_up = [None], []
    blocked = lambda value: value.reshape(2, links.shards, half, value.shape[2])

    def feed(start, up_weights, down_weights):
        act, du, own, sib, gbias = run_feed(
            up_weights,
            down_weights,
            low_two,
            turned_two,
            dy,
            dyt,
            small,
            BIAS_UP * width + start,
            start,
            block,
            passed[-1],
            after=side.order,
        )
        side.order = (own,)
        passed.append((act, du))
        grad_bias_up.append(gbias)
        return own, sib

    def unit(way, own, sib, bits=((1, 2), (2, 1))):
        if links.fast:
            return Reduce(links, way, bits).add(own, sib)
        return Wide(links, side.jobs([join(own, links.swap(sib))], steps=4)[0])

    def join(own, received):
        return job_join(blocked(own), blocked(received), 4, links.fast)

    def reduce(units, jobs=(), steps=2):
        if links.fast:
            return side.reduce(units, jobs, steps)
        return side.jobs(jobs, steps) if jobs else None

    group_a = feed(0, wide, wide.at(block))
    more_wide = links.gathered(more_wide, grad_bias_up[0])
    unit_a = unit(LINE, *group_a)
    reduce([unit_a], steps=4)
    unit_b = unit(AT_ONCE, *feed(block, more_wide, more_wide.at(block)))
    reduce([unit_a], steps=4)
    (
        grad_after,
        dmix,
        own_out,
        sib_out,
        grad_bias_o,
        grad_gain_two,
        grad_shift_two,
    ) = side.then(
        run_middle(
            [(block, wide), (block, more_wide)],
            attn_weights.at(3 * width),
            passed[-1][1],
            after,
            dy,
            small,
            GAIN_TWO,
            turned_mixed,
            after=side.order,
        )
    )
    received_out = links.swap(sib_out)
    reduce([unit_a, unit_b], steps=4)
    grads, biases = [], []

    def attend_back(first):
        dq, dk, dv, gq, gv = side.then(
            run_attend_back(ends, qkv, mixed, dmix, lse, first, pairs // 2, after=side.order)
        )
        grads.append((dq, dk, dv))
        biases.append((gq, gv))

    def project(group):
        return side.then(run_project(turned_one, *grads[group], after=side.order))

    attend_back(0)
    (joined,) = reduce([unit_a, unit_b], [join(own_out, received_out)], steps=4)
    unit_e = Wide(links, joined)
    unit_c = unit(EXCHANGE, *project(0), ((1, 2),))
    attend_back(pairs // 2)
    if links.fast:
        side.order += (unit_e.own,)
    reduce([unit_a, unit_b, unit_c], steps=4)
    if links.fast:
        unit_b.own, unit_e.own = links.over_dp((unit_b.own, unit_e.own.reshape(unit_e.shape)))
    unit_d = unit(EXCHANGE, *project(1), ((2, 1),))
    grad_input, grad_gain_one, grad_shift_one = side.then(
        run_input(attn_weights, grads, tokens, grad_after, small, GAIN_ONE, after=side.order)
    )
    small_grads = [biases[0][0], biases[1][0], biases[0][1], biases[1][1], grad_bias_o]
    small_grads += grad_bias_up
    small_grads += [grad_bias_dn, grad_gain_one, grad_shift_one, grad_gain_two, grad_shift_two]
    (grad_small,) = reduce([unit_a, unit_c, unit_d], [job_lay(small_grads)])

    def pick_feed(number, arrays):
        return [arrays[0][number]]

    def adam_mlp(number, item, earlier):
        return side.then(
            run_adam(
                core_arr,
                mlp_state,
                [item.grads],
                block,
                [number, 2 + number],
                pick_feed,
                earlier,
                after=side.order,
            )
        )

    out_block = width // 2

    def pick_heads(number, arrays):
        left, right = arrays[0][0], arrays[0][1]
        split = out_block // 2
        if number > 2:
            return [arrays[1][number - 3]]
        return (
            [left[:, :out_block]],
            [left[:, out_block:], right[:, :split]],
            [right[:, split:]],
        )[number]

    def adam_attn(items, places, earlier):
        return side.then(
            run_adam(
                core_arr,
                attn_state,
                [item.grads for item in items],
                out_block,
                places,
                pick_heads,
                earlier,
                after=side.order,
            )
        )

    def output_now():
        out = run_output(
            [(block, wide.at(block)), (block, more_wide.at(block))],
            passed[-1][0],
            after,
            small,
            BIAS_DN,
            after=side.order,
        )
        side.then([out])
        return out

    if links.fast:
        shard_move = lambda bit: functools.partial(links.across_shard, bit=bit)
        dp_move = lambda bit: functools.partial(links.across_dp, bit=bit)
        moved = links.across_shard(grad_small, 1)

        def step(units, move):
            (total,) = reduce(units, [job_add(grad_small, moved, 2)])
            return total, move(total) if move else None

        mlp_new = adam_mlp(0, unit_a, None)
        grad_small, moved = step([unit_c, unit_d], shard_move(2))
        output = output_now()
        grad_small, moved = step([unit_c, unit_d], links.swap)
        unit_b.close(grad_small)
        unit_e.close(grad_small)
        mlp_new = adam_mlp(1, unit_b, mlp_new)
        grad_small, moved = step([unit_c, unit_d], dp_move(2))
        attn_new = adam_attn([unit_c], [0, 2, 4], None)
        grad_small, moved = step([unit_d], dp_move(4))
        attn_new = adam_attn([unit_d, unit_e], [1, 3, 5, 6, 7], attn_new)
        grad_small, _ = step([], None)
    else:
        for item in (unit_a, unit_b, unit_c, unit_d, unit_e):
            item.finish()
            item.close(grad_input)
        grad_small = lax.psum(grad_small, ("dp", "shard"))
        output = output_now()
        mlp_new = adam_mlp(1, unit_b, adam_mlp(0, unit_a, None))
        attn_new = adam_attn([unit_c], [0, 2, 4], None)
        attn_new = adam_attn([unit_d, unit_e], [1, 3, 5, 6, 7], attn_new)
    grad_small = lax.dynamic_slice_in_dim(grad_small, links.shard * small_size, small_size, 1)[0]
    small_new = adamw(*small_state, grad_small, 0.4, 0.0)
    return (output, grad_input, *attn_new, *mlp_new, *small_new)


def solution(mesh):
    tokens = P(("dp", "shard"), None)
    state = P("shard", None)
    vector = P("shard")
    return jax.shard_map(
        functools.partial(body, (mesh.shape["dp"], mesh.shape["shard"])),
        mesh=mesh,
        in_specs=(tokens,) * 3 + (state,) * 6 + (vector,) * 3,
        out_specs=(tokens,) * 2 + (state,) * 6 + (vector,) * 3,
        check_vma=False,
    )
```

```python
import functools

import jax
import jax.numpy as jnp
from jax import lax
from jax.experimental import pallas as pl
from jax.experimental.pallas import tpu as pltpu
from jax.sharding import PartitionSpec as P

HD = 64
STEP = 10
LANES = 128
MASKED = -1e30
SAFE = 60.0
GELU_IN = 0.7978845608028654
GELU_CUBE = 0.044715

beta_one = 0.9
beta_two = 0.95
adam_eps = 1e-08
norm_eps = 1e-05

F32 = jnp.float32
BF16 = jnp.bfloat16
MIB = 1024 * 1024
VMEM_MIB = 64

ANY = pl.BlockSpec(memory_space=pl.ANY)
SMEM = pl.BlockSpec(memory_space=pltpu.SMEM)


def dot_nn(left, right):
    return lax.dot_general(left, right, (((1,), (0,)), ((), ())), preferred_element_type=F32)


def dot_nt(left, right):
    return lax.dot_general(left, right, (((1,), (1,)), ((), ())), preferred_element_type=F32)


def dot_tn(left, right):
    return lax.dot_general(left, right, (((0,), (0,)), ((), ())), preferred_element_type=F32)


def whole(shape):
    return pl.BlockSpec(shape, lambda *_: (0,) * len(shape))


def call(kernel, grid, ins, outs, after=(), reuse=(), prefetch=(), scratch=(), cost=None, name=None):
    known = len(prefetch) + len(ins)
    idle = [*after, *(array for array, _ in reuse)]

    def run(*refs):
        kernel(*refs[:known], *refs[known + len(idle) :])

    def placed(array, spec):
        if spec is SMEM:
            return array
        return pltpu.with_memory_space_constraint(array, pltpu.HBM)

    return pl.pallas_call(
        run,
        grid_spec=pltpu.PrefetchScalarGridSpec(
            num_scalar_prefetch=len(prefetch),
            grid=grid,
            in_specs=[spec for _, spec in ins] + [ANY] * len(idle),
            out_specs=[spec for _, _, spec in outs],
            scratch_shapes=list(scratch),
        ),
        out_shape=[pltpu.HBM(shape, dtype) for shape, dtype, _ in outs],
        input_output_aliases={
            known + len(after) + number: output for number, (_, output) in enumerate(reuse)
        },
        compiler_params=pltpu.CompilerParams(vmem_limit_bytes=VMEM_MIB * MIB),
        cost_estimate=cost,
        name=name,
    )(*prefetch, *(placed(*item) for item in ins), *(placed(array, ANY) for array in idle))


def param(small, number, width):
    return (small, pl.BlockSpec((1, width), lambda *_: (0, number)))


def cost(flops, moved, exps=0):
    return pl.CostEstimate(flops=int(flops), bytes_accessed=int(moved), transcendentals=int(exps))


def store_turned(turned_ref, toff, block, half, value, columns):
    turned = value.astype(BF16).T
    for part in range(LANES // half):
        offset = pl.multiple_of(toff[block * (LANES // half) + part], half)
        turned_ref[pl.ds(offset, half), columns] = turned[part * half : (part + 1) * half]


def norm_stats(values):
    center = values - jnp.mean(values, axis=-1, keepdims=True)
    spread = jnp.mean(center * center, axis=-1, keepdims=True)
    scale = lax.rsqrt(spread + norm_eps)
    return center * scale, scale


def norm_back(hat, scale, grad_hat):
    mean = jnp.mean(grad_hat, axis=-1, keepdims=True)
    along = jnp.mean(grad_hat * hat, axis=-1, keepdims=True)
    return scale * (grad_hat - mean - hat * along)


def accumulate(ref, value, first):
    @pl.when(first)
    def _():
        ref[...] = value

    @pl.when(jnp.logical_not(first))
    def _():
        ref[...] += value


class Weights:
    def __init__(self, pieces, plan, offs, first=0):
        self.pieces, self.plan, self.offs, self.first = pieces, plan, offs, first

    def at(self, first):
        return Weights(self.pieces, self.plan, self.offs, self.first + first)

    def inputs(self):
        return [(self.offs, SMEM)] + [(piece, ANY) for piece in self.pieces]

    def sems(self):
        return pltpu.SemaphoreType.DMA((len(self.plan),))

    def rest(self, refs):
        return refs[1 + len(self.pieces) :]

    def copies(self, refs, size, target, sems, start=None):
        offs, refs = refs[0], refs[1:]
        columns = slice(self.first, self.first + size)
        if start is not None:
            columns = pl.ds(pl.multiple_of(self.first + start, LANES), size)
        made = []
        for number, (piece, first, rows, index) in enumerate(self.plan):
            offset = pl.multiple_of(offs[index], rows)
            made.append(
                pltpu.make_async_copy(
                    refs[piece].at[pl.ds(first, rows), columns],
                    target(offset, rows),
                    sems.at[number],
                )
            )
        return made, refs[len(self.pieces) :]


def start_all(copies):
    @pl.when(pl.program_id(0) == 0)
    def _():
        for copy in copies:
            copy.start()


def wait_all(copies):
    @pl.when(pl.program_id(0) == 0)
    def _():
        for copy in copies:
            copy.wait()


def cot_kernel(half, toff, ends, cot_ref, dy_ref, turned_ref, bias_ref):
    rows = cot_ref.shape[0]
    place = lax.broadcasted_iota(jnp.int32, (rows, LANES), 0)
    live = (place < ends[ends.shape[0] - 1]).astype(F32)
    for block in range(cot_ref.shape[1] // LANES):
        columns = slice(block * LANES, (block + 1) * LANES)
        value = cot_ref[:, columns].astype(F32) * live
        dy_ref[:, columns] = value.astype(BF16)
        bias_ref[:, columns] = jnp.sum(value, axis=0, keepdims=True)
        store_turned(turned_ref, toff, block, half, value, slice(None))


def run_cot(half, toff, ends, cot, after=()):
    rows, width = cot.shape
    return call(
        functools.partial(cot_kernel, half),
        (1,),
        [(toff, SMEM), (ends, SMEM), (cot, whole(cot.shape))],
        [
            ((rows, width), BF16, whole((rows, width))),
            ((width, rows), BF16, whole((width, rows))),
            ((1, width), F32, whole((1, width))),
        ],
        after=after,
        cost=cost(0, 6 * rows * width),
        name="cotangent",
    )


def run_qkv(half, weights, toff, x, small, numbers, after=()):
    rows, width = x.shape
    span = 256

    def kernel(*refs):
        weight, sems = refs[-2:]
        copies, refs = weights.copies(
            refs, 3 * width, lambda at, size: weight.at[pl.ds(at, size), :], sems
        )
        toff_ref, x_ref, bias_q, bias_v, gain_ref, shift_ref, qkv_ref, turned_ref = refs[:8]
        start_all(copies)
        hat, _ = norm_stats(x_ref[...].astype(F32))
        normed = hat * gain_ref[...] + shift_ref[...]
        for block in range(width // LANES):
            columns = slice(block * LANES, (block + 1) * LANES)
            store_turned(turned_ref, toff_ref, block, half, normed[:, columns], slice(None))
        wait_all(copies)
        low = normed.astype(BF16)
        for part in range(3):
            columns = slice(part * width, (part + 1) * width)
            value = dot_nn(low, weight[:, columns])
            if part == 2:
                value += bias_v[...]
            if part == 0:
                value = (value + bias_q[...]).astype(BF16).astype(F32) * HD ** (-0.5)
            qkv_ref[:, columns] = value.astype(BF16)

    return call(
        kernel,
        (rows // span,),
        weights.inputs()
        + [
            (toff, SMEM),
            (x, pl.BlockSpec((span, width), lambda i: (i, 0))),
        ]
        + [param(small, number, width) for number in numbers],
        [
            ((rows, 3 * width), BF16, pl.BlockSpec((span, 3 * width), lambda i: (i, 0))),
            ((width, rows), BF16, pl.BlockSpec((width, span), lambda i: (0, i))),
        ],
        after=after,
        scratch=[pltpu.VMEM((width, 3 * width), BF16), weights.sems()],
        cost=cost(6 * rows * width * width, 16 * rows * width),
        name="qkv",
    )


def first_of_row(ends, place):
    first = jnp.zeros_like(place)
    for number in range(ends.shape[0]):
        first = jnp.where(place >= ends[number], ends[number], first)
    return first


def attend_kernel(ends, q_ref, k_ref, v_ref, o_ref, lse_ref, allow):
    rows = q_ref.shape[0]
    span = min(256, rows)

    @pl.when(pl.program_id(0) == 0)
    def _():
        for start in range(0, rows, span):
            keys = start + span
            place = lax.broadcasted_iota(jnp.int32, (span, 1), 0) + start
            first = first_of_row(ends, place)
            key = lax.broadcasted_iota(jnp.int32, (span, keys), 1)
            allow[start:keys, :keys] = jnp.where((key <= place) & (key >= first), 0.0, MASKED)

    lane = lax.broadcasted_iota(jnp.int32, (1, LANES), 1)
    low_lane = lane < HD
    one = low_lane.astype(BF16)
    masks = (one, 1 - one)

    same = (lax.broadcasted_iota(jnp.int32, (LANES, LANES), 0) < HD) == (
        lax.broadcasted_iota(jnp.int32, (LANES, LANES), 1) < HD
    )
    same = same.astype(F32).astype(BF16)
    longest = [
        jnp.max(dot_nn(ref[...] * ref[...], same), axis=0, keepdims=True) for ref in (q_ref, k_ref)
    ]
    bounded = jnp.max(longest[0] * longest[1]) < SAFE * SAFE

    def attend(shift):
        mixed = [v_ref[...] * mask + (1 - mask) for mask in masks]
        for start in range(0, rows, span):
            keys = start + span
            sums = []
            tops = []
            for head in range(2):
                query = q_ref[start:keys, :] * masks[head]
                scores = dot_nt(query, k_ref[:keys, :]) + allow[start:keys, :keys]
                if shift:
                    top = jnp.max(scores, axis=1, keepdims=True)
                    tops.append(top)
                    scores = scores - top
                probs = jnp.exp(scores).astype(BF16)
                sums.append(dot_nn(probs, mixed[head][:keys]))
            total = pltpu.roll(jnp.where(low_lane, sums[1], sums[0]), HD, 1)
            out = jnp.where(low_lane, sums[0], sums[1]) / total
            o_ref[start:keys, :] = out.astype(BF16)
            lse = jnp.log(total)
            if shift:
                lse += jnp.where(low_lane, tops[0], tops[1])
            lse = lse.T
            lse_ref[0, 0:1, start:keys] = lse[0:1]
            lse_ref[0, 1:2, start:keys] = lse[HD : HD + 1]

    @pl.when(bounded)
    def _():
        attend(False)

    @pl.when(jnp.logical_not(bounded))
    def _():
        attend(True)


def run_attend(ends, qkv, first, count, earlier=None, after=()):
    rows = qkv.shape[0]
    width = qkv.shape[1] // 3
    pairs = width // LANES
    column = lambda shift: pl.BlockSpec((rows, LANES), lambda i: (0, i + shift))
    return call(
        attend_kernel,
        (count,),
        [(ends, SMEM)] + [(qkv, column(first + part * pairs)) for part in range(3)],
        [
            ((rows, width), BF16, column(first)),
            ((pairs, 2, rows), F32, pl.BlockSpec((1, 2, rows), lambda i: (i + first, 0, 0))),
        ],
        after=after,
        reuse=[] if earlier is None else [(earlier[0], 0), (earlier[1], 1)],
        scratch=[pltpu.VMEM((rows, rows), F32)],
        cost=cost(8 * rows * rows * LANES * count, 8 * rows * LANES * count, 2 * rows * rows * count),
        name="attend",
    )


def run_after(half, weights, toffs, mixed, x, small, numbers, after=()):
    rows, width = x.shape
    span = 256

    def kernel(*refs):
        weight, sems = refs[-2:]
        copies, refs = weights.copies(
            refs, width, lambda at, size: weight.at[pl.ds(at, size), :], sems
        )
        mixed_toff, low_toff, mixed_ref, x_ref, bias_ref, gain_ref, shift_ref = refs[:7]
        after_ref, low_ref, turned_ref, mixed_turned_ref = refs[7:11]
        start_all(copies)
        for block in range(width // LANES):
            columns = slice(block * LANES, (block + 1) * LANES)
            store_turned(mixed_turned_ref, mixed_toff, block, half, mixed_ref[:, columns], slice(None))
        wait_all(copies)
        value = x_ref[...].astype(F32) + dot_nn(mixed_ref[...], weight[...]) + bias_ref[...]
        after_ref[...] = value
        hat, _ = norm_stats(value)
        normed = hat * gain_ref[...] + shift_ref[...]
        low_ref[...] = normed.astype(BF16)
        for block in range(width // LANES):
            columns = slice(block * LANES, (block + 1) * LANES)
            store_turned(turned_ref, low_toff, block, half, normed[:, columns], slice(None))

    by_row = pl.BlockSpec((span, width), lambda i: (i, 0))
    by_column = pl.BlockSpec((width, span), lambda i: (0, i))
    return call(
        kernel,
        (rows // span,),
        weights.inputs()
        + [(toff, SMEM) for toff in toffs]
        + [(mixed, by_row), (x, by_row)]
        + [param(small, number, width) for number in numbers],
        [
            ((rows, width), F32, by_row),
            ((rows, width), BF16, by_row),
            ((width, rows), BF16, by_column),
            ((width, rows), BF16, by_column),
        ],
        after=after,
        scratch=[pltpu.VMEM((width, width), BF16), weights.sems()],
        cost=cost(2 * rows * width * width, 14 * rows * width),
        name="after",
    )


def run_feed(up_weights, down_weights, low, turned, dy, dyt, small, first, begin, block, earlier, after=()):
    rows, width = low.shape
    hidden = earlier[0].shape[1] if earlier is not None else block_total(small, width)
    span = 256
    mid = width // 2
    count = block // span
    by_column = lambda size: pl.BlockSpec((size, span), lambda i: (0, i))
    shifted = pl.BlockSpec((rows, span), lambda i: (0, begin // span + i))
    grad = ((2, mid, block), BF16, pl.BlockSpec((2, mid, span), lambda i: (0, 0, i)))

    def kernel(*refs):
        up, down, up_sems, down_sems = refs[-4:]
        step = pl.program_id(0)

        def copies(number):
            columns = pl.ds(pl.multiple_of(number * span, span), span)
            made, rest = up_weights.copies(
                refs,
                span,
                lambda at, size: up.at[pl.ds(at, size), columns],
                up_sems.at[number],
                number * span,
            )
            more, _ = down_weights.copies(
                rest,
                span,
                lambda at, size: down.at[pl.ds(at, size), columns],
                down_sems.at[number],
                number * span,
            )
            return made + more

        @pl.when(step == 0)
        def _():
            for copy in copies(0):
                copy.start()

        @pl.when(step + 1 < count)
        def _():
            for copy in copies(step + 1):
                copy.start()

        for copy in copies(step):
            copy.wait()
        low_ref, turned_ref, dy_ref, dyt_ref, bias_ref, act_ref, du_ref, own_ref, sib_ref, gbias_ref = (
            down_weights.rest(up_weights.rest(refs))[:10]
        )
        columns = pl.ds(pl.multiple_of(step * span, span), span)
        upper = dot_nn(low_ref[...], up[:, columns]) + bias_ref[...]
        grad_act = dot_nn(dy_ref[...], down[:, columns])
        square = (GELU_IN * GELU_CUBE) * (upper * upper)
        tanh = jnp.tanh(upper * (GELU_IN + square))
        share = 0.5 + 0.5 * tanh
        act = upper * share
        slope = share + act * (1.0 - tanh) * (GELU_IN + 3.0 * square)
        act = act.astype(BF16)
        du = (grad_act * slope).astype(BF16)
        act_ref[...] = act
        du_ref[...] = du
        gbias_ref[...] = jnp.sum(du.astype(F32), axis=0, keepdims=True)
        grad_up = dot_nn(turned_ref[...], du).astype(BF16)
        own_ref[0] = grad_up[:mid]
        sib_ref[0] = grad_up[mid:]
        grad_dn = dot_nn(dyt_ref[...], act).astype(BF16)
        own_ref[1] = grad_dn[:mid]
        sib_ref[1] = grad_dn[mid:]

    return call(
        kernel,
        (count,),
        up_weights.inputs()
        + down_weights.inputs()
        + [
            (low, whole((rows, width))),
            (turned, whole((width, rows))),
            (dy, whole((rows, width))),
            (dyt, whole((width, rows))),
            (small, pl.BlockSpec((1, span), lambda i: (0, first // span + i))),
        ],
        [
            ((rows, hidden), BF16, shifted),
            ((rows, hidden), BF16, shifted),
            grad,
            grad,
            ((1, block), F32, by_column(1)),
        ],
        after=after,
        reuse=[] if earlier is None else [(earlier[0], 0), (earlier[1], 1)],
        scratch=[
            pltpu.VMEM((width, block), BF16),
            pltpu.VMEM((width, block), BF16),
            pltpu.SemaphoreType.DMA((count, len(up_weights.plan))),
            pltpu.SemaphoreType.DMA((count, len(down_weights.plan))),
        ],
        cost=cost(8 * rows * width * block, 24 * width * block, rows * block),
        name="feed",
    )


def block_total(small, width):
    return small.shape[1] - 8 * width


class Stream:
    def __init__(self):
        self.parts = []

    def add(self, copies):
        self.parts.append(copies)

    def start(self):
        for copies in self.parts:
            for copy in copies:
                copy.start()

    def wait(self, number):
        for copy in self.parts[number]:
            copy.wait()


def run_output(weights, acts, after_value, small, number, after=()):
    rows, width = after_value.shape
    hidden = acts.shape[1]
    span = 256
    bounds = [0]
    for size, _ in weights:
        bounds.append(bounds[-1] + size)
    by_row = lambda size: pl.BlockSpec((span, size), lambda i: (i, 0))

    def kernel(*refs):
        down = refs[-1 - len(weights)]
        sems = refs[-len(weights) :]
        stream = []
        for index, (size, item) in enumerate(weights):
            columns = slice(bounds[index], bounds[index + 1])
            copies, refs = item.copies(
                refs,
                size,
                lambda at, lines, columns=columns: down.at[pl.ds(at, lines), columns],
                sems[index],
            )
            stream.append(copies)
        act_ref, after_ref, bias_ref, out_ref = refs[:4]
        for copies in stream:
            start_all(copies)
        total = after_ref[...] + bias_ref[...]
        for index, copies in enumerate(stream):
            wait_all(copies)
            columns = slice(bounds[index], bounds[index + 1])
            total += dot_nt(act_ref[:, columns], down[:, columns])
        out_ref[...] = total.astype(BF16)

    (out,) = call(
        kernel,
        (rows // span,),
        [item for _, weight in weights for item in weight.inputs()]
        + [(acts, by_row(hidden)), (after_value, by_row(width)), param(small, number, width)],
        [((rows, width), BF16, by_row(width))],
        after=after,
        scratch=[pltpu.VMEM((width, hidden), BF16)] + [weight.sems() for _, weight in weights],
        cost=cost(rows * width * hidden // 5, 2 * rows * width),
        name="output",
    )
    return out


def run_middle(weights, out_weights, dus, after_value, dy, small, number, turned, after=()):
    rows, width = after_value.shape
    hidden = dus.shape[1]
    part = width
    parts = hidden // part
    span = 256
    mid = width // 2
    places = [
        (item.at(start)) for size, item in weights for start in range(0, size, part)
    ]
    most = max(len(item.plan) for item in places)

    def kernel(*refs):
        du, up, value_in, dy_in, turned_in, out_weight, branch, sems, out_sems, own_sems = refs[-10:]
        stream = Stream()
        for index, item in enumerate(places):
            columns = slice(index * part, (index + 1) * part)
            copies, refs = item.copies(
                refs,
                part,
                lambda at, size, columns=columns: up.at[pl.ds(at, size), columns],
                sems.at[index],
            )
            stream.add(copies)
        more, refs = out_weights.copies(
            refs, width, lambda at, size: out_weight.at[pl.ds(at, size), :], out_sems
        )
        du_ref, after_ref, dy_ref, gain_ref, turned_ref = refs[:5]
        grad_ref, dmix_ref, own_ref, sib_ref, gbias_ref, ggain_ref, gshift_ref = refs[5:12]
        for index in range(parts):
            columns = slice(index * part, (index + 1) * part)
            stream.parts[index].append(
                pltpu.make_async_copy(du_ref.at[:, columns], du.at[:, columns], own_sems.at[index])
            )
        stream.add(
            [
                pltpu.make_async_copy(after_ref, value_in, own_sems.at[parts]),
                pltpu.make_async_copy(dy_ref, dy_in, own_sems.at[parts + 1]),
            ]
        )
        stream.add([pltpu.make_async_copy(turned_ref, turned_in, own_sems.at[parts + 2]), *more])
        stream.start()
        total = None
        for index in range(parts):
            columns = slice(index * part, (index + 1) * part)
            stream.wait(index)
            value = dot_nt(du[:, columns], up[:, columns])
            total = value if total is None else total + value
        stream.wait(parts)
        gain = gain_ref[...]
        sums = [jnp.zeros((1, width), F32)] * 3
        for start in range(0, rows, span):
            lines = slice(start, start + span)
            grad = total[lines]
            hat, scale = norm_stats(value_in[lines, :])
            full = dy_in[lines, :].astype(F32) + norm_back(hat, scale, grad * gain)
            grad_ref[lines, :] = full
            low = full.astype(BF16)
            branch[lines, :] = low
            for index, value in enumerate((low.astype(F32), grad * hat, grad)):
                sums[index] = sums[index] + jnp.sum(value, axis=0, keepdims=True)
        gbias_ref[...], ggain_ref[...], gshift_ref[...] = sums
        stream.wait(parts + 1)
        dmix_ref[...] = dot_nt(branch[...], out_weight[...]).astype(BF16)
        for side in range(2):
            columns = slice(side * (width // 2), (side + 1) * (width // 2))
            value = dot_nn(turned_in[...], branch[:, columns]).astype(BF16)
            own_ref[side] = value[:mid]
            sib_ref[side] = value[mid:]

    grads = ((2, mid, width // 2), BF16, whole((2, mid, width // 2)))
    vector = ((1, width), F32, whole((1, width)))
    full = whole((rows, width))
    return call(
        kernel,
        (1,),
        [item for place in places for item in place.inputs()]
        + out_weights.inputs()
        + [(dus, ANY), (after_value, ANY), (dy, ANY), param(small, number, width), (turned, ANY)],
        [((rows, width), F32, full), ((rows, width), BF16, full), grads, grads] + [vector] * 3,
        after=after,
        scratch=[
            pltpu.VMEM((rows, hidden), BF16),
            pltpu.VMEM((width, hidden), BF16),
            pltpu.VMEM((rows, width), F32),
            pltpu.VMEM((rows, width), BF16),
            pltpu.VMEM((width, rows), BF16),
            pltpu.VMEM((width, width), BF16),
            pltpu.VMEM((rows, width), BF16),
            pltpu.SemaphoreType.DMA((parts, most)),
            out_weights.sems(),
            pltpu.SemaphoreType.DMA((parts + 3,)),
        ],
        cost=cost(8 * rows * width * (hidden + 2 * width), 120 * rows * width),
        name="middle",
    )


def attend_back_kernel(
    ends,
    q_ref,
    k_ref,
    v_ref,
    o_ref,
    do_ref,
    lse_ref,
    dq_ref,
    dk_ref,
    dv_ref,
    gq_ref,
    gv_ref,
    allow,
    total,
):
    rows = q_ref.shape[0]
    span = min(256, rows)

    @pl.when(pl.program_id(0) == 0)
    def _():
        for start in range(0, rows, span):
            query = lax.broadcasted_iota(jnp.int32, (1, rows - start), 1) + start
            first = first_of_row(ends, query)
            key = lax.broadcasted_iota(jnp.int32, (span, rows - start), 0) + start
            allow[start : start + span, start:] = jnp.where(
                (key <= query) & (key >= first), 0.0, MASKED
            )

    lane = lax.broadcasted_iota(jnp.int32, (1, LANES), 1)
    low_lane = lane < HD
    one = low_lane.astype(BF16)
    masks = (one, 1 - one)
    product = (o_ref[...].astype(F32) * do_ref[...].astype(F32)).T
    inner = (
        jnp.sum(product[:HD], axis=0, keepdims=True),
        jnp.sum(product[HD:], axis=0, keepdims=True),
    )
    for start in range(0, rows, span):
        stop = start + span
        grads = []
        for head in range(2):
            keys = k_ref[start:stop, :] * masks[head]
            vals = v_ref[start:stop, :] * masks[head]
            scores = dot_nt(keys, q_ref[start:, :]) + allow[start:stop, start:]
            probs = jnp.exp(scores - lse_ref[0, head : head + 1, start:])
            grad_probs = dot_nt(vals, do_ref[start:, :])
            grad_scores = (probs * (grad_probs - inner[head][:, start:])).astype(BF16)
            grad_vals = dot_nn(probs.astype(BF16), do_ref[start:, :])
            grad_keys = dot_nn(grad_scores, q_ref[start:, :])
            grads.append((grad_keys, grad_vals))
            update = dot_tn(grad_scores, keys)
            if start == 0 and head == 0:
                total[...] = update
            else:
                total[start:, :] += update
        dk_ref[start:stop, :] = jnp.where(low_lane, grads[0][0], grads[1][0]).astype(BF16)
        dv_ref[start:stop, :] = jnp.where(low_lane, grads[0][1], grads[1][1]).astype(BF16)
    grad_query = (total[...] * HD ** (-0.5)).astype(BF16)
    dq_ref[...] = grad_query
    gq_ref[...] = jnp.sum(grad_query.astype(F32), axis=0, keepdims=True)
    gv_ref[...] = jnp.sum(dv_ref[...].astype(F32), axis=0, keepdims=True)


def run_attend_back(ends, qkv, mixed, dmix, lse, first, count, after=()):
    rows, width = mixed.shape
    pairs = width // LANES
    column = lambda shift: pl.BlockSpec((rows, LANES), lambda i: (0, i + shift))
    return call(
        attend_back_kernel,
        (count,),
        [(ends, SMEM)]
        + [(qkv, column(first + part * pairs)) for part in range(3)]
        + [
            (mixed, column(first)),
            (dmix, column(first)),
            (lse, pl.BlockSpec((1, 2, rows), lambda i: (i + first, 0, 0))),
        ],
        [((rows, LANES * count), BF16, column(0))] * 3
        + [((1, LANES * count), F32, pl.BlockSpec((1, LANES), lambda i: (0, i)))] * 2,
        after=after,
        scratch=[pltpu.VMEM((rows, rows), F32), pltpu.VMEM((rows, LANES), F32)],
        cost=cost(
            80 * rows * rows * LANES * count, rows * LANES * count
        ),
        name="attend_back",
    )


def project_kernel(turned_ref, dq_ref, dk_ref, dv_ref, own_ref, sib_ref):
    mid = own_ref.shape[1]
    size = dq_ref.shape[1]
    left = jnp.concatenate([dq_ref[...], dk_ref[:, : size // 2]], axis=1)
    right = jnp.concatenate([dk_ref[:, size // 2 :], dv_ref[...]], axis=1)
    for side, columns in enumerate((left, right)):
        own_ref[side] = dot_nn(turned_ref[:mid], columns).astype(BF16)
        sib_ref[side] = dot_nn(turned_ref[mid:], columns).astype(BF16)


def run_project(turned, dq, dk, dv, after=()):
    width, rows = turned.shape
    size = dq.shape[1]
    mid = width // 2
    grad = ((2, mid, 3 * size // 2), BF16, whole((2, mid, 3 * size // 2)))
    return call(
        project_kernel,
        (1,),
        [(turned, whole((width, rows)))] + [(value, whole((rows, size))) for value in (dq, dk, dv)],
        [grad, grad],
        after=after,
        cost=cost(6 * rows * width * size, 14 * rows * size),
        name="project",
    )


def run_input(weights, grads, x, grad_after, small, number, after=()):
    rows, width = x.shape
    span = 256
    size = grads[0][0].shape[1]
    flat = [value for group in grads for value in group]
    count = len(flat)
    by_row = lambda size: pl.BlockSpec((span, size), lambda i: (i, 0))

    def kernel(*refs):
        weight, sems = refs[-2:]
        stream = []
        for part in range(3):
            columns = slice(part * width, (part + 1) * width)
            copies, rest = weights.at(part * width).copies(
                refs,
                width,
                lambda at, lines, columns=columns: weight.at[pl.ds(at, lines), columns],
                sems.at[part],
            )
            stream.append(copies)
        refs = rest
        for copies in stream:
            start_all(copies)
        x_ref, grad_ref, gain_ref, out_ref, ggain_ref, gshift_ref = refs[count : count + 6]
        step = pl.program_id(0)
        total = None
        for part in range(3):
            wait_all(stream[part])
            for group in range(len(grads)):
                begin = part * width + group * size
                value = dot_nt(refs[3 * group + part][...], weight[:, begin : begin + size])
                total = value if total is None else total + value
        hat, scale = norm_stats(x_ref[...].astype(F32))
        accumulate(gshift_ref, jnp.sum(total, axis=0, keepdims=True), step == 0)
        accumulate(ggain_ref, jnp.sum(total * hat, axis=0, keepdims=True), step == 0)
        out_ref[...] = grad_ref[...] + norm_back(hat, scale, total * gain_ref[...])

    vector = ((1, width), F32, whole((1, width)))
    return call(
        kernel,
        (rows // span,),
        weights.inputs()
        + [(value, by_row(size)) for value in flat]
        + [(x, by_row(width)), (grad_after, by_row(width)), param(small, number, width)],
        [((rows, width), F32, by_row(width)), vector, vector],
        after=after,
        scratch=[
            pltpu.VMEM((width, 3 * width), BF16),
            pltpu.SemaphoreType.DMA((3, len(weights.plan))),
        ],
        cost=cost(24 * rows * width * width, 88 * rows * width),
        name="grad_input",
    )


def adamw(weight, first, second, grad, rate, decay):
    first_new = beta_one * first + (1.0 - beta_one) * grad
    second_new = beta_two * second + (1.0 - beta_two) * grad * grad
    first_hat = first_new / (1.0 - beta_one**STEP)
    second_hat = second_new / (1.0 - beta_two**STEP)
    weight_new = weight - rate * (first_hat / (jnp.sqrt(second_hat) + adam_eps) + decay * weight)
    return (weight_new, first_new, second_new)


def run_adam(core, state, groups, span, places, pick, earlier, after=()):
    half = groups[0][0].shape[-2]
    count = len(places)
    table = jnp.array(places, jnp.int32)
    place = pl.BlockSpec((half, span), lambda p, h, c, t: (jnp.bitwise_xor(h, c[0]), t[p]))
    flat = [value for group in groups for value in group]

    def kernel(core_ref, table_ref, w_ref, m_ref, v_ref, *refs):
        w_out, m_out, v_out, grad_ref = refs[-4:]
        for side in range(2):
            mine = refs[side : 2 * len(groups) : 2]
            for block in range(count):

                @pl.when((pl.program_id(1) == side) & (pl.program_id(0) == block))
                def _(mine=mine, block=block):
                    start = 0
                    for value in pick(block, mine):
                        grad_ref[:, start : start + value.shape[1]] = value
                        start += value.shape[1]

        w_out[...], m_out[...], v_out[...] = adamw(
            w_ref[...], m_ref[...], v_ref[...], grad_ref[...].astype(F32), 0.05, 0.1
        )

    moved = 2 * half * count * span
    return call(
        kernel,
        (count, 2),
        [(value, place) for value in state] + [(value, whole(value.shape)) for value in flat],
        [(state[0].shape, F32, place)] * 3,
        after=after,
        reuse=[] if earlier is None else [(value, n) for n, value in enumerate(earlier)],
        prefetch=(core, table),
        scratch=[pltpu.VMEM((half, span), BF16)],
        cost=cost(2 * moved, 2 * moved),
        name="adam",
    )


def run_side(core, jobs, after=(), steps=4):
    counts = [(len(job[0]), len(job[1])) for job in jobs]
    total_in = sum(count[0] for count in counts)

    def kernel(core_ref, *refs):
        ins = refs[:total_in]
        outs = refs[total_in:]
        for job, (have, give) in zip(jobs, counts):
            more = (core_ref,) if "places" in job[2].__code__.co_varnames else ()
            job[2](ins[:have], outs[:give], *more)
            ins = ins[have:]
            outs = outs[give:]

    def spec(block, index):
        return pl.BlockSpec(block, lambda i, c: index(i, c))

    moved = sum(array.size * 2 for job in jobs for array, _, _ in job[0])
    results = call(
        kernel,
        (steps,),
        [(array, spec(block, index)) for job in jobs for array, block, index in job[0]],
        [(shape, dtype, spec(block, index)) for job in jobs for shape, dtype, block, index in job[1]],
        after=after,
        prefetch=(core,),
        cost=cost(0, 2 * moved),
        name="side",
    )
    split = []
    for _, give in counts:
        split.append(results[:give])
        results = results[give:]
    return split


def job_cast(rows, columns, by_core, steps):
    span = rows // steps
    total = sum(size for _, _, size in columns)
    ins = []
    for state, number, size in columns:
        index = lambda i, c, number=number: (c[0] * steps * by_core + i, number)
        ins.append((state, (span, size), index))
    outs = [((rows, total), BF16, (span, total), lambda i, c: (i, 0))]

    def run(have, give):
        start = 0
        for ref, (_, _, size) in zip(have, columns):
            give[0][:, start : start + size] = ref[...].astype(BF16)
            start += size

    return ins, outs, run


def job_join(left, right, steps, around):
    _, blocks, rows, size = left.shape
    span = rows // steps
    four = lambda i, c: (0, 0, i, 0)
    ins = [(value, (2, blocks, span, size), four) for value in (left, right)]
    outs = [((blocks, 2, rows, size), BF16, (blocks, 2, span, size), four)]

    def run(have, give, places):
        for side in range(2):
            for block in range(blocks):
                owner = jnp.bitwise_xor(places[1], block) if around else block
                give[0][owner, side] = have[0][side, block] + have[1][side, block]

    return ins, outs, run


def job_copy(value, first, rows):
    size = value.shape[1]
    ins = [(value, value.shape, lambda i, c: (0, 0))]
    outs = [((rows, size), value.dtype, (rows, size), lambda i, c: (0, 0))]

    def run(have, give):
        give[0][...] = have[0][first : first + rows, :]

    return ins, outs, run


def job_add(left, right, steps):
    at = left.ndim - 2
    if left.shape[at] == 1:
        same = lambda i, c: (0,) * left.ndim

        def run_whole(have, give):
            give[0][...] = have[0][...] + have[1][...]

        return (
            [(left, left.shape, same), (right, right.shape, same)],
            [(left.shape, left.dtype, left.shape, same)],
            run_whole,
        )
    block = tuple(size // steps if axis == at else size for axis, size in enumerate(left.shape))
    index = lambda i, c: (0,) * at + (i, 0)

    def run(have, give):
        give[0][...] = have[0][...] + have[1][...]

    return [(left, block, index), (right, block, index)], [(left.shape, left.dtype, block, index)], run


def job_pick(own, received, steps):
    at = own.ndim - 2
    block = tuple(size // steps if axis == at else size for axis, size in enumerate(own.shape))
    index = lambda i, c: (0,) * at + (i, 0)

    def run(have, give, places):
        give[0][...] = jnp.where(places[2] == 1, have[0][...], have[1][...])

    return [(own, block, index), (received, block, index)], [(own.shape, own.dtype, block, index)], run


def job_sum(groups, keep, send, steps):
    _, blocks, rows, _ = groups[0][0].shape
    span = rows // steps
    total = sum(own.shape[3] for own, _ in groups)
    four = lambda i, c: (0, 0, i, 0)
    three = lambda i, c: (0, i, 0)
    ins = []
    for own, received in groups:
        size = own.shape[3]
        ins.append((own, (2, blocks, span, size), four))
        if len(received) == 1:
            ins.append((received[0], (2, blocks, span, size), four))
        else:
            ins += [(value, (blocks, span, size), three) for value in received]
    kept = len(keep[0])
    outs = [((2, kept, rows, total), BF16, (2, kept, span, total), four)]
    if len(send) == 1:
        gone = len(send[0])
        outs.append(((2, gone, rows, total), BF16, (2, gone, span, total), four))
    else:
        for side in range(2):
            if send[side]:
                gone = len(send[side])
                outs.append(((gone, rows, total), BF16, (gone, span, total), three))

    def run(have, give):
        start = 0
        for own, received in groups:
            size = own.shape[3]
            columns = slice(start, start + size)
            start += size
            for side in range(2):
                for block in range(blocks):
                    other = have[1][side, block] if len(received) == 1 else have[1 + side][block]
                    value = have[0][side, block] + other
                    if block in keep[side]:
                        give[0][side, keep[side].index(block), :, columns] = value
                    elif len(send) == 1:
                        give[1][side, send[0].index(block), :, columns] = value
                    else:
                        give[1 + side][send[side].index(block), :, columns] = value
            have = have[1 + len(received) :]

    return ins, outs, run


def job_params(rows, shards, small_size):
    ins = []
    for array, row in rows:
        if array.shape[0] == 1:
            ins.append((array, array.shape, lambda i, c: (0, 0)))
        else:
            size = array.shape[1]
            ins.append((array, (16, size), lambda i, c, row=row: (row // 16, 0)))
    shape = (1, shards * small_size)
    outs = [(shape, F32, shape, lambda i, c: (0, 0))]

    def run(have, give, places):
        for number, ref in enumerate(have):
            owner = jnp.bitwise_xor(places[1], number)
            start = pl.multiple_of(owner * small_size, LANES)
            value = ref[0:1, :small_size].astype(BF16).astype(F32)
            give[0][:, pl.ds(start, small_size)] = value

    return ins, outs, run


def job_lay(values):
    total = sum(value.shape[1] for value in values)
    same = lambda i, c: (0, 0)
    ins = [(value, value.shape, same) for value in values]

    def run(have, give):
        start = 0
        for ref in have:
            give[0][:, start : start + ref.shape[1]] = ref[...]
            start += ref.shape[1]

    return ins, [((1, total), F32, (1, total), same)], run


class Links:
    def __init__(self, sizes, shard_rows):
        self.replicas, self.shards = sizes
        dp = lax.axis_index("dp")
        self.shard = lax.axis_index("shard")
        self.core = lax.rem(dp, 2)
        place = dp // 2
        self.inner = (place > 0) & (place < sizes[0] // 2 - 1)
        self.core_arr = jnp.stack([self.core, self.shard, self.inner]).astype(jnp.int32)
        self.rows = shard_rows
        self.half = shard_rows // 2
        self.fast = sizes == (8, 4)

    def swap(self, value):
        return self.across_dp(value, 1)

    def across_dp(self, value, bit):
        return lax.ppermute(value, "dp", [(d, d ^ bit) for d in range(self.replicas)])

    def along_dp(self, value, step):
        hops = ([(0, 1), (3, 2)], [(1, 2), (2, 1)], [(1, 0), (2, 3)])[step]
        pairs = [(2 * a + core, 2 * b + core) for a, b in hops for core in range(2)]
        return lax.ppermute(value, "dp", pairs)

    def across_shard(self, value, bit):
        return lax.ppermute(value, "shard", [(s, s ^ bit) for s in range(self.shards)])

    def turned_offsets(self, around):
        blocks = jnp.arange(2 * self.shards, dtype=jnp.int32)
        owner = blocks // 2
        if around:
            owner = jnp.bitwise_xor(owner, self.shard)
        away = jnp.bitwise_xor(lax.rem(blocks, 2), self.core)
        return away * (self.shards * self.half) + owner * self.half

    def gather(self, half_rows):
        return lax.all_gather(half_rows, "shard", axis=0, tiled=True)

    def gathered(self, mine, behind=None):
        if behind is not None:
            mine, _ = lax.optimization_barrier((mine, behind))
        first = jnp.arange(self.shards, dtype=jnp.int32) * self.rows
        offs = jnp.concatenate([first + self.core * self.half, first + (1 - self.core) * self.half])
        stride = mine.shape[0] // self.shards
        plan = tuple((0, t * stride, self.half, t) for t in range(self.shards)) + tuple(
            (1, t * stride, self.half, self.shards + t) for t in range(self.shards)
        )
        return Weights((mine, self.swap(mine)), plan, offs.astype(jnp.int32))

    def over_dp(self, values):
        groups = [[d for d in range(self.replicas) if d % 2 == c] for c in range(2)]
        return lax.psum(values, "dp", axis_index_groups=groups)


class Gather:
    def __init__(self, links, half_rows, own):
        self.links = links
        self.own = own
        self.by_x = links.across_shard(half_rows, 1)
        self.by_y = links.across_shard(half_rows, 2)

    def jobs(self):
        part = self.links.half // 2
        rest = self.by_x.shape[0] - part
        return [job_copy(self.by_y, 0, part), job_copy(self.by_x, part, rest)]

    def forward(self, results):
        links = self.links
        self.far = (
            links.across_shard(results[0], 1),
            links.across_shard(results[1], 2),
        )
        self.near = (links.swap(self.by_x), links.swap(self.by_y))

    def weights(self):
        links = self.links
        half, rows = links.half, links.rows
        part = half // 2
        far = tuple(links.swap(value) for value in self.far)
        pieces = (self.own, self.by_x, self.by_y, *self.near, *self.far, *far)
        plan = ((0, 0, rows, 0),)
        plan += tuple((n, 0, half, n) for n in range(1, 5))
        plan += tuple((n, 0, part, n) for n in range(5, 9))
        at = lambda bits: jnp.bitwise_xor(links.shard, bits) * rows
        mine = links.core * half
        other = (1 - links.core) * half
        offs = [at(0), at(1) + mine, at(2) + mine, at(1) + other, at(2) + other]
        offs += [at(3) + mine, at(3) + mine + part, at(3) + other, at(3) + other + part]
        return Weights(pieces, plan, jnp.stack(offs).astype(jnp.int32))


LINE, AT_ONCE, EXCHANGE = range(3)


class Reduce:
    def __init__(self, links, way, bits=((1, 2), (2, 1))):
        self.links = links
        self.way = way
        self.bits = bits
        self.stage = 0
        self.groups = []

    def add(self, own, sib):
        shape = (2, self.links.shards, self.links.half, own.shape[2])
        self.groups.append((own.reshape(shape), (self.links.swap(sib).reshape(shape),)))
        return self

    def job(self, steps):
        if self.stage > 2:
            own, received = self.groups[0]
            if self.way == LINE and self.stage == 5:
                return job_pick(own, received, steps)
            return job_add(own, received, steps)
        blocks = self.groups[0][0].shape[1]
        sides = []
        for number in range(2):
            order = self.bits[number % len(self.bits)]
            if blocks == 1:
                sides.append(())
            elif blocks == 2:
                sides.append((1,))
            else:
                sides.append(tuple(block for block in range(blocks) if block & order[0]))
        keep = [[block for block in range(blocks) if block not in gone] for gone in sides]
        send = [list(gone) for gone in sides]
        if len(self.bits) == 1 and blocks > 1:
            send = send[:1]
        return job_sum(self.groups, keep, send, steps)

    def advance(self, results):
        links = self.links
        own = results[0]
        stage = self.stage
        self.stage += 1
        if stage < 2:
            received = tuple(
                links.across_shard(value, order[stage])
                for value, order in zip(results[1:], self.bits)
            )
            self.groups = [(own, received)]
            return
        if stage == 2:
            own = own.reshape(2, own.shape[2], own.shape[3])
        if self.way == AT_ONCE:
            self.own = own
        elif self.way == LINE and stage < 5:
            self.groups = [(own, links.along_dp(own, stage - 2))]
        elif self.way == EXCHANGE and stage < 4:
            self.groups = [(own, links.across_dp(own, 2 * (stage - 1)))]
        else:
            self.grads = (own, links.swap(own))

    def close(self, behind):
        mine, _ = lax.optimization_barrier((self.own, behind))
        self.grads = (mine, self.links.swap(mine))


class Wide:
    def __init__(self, links, joined):
        self.links = links
        self.shape = joined.shape[1:]
        flat = joined.reshape(-1, joined.shape[3])
        self.own = lax.psum_scatter(flat, "shard", scatter_dimension=0, tiled=True)

    def finish(self):
        self.own = self.links.over_dp(self.own).reshape(self.shape)

    def close(self, behind):
        mine, _ = lax.optimization_barrier((self.own, behind))
        self.grads = (mine, self.links.swap(mine))


class Side:
    def __init__(self, links):
        self.links = links
        self.order = ()

    def jobs(self, jobs, steps=1, after=()):
        results = run_side(self.links.core_arr, jobs, after=(*self.order, *after), steps=steps)
        self.order = (results[0][0],)
        return [result[0] for result in results]

    def reduce(self, reduces, jobs=(), steps=2):
        work = [item.job(steps) for item in reduces] + list(jobs)
        results = run_side(self.links.core_arr, work, after=self.order, steps=steps)
        for item, result in zip(reduces, results):
            item.advance(result)
        self.order = (results[0][0],)
        return [result[0] for result in results[len(reduces) :]]

    def then(self, results):
        self.order = (results[0],)
        return results


def small_parts(small, width, hidden):
    bounds = [width] * 3 + [hidden] + [width] * 5
    parts = []
    start = 0
    for size in bounds:
        parts.append(small[:, start : start + size])
        start += size
    return parts


def body(sizes, *args):
    tokens, cotangent, lengths = args[:3]
    attn_state, mlp_state, small_state = args[3:6], args[6:9], args[9:12]
    rows, width = tokens.shape
    links = Links(sizes, attn_state[0].shape[0])
    half = links.half
    hidden = mlp_state[0].shape[1] // 2
    pairs = width // LANES
    pad = 16
    core_arr = links.core_arr
    around = links.turned_offsets(links.fast)
    side = Side(links)

    ends = jnp.cumsum(lengths[0], dtype=jnp.int32)
    small_own = small_state[0][None]
    small_size = small_own.shape[1]
    (
        BIAS_Q,
        BIAS_V,
        BIAS_O,
        BIAS_UP,
    ) = range(4)
    BIAS_DN, GAIN_ONE, SHIFT_ONE, GAIN_TWO, SHIFT_TWO = range(
        BIAS_UP + hidden // width, BIAS_UP + hidden // width + 5
    )

    def first_job():
        ins = [
            (attn_state[0], (half, 4 * width), lambda i, c: (c[0], 0)),
            (small_own, (1, small_size), lambda i, c: (0, 0)),
        ]
        outs = [((half + pad, 4 * width), BF16, (half + pad, 4 * width), lambda i, c: (0, 0))]

        def job(have, give):
            give[0][:half] = have[0][...].astype(BF16)
            row = have[1][...].astype(BF16)
            give[0][half:, :small_size] = jnp.broadcast_to(row, (pad, small_size))

        return ins, outs, job

    block = hidden // 2
    groups = [[(mlp_state[0], number, block) for number in pair] for pair in ((0, 2), (1, 3))]
    (first_half,) = side.jobs([first_job()])
    if links.fast:
        attn_gather = Gather(links, first_half, None)
    else:
        attn_weights = links.gathered(links.gather(first_half))
    dy, dyt, grad_bias_dn = side.then(run_cot(half, around, ends, cotangent, after=side.order))
    (more_half,) = side.jobs([job_cast(half, groups[1], 1, 4)], steps=4)
    if links.fast:
        (attn_gather.own,) = side.jobs(
            [job_cast(links.rows, [(attn_state[0], 0, 4 * width)], 0, 4)], steps=4
        )
        *copied, feed_half = side.jobs([*attn_gather.jobs(), job_cast(half, groups[0], 1, 1)])
        attn_gather.forward(copied)
    else:
        (feed_half,) = side.jobs([job_cast(half, groups[0], 1, 1)])
    wide = links.gather(feed_half)
    more_wide = links.gather(more_half)
    if links.fast:
        attn_weights = attn_gather.weights()
        rows_of = [
            (small_own, 0),
            (attn_gather.by_x, half),
            (attn_gather.by_y, half),
            (attn_gather.far[1], half // 2),
        ]
        (small,) = side.jobs([job_params(rows_of, links.shards, small_size)])
    else:
        small = attn_weights.pieces[0].reshape(links.shards, half + pad, 4 * width)
        small = small[:, half, :small_size].astype(F32).reshape(1, -1)

    qkv, turned_one = side.then(
        run_qkv(
            half,
            attn_weights,
            around,
            tokens,
            small,
            (BIAS_Q, BIAS_V, GAIN_ONE, SHIFT_ONE),
            after=side.order,
        )
    )
    mixed, lse = side.then(run_attend(ends, qkv, 0, pairs, after=side.order))
    wide = links.gathered(wide, lse)
    side.order += (wide.pieces[0],)
    after, low_two, turned_two, turned_mixed = side.then(
        run_after(
            half,
            attn_weights.at(3 * width),
            (around, around),
            mixed,
            tokens,
            small,
            (BIAS_O, GAIN_TWO, SHIFT_TWO),
            after=side.order,
        )
    )

    passed, grad_bias_up = [None], []
    blocked = lambda value: value.reshape(2, links.shards, half, value.shape[2])

    def feed(start, up_weights, down_weights):
        act, du, own, sib, gbias = run_feed(
            up_weights,
            down_weights,
            low_two,
            turned_two,
            dy,
            dyt,
            small,
            BIAS_UP * width + start,
            start,
            block,
            passed[-1],
            after=side.order,
        )
        side.order = (own,)
        passed.append((act, du))
        grad_bias_up.append(gbias)
        return own, sib

    def unit(way, own, sib, bits=((1, 2), (2, 1))):
        if links.fast:
            return Reduce(links, way, bits).add(own, sib)
        return Wide(links, side.jobs([join(own, links.swap(sib))], steps=4)[0])

    def join(own, received):
        return job_join(blocked(own), blocked(received), 4, links.fast)

    def reduce(units, jobs=(), steps=2):
        if links.fast:
            return side.reduce(units, jobs, steps)
        return side.jobs(jobs, steps) if jobs else None

    group_a = feed(0, wide, wide.at(block))
    more_wide = links.gathered(more_wide, grad_bias_up[0])
    unit_a = unit(LINE, *group_a)
    reduce([unit_a], steps=4)
    unit_b = unit(AT_ONCE, *feed(block, more_wide, more_wide.at(block)))
    reduce([unit_a], steps=4)
    (
        grad_after,
        dmix,
        own_out,
        sib_out,
        grad_bias_o,
        grad_gain_two,
        grad_shift_two,
    ) = side.then(
        run_middle(
            [(block, wide), (block, more_wide)],
            attn_weights.at(3 * width),
            passed[-1][1],
            after,
            dy,
            small,
            GAIN_TWO,
            turned_mixed,
            after=side.order,
        )
    )
    received_out = links.swap(sib_out)
    reduce([unit_a, unit_b], steps=4)
    grads, biases = [], []

    def attend_back(first):
        dq, dk, dv, gq, gv = side.then(
            run_attend_back(ends, qkv, mixed, dmix, lse, first, pairs // 2, after=side.order)
        )
        grads.append((dq, dk, dv))
        biases.append((gq, gv))

    def project(group):
        return side.then(run_project(turned_one, *grads[group], after=side.order))

    attend_back(0)
    (joined,) = reduce([unit_a, unit_b], [join(own_out, received_out)], steps=4)
    unit_e = Wide(links, joined)
    unit_c = unit(EXCHANGE, *project(0), ((1, 2),))
    attend_back(pairs // 2)
    if links.fast:
        side.order += (unit_e.own,)
    reduce([unit_a, unit_b, unit_c], steps=4)
    if links.fast:
        unit_b.own, unit_e.own = links.over_dp((unit_b.own, unit_e.own.reshape(unit_e.shape)))
    unit_d = unit(EXCHANGE, *project(1), ((1, 2),))
    grad_input, grad_gain_one, grad_shift_one = side.then(
        run_input(attn_weights, grads, tokens, grad_after, small, GAIN_ONE, after=side.order)
    )
    small_grads = [biases[0][0], biases[1][0], biases[0][1], biases[1][1], grad_bias_o]
    small_grads += grad_bias_up
    small_grads += [grad_bias_dn, grad_gain_one, grad_shift_one, grad_gain_two, grad_shift_two]
    (grad_small,) = reduce([unit_a, unit_c, unit_d], [job_lay(small_grads)])

    def pick_feed(number, arrays):
        return [arrays[0][number]]

    def adam_mlp(number, item, earlier):
        return side.then(
            run_adam(
                core_arr,
                mlp_state,
                [item.grads],
                block,
                [number, 2 + number],
                pick_feed,
                earlier,
                after=side.order,
            )
        )

    out_block = width // 2

    def pick_heads(number, arrays):
        left, right = arrays[0][0], arrays[0][1]
        split = out_block // 2
        if number > 2:
            return [arrays[1][number - 3]]
        return (
            [left[:, :out_block]],
            [left[:, out_block:], right[:, :split]],
            [right[:, split:]],
        )[number]

    def adam_attn(items, places, earlier):
        return side.then(
            run_adam(
                core_arr,
                attn_state,
                [item.grads for item in items],
                out_block,
                places,
                pick_heads,
                earlier,
                after=side.order,
            )
        )

    def output_now():
        out = run_output(
            [(block, wide.at(block)), (block, more_wide.at(block))],
            passed[-1][0],
            after,
            small,
            BIAS_DN,
            after=side.order,
        )
        side.then([out])
        return out

    if links.fast:
        shard_move = lambda bit: functools.partial(links.across_shard, bit=bit)
        dp_move = lambda bit: functools.partial(links.across_dp, bit=bit)
        moved = links.across_shard(grad_small, 1)

        def step(units, move):
            (total,) = reduce(units, [job_add(grad_small, moved, 2)])
            return total, move(total) if move else None

        mlp_new = adam_mlp(0, unit_a, None)
        side.order += (unit_b.own,)
        grad_small, moved = step([unit_c, unit_d], shard_move(2))
        output = output_now()
        grad_small, moved = step([unit_c, unit_d], links.swap)
        unit_b.close(grad_small)
        unit_e.close(grad_small)
        mlp_new = adam_mlp(1, unit_b, mlp_new)
        grad_small, moved = step([unit_c, unit_d], dp_move(2))
        attn_new = adam_attn([unit_c], [0, 2, 4], None)
        grad_small, moved = step([unit_d], dp_move(4))
        attn_new = adam_attn([unit_d, unit_e], [1, 3, 5, 6, 7], attn_new)
        grad_small, _ = step([], None)
    else:
        for item in (unit_a, unit_b, unit_c, unit_d, unit_e):
            item.finish()
            item.close(grad_input)
        grad_small = lax.psum(grad_small, ("dp", "shard"))
        output = output_now()
        mlp_new = adam_mlp(1, unit_b, adam_mlp(0, unit_a, None))
        attn_new = adam_attn([unit_c], [0, 2, 4], None)
        attn_new = adam_attn([unit_d, unit_e], [1, 3, 5, 6, 7], attn_new)
    grad_small = lax.dynamic_slice_in_dim(grad_small, links.shard * small_size, small_size, 1)[0]
    small_new = adamw(*small_state, grad_small, 0.4, 0.0)
    return (output, grad_input, *attn_new, *mlp_new, *small_new)


def solution(mesh):
    tokens = P(("dp", "shard"), None)
    state = P("shard", None)
    vector = P("shard")
    return jax.shard_map(
        functools.partial(body, (mesh.shape["dp"], mesh.shape["shard"])),
        mesh=mesh,
        in_specs=(tokens,) * 3 + (state,) * 6 + (vector,) * 3,
        out_specs=(tokens,) * 2 + (state,) * 6 + (vector,) * 3,
        check_vma=False,
    )
```

```python
import functools

import jax
import jax.numpy as jnp
from jax import lax
from jax.experimental import pallas as pl
from jax.experimental.pallas import tpu as pltpu
from jax.sharding import PartitionSpec as P

HD = 64
STEP = 10
LANES = 128
MASKED = -1e30
SAFE = 60.0
GELU_IN = 0.7978845608028654
GELU_CUBE = 0.044715

beta_one = 0.9
beta_two = 0.95
adam_eps = 1e-08
norm_eps = 1e-05

F32 = jnp.float32
BF16 = jnp.bfloat16
MIB = 1024 * 1024
VMEM_MIB = 64

ANY = pl.BlockSpec(memory_space=pl.ANY)
SMEM = pl.BlockSpec(memory_space=pltpu.SMEM)


def dot_nn(left, right):
    return lax.dot_general(left, right, (((1,), (0,)), ((), ())), preferred_element_type=F32)


def dot_nt(left, right):
    return lax.dot_general(left, right, (((1,), (1,)), ((), ())), preferred_element_type=F32)


def dot_tn(left, right):
    return lax.dot_general(left, right, (((0,), (0,)), ((), ())), preferred_element_type=F32)


def whole(shape):
    return pl.BlockSpec(shape, lambda *_: (0,) * len(shape))


def call(kernel, grid, ins, outs, after=(), reuse=(), prefetch=(), scratch=(), cost=None, name=None):
    known = len(prefetch) + len(ins)
    idle = [*after, *(array for array, _ in reuse)]

    def run(*refs):
        kernel(*refs[:known], *refs[known + len(idle) :])

    def placed(array, spec):
        if spec is SMEM:
            return array
        return pltpu.with_memory_space_constraint(array, pltpu.HBM)

    return pl.pallas_call(
        run,
        grid_spec=pltpu.PrefetchScalarGridSpec(
            num_scalar_prefetch=len(prefetch),
            grid=grid,
            in_specs=[spec for _, spec in ins] + [ANY] * len(idle),
            out_specs=[spec for _, _, spec in outs],
            scratch_shapes=list(scratch),
        ),
        out_shape=[pltpu.HBM(shape, dtype) for shape, dtype, _ in outs],
        input_output_aliases={
            known + len(after) + number: output for number, (_, output) in enumerate(reuse)
        },
        compiler_params=pltpu.CompilerParams(vmem_limit_bytes=VMEM_MIB * MIB),
        cost_estimate=cost,
        name=name,
    )(*prefetch, *(placed(*item) for item in ins), *(placed(array, ANY) for array in idle))


def param(small, number, width):
    return (small, pl.BlockSpec((1, width), lambda *_: (0, number)))


def cost(flops, moved, exps=0):
    return pl.CostEstimate(flops=int(flops), bytes_accessed=int(moved), transcendentals=int(exps))


def store_turned(turned_ref, toff, block, half, value, columns):
    turned = value.astype(BF16).T
    for part in range(LANES // half):
        offset = pl.multiple_of(toff[block * (LANES // half) + part], half)
        turned_ref[pl.ds(offset, half), columns] = turned[part * half : (part + 1) * half]


def norm_stats(values):
    center = values - jnp.mean(values, axis=-1, keepdims=True)
    spread = jnp.mean(center * center, axis=-1, keepdims=True)
    scale = lax.rsqrt(spread + norm_eps)
    return center * scale, scale


def norm_back(hat, scale, grad_hat):
    mean = jnp.mean(grad_hat, axis=-1, keepdims=True)
    along = jnp.mean(grad_hat * hat, axis=-1, keepdims=True)
    return scale * (grad_hat - mean - hat * along)


def accumulate(ref, value, first):
    @pl.when(first)
    def _():
        ref[...] = value

    @pl.when(jnp.logical_not(first))
    def _():
        ref[...] += value


class Weights:
    def __init__(self, pieces, plan, offs, first=0):
        self.pieces, self.plan, self.offs, self.first = pieces, plan, offs, first

    def at(self, first):
        return Weights(self.pieces, self.plan, self.offs, self.first + first)

    def inputs(self):
        return [(self.offs, SMEM)] + [(piece, ANY) for piece in self.pieces]

    def sems(self):
        return pltpu.SemaphoreType.DMA((len(self.plan),))

    def rest(self, refs):
        return refs[1 + len(self.pieces) :]

    def copies(self, refs, size, target, sems, start=None):
        offs, refs = refs[0], refs[1:]
        columns = slice(self.first, self.first + size)
        if start is not None:
            columns = pl.ds(pl.multiple_of(self.first + start, LANES), size)
        made = []
        for number, (piece, first, rows, index) in enumerate(self.plan):
            offset = pl.multiple_of(offs[index], rows)
            made.append(
                pltpu.make_async_copy(
                    refs[piece].at[pl.ds(first, rows), columns],
                    target(offset, rows),
                    sems.at[number],
                )
            )
        return made, refs[len(self.pieces) :]


def start_all(copies):
    @pl.when(pl.program_id(0) == 0)
    def _():
        for copy in copies:
            copy.start()


def wait_all(copies):
    @pl.when(pl.program_id(0) == 0)
    def _():
        for copy in copies:
            copy.wait()


def cot_kernel(half, toff, ends, cot_ref, dy_ref, turned_ref, bias_ref):
    rows = cot_ref.shape[0]
    place = lax.broadcasted_iota(jnp.int32, (rows, LANES), 0)
    live = (place < ends[ends.shape[0] - 1]).astype(F32)
    for block in range(cot_ref.shape[1] // LANES):
        columns = slice(block * LANES, (block + 1) * LANES)
        value = cot_ref[:, columns].astype(F32) * live
        dy_ref[:, columns] = value.astype(BF16)
        bias_ref[:, columns] = jnp.sum(value, axis=0, keepdims=True)
        store_turned(turned_ref, toff, block, half, value, slice(None))


def run_cot(half, toff, ends, cot, after=()):
    rows, width = cot.shape
    return call(
        functools.partial(cot_kernel, half),
        (1,),
        [(toff, SMEM), (ends, SMEM), (cot, whole(cot.shape))],
        [
            ((rows, width), BF16, whole((rows, width))),
            ((width, rows), BF16, whole((width, rows))),
            ((1, width), F32, whole((1, width))),
        ],
        after=after,
        cost=cost(0, 6 * rows * width),
        name="cotangent",
    )


def run_qkv(half, weights, toff, x, small, numbers, after=()):
    rows, width = x.shape
    span = 256

    def kernel(*refs):
        weight, sems = refs[-2:]
        copies, refs = weights.copies(
            refs, 3 * width, lambda at, size: weight.at[pl.ds(at, size), :], sems
        )
        toff_ref, x_ref, bias_q, bias_v, gain_ref, shift_ref, qkv_ref, turned_ref = refs[:8]
        start_all(copies)
        hat, _ = norm_stats(x_ref[...].astype(F32))
        normed = hat * gain_ref[...] + shift_ref[...]
        for block in range(width // LANES):
            columns = slice(block * LANES, (block + 1) * LANES)
            store_turned(turned_ref, toff_ref, block, half, normed[:, columns], slice(None))
        wait_all(copies)
        low = normed.astype(BF16)
        for part in range(3):
            columns = slice(part * width, (part + 1) * width)
            value = dot_nn(low, weight[:, columns])
            if part == 2:
                value += bias_v[...]
            if part == 0:
                value = (value + bias_q[...]).astype(BF16).astype(F32) * HD ** (-0.5)
            qkv_ref[:, columns] = value.astype(BF16)

    return call(
        kernel,
        (rows // span,),
        weights.inputs()
        + [
            (toff, SMEM),
            (x, pl.BlockSpec((span, width), lambda i: (i, 0))),
        ]
        + [param(small, number, width) for number in numbers],
        [
            ((rows, 3 * width), BF16, pl.BlockSpec((span, 3 * width), lambda i: (i, 0))),
            ((width, rows), BF16, pl.BlockSpec((width, span), lambda i: (0, i))),
        ],
        after=after,
        scratch=[pltpu.VMEM((width, 3 * width), BF16), weights.sems()],
        cost=cost(6 * rows * width * width, 16 * rows * width),
        name="qkv",
    )


def first_of_row(ends, place):
    first = jnp.zeros_like(place)
    for number in range(ends.shape[0]):
        first = jnp.where(place >= ends[number], ends[number], first)
    return first


def attend_kernel(ends, q_ref, k_ref, v_ref, o_ref, lse_ref, allow):
    rows = q_ref.shape[0]
    span = min(256, rows)

    @pl.when(pl.program_id(0) == 0)
    def _():
        for start in range(0, rows, span):
            keys = start + span
            place = lax.broadcasted_iota(jnp.int32, (span, 1), 0) + start
            first = first_of_row(ends, place)
            key = lax.broadcasted_iota(jnp.int32, (span, keys), 1)
            allow[start:keys, :keys] = jnp.where((key <= place) & (key >= first), 0.0, MASKED)

    lane = lax.broadcasted_iota(jnp.int32, (1, LANES), 1)
    low_lane = lane < HD
    one = low_lane.astype(BF16)
    masks = (one, 1 - one)

    same = (lax.broadcasted_iota(jnp.int32, (LANES, LANES), 0) < HD) == (
        lax.broadcasted_iota(jnp.int32, (LANES, LANES), 1) < HD
    )
    same = same.astype(F32).astype(BF16)
    longest = [
        jnp.max(dot_nn(ref[...] * ref[...], same), axis=0, keepdims=True) for ref in (q_ref, k_ref)
    ]
    bounded = jnp.max(longest[0] * longest[1]) < SAFE * SAFE

    def attend(shift):
        mixed = [v_ref[...] * mask + (1 - mask) for mask in masks]
        for start in range(0, rows, span):
            keys = start + span
            sums = []
            tops = []
            for head in range(2):
                query = q_ref[start:keys, :] * masks[head]
                scores = dot_nt(query, k_ref[:keys, :]) + allow[start:keys, :keys]
                if shift:
                    top = jnp.max(scores, axis=1, keepdims=True)
                    tops.append(top)
                    scores = scores - top
                probs = jnp.exp(scores).astype(BF16)
                sums.append(dot_nn(probs, mixed[head][:keys]))
            total = pltpu.roll(jnp.where(low_lane, sums[1], sums[0]), HD, 1)
            out = jnp.where(low_lane, sums[0], sums[1]) / total
            o_ref[start:keys, :] = out.astype(BF16)
            lse = jnp.log(total)
            if shift:
                lse += jnp.where(low_lane, tops[0], tops[1])
            lse = lse.T
            lse_ref[0, 0:1, start:keys] = lse[0:1]
            lse_ref[0, 1:2, start:keys] = lse[HD : HD + 1]

    @pl.when(bounded)
    def _():
        attend(False)

    @pl.when(jnp.logical_not(bounded))
    def _():
        attend(True)


def run_attend(ends, qkv, first, count, earlier=None, after=()):
    rows = qkv.shape[0]
    width = qkv.shape[1] // 3
    pairs = width // LANES
    column = lambda shift: pl.BlockSpec((rows, LANES), lambda i: (0, i + shift))
    return call(
        attend_kernel,
        (count,),
        [(ends, SMEM)] + [(qkv, column(first + part * pairs)) for part in range(3)],
        [
            ((rows, width), BF16, column(first)),
            ((pairs, 2, rows), F32, pl.BlockSpec((1, 2, rows), lambda i: (i + first, 0, 0))),
        ],
        after=after,
        reuse=[] if earlier is None else [(earlier[0], 0), (earlier[1], 1)],
        scratch=[pltpu.VMEM((rows, rows), F32)],
        cost=cost(8 * rows * rows * LANES * count, 8 * rows * LANES * count, 2 * rows * rows * count),
        name="attend",
    )


def run_after(half, weights, toffs, mixed, x, small, numbers, after=()):
    rows, width = x.shape
    span = 256

    def kernel(*refs):
        weight, sems = refs[-2:]
        copies, refs = weights.copies(
            refs, width, lambda at, size: weight.at[pl.ds(at, size), :], sems
        )
        mixed_toff, low_toff, mixed_ref, x_ref, bias_ref, gain_ref, shift_ref = refs[:7]
        after_ref, low_ref, turned_ref, mixed_turned_ref = refs[7:11]
        start_all(copies)
        for block in range(width // LANES):
            columns = slice(block * LANES, (block + 1) * LANES)
            store_turned(mixed_turned_ref, mixed_toff, block, half, mixed_ref[:, columns], slice(None))
        wait_all(copies)
        value = x_ref[...].astype(F32) + dot_nn(mixed_ref[...], weight[...]) + bias_ref[...]
        after_ref[...] = value
        hat, _ = norm_stats(value)
        normed = hat * gain_ref[...] + shift_ref[...]
        low_ref[...] = normed.astype(BF16)
        for block in range(width // LANES):
            columns = slice(block * LANES, (block + 1) * LANES)
            store_turned(turned_ref, low_toff, block, half, normed[:, columns], slice(None))

    by_row = pl.BlockSpec((span, width), lambda i: (i, 0))
    by_column = pl.BlockSpec((width, span), lambda i: (0, i))
    return call(
        kernel,
        (rows // span,),
        weights.inputs()
        + [(toff, SMEM) for toff in toffs]
        + [(mixed, by_row), (x, by_row)]
        + [param(small, number, width) for number in numbers],
        [
            ((rows, width), F32, by_row),
            ((rows, width), BF16, by_row),
            ((width, rows), BF16, by_column),
            ((width, rows), BF16, by_column),
        ],
        after=after,
        scratch=[pltpu.VMEM((width, width), BF16), weights.sems()],
        cost=cost(2 * rows * width * width, 14 * rows * width),
        name="after",
    )


def run_feed(up_weights, down_weights, low, turned, dy, dyt, small, first, begin, block, earlier, after=()):
    rows, width = low.shape
    hidden = earlier[0].shape[1] if earlier is not None else block_total(small, width)
    span = 256
    mid = width // 2
    count = block // span
    by_column = lambda size: pl.BlockSpec((size, span), lambda i: (0, i))
    shifted = pl.BlockSpec((rows, span), lambda i: (0, begin // span + i))
    grad = ((2, mid, block), BF16, pl.BlockSpec((2, mid, span), lambda i: (0, 0, i)))

    def kernel(*refs):
        up, down, up_sems, down_sems = refs[-4:]
        step = pl.program_id(0)

        def copies(number):
            columns = pl.ds(pl.multiple_of(number * span, span), span)
            made, rest = up_weights.copies(
                refs,
                span,
                lambda at, size: up.at[pl.ds(at, size), columns],
                up_sems.at[number],
                number * span,
            )
            more, _ = down_weights.copies(
                rest,
                span,
                lambda at, size: down.at[pl.ds(at, size), columns],
                down_sems.at[number],
                number * span,
            )
            return made + more

        @pl.when(step == 0)
        def _():
            for copy in copies(0):
                copy.start()

        @pl.when(step + 1 < count)
        def _():
            for copy in copies(step + 1):
                copy.start()

        for copy in copies(step):
            copy.wait()
        low_ref, turned_ref, dy_ref, dyt_ref, bias_ref, act_ref, du_ref, own_ref, sib_ref, gbias_ref = (
            down_weights.rest(up_weights.rest(refs))[:10]
        )
        columns = pl.ds(pl.multiple_of(step * span, span), span)
        upper = dot_nn(low_ref[...], up[:, columns]) + bias_ref[...]
        grad_act = dot_nn(dy_ref[...], down[:, columns])
        square = (GELU_IN * GELU_CUBE) * (upper * upper)
        tanh = jnp.tanh(upper * (GELU_IN + square))
        share = 0.5 + 0.5 * tanh
        act = upper * share
        slope = share + act * (1.0 - tanh) * (GELU_IN + 3.0 * square)
        act = act.astype(BF16)
        du = (grad_act * slope).astype(BF16)
        act_ref[...] = act
        du_ref[...] = du
        gbias_ref[...] = jnp.sum(du.astype(F32), axis=0, keepdims=True)
        grad_up = dot_nn(turned_ref[...], du).astype(BF16)
        own_ref[0] = grad_up[:mid]
        sib_ref[0] = grad_up[mid:]
        grad_dn = dot_nn(dyt_ref[...], act).astype(BF16)
        own_ref[1] = grad_dn[:mid]
        sib_ref[1] = grad_dn[mid:]

    return call(
        kernel,
        (count,),
        up_weights.inputs()
        + down_weights.inputs()
        + [
            (low, whole((rows, width))),
            (turned, whole((width, rows))),
            (dy, whole((rows, width))),
            (dyt, whole((width, rows))),
            (small, pl.BlockSpec((1, span), lambda i: (0, first // span + i))),
        ],
        [
            ((rows, hidden), BF16, shifted),
            ((rows, hidden), BF16, shifted),
            grad,
            grad,
            ((1, block), F32, by_column(1)),
        ],
        after=after,
        reuse=[] if earlier is None else [(earlier[0], 0), (earlier[1], 1)],
        scratch=[
            pltpu.VMEM((width, block), BF16),
            pltpu.VMEM((width, block), BF16),
            pltpu.SemaphoreType.DMA((count, len(up_weights.plan))),
            pltpu.SemaphoreType.DMA((count, len(down_weights.plan))),
        ],
        cost=cost(8 * rows * width * block, 24 * width * block, rows * block),
        name="feed",
    )


def block_total(small, width):
    return small.shape[1] - 8 * width


class Stream:
    def __init__(self):
        self.parts = []

    def add(self, copies):
        self.parts.append(copies)

    def start(self):
        for copies in self.parts:
            for copy in copies:
                copy.start()

    def wait(self, number):
        for copy in self.parts[number]:
            copy.wait()


def run_output(weights, acts, after_value, small, number, after=()):
    rows, width = after_value.shape
    hidden = acts.shape[1]
    span = 256
    bounds = [0]
    for size, _ in weights:
        bounds.append(bounds[-1] + size)
    by_row = lambda size: pl.BlockSpec((span, size), lambda i: (i, 0))

    def kernel(*refs):
        down = refs[-1 - len(weights)]
        sems = refs[-len(weights) :]
        stream = []
        for index, (size, item) in enumerate(weights):
            columns = slice(bounds[index], bounds[index + 1])
            copies, refs = item.copies(
                refs,
                size,
                lambda at, lines, columns=columns: down.at[pl.ds(at, lines), columns],
                sems[index],
            )
            stream.append(copies)
        act_ref, after_ref, bias_ref, out_ref = refs[:4]
        for copies in stream:
            start_all(copies)
        total = after_ref[...] + bias_ref[...]
        for index, copies in enumerate(stream):
            wait_all(copies)
            columns = slice(bounds[index], bounds[index + 1])
            total += dot_nt(act_ref[:, columns], down[:, columns])
        out_ref[...] = total.astype(BF16)

    (out,) = call(
        kernel,
        (rows // span,),
        [item for _, weight in weights for item in weight.inputs()]
        + [(acts, by_row(hidden)), (after_value, by_row(width)), param(small, number, width)],
        [((rows, width), BF16, by_row(width))],
        after=after,
        scratch=[pltpu.VMEM((width, hidden), BF16)] + [weight.sems() for _, weight in weights],
        cost=cost(rows * width * hidden // 5, 2 * rows * width),
        name="output",
    )
    return out


def run_middle(weights, out_weights, dus, after_value, dy, small, number, turned, after=()):
    rows, width = after_value.shape
    hidden = dus.shape[1]
    part = width
    parts = hidden // part
    span = 256
    mid = width // 2
    places = [
        (item.at(start)) for size, item in weights for start in range(0, size, part)
    ]
    most = max(len(item.plan) for item in places)

    def kernel(*refs):
        du, up, value_in, dy_in, turned_in, out_weight, branch, sems, out_sems, own_sems = refs[-10:]
        stream = Stream()
        for index, item in enumerate(places):
            columns = slice(index * part, (index + 1) * part)
            copies, refs = item.copies(
                refs,
                part,
                lambda at, size, columns=columns: up.at[pl.ds(at, size), columns],
                sems.at[index],
            )
            stream.add(copies)
        more, refs = out_weights.copies(
            refs, width, lambda at, size: out_weight.at[pl.ds(at, size), :], out_sems
        )
        du_ref, after_ref, dy_ref, gain_ref, turned_ref = refs[:5]
        grad_ref, dmix_ref, own_ref, sib_ref, gbias_ref, ggain_ref, gshift_ref = refs[5:12]
        for index in range(parts):
            columns = slice(index * part, (index + 1) * part)
            stream.parts[index].append(
                pltpu.make_async_copy(du_ref.at[:, columns], du.at[:, columns], own_sems.at[index])
            )
        stream.add(
            [
                pltpu.make_async_copy(after_ref, value_in, own_sems.at[parts]),
                pltpu.make_async_copy(dy_ref, dy_in, own_sems.at[parts + 1]),
            ]
        )
        stream.add([pltpu.make_async_copy(turned_ref, turned_in, own_sems.at[parts + 2]), *more])
        stream.start()
        total = None
        for index in range(parts):
            columns = slice(index * part, (index + 1) * part)
            stream.wait(index)
            value = dot_nt(du[:, columns], up[:, columns])
            total = value if total is None else total + value
        stream.wait(parts)
        gain = gain_ref[...]
        sums = [jnp.zeros((1, width), F32)] * 3
        for start in range(0, rows, span):
            lines = slice(start, start + span)
            grad = total[lines]
            hat, scale = norm_stats(value_in[lines, :])
            full = dy_in[lines, :].astype(F32) + norm_back(hat, scale, grad * gain)
            grad_ref[lines, :] = full
            low = full.astype(BF16)
            branch[lines, :] = low
            for index, value in enumerate((low.astype(F32), grad * hat, grad)):
                sums[index] = sums[index] + jnp.sum(value, axis=0, keepdims=True)
        gbias_ref[...], ggain_ref[...], gshift_ref[...] = sums
        stream.wait(parts + 1)
        dmix_ref[...] = dot_nt(branch[...], out_weight[...]).astype(BF16)
        for side in range(2):
            columns = slice(side * (width // 2), (side + 1) * (width // 2))
            value = dot_nn(turned_in[...], branch[:, columns]).astype(BF16)
            own_ref[side] = value[:mid]
            sib_ref[side] = value[mid:]

    grads = ((2, mid, width // 2), BF16, whole((2, mid, width // 2)))
    vector = ((1, width), F32, whole((1, width)))
    full = whole((rows, width))
    return call(
        kernel,
        (1,),
        [item for place in places for item in place.inputs()]
        + out_weights.inputs()
        + [(dus, ANY), (after_value, ANY), (dy, ANY), param(small, number, width), (turned, ANY)],
        [((rows, width), F32, full), ((rows, width), BF16, full), grads, grads] + [vector] * 3,
        after=after,
        scratch=[
            pltpu.VMEM((rows, hidden), BF16),
            pltpu.VMEM((width, hidden), BF16),
            pltpu.VMEM((rows, width), F32),
            pltpu.VMEM((rows, width), BF16),
            pltpu.VMEM((width, rows), BF16),
            pltpu.VMEM((width, width), BF16),
            pltpu.VMEM((rows, width), BF16),
            pltpu.SemaphoreType.DMA((parts, most)),
            out_weights.sems(),
            pltpu.SemaphoreType.DMA((parts + 3,)),
        ],
        cost=cost(8 * rows * width * (hidden + 2 * width), 120 * rows * width),
        name="middle",
    )


def attend_back_kernel(
    ends,
    q_ref,
    k_ref,
    v_ref,
    o_ref,
    do_ref,
    lse_ref,
    dq_ref,
    dk_ref,
    dv_ref,
    gq_ref,
    gv_ref,
    allow,
    total,
):
    rows = q_ref.shape[0]
    span = min(256, rows)

    @pl.when(pl.program_id(0) == 0)
    def _():
        for start in range(0, rows, span):
            query = lax.broadcasted_iota(jnp.int32, (1, rows - start), 1) + start
            first = first_of_row(ends, query)
            key = lax.broadcasted_iota(jnp.int32, (span, rows - start), 0) + start
            allow[start : start + span, start:] = jnp.where(
                (key <= query) & (key >= first), 0.0, MASKED
            )

    lane = lax.broadcasted_iota(jnp.int32, (1, LANES), 1)
    low_lane = lane < HD
    one = low_lane.astype(BF16)
    masks = (one, 1 - one)
    product = (o_ref[...].astype(F32) * do_ref[...].astype(F32)).T
    inner = (
        jnp.sum(product[:HD], axis=0, keepdims=True),
        jnp.sum(product[HD:], axis=0, keepdims=True),
    )
    for start in range(0, rows, span):
        stop = start + span
        grads = []
        for head in range(2):
            keys = k_ref[start:stop, :] * masks[head]
            vals = v_ref[start:stop, :] * masks[head]
            scores = dot_nt(keys, q_ref[start:, :]) + allow[start:stop, start:]
            probs = jnp.exp(scores - lse_ref[0, head : head + 1, start:])
            grad_probs = dot_nt(vals, do_ref[start:, :])
            grad_scores = (probs * (grad_probs - inner[head][:, start:])).astype(BF16)
            grad_vals = dot_nn(probs.astype(BF16), do_ref[start:, :])
            grad_keys = dot_nn(grad_scores, q_ref[start:, :])
            grads.append((grad_keys, grad_vals))
            update = dot_tn(grad_scores, keys)
            if start == 0 and head == 0:
                total[...] = update
            else:
                total[start:, :] += update
        dk_ref[start:stop, :] = jnp.where(low_lane, grads[0][0], grads[1][0]).astype(BF16)
        dv_ref[start:stop, :] = jnp.where(low_lane, grads[0][1], grads[1][1]).astype(BF16)
    grad_query = (total[...] * HD ** (-0.5)).astype(BF16)
    dq_ref[...] = grad_query
    gq_ref[...] = jnp.sum(grad_query.astype(F32), axis=0, keepdims=True)
    gv_ref[...] = jnp.sum(dv_ref[...].astype(F32), axis=0, keepdims=True)


def run_attend_back(ends, qkv, mixed, dmix, lse, first, count, after=()):
    rows, width = mixed.shape
    pairs = width // LANES
    column = lambda shift: pl.BlockSpec((rows, LANES), lambda i: (0, i + shift))
    return call(
        attend_back_kernel,
        (count,),
        [(ends, SMEM)]
        + [(qkv, column(first + part * pairs)) for part in range(3)]
        + [
            (mixed, column(first)),
            (dmix, column(first)),
            (lse, pl.BlockSpec((1, 2, rows), lambda i: (i + first, 0, 0))),
        ],
        [((rows, LANES * count), BF16, column(0))] * 3
        + [((1, LANES * count), F32, pl.BlockSpec((1, LANES), lambda i: (0, i)))] * 2,
        after=after,
        scratch=[pltpu.VMEM((rows, rows), F32), pltpu.VMEM((rows, LANES), F32)],
        cost=cost(
            80 * rows * rows * LANES * count, rows * LANES * count
        ),
        name="attend_back",
    )


def project_kernel(turned_ref, dq_ref, dk_ref, dv_ref, own_ref, sib_ref):
    mid = own_ref.shape[1]
    size = dq_ref.shape[1]
    left = jnp.concatenate([dq_ref[...], dk_ref[:, : size // 2]], axis=1)
    right = jnp.concatenate([dk_ref[:, size // 2 :], dv_ref[...]], axis=1)
    for side, columns in enumerate((left, right)):
        own_ref[side] = dot_nn(turned_ref[:mid], columns).astype(BF16)
        sib_ref[side] = dot_nn(turned_ref[mid:], columns).astype(BF16)


def run_project(turned, dq, dk, dv, after=()):
    width, rows = turned.shape
    size = dq.shape[1]
    mid = width // 2
    grad = ((2, mid, 3 * size // 2), BF16, whole((2, mid, 3 * size // 2)))
    return call(
        project_kernel,
        (1,),
        [(turned, whole((width, rows)))] + [(value, whole((rows, size))) for value in (dq, dk, dv)],
        [grad, grad],
        after=after,
        cost=cost(6 * rows * width * size, 14 * rows * size),
        name="project",
    )


def run_input(weights, grads, x, grad_after, small, number, after=()):
    rows, width = x.shape
    span = 256
    size = grads[0][0].shape[1]
    flat = [value for group in grads for value in group]
    count = len(flat)
    by_row = lambda size: pl.BlockSpec((span, size), lambda i: (i, 0))

    def kernel(*refs):
        weight, sems = refs[-2:]
        stream = []
        for part in range(3):
            columns = slice(part * width, (part + 1) * width)
            copies, rest = weights.at(part * width).copies(
                refs,
                width,
                lambda at, lines, columns=columns: weight.at[pl.ds(at, lines), columns],
                sems.at[part],
            )
            stream.append(copies)
        refs = rest
        for copies in stream:
            start_all(copies)
        x_ref, grad_ref, gain_ref, out_ref, ggain_ref, gshift_ref = refs[count : count + 6]
        step = pl.program_id(0)
        total = None
        for part in range(3):
            wait_all(stream[part])
            for group in range(len(grads)):
                begin = part * width + group * size
                value = dot_nt(refs[3 * group + part][...], weight[:, begin : begin + size])
                total = value if total is None else total + value
        hat, scale = norm_stats(x_ref[...].astype(F32))
        accumulate(gshift_ref, jnp.sum(total, axis=0, keepdims=True), step == 0)
        accumulate(ggain_ref, jnp.sum(total * hat, axis=0, keepdims=True), step == 0)
        out_ref[...] = grad_ref[...] + norm_back(hat, scale, total * gain_ref[...])

    vector = ((1, width), F32, whole((1, width)))
    return call(
        kernel,
        (rows // span,),
        weights.inputs()
        + [(value, by_row(size)) for value in flat]
        + [(x, by_row(width)), (grad_after, by_row(width)), param(small, number, width)],
        [((rows, width), F32, by_row(width)), vector, vector],
        after=after,
        scratch=[
            pltpu.VMEM((width, 3 * width), BF16),
            pltpu.SemaphoreType.DMA((3, len(weights.plan))),
        ],
        cost=cost(24 * rows * width * width, 88 * rows * width),
        name="grad_input",
    )


def adamw(weight, first, second, grad, rate, decay):
    first_new = beta_one * first + (1.0 - beta_one) * grad
    second_new = beta_two * second + (1.0 - beta_two) * grad * grad
    first_hat = first_new / (1.0 - beta_one**STEP)
    second_hat = second_new / (1.0 - beta_two**STEP)
    weight_new = weight - rate * (first_hat / (jnp.sqrt(second_hat) + adam_eps) + decay * weight)
    return (weight_new, first_new, second_new)


def run_adam(core, state, groups, span, places, pick, earlier, after=()):
    half = groups[0][0].shape[-2]
    count = len(places)
    table = jnp.array(places, jnp.int32)
    place = pl.BlockSpec((half, span), lambda p, h, c, t: (jnp.bitwise_xor(h, c[0]), t[p]))
    flat = [value for group in groups for value in group]

    def kernel(core_ref, table_ref, w_ref, m_ref, v_ref, *refs):
        w_out, m_out, v_out, grad_ref = refs[-4:]
        for side in range(2):
            mine = refs[side : 2 * len(groups) : 2]
            for block in range(count):

                @pl.when((pl.program_id(1) == side) & (pl.program_id(0) == block))
                def _(mine=mine, block=block):
                    start = 0
                    for value in pick(block, mine):
                        grad_ref[:, start : start + value.shape[1]] = value
                        start += value.shape[1]

        w_out[...], m_out[...], v_out[...] = adamw(
            w_ref[...], m_ref[...], v_ref[...], grad_ref[...].astype(F32), 0.05, 0.1
        )

    moved = 2 * half * count * span
    return call(
        kernel,
        (count, 2),
        [(value, place) for value in state] + [(value, whole(value.shape)) for value in flat],
        [(state[0].shape, F32, place)] * 3,
        after=after,
        reuse=[] if earlier is None else [(value, n) for n, value in enumerate(earlier)],
        prefetch=(core, table),
        scratch=[pltpu.VMEM((half, span), BF16)],
        cost=cost(2 * moved, 2 * moved),
        name="adam",
    )


def run_side(core, jobs, after=(), steps=4):
    counts = [(len(job[0]), len(job[1])) for job in jobs]
    total_in = sum(count[0] for count in counts)

    def kernel(core_ref, *refs):
        ins = refs[:total_in]
        outs = refs[total_in:]
        for job, (have, give) in zip(jobs, counts):
            more = (core_ref,) if "places" in job[2].__code__.co_varnames else ()
            job[2](ins[:have], outs[:give], *more)
            ins = ins[have:]
            outs = outs[give:]

    def spec(block, index):
        return pl.BlockSpec(block, lambda i, c: index(i, c))

    moved = sum(array.size * 2 for job in jobs for array, _, _ in job[0])
    results = call(
        kernel,
        (steps,),
        [(array, spec(block, index)) for job in jobs for array, block, index in job[0]],
        [(shape, dtype, spec(block, index)) for job in jobs for shape, dtype, block, index in job[1]],
        after=after,
        prefetch=(core,),
        cost=cost(0, 2 * moved),
        name="side",
    )
    split = []
    for _, give in counts:
        split.append(results[:give])
        results = results[give:]
    return split


def job_cast(rows, columns, by_core, steps):
    span = rows // steps
    total = sum(size for _, _, size in columns)
    ins = []
    for state, number, size in columns:
        index = lambda i, c, number=number: (c[0] * steps * by_core + i, number)
        ins.append((state, (span, size), index))
    outs = [((rows, total), BF16, (span, total), lambda i, c: (i, 0))]

    def run(have, give):
        start = 0
        for ref, (_, _, size) in zip(have, columns):
            give[0][:, start : start + size] = ref[...].astype(BF16)
            start += size

    return ins, outs, run


def job_join(left, right, steps, around):
    _, blocks, rows, size = left.shape
    span = rows // steps
    four = lambda i, c: (0, 0, i, 0)
    ins = [(value, (2, blocks, span, size), four) for value in (left, right)]
    outs = [((blocks, 2, rows, size), BF16, (blocks, 2, span, size), four)]

    def run(have, give, places):
        for side in range(2):
            for block in range(blocks):
                owner = jnp.bitwise_xor(places[1], block) if around else block
                give[0][owner, side] = have[0][side, block] + have[1][side, block]

    return ins, outs, run


def job_copy(value, first, rows):
    size = value.shape[1]
    ins = [(value, value.shape, lambda i, c: (0, 0))]
    outs = [((rows, size), value.dtype, (rows, size), lambda i, c: (0, 0))]

    def run(have, give):
        give[0][...] = have[0][first : first + rows, :]

    return ins, outs, run


def job_add(left, right, steps):
    at = left.ndim - 2
    if left.shape[at] == 1:
        same = lambda i, c: (0,) * left.ndim

        def run_whole(have, give):
            give[0][...] = have[0][...] + have[1][...]

        return (
            [(left, left.shape, same), (right, right.shape, same)],
            [(left.shape, left.dtype, left.shape, same)],
            run_whole,
        )
    block = tuple(size // steps if axis == at else size for axis, size in enumerate(left.shape))
    index = lambda i, c: (0,) * at + (i, 0)

    def run(have, give):
        give[0][...] = have[0][...] + have[1][...]

    return [(left, block, index), (right, block, index)], [(left.shape, left.dtype, block, index)], run


def job_pick(own, received, steps):
    at = own.ndim - 2
    block = tuple(size // steps if axis == at else size for axis, size in enumerate(own.shape))
    index = lambda i, c: (0,) * at + (i, 0)

    def run(have, give, places):
        give[0][...] = jnp.where(places[2] == 1, have[0][...], have[1][...])

    return [(own, block, index), (received, block, index)], [(own.shape, own.dtype, block, index)], run


def job_sum(groups, keep, send, steps):
    _, blocks, rows, _ = groups[0][0].shape
    span = rows // steps
    total = sum(own.shape[3] for own, _ in groups)
    four = lambda i, c: (0, 0, i, 0)
    three = lambda i, c: (0, i, 0)
    ins = []
    for own, received in groups:
        size = own.shape[3]
        ins.append((own, (2, blocks, span, size), four))
        if len(received) == 1:
            ins.append((received[0], (2, blocks, span, size), four))
        else:
            ins += [(value, (blocks, span, size), three) for value in received]
    kept = len(keep[0])
    outs = [((2, kept, rows, total), BF16, (2, kept, span, total), four)]
    if len(send) == 1:
        gone = len(send[0])
        outs.append(((2, gone, rows, total), BF16, (2, gone, span, total), four))
    else:
        for side in range(2):
            if send[side]:
                gone = len(send[side])
                outs.append(((gone, rows, total), BF16, (gone, span, total), three))

    def run(have, give):
        start = 0
        for own, received in groups:
            size = own.shape[3]
            columns = slice(start, start + size)
            start += size
            for side in range(2):
                for block in range(blocks):
                    other = have[1][side, block] if len(received) == 1 else have[1 + side][block]
                    value = have[0][side, block] + other
                    if block in keep[side]:
                        give[0][side, keep[side].index(block), :, columns] = value
                    elif len(send) == 1:
                        give[1][side, send[0].index(block), :, columns] = value
                    else:
                        give[1 + side][send[side].index(block), :, columns] = value
            have = have[1 + len(received) :]

    return ins, outs, run


def job_params(rows, shards, small_size):
    ins = []
    for array, row in rows:
        if array.shape[0] == 1:
            ins.append((array, array.shape, lambda i, c: (0, 0)))
        else:
            size = array.shape[1]
            ins.append((array, (16, size), lambda i, c, row=row: (row // 16, 0)))
    shape = (1, shards * small_size)
    outs = [(shape, F32, shape, lambda i, c: (0, 0))]

    def run(have, give, places):
        for number, ref in enumerate(have):
            owner = jnp.bitwise_xor(places[1], number)
            start = pl.multiple_of(owner * small_size, LANES)
            value = ref[0:1, :small_size].astype(BF16).astype(F32)
            give[0][:, pl.ds(start, small_size)] = value

    return ins, outs, run


def job_lay(values):
    total = sum(value.shape[1] for value in values)
    same = lambda i, c: (0, 0)
    ins = [(value, value.shape, same) for value in values]

    def run(have, give):
        start = 0
        for ref in have:
            give[0][:, start : start + ref.shape[1]] = ref[...]
            start += ref.shape[1]

    return ins, [((1, total), F32, (1, total), same)], run


class Links:
    def __init__(self, sizes, shard_rows):
        self.replicas, self.shards = sizes
        dp = lax.axis_index("dp")
        self.shard = lax.axis_index("shard")
        self.core = lax.rem(dp, 2)
        place = dp // 2
        self.inner = (place > 0) & (place < sizes[0] // 2 - 1)
        self.core_arr = jnp.stack([self.core, self.shard, self.inner]).astype(jnp.int32)
        self.rows = shard_rows
        self.half = shard_rows // 2
        self.fast = sizes == (8, 4)

    def swap(self, value):
        return self.across_dp(value, 1)

    def across_dp(self, value, bit):
        return lax.ppermute(value, "dp", [(d, d ^ bit) for d in range(self.replicas)])

    def along_dp(self, value, step):
        hops = ([(0, 1), (3, 2)], [(1, 2), (2, 1)], [(1, 0), (2, 3)])[step]
        pairs = [(2 * a + core, 2 * b + core) for a, b in hops for core in range(2)]
        return lax.ppermute(value, "dp", pairs)

    def across_shard(self, value, bit):
        return lax.ppermute(value, "shard", [(s, s ^ bit) for s in range(self.shards)])

    def turned_offsets(self, around):
        blocks = jnp.arange(2 * self.shards, dtype=jnp.int32)
        owner = blocks // 2
        if around:
            owner = jnp.bitwise_xor(owner, self.shard)
        away = jnp.bitwise_xor(lax.rem(blocks, 2), self.core)
        return away * (self.shards * self.half) + owner * self.half

    def gather(self, half_rows):
        return lax.all_gather(half_rows, "shard", axis=0, tiled=True)

    def gathered(self, mine, behind=None):
        if behind is not None:
            mine, _ = lax.optimization_barrier((mine, behind))
        first = jnp.arange(self.shards, dtype=jnp.int32) * self.rows
        offs = jnp.concatenate([first + self.core * self.half, first + (1 - self.core) * self.half])
        stride = mine.shape[0] // self.shards
        plan = tuple((0, t * stride, self.half, t) for t in range(self.shards)) + tuple(
            (1, t * stride, self.half, self.shards + t) for t in range(self.shards)
        )
        return Weights((mine, self.swap(mine)), plan, offs.astype(jnp.int32))

    def over_dp(self, values):
        groups = [[d for d in range(self.replicas) if d % 2 == c] for c in range(2)]
        return lax.psum(values, "dp", axis_index_groups=groups)


class Gather:
    def __init__(self, links, half_rows, own):
        self.links = links
        self.own = own
        self.by_x = links.across_shard(half_rows, 1)
        self.by_y = links.across_shard(half_rows, 2)

    def jobs(self):
        part = self.links.half // 2
        rest = self.by_x.shape[0] - part
        return [job_copy(self.by_y, 0, part), job_copy(self.by_x, part, rest)]

    def forward(self, results):
        links = self.links
        self.far = (
            links.across_shard(results[0], 1),
            links.across_shard(results[1], 2),
        )
        self.near = (links.swap(self.by_x), links.swap(self.by_y))

    def weights(self):
        links = self.links
        half, rows = links.half, links.rows
        part = half // 2
        far = tuple(links.swap(value) for value in self.far)
        pieces = (self.own, self.by_x, self.by_y, *self.near, *self.far, *far)
        plan = ((0, 0, rows, 0),)
        plan += tuple((n, 0, half, n) for n in range(1, 5))
        plan += tuple((n, 0, part, n) for n in range(5, 9))
        at = lambda bits: jnp.bitwise_xor(links.shard, bits) * rows
        mine = links.core * half
        other = (1 - links.core) * half
        offs = [at(0), at(1) + mine, at(2) + mine, at(1) + other, at(2) + other]
        offs += [at(3) + mine, at(3) + mine + part, at(3) + other, at(3) + other + part]
        return Weights(pieces, plan, jnp.stack(offs).astype(jnp.int32))


LINE, AT_ONCE, EXCHANGE = range(3)


class Reduce:
    def __init__(self, links, way, bits=((1, 2), (2, 1))):
        self.links = links
        self.way = way
        self.bits = bits
        self.stage = 0
        self.groups = []

    def add(self, own, sib):
        shape = (2, self.links.shards, self.links.half, own.shape[2])
        self.groups.append((own.reshape(shape), (self.links.swap(sib).reshape(shape),)))
        return self

    def job(self, steps):
        if self.stage > 2:
            own, received = self.groups[0]
            if self.way == LINE and self.stage == 5:
                return job_pick(own, received, steps)
            return job_add(own, received, steps)
        blocks = self.groups[0][0].shape[1]
        sides = []
        for number in range(2):
            order = self.bits[number % len(self.bits)]
            if blocks == 1:
                sides.append(())
            elif blocks == 2:
                sides.append((1,))
            else:
                sides.append(tuple(block for block in range(blocks) if block & order[0]))
        keep = [[block for block in range(blocks) if block not in gone] for gone in sides]
        send = [list(gone) for gone in sides]
        if len(self.bits) == 1 and blocks > 1:
            send = send[:1]
        return job_sum(self.groups, keep, send, steps)

    def advance(self, results):
        links = self.links
        own = results[0]
        stage = self.stage
        self.stage += 1
        if stage < 2:
            received = tuple(
                links.across_shard(value, order[stage])
                for value, order in zip(results[1:], self.bits)
            )
            self.groups = [(own, received)]
            return
        if stage == 2:
            own = own.reshape(2, own.shape[2], own.shape[3])
        if self.way == AT_ONCE:
            self.own = own
        elif self.way == LINE and stage < 5:
            self.groups = [(own, links.along_dp(own, stage - 2))]
        elif self.way == EXCHANGE and stage < 4:
            self.groups = [(own, links.across_dp(own, 2 * (stage - 1)))]
        else:
            self.grads = (own, links.swap(own))

    def close(self, behind):
        mine, _ = lax.optimization_barrier((self.own, behind))
        self.grads = (mine, self.links.swap(mine))


class Wide:
    def __init__(self, links, joined):
        self.links = links
        self.shape = joined.shape[1:]
        flat = joined.reshape(-1, joined.shape[3])
        self.own = lax.psum_scatter(flat, "shard", scatter_dimension=0, tiled=True)

    def finish(self):
        self.own = self.links.over_dp(self.own).reshape(self.shape)

    def close(self, behind):
        mine, _ = lax.optimization_barrier((self.own, behind))
        self.grads = (mine, self.links.swap(mine))


class Side:
    def __init__(self, links):
        self.links = links
        self.order = ()

    def jobs(self, jobs, steps=1, after=()):
        results = run_side(self.links.core_arr, jobs, after=(*self.order, *after), steps=steps)
        self.order = (results[0][0],)
        return [result[0] for result in results]

    def reduce(self, reduces, jobs=(), steps=2):
        work = [item.job(steps) for item in reduces] + list(jobs)
        results = run_side(self.links.core_arr, work, after=self.order, steps=steps)
        for item, result in zip(reduces, results):
            item.advance(result)
        self.order = (results[0][0],)
        return [result[0] for result in results[len(reduces) :]]

    def then(self, results):
        self.order = (results[0],)
        return results


def small_parts(small, width, hidden):
    bounds = [width] * 3 + [hidden] + [width] * 5
    parts = []
    start = 0
    for size in bounds:
        parts.append(small[:, start : start + size])
        start += size
    return parts


def body(sizes, *args):
    tokens, cotangent, lengths = args[:3]
    attn_state, mlp_state, small_state = args[3:6], args[6:9], args[9:12]
    rows, width = tokens.shape
    links = Links(sizes, attn_state[0].shape[0])
    half = links.half
    hidden = mlp_state[0].shape[1] // 2
    pairs = width // LANES
    pad = 16
    core_arr = links.core_arr
    around = links.turned_offsets(links.fast)
    side = Side(links)

    ends = jnp.cumsum(lengths[0], dtype=jnp.int32)
    small_own = small_state[0][None]
    small_size = small_own.shape[1]
    (
        BIAS_Q,
        BIAS_V,
        BIAS_O,
        BIAS_UP,
    ) = range(4)
    BIAS_DN, GAIN_ONE, SHIFT_ONE, GAIN_TWO, SHIFT_TWO = range(
        BIAS_UP + hidden // width, BIAS_UP + hidden // width + 5
    )

    def first_job():
        ins = [
            (attn_state[0], (half, 4 * width), lambda i, c: (c[0], 0)),
            (small_own, (1, small_size), lambda i, c: (0, 0)),
        ]
        outs = [((half + pad, 4 * width), BF16, (half + pad, 4 * width), lambda i, c: (0, 0))]

        def job(have, give):
            give[0][:half] = have[0][...].astype(BF16)
            row = have[1][...].astype(BF16)
            give[0][half:, :small_size] = jnp.broadcast_to(row, (pad, small_size))

        return ins, outs, job

    block = hidden // 2
    groups = [[(mlp_state[0], number, block) for number in pair] for pair in ((0, 2), (1, 3))]
    (first_half,) = side.jobs([first_job()])
    if links.fast:
        attn_gather = Gather(links, first_half, None)
    else:
        attn_weights = links.gathered(links.gather(first_half))
    dy, dyt, grad_bias_dn = side.then(run_cot(half, around, ends, cotangent, after=side.order))
    (more_half,) = side.jobs([job_cast(half, groups[1], 1, 4)], steps=4)
    if links.fast:
        (attn_gather.own,) = side.jobs(
            [job_cast(links.rows, [(attn_state[0], 0, 4 * width)], 0, 4)], steps=4
        )
        *copied, feed_half = side.jobs([*attn_gather.jobs(), job_cast(half, groups[0], 1, 1)])
        attn_gather.forward(copied)
    else:
        (feed_half,) = side.jobs([job_cast(half, groups[0], 1, 1)])
    wide = links.gather(feed_half)
    more_wide = links.gather(more_half)
    if links.fast:
        attn_weights = attn_gather.weights()
        rows_of = [
            (small_own, 0),
            (attn_gather.by_x, half),
            (attn_gather.by_y, half),
            (attn_gather.far[1], half // 2),
        ]
        (small,) = side.jobs([job_params(rows_of, links.shards, small_size)])
    else:
        small = attn_weights.pieces[0].reshape(links.shards, half + pad, 4 * width)
        small = small[:, half, :small_size].astype(F32).reshape(1, -1)

    qkv, turned_one = side.then(
        run_qkv(
            half,
            attn_weights,
            around,
            tokens,
            small,
            (BIAS_Q, BIAS_V, GAIN_ONE, SHIFT_ONE),
            after=side.order,
        )
    )
    mixed, lse = side.then(run_attend(ends, qkv, 0, pairs, after=side.order))
    wide = links.gathered(wide, lse)
    side.order += (wide.pieces[0],)
    after, low_two, turned_two, turned_mixed = side.then(
        run_after(
            half,
            attn_weights.at(3 * width),
            (around, around),
            mixed,
            tokens,
            small,
            (BIAS_O, GAIN_TWO, SHIFT_TWO),
            after=side.order,
        )
    )

    passed, grad_bias_up = [None], []
    blocked = lambda value: value.reshape(2, links.shards, half, value.shape[2])

    def feed(start, up_weights, down_weights):
        act, du, own, sib, gbias = run_feed(
            up_weights,
            down_weights,
            low_two,
            turned_two,
            dy,
            dyt,
            small,
            BIAS_UP * width + start,
            start,
            block,
            passed[-1],
            after=side.order,
        )
        side.order = (own,)
        passed.append((act, du))
        grad_bias_up.append(gbias)
        return own, sib

    def unit(way, own, sib, bits=((1, 2), (2, 1))):
        if links.fast:
            return Reduce(links, way, bits).add(own, sib)
        return Wide(links, side.jobs([join(own, links.swap(sib))], steps=4)[0])

    def join(own, received):
        return job_join(blocked(own), blocked(received), 4, links.fast)

    def reduce(units, jobs=(), steps=2):
        if links.fast:
            return side.reduce(units, jobs, steps)
        return side.jobs(jobs, steps) if jobs else None

    group_a = feed(0, wide, wide.at(block))
    more_wide = links.gathered(more_wide, grad_bias_up[0])
    unit_a = unit(LINE, *group_a)
    reduce([unit_a], steps=4)
    unit_b = unit(AT_ONCE, *feed(block, more_wide, more_wide.at(block)))
    reduce([unit_a], steps=4)
    (
        grad_after,
        dmix,
        own_out,
        sib_out,
        grad_bias_o,
        grad_gain_two,
        grad_shift_two,
    ) = side.then(
        run_middle(
            [(block, wide), (block, more_wide)],
            attn_weights.at(3 * width),
            passed[-1][1],
            after,
            dy,
            small,
            GAIN_TWO,
            turned_mixed,
            after=side.order,
        )
    )
    received_out = links.swap(sib_out)
    reduce([unit_a, unit_b], steps=4)
    grads, biases = [], []

    def attend_back(first):
        dq, dk, dv, gq, gv = side.then(
            run_attend_back(ends, qkv, mixed, dmix, lse, first, pairs // 2, after=side.order)
        )
        grads.append((dq, dk, dv))
        biases.append((gq, gv))

    def project(group):
        return side.then(run_project(turned_one, *grads[group], after=side.order))

    attend_back(0)
    (joined,) = reduce([unit_a, unit_b], [join(own_out, received_out)], steps=4)
    unit_e = Wide(links, joined)
    unit_c = unit(EXCHANGE, *project(0), ((1, 2),))
    attend_back(pairs // 2)
    reduce([unit_a, unit_b, unit_c], steps=4)
    if links.fast:
        unit_b.own = links.over_dp(unit_b.own)
    unit_d = unit(EXCHANGE, *project(1), ((1, 2),))
    grad_input, grad_gain_one, grad_shift_one = side.then(
        run_input(attn_weights, grads, tokens, grad_after, small, GAIN_ONE, after=side.order)
    )
    small_grads = [biases[0][0], biases[1][0], biases[0][1], biases[1][1], grad_bias_o]
    small_grads += grad_bias_up
    small_grads += [grad_bias_dn, grad_gain_one, grad_shift_one, grad_gain_two, grad_shift_two]
    if links.fast:
        side.order += (unit_e.own,)
    (grad_small,) = reduce([unit_a, unit_c, unit_d], [job_lay(small_grads)])

    def pick_feed(number, arrays):
        return [arrays[0][number]]

    def adam_mlp(number, item, earlier):
        return side.then(
            run_adam(
                core_arr,
                mlp_state,
                [item.grads],
                block,
                [number, 2 + number],
                pick_feed,
                earlier,
                after=side.order,
            )
        )

    out_block = width // 2

    def pick_heads(number, arrays):
        left, right = arrays[0][0], arrays[0][1]
        split = out_block // 2
        if number > 2:
            return [arrays[1][number - 3]]
        return (
            [left[:, :out_block]],
            [left[:, out_block:], right[:, :split]],
            [right[:, split:]],
        )[number]

    def adam_attn(items, places, earlier):
        return side.then(
            run_adam(
                core_arr,
                attn_state,
                [item.grads for item in items],
                out_block,
                places,
                pick_heads,
                earlier,
                after=side.order,
            )
        )

    def output_now():
        out = run_output(
            [(block, wide.at(block)), (block, more_wide.at(block))],
            passed[-1][0],
            after,
            small,
            BIAS_DN,
            after=side.order,
        )
        side.then([out])
        return out

    if links.fast:
        shard_move = lambda bit: functools.partial(links.across_shard, bit=bit)
        dp_move = lambda bit: functools.partial(links.across_dp, bit=bit)
        moved = links.across_shard(grad_small, 1)

        def step(units, move):
            (total,) = reduce(units, [job_add(grad_small, moved, 2)])
            return total, move(total) if move else None

        mlp_new = adam_mlp(0, unit_a, None)
        grad_small, moved = step([unit_c, unit_d], shard_move(2))
        output = output_now()
        grad_small, moved = step([unit_c, unit_d], links.swap)
        unit_b.close(grad_small)
        unit_e.own, _ = lax.optimization_barrier((unit_e.own, unit_b.own))
        unit_e.finish()
        mlp_new = adam_mlp(1, unit_b, mlp_new)
        grad_small, moved = step([unit_c, unit_d], dp_move(2))
        unit_e.close(grad_small)
        attn_new = adam_attn([unit_c], [0, 2, 4], None)
        grad_small, moved = step([unit_d], dp_move(4))
        attn_new = adam_attn([unit_d, unit_e], [1, 3, 5, 6, 7], attn_new)
        grad_small, _ = step([], None)
    else:
        for item in (unit_a, unit_b, unit_c, unit_d, unit_e):
            item.finish()
            item.close(grad_input)
        grad_small = lax.psum(grad_small, ("dp", "shard"))
        output = output_now()
        mlp_new = adam_mlp(1, unit_b, adam_mlp(0, unit_a, None))
        attn_new = adam_attn([unit_c], [0, 2, 4], None)
        attn_new = adam_attn([unit_d, unit_e], [1, 3, 5, 6, 7], attn_new)
    grad_small = lax.dynamic_slice_in_dim(grad_small, links.shard * small_size, small_size, 1)[0]
    small_new = adamw(*small_state, grad_small, 0.4, 0.0)
    return (output, grad_input, *attn_new, *mlp_new, *small_new)


def solution(mesh):
    tokens = P(("dp", "shard"), None)
    state = P("shard", None)
    vector = P("shard")
    return jax.shard_map(
        functools.partial(body, (mesh.shape["dp"], mesh.shape["shard"])),
        mesh=mesh,
        in_specs=(tokens,) * 3 + (state,) * 6 + (vector,) * 3,
        out_specs=(tokens,) * 2 + (state,) * 6 + (vector,) * 3,
        check_vma=False,
    )
```

```python
import functools

import jax
import jax.numpy as jnp
from jax import lax
from jax.experimental import pallas as pl
from jax.experimental.pallas import tpu as pltpu
from jax.sharding import PartitionSpec as P

HD = 64
STEP = 10
LANES = 128
MASKED = -1e30
SAFE = 60.0
GELU_IN = 0.7978845608028654
GELU_CUBE = 0.044715

beta_one = 0.9
beta_two = 0.95
adam_eps = 1e-08
norm_eps = 1e-05

F32 = jnp.float32
BF16 = jnp.bfloat16
MIB = 1024 * 1024
VMEM_MIB = 64

ANY = pl.BlockSpec(memory_space=pl.ANY)
SMEM = pl.BlockSpec(memory_space=pltpu.SMEM)


def dot_nn(left, right):
    return lax.dot_general(left, right, (((1,), (0,)), ((), ())), preferred_element_type=F32)


def dot_nt(left, right):
    return lax.dot_general(left, right, (((1,), (1,)), ((), ())), preferred_element_type=F32)


def dot_tn(left, right):
    return lax.dot_general(left, right, (((0,), (0,)), ((), ())), preferred_element_type=F32)


def whole(shape):
    return pl.BlockSpec(shape, lambda *_: (0,) * len(shape))


def call(kernel, grid, ins, outs, after=(), reuse=(), prefetch=(), scratch=(), cost=None, name=None):
    known = len(prefetch) + len(ins)
    idle = [*after, *(array for array, _ in reuse)]

    def run(*refs):
        kernel(*refs[:known], *refs[known + len(idle) :])

    def placed(array, spec):
        if spec is SMEM:
            return array
        return pltpu.with_memory_space_constraint(array, pltpu.HBM)

    return pl.pallas_call(
        run,
        grid_spec=pltpu.PrefetchScalarGridSpec(
            num_scalar_prefetch=len(prefetch),
            grid=grid,
            in_specs=[spec for _, spec in ins] + [ANY] * len(idle),
            out_specs=[spec for _, _, spec in outs],
            scratch_shapes=list(scratch),
        ),
        out_shape=[pltpu.HBM(shape, dtype) for shape, dtype, _ in outs],
        input_output_aliases={
            known + len(after) + number: output for number, (_, output) in enumerate(reuse)
        },
        compiler_params=pltpu.CompilerParams(vmem_limit_bytes=VMEM_MIB * MIB),
        cost_estimate=cost,
        name=name,
    )(*prefetch, *(placed(*item) for item in ins), *(placed(array, ANY) for array in idle))


def param(small, number, width):
    return (small, pl.BlockSpec((1, width), lambda *_: (0, number)))


def cost(flops, moved, exps=0):
    return pl.CostEstimate(flops=int(flops), bytes_accessed=int(moved), transcendentals=int(exps))


def store_turned(turned_ref, toff, block, half, value, columns):
    turned = value.astype(BF16).T
    for part in range(LANES // half):
        offset = pl.multiple_of(toff[block * (LANES // half) + part], half)
        turned_ref[pl.ds(offset, half), columns] = turned[part * half : (part + 1) * half]


def norm_stats(values):
    center = values - jnp.mean(values, axis=-1, keepdims=True)
    spread = jnp.mean(center * center, axis=-1, keepdims=True)
    scale = lax.rsqrt(spread + norm_eps)
    return center * scale, scale


def norm_back(hat, scale, grad_hat):
    mean = jnp.mean(grad_hat, axis=-1, keepdims=True)
    along = jnp.mean(grad_hat * hat, axis=-1, keepdims=True)
    return scale * (grad_hat - mean - hat * along)


def accumulate(ref, value, first):
    @pl.when(first)
    def _():
        ref[...] = value

    @pl.when(jnp.logical_not(first))
    def _():
        ref[...] += value


class Weights:
    def __init__(self, pieces, plan, offs, first=0):
        self.pieces, self.plan, self.offs, self.first = pieces, plan, offs, first

    def at(self, first):
        return Weights(self.pieces, self.plan, self.offs, self.first + first)

    def inputs(self):
        return [(self.offs, SMEM)] + [(piece, ANY) for piece in self.pieces]

    def sems(self):
        return pltpu.SemaphoreType.DMA((len(self.plan),))

    def rest(self, refs):
        return refs[1 + len(self.pieces) :]

    def copies(self, refs, size, target, sems, start=None):
        offs, refs = refs[0], refs[1:]
        columns = slice(self.first, self.first + size)
        if start is not None:
            columns = pl.ds(pl.multiple_of(self.first + start, LANES), size)
        made = []
        for number, (piece, first, rows, index) in enumerate(self.plan):
            offset = pl.multiple_of(offs[index], rows)
            made.append(
                pltpu.make_async_copy(
                    refs[piece].at[pl.ds(first, rows), columns],
                    target(offset, rows),
                    sems.at[number],
                )
            )
        return made, refs[len(self.pieces) :]


def start_all(copies):
    @pl.when(pl.program_id(0) == 0)
    def _():
        for copy in copies:
            copy.start()


def wait_all(copies):
    @pl.when(pl.program_id(0) == 0)
    def _():
        for copy in copies:
            copy.wait()


def cot_kernel(half, toff, ends, cot_ref, dy_ref, turned_ref, bias_ref):
    rows = cot_ref.shape[0]
    place = lax.broadcasted_iota(jnp.int32, (rows, LANES), 0)
    live = (place < ends[ends.shape[0] - 1]).astype(F32)
    for block in range(cot_ref.shape[1] // LANES):
        columns = slice(block * LANES, (block + 1) * LANES)
        value = cot_ref[:, columns].astype(F32) * live
        dy_ref[:, columns] = value.astype(BF16)
        bias_ref[:, columns] = jnp.sum(value, axis=0, keepdims=True)
        store_turned(turned_ref, toff, block, half, value, slice(None))


def run_cot(half, toff, ends, cot, after=()):
    rows, width = cot.shape
    return call(
        functools.partial(cot_kernel, half),
        (1,),
        [(toff, SMEM), (ends, SMEM), (cot, whole(cot.shape))],
        [
            ((rows, width), BF16, whole((rows, width))),
            ((width, rows), BF16, whole((width, rows))),
            ((1, width), F32, whole((1, width))),
        ],
        after=after,
        cost=cost(0, 6 * rows * width),
        name="cotangent",
    )


def run_qkv(half, weights, toff, x, small, numbers, after=()):
    rows, width = x.shape
    span = 256

    def kernel(*refs):
        weight, sems = refs[-2:]
        copies, refs = weights.copies(
            refs, 3 * width, lambda at, size: weight.at[pl.ds(at, size), :], sems
        )
        toff_ref, x_ref, bias_q, bias_v, gain_ref, shift_ref, qkv_ref, turned_ref = refs[:8]
        start_all(copies)
        hat, _ = norm_stats(x_ref[...].astype(F32))
        normed = hat * gain_ref[...] + shift_ref[...]
        for block in range(width // LANES):
            columns = slice(block * LANES, (block + 1) * LANES)
            store_turned(turned_ref, toff_ref, block, half, normed[:, columns], slice(None))
        wait_all(copies)
        low = normed.astype(BF16)
        for part in range(3):
            columns = slice(part * width, (part + 1) * width)
            value = dot_nn(low, weight[:, columns])
            if part == 2:
                value += bias_v[...]
            if part == 0:
                value = (value + bias_q[...]).astype(BF16).astype(F32) * HD ** (-0.5)
            qkv_ref[:, columns] = value.astype(BF16)

    return call(
        kernel,
        (rows // span,),
        weights.inputs()
        + [
            (toff, SMEM),
            (x, pl.BlockSpec((span, width), lambda i: (i, 0))),
        ]
        + [param(small, number, width) for number in numbers],
        [
            ((rows, 3 * width), BF16, pl.BlockSpec((span, 3 * width), lambda i: (i, 0))),
            ((width, rows), BF16, pl.BlockSpec((width, span), lambda i: (0, i))),
        ],
        after=after,
        scratch=[pltpu.VMEM((width, 3 * width), BF16), weights.sems()],
        cost=cost(6 * rows * width * width, 16 * rows * width),
        name="qkv",
    )


def first_of_row(ends, place):
    first = jnp.zeros_like(place)
    for number in range(ends.shape[0]):
        first = jnp.where(place >= ends[number], ends[number], first)
    return first


def attend_kernel(ends, q_ref, k_ref, v_ref, o_ref, lse_ref, allow):
    rows = q_ref.shape[0]
    span = min(256, rows)

    @pl.when(pl.program_id(0) == 0)
    def _():
        for start in range(0, rows, span):
            keys = start + span
            place = lax.broadcasted_iota(jnp.int32, (span, 1), 0) + start
            first = first_of_row(ends, place)
            key = lax.broadcasted_iota(jnp.int32, (span, keys), 1)
            allow[start:keys, :keys] = jnp.where((key <= place) & (key >= first), 0.0, MASKED)

    lane = lax.broadcasted_iota(jnp.int32, (1, LANES), 1)
    low_lane = lane < HD
    one = low_lane.astype(BF16)
    masks = (one, 1 - one)

    same = (lax.broadcasted_iota(jnp.int32, (LANES, LANES), 0) < HD) == (
        lax.broadcasted_iota(jnp.int32, (LANES, LANES), 1) < HD
    )
    same = same.astype(F32).astype(BF16)
    longest = [
        jnp.max(dot_nn(ref[...] * ref[...], same), axis=0, keepdims=True) for ref in (q_ref, k_ref)
    ]
    bounded = jnp.max(longest[0] * longest[1]) < SAFE * SAFE

    def attend(shift):
        mixed = [v_ref[...] * mask + (1 - mask) for mask in masks]
        for start in range(0, rows, span):
            keys = start + span
            sums = []
            tops = []
            for head in range(2):
                query = q_ref[start:keys, :] * masks[head]
                scores = dot_nt(query, k_ref[:keys, :]) + allow[start:keys, :keys]
                if shift:
                    top = jnp.max(scores, axis=1, keepdims=True)
                    tops.append(top)
                    scores = scores - top
                probs = jnp.exp(scores).astype(BF16)
                sums.append(dot_nn(probs, mixed[head][:keys]))
            total = pltpu.roll(jnp.where(low_lane, sums[1], sums[0]), HD, 1)
            out = jnp.where(low_lane, sums[0], sums[1]) / total
            o_ref[start:keys, :] = out.astype(BF16)
            lse = jnp.log(total)
            if shift:
                lse += jnp.where(low_lane, tops[0], tops[1])
            lse = lse.T
            lse_ref[0, 0:1, start:keys] = lse[0:1]
            lse_ref[0, 1:2, start:keys] = lse[HD : HD + 1]

    @pl.when(bounded)
    def _():
        attend(False)

    @pl.when(jnp.logical_not(bounded))
    def _():
        attend(True)


def run_attend(ends, qkv, first, count, earlier=None, after=()):
    rows = qkv.shape[0]
    width = qkv.shape[1] // 3
    pairs = width // LANES
    column = lambda shift: pl.BlockSpec((rows, LANES), lambda i: (0, i + shift))
    return call(
        attend_kernel,
        (count,),
        [(ends, SMEM)] + [(qkv, column(first + part * pairs)) for part in range(3)],
        [
            ((rows, width), BF16, column(first)),
            ((pairs, 2, rows), F32, pl.BlockSpec((1, 2, rows), lambda i: (i + first, 0, 0))),
        ],
        after=after,
        reuse=[] if earlier is None else [(earlier[0], 0), (earlier[1], 1)],
        scratch=[pltpu.VMEM((rows, rows), F32)],
        cost=cost(8 * rows * rows * LANES * count, 8 * rows * LANES * count, 2 * rows * rows * count),
        name="attend",
    )


def run_after(half, weights, toffs, mixed, x, small, numbers, after=()):
    rows, width = x.shape
    span = 256

    def kernel(*refs):
        weight, sems = refs[-2:]
        copies, refs = weights.copies(
            refs, width, lambda at, size: weight.at[pl.ds(at, size), :], sems
        )
        mixed_toff, low_toff, mixed_ref, x_ref, bias_ref, gain_ref, shift_ref = refs[:7]
        after_ref, low_ref, turned_ref, mixed_turned_ref = refs[7:11]
        start_all(copies)
        for block in range(width // LANES):
            columns = slice(block * LANES, (block + 1) * LANES)
            store_turned(mixed_turned_ref, mixed_toff, block, half, mixed_ref[:, columns], slice(None))
        wait_all(copies)
        value = x_ref[...].astype(F32) + dot_nn(mixed_ref[...], weight[...]) + bias_ref[...]
        after_ref[...] = value
        hat, _ = norm_stats(value)
        normed = hat * gain_ref[...] + shift_ref[...]
        low_ref[...] = normed.astype(BF16)
        for block in range(width // LANES):
            columns = slice(block * LANES, (block + 1) * LANES)
            store_turned(turned_ref, low_toff, block, half, normed[:, columns], slice(None))

    by_row = pl.BlockSpec((span, width), lambda i: (i, 0))
    by_column = pl.BlockSpec((width, span), lambda i: (0, i))
    return call(
        kernel,
        (rows // span,),
        weights.inputs()
        + [(toff, SMEM) for toff in toffs]
        + [(mixed, by_row), (x, by_row)]
        + [param(small, number, width) for number in numbers],
        [
            ((rows, width), F32, by_row),
            ((rows, width), BF16, by_row),
            ((width, rows), BF16, by_column),
            ((width, rows), BF16, by_column),
        ],
        after=after,
        scratch=[pltpu.VMEM((width, width), BF16), weights.sems()],
        cost=cost(2 * rows * width * width, 14 * rows * width),
        name="after",
    )


def run_feed(up_weights, down_weights, low, turned, dy, dyt, small, first, begin, block, earlier, after=()):
    rows, width = low.shape
    hidden = earlier[0].shape[1] if earlier is not None else block_total(small, width)
    span = 256
    mid = width // 2
    count = block // span
    by_column = lambda size: pl.BlockSpec((size, span), lambda i: (0, i))
    shifted = pl.BlockSpec((rows, span), lambda i: (0, begin // span + i))
    grad = ((2, mid, block), BF16, pl.BlockSpec((2, mid, span), lambda i: (0, 0, i)))

    def kernel(*refs):
        up, down, up_sems, down_sems = refs[-4:]
        step = pl.program_id(0)

        def copies(number):
            columns = pl.ds(pl.multiple_of(number * span, span), span)
            made, rest = up_weights.copies(
                refs,
                span,
                lambda at, size: up.at[pl.ds(at, size), columns],
                up_sems.at[number],
                number * span,
            )
            more, _ = down_weights.copies(
                rest,
                span,
                lambda at, size: down.at[pl.ds(at, size), columns],
                down_sems.at[number],
                number * span,
            )
            return made + more

        @pl.when(step == 0)
        def _():
            for copy in copies(0):
                copy.start()

        @pl.when(step + 1 < count)
        def _():
            for copy in copies(step + 1):
                copy.start()

        for copy in copies(step):
            copy.wait()
        low_ref, turned_ref, dy_ref, dyt_ref, bias_ref, act_ref, du_ref, own_ref, sib_ref, gbias_ref = (
            down_weights.rest(up_weights.rest(refs))[:10]
        )
        columns = pl.ds(pl.multiple_of(step * span, span), span)
        upper = dot_nn(low_ref[...], up[:, columns]) + bias_ref[...]
        grad_act = dot_nn(dy_ref[...], down[:, columns])
        square = (GELU_IN * GELU_CUBE) * (upper * upper)
        tanh = jnp.tanh(upper * (GELU_IN + square))
        share = 0.5 + 0.5 * tanh
        act = upper * share
        slope = share + act * (1.0 - tanh) * (GELU_IN + 3.0 * square)
        act = act.astype(BF16)
        du = (grad_act * slope).astype(BF16)
        act_ref[...] = act
        du_ref[...] = du
        gbias_ref[...] = jnp.sum(du.astype(F32), axis=0, keepdims=True)
        grad_up = dot_nn(turned_ref[...], du).astype(BF16)
        own_ref[0] = grad_up[:mid]
        sib_ref[0] = grad_up[mid:]
        grad_dn = dot_nn(dyt_ref[...], act).astype(BF16)
        own_ref[1] = grad_dn[:mid]
        sib_ref[1] = grad_dn[mid:]

    return call(
        kernel,
        (count,),
        up_weights.inputs()
        + down_weights.inputs()
        + [
            (low, whole((rows, width))),
            (turned, whole((width, rows))),
            (dy, whole((rows, width))),
            (dyt, whole((width, rows))),
            (small, pl.BlockSpec((1, span), lambda i: (0, first // span + i))),
        ],
        [
            ((rows, hidden), BF16, shifted),
            ((rows, hidden), BF16, shifted),
            grad,
            grad,
            ((1, block), F32, by_column(1)),
        ],
        after=after,
        reuse=[] if earlier is None else [(earlier[0], 0), (earlier[1], 1)],
        scratch=[
            pltpu.VMEM((width, block), BF16),
            pltpu.VMEM((width, block), BF16),
            pltpu.SemaphoreType.DMA((count, len(up_weights.plan))),
            pltpu.SemaphoreType.DMA((count, len(down_weights.plan))),
        ],
        cost=cost(8 * rows * width * block, 24 * width * block, rows * block),
        name="feed",
    )


def block_total(small, width):
    return small.shape[1] - 8 * width


class Stream:
    def __init__(self):
        self.parts = []

    def add(self, copies):
        self.parts.append(copies)

    def start(self):
        for copies in self.parts:
            for copy in copies:
                copy.start()

    def wait(self, number):
        for copy in self.parts[number]:
            copy.wait()


def run_output(weights, acts, after_value, small, number, after=()):
    rows, width = after_value.shape
    hidden = acts.shape[1]
    span = 256
    bounds = [0]
    for size, _ in weights:
        bounds.append(bounds[-1] + size)
    by_row = lambda size: pl.BlockSpec((span, size), lambda i: (i, 0))

    def kernel(*refs):
        down = refs[-1 - len(weights)]
        sems = refs[-len(weights) :]
        stream = []
        for index, (size, item) in enumerate(weights):
            columns = slice(bounds[index], bounds[index + 1])
            copies, refs = item.copies(
                refs,
                size,
                lambda at, lines, columns=columns: down.at[pl.ds(at, lines), columns],
                sems[index],
            )
            stream.append(copies)
        act_ref, after_ref, bias_ref, out_ref = refs[:4]
        for copies in stream:
            start_all(copies)
        total = after_ref[...] + bias_ref[...]
        for index, copies in enumerate(stream):
            wait_all(copies)
            columns = slice(bounds[index], bounds[index + 1])
            total += dot_nt(act_ref[:, columns], down[:, columns])
        out_ref[...] = total.astype(BF16)

    (out,) = call(
        kernel,
        (rows // span,),
        [item for _, weight in weights for item in weight.inputs()]
        + [(acts, by_row(hidden)), (after_value, by_row(width)), param(small, number, width)],
        [((rows, width), BF16, by_row(width))],
        after=after,
        scratch=[pltpu.VMEM((width, hidden), BF16)] + [weight.sems() for _, weight in weights],
        cost=cost(rows * width * hidden // 5, 2 * rows * width),
        name="output",
    )
    return out


def run_middle(weights, out_weights, dus, after_value, dy, small, number, turned, after=()):
    rows, width = after_value.shape
    hidden = dus.shape[1]
    part = width
    parts = hidden // part
    span = 256
    mid = width // 2
    places = [
        (item.at(start)) for size, item in weights for start in range(0, size, part)
    ]
    most = max(len(item.plan) for item in places)

    def kernel(*refs):
        du, up, value_in, dy_in, turned_in, out_weight, branch, sems, out_sems, own_sems = refs[-10:]
        stream = Stream()
        for index, item in enumerate(places):
            columns = slice(index * part, (index + 1) * part)
            copies, refs = item.copies(
                refs,
                part,
                lambda at, size, columns=columns: up.at[pl.ds(at, size), columns],
                sems.at[index],
            )
            stream.add(copies)
        more, refs = out_weights.copies(
            refs, width, lambda at, size: out_weight.at[pl.ds(at, size), :], out_sems
        )
        du_ref, after_ref, dy_ref, gain_ref, turned_ref = refs[:5]
        grad_ref, dmix_ref, own_ref, sib_ref, gbias_ref, ggain_ref, gshift_ref = refs[5:12]
        for index in range(parts):
            columns = slice(index * part, (index + 1) * part)
            stream.parts[index].append(
                pltpu.make_async_copy(du_ref.at[:, columns], du.at[:, columns], own_sems.at[index])
            )
        stream.add(
            [
                pltpu.make_async_copy(after_ref, value_in, own_sems.at[parts]),
                pltpu.make_async_copy(dy_ref, dy_in, own_sems.at[parts + 1]),
            ]
        )
        stream.add([pltpu.make_async_copy(turned_ref, turned_in, own_sems.at[parts + 2]), *more])
        stream.start()
        total = None
        for index in range(parts):
            columns = slice(index * part, (index + 1) * part)
            stream.wait(index)
            value = dot_nt(du[:, columns], up[:, columns])
            total = value if total is None else total + value
        stream.wait(parts)
        gain = gain_ref[...]
        sums = [jnp.zeros((1, width), F32)] * 3
        for start in range(0, rows, span):
            lines = slice(start, start + span)
            grad = total[lines]
            hat, scale = norm_stats(value_in[lines, :])
            full = dy_in[lines, :].astype(F32) + norm_back(hat, scale, grad * gain)
            grad_ref[lines, :] = full
            low = full.astype(BF16)
            branch[lines, :] = low
            for index, value in enumerate((low.astype(F32), grad * hat, grad)):
                sums[index] = sums[index] + jnp.sum(value, axis=0, keepdims=True)
        gbias_ref[...], ggain_ref[...], gshift_ref[...] = sums
        stream.wait(parts + 1)
        dmix_ref[...] = dot_nt(branch[...], out_weight[...]).astype(BF16)
        for side in range(2):
            columns = slice(side * (width // 2), (side + 1) * (width // 2))
            value = dot_nn(turned_in[...], branch[:, columns]).astype(BF16)
            own_ref[side] = value[:mid]
            sib_ref[side] = value[mid:]

    grads = ((2, mid, width // 2), BF16, whole((2, mid, width // 2)))
    vector = ((1, width), F32, whole((1, width)))
    full = whole((rows, width))
    return call(
        kernel,
        (1,),
        [item for place in places for item in place.inputs()]
        + out_weights.inputs()
        + [(dus, ANY), (after_value, ANY), (dy, ANY), param(small, number, width), (turned, ANY)],
        [((rows, width), F32, full), ((rows, width), BF16, full), grads, grads] + [vector] * 3,
        after=after,
        scratch=[
            pltpu.VMEM((rows, hidden), BF16),
            pltpu.VMEM((width, hidden), BF16),
            pltpu.VMEM((rows, width), F32),
            pltpu.VMEM((rows, width), BF16),
            pltpu.VMEM((width, rows), BF16),
            pltpu.VMEM((width, width), BF16),
            pltpu.VMEM((rows, width), BF16),
            pltpu.SemaphoreType.DMA((parts, most)),
            out_weights.sems(),
            pltpu.SemaphoreType.DMA((parts + 3,)),
        ],
        cost=cost(8 * rows * width * (hidden + 2 * width), 120 * rows * width),
        name="middle",
    )


def attend_back_kernel(
    ends,
    q_ref,
    k_ref,
    v_ref,
    o_ref,
    do_ref,
    lse_ref,
    dq_ref,
    dk_ref,
    dv_ref,
    gq_ref,
    gv_ref,
    allow,
    total,
):
    rows = q_ref.shape[0]
    span = min(256, rows)

    @pl.when(pl.program_id(0) == 0)
    def _():
        for start in range(0, rows, span):
            query = lax.broadcasted_iota(jnp.int32, (1, rows - start), 1) + start
            first = first_of_row(ends, query)
            key = lax.broadcasted_iota(jnp.int32, (span, rows - start), 0) + start
            allow[start : start + span, start:] = jnp.where(
                (key <= query) & (key >= first), 0.0, MASKED
            )

    lane = lax.broadcasted_iota(jnp.int32, (1, LANES), 1)
    low_lane = lane < HD
    one = low_lane.astype(BF16)
    masks = (one, 1 - one)
    product = (o_ref[...].astype(F32) * do_ref[...].astype(F32)).T
    inner = (
        jnp.sum(product[:HD], axis=0, keepdims=True),
        jnp.sum(product[HD:], axis=0, keepdims=True),
    )
    for start in range(0, rows, span):
        stop = start + span
        grads = []
        for head in range(2):
            keys = k_ref[start:stop, :] * masks[head]
            vals = v_ref[start:stop, :] * masks[head]
            scores = dot_nt(keys, q_ref[start:, :]) + allow[start:stop, start:]
            probs = jnp.exp(scores - lse_ref[0, head : head + 1, start:])
            grad_probs = dot_nt(vals, do_ref[start:, :])
            grad_scores = (probs * (grad_probs - inner[head][:, start:])).astype(BF16)
            grad_vals = dot_nn(probs.astype(BF16), do_ref[start:, :])
            grad_keys = dot_nn(grad_scores, q_ref[start:, :])
            grads.append((grad_keys, grad_vals))
            update = dot_tn(grad_scores, keys)
            if start == 0 and head == 0:
                total[...] = update
            else:
                total[start:, :] += update
        dk_ref[start:stop, :] = jnp.where(low_lane, grads[0][0], grads[1][0]).astype(BF16)
        dv_ref[start:stop, :] = jnp.where(low_lane, grads[0][1], grads[1][1]).astype(BF16)
    grad_query = (total[...] * HD ** (-0.5)).astype(BF16)
    dq_ref[...] = grad_query
    gq_ref[...] = jnp.sum(grad_query.astype(F32), axis=0, keepdims=True)
    gv_ref[...] = jnp.sum(dv_ref[...].astype(F32), axis=0, keepdims=True)


def run_attend_back(ends, qkv, mixed, dmix, lse, first, count, after=()):
    rows, width = mixed.shape
    pairs = width // LANES
    column = lambda shift: pl.BlockSpec((rows, LANES), lambda i: (0, i + shift))
    return call(
        attend_back_kernel,
        (count,),
        [(ends, SMEM)]
        + [(qkv, column(first + part * pairs)) for part in range(3)]
        + [
            (mixed, column(first)),
            (dmix, column(first)),
            (lse, pl.BlockSpec((1, 2, rows), lambda i: (i + first, 0, 0))),
        ],
        [((rows, LANES * count), BF16, column(0))] * 3
        + [((1, LANES * count), F32, pl.BlockSpec((1, LANES), lambda i: (0, i)))] * 2,
        after=after,
        scratch=[pltpu.VMEM((rows, rows), F32), pltpu.VMEM((rows, LANES), F32)],
        cost=cost(
            80 * rows * rows * LANES * count, rows * LANES * count
        ),
        name="attend_back",
    )


def project_kernel(turned_ref, dq_ref, dk_ref, dv_ref, own_ref, sib_ref):
    mid = own_ref.shape[1]
    size = dq_ref.shape[1]
    left = jnp.concatenate([dq_ref[...], dk_ref[:, : size // 2]], axis=1)
    right = jnp.concatenate([dk_ref[:, size // 2 :], dv_ref[...]], axis=1)
    for side, columns in enumerate((left, right)):
        own_ref[side] = dot_nn(turned_ref[:mid], columns).astype(BF16)
        sib_ref[side] = dot_nn(turned_ref[mid:], columns).astype(BF16)


def run_project(turned, dq, dk, dv, after=()):
    width, rows = turned.shape
    size = dq.shape[1]
    mid = width // 2
    grad = ((2, mid, 3 * size // 2), BF16, whole((2, mid, 3 * size // 2)))
    return call(
        project_kernel,
        (1,),
        [(turned, whole((width, rows)))] + [(value, whole((rows, size))) for value in (dq, dk, dv)],
        [grad, grad],
        after=after,
        cost=cost(6 * rows * width * size, 14 * rows * size),
        name="project",
    )


def run_input(weights, grads, x, grad_after, small, number, after=()):
    rows, width = x.shape
    span = 256
    size = grads[0][0].shape[1]
    flat = [value for group in grads for value in group]
    count = len(flat)
    by_row = lambda size: pl.BlockSpec((span, size), lambda i: (i, 0))

    def kernel(*refs):
        weight, sems = refs[-2:]
        stream = []
        for part in range(3):
            columns = slice(part * width, (part + 1) * width)
            copies, rest = weights.at(part * width).copies(
                refs,
                width,
                lambda at, lines, columns=columns: weight.at[pl.ds(at, lines), columns],
                sems.at[part],
            )
            stream.append(copies)
        refs = rest
        for copies in stream:
            start_all(copies)
        x_ref, grad_ref, gain_ref, out_ref, ggain_ref, gshift_ref = refs[count : count + 6]
        step = pl.program_id(0)
        total = None
        for part in range(3):
            wait_all(stream[part])
            for group in range(len(grads)):
                begin = part * width + group * size
                value = dot_nt(refs[3 * group + part][...], weight[:, begin : begin + size])
                total = value if total is None else total + value
        hat, scale = norm_stats(x_ref[...].astype(F32))
        accumulate(gshift_ref, jnp.sum(total, axis=0, keepdims=True), step == 0)
        accumulate(ggain_ref, jnp.sum(total * hat, axis=0, keepdims=True), step == 0)
        out_ref[...] = grad_ref[...] + norm_back(hat, scale, total * gain_ref[...])

    vector = ((1, width), F32, whole((1, width)))
    return call(
        kernel,
        (rows // span,),
        weights.inputs()
        + [(value, by_row(size)) for value in flat]
        + [(x, by_row(width)), (grad_after, by_row(width)), param(small, number, width)],
        [((rows, width), F32, by_row(width)), vector, vector],
        after=after,
        scratch=[
            pltpu.VMEM((width, 3 * width), BF16),
            pltpu.SemaphoreType.DMA((3, len(weights.plan))),
        ],
        cost=cost(24 * rows * width * width, 88 * rows * width),
        name="grad_input",
    )


def adamw(weight, first, second, grad, rate, decay):
    first_new = beta_one * first + (1.0 - beta_one) * grad
    second_new = beta_two * second + (1.0 - beta_two) * grad * grad
    first_hat = first_new / (1.0 - beta_one**STEP)
    second_hat = second_new / (1.0 - beta_two**STEP)
    weight_new = weight - rate * (first_hat / (jnp.sqrt(second_hat) + adam_eps) + decay * weight)
    return (weight_new, first_new, second_new)


def run_adam(core, state, groups, span, places, pick, earlier, after=()):
    half = groups[0][0].shape[-2]
    count = len(places)
    table = jnp.array(places, jnp.int32)
    place = pl.BlockSpec((half, span), lambda p, h, c, t: (jnp.bitwise_xor(h, c[0]), t[p]))
    flat = [value for group in groups for value in group]

    def kernel(core_ref, table_ref, w_ref, m_ref, v_ref, *refs):
        w_out, m_out, v_out, grad_ref = refs[-4:]
        for side in range(2):
            mine = refs[side : 2 * len(groups) : 2]
            for block in range(count):

                @pl.when((pl.program_id(1) == side) & (pl.program_id(0) == block))
                def _(mine=mine, block=block):
                    start = 0
                    for value in pick(block, mine):
                        grad_ref[:, start : start + value.shape[1]] = value
                        start += value.shape[1]

        w_out[...], m_out[...], v_out[...] = adamw(
            w_ref[...], m_ref[...], v_ref[...], grad_ref[...].astype(F32), 0.05, 0.1
        )

    moved = 2 * half * count * span
    return call(
        kernel,
        (count, 2),
        [(value, place) for value in state] + [(value, whole(value.shape)) for value in flat],
        [(state[0].shape, F32, place)] * 3,
        after=after,
        reuse=[] if earlier is None else [(value, n) for n, value in enumerate(earlier)],
        prefetch=(core, table),
        scratch=[pltpu.VMEM((half, span), BF16)],
        cost=cost(2 * moved, 2 * moved),
        name="adam",
    )


def run_side(core, jobs, after=(), steps=4):
    counts = [(len(job[0]), len(job[1])) for job in jobs]
    total_in = sum(count[0] for count in counts)

    def kernel(core_ref, *refs):
        ins = refs[:total_in]
        outs = refs[total_in:]
        for job, (have, give) in zip(jobs, counts):
            more = (core_ref,) if "places" in job[2].__code__.co_varnames else ()
            job[2](ins[:have], outs[:give], *more)
            ins = ins[have:]
            outs = outs[give:]

    def spec(block, index):
        return pl.BlockSpec(block, lambda i, c: index(i, c))

    moved = sum(array.size * 2 for job in jobs for array, _, _ in job[0])
    results = call(
        kernel,
        (steps,),
        [(array, spec(block, index)) for job in jobs for array, block, index in job[0]],
        [(shape, dtype, spec(block, index)) for job in jobs for shape, dtype, block, index in job[1]],
        after=after,
        prefetch=(core,),
        cost=cost(0, 2 * moved),
        name="side",
    )
    split = []
    for _, give in counts:
        split.append(results[:give])
        results = results[give:]
    return split


def job_cast(rows, columns, by_core, steps):
    span = rows // steps
    total = sum(size for _, _, size in columns)
    ins = []
    for state, number, size in columns:
        index = lambda i, c, number=number: (c[0] * steps * by_core + i, number)
        ins.append((state, (span, size), index))
    outs = [((rows, total), BF16, (span, total), lambda i, c: (i, 0))]

    def run(have, give):
        start = 0
        for ref, (_, _, size) in zip(have, columns):
            give[0][:, start : start + size] = ref[...].astype(BF16)
            start += size

    return ins, outs, run


def job_join(left, right, steps, around):
    _, blocks, rows, size = left.shape
    span = rows // steps
    four = lambda i, c: (0, 0, i, 0)
    ins = [(value, (2, blocks, span, size), four) for value in (left, right)]
    outs = [((blocks, 2, rows, size), BF16, (blocks, 2, span, size), four)]

    def run(have, give, places):
        for side in range(2):
            for block in range(blocks):
                owner = jnp.bitwise_xor(places[1], block) if around else block
                give[0][owner, side] = have[0][side, block] + have[1][side, block]

    return ins, outs, run


def job_copy(value, first, rows):
    size = value.shape[1]
    ins = [(value, value.shape, lambda i, c: (0, 0))]
    outs = [((rows, size), value.dtype, (rows, size), lambda i, c: (0, 0))]

    def run(have, give):
        give[0][...] = have[0][first : first + rows, :]

    return ins, outs, run


def job_add(left, right, steps):
    at = left.ndim - 2
    if left.shape[at] == 1:
        same = lambda i, c: (0,) * left.ndim

        def run_whole(have, give):
            give[0][...] = have[0][...] + have[1][...]

        return (
            [(left, left.shape, same), (right, right.shape, same)],
            [(left.shape, left.dtype, left.shape, same)],
            run_whole,
        )
    block = tuple(size // steps if axis == at else size for axis, size in enumerate(left.shape))
    index = lambda i, c: (0,) * at + (i, 0)

    def run(have, give):
        give[0][...] = have[0][...] + have[1][...]

    return [(left, block, index), (right, block, index)], [(left.shape, left.dtype, block, index)], run


def job_pick(own, received, steps):
    at = own.ndim - 2
    block = tuple(size // steps if axis == at else size for axis, size in enumerate(own.shape))
    index = lambda i, c: (0,) * at + (i, 0)

    def run(have, give, places):
        give[0][...] = jnp.where(places[2] == 1, have[0][...], have[1][...])

    return [(own, block, index), (received, block, index)], [(own.shape, own.dtype, block, index)], run


def job_sum(groups, keep, send, steps):
    _, blocks, rows, _ = groups[0][0].shape
    span = rows // steps
    total = sum(own.shape[3] for own, _ in groups)
    four = lambda i, c: (0, 0, i, 0)
    three = lambda i, c: (0, i, 0)
    ins = []
    for own, received in groups:
        size = own.shape[3]
        ins.append((own, (2, blocks, span, size), four))
        if len(received) == 1:
            ins.append((received[0], (2, blocks, span, size), four))
        else:
            ins += [(value, (blocks, span, size), three) for value in received]
    kept = len(keep[0])
    outs = [((2, kept, rows, total), BF16, (2, kept, span, total), four)]
    if len(send) == 1:
        gone = len(send[0])
        outs.append(((2, gone, rows, total), BF16, (2, gone, span, total), four))
    else:
        for side in range(2):
            if send[side]:
                gone = len(send[side])
                outs.append(((gone, rows, total), BF16, (gone, span, total), three))

    def run(have, give):
        start = 0
        for own, received in groups:
            size = own.shape[3]
            columns = slice(start, start + size)
            start += size
            for side in range(2):
                for block in range(blocks):
                    other = have[1][side, block] if len(received) == 1 else have[1 + side][block]
                    value = have[0][side, block] + other
                    if block in keep[side]:
                        give[0][side, keep[side].index(block), :, columns] = value
                    elif len(send) == 1:
                        give[1][side, send[0].index(block), :, columns] = value
                    else:
                        give[1 + side][send[side].index(block), :, columns] = value
            have = have[1 + len(received) :]

    return ins, outs, run


def job_params(rows, shards, small_size):
    ins = []
    for array, row in rows:
        if array.shape[0] == 1:
            ins.append((array, array.shape, lambda i, c: (0, 0)))
        else:
            size = array.shape[1]
            ins.append((array, (16, size), lambda i, c, row=row: (row // 16, 0)))
    shape = (1, shards * small_size)
    outs = [(shape, F32, shape, lambda i, c: (0, 0))]

    def run(have, give, places):
        for number, ref in enumerate(have):
            owner = jnp.bitwise_xor(places[1], number)
            start = pl.multiple_of(owner * small_size, LANES)
            value = ref[0:1, :small_size].astype(BF16).astype(F32)
            give[0][:, pl.ds(start, small_size)] = value

    return ins, outs, run


def job_lay(values):
    total = sum(value.shape[1] for value in values)
    same = lambda i, c: (0, 0)
    ins = [(value, value.shape, same) for value in values]

    def run(have, give):
        start = 0
        for ref in have:
            give[0][:, start : start + ref.shape[1]] = ref[...]
            start += ref.shape[1]

    return ins, [((1, total), F32, (1, total), same)], run


class Links:
    def __init__(self, sizes, shard_rows):
        self.replicas, self.shards = sizes
        dp = lax.axis_index("dp")
        self.shard = lax.axis_index("shard")
        self.core = lax.rem(dp, 2)
        place = dp // 2
        self.inner = (place > 0) & (place < sizes[0] // 2 - 1)
        self.core_arr = jnp.stack([self.core, self.shard, self.inner]).astype(jnp.int32)
        self.rows = shard_rows
        self.half = shard_rows // 2
        self.fast = sizes == (8, 4)

    def swap(self, value):
        return self.across_dp(value, 1)

    def across_dp(self, value, bit):
        return lax.ppermute(value, "dp", [(d, d ^ bit) for d in range(self.replicas)])

    def along_dp(self, value, step):
        hops = ([(0, 1), (3, 2)], [(1, 2), (2, 1)], [(1, 0), (2, 3)])[step]
        pairs = [(2 * a + core, 2 * b + core) for a, b in hops for core in range(2)]
        return lax.ppermute(value, "dp", pairs)

    def across_shard(self, value, bit):
        return lax.ppermute(value, "shard", [(s, s ^ bit) for s in range(self.shards)])

    def turned_offsets(self, around):
        blocks = jnp.arange(2 * self.shards, dtype=jnp.int32)
        owner = blocks // 2
        if around:
            owner = jnp.bitwise_xor(owner, self.shard)
        away = jnp.bitwise_xor(lax.rem(blocks, 2), self.core)
        return away * (self.shards * self.half) + owner * self.half

    def gather(self, half_rows):
        return lax.all_gather(half_rows, "shard", axis=0, tiled=True)

    def gathered(self, mine, behind=None):
        if behind is not None:
            mine, _ = lax.optimization_barrier((mine, behind))
        first = jnp.arange(self.shards, dtype=jnp.int32) * self.rows
        offs = jnp.concatenate([first + self.core * self.half, first + (1 - self.core) * self.half])
        stride = mine.shape[0] // self.shards
        plan = tuple((0, t * stride, self.half, t) for t in range(self.shards)) + tuple(
            (1, t * stride, self.half, self.shards + t) for t in range(self.shards)
        )
        return Weights((mine, self.swap(mine)), plan, offs.astype(jnp.int32))

    def over_dp(self, values):
        groups = [[d for d in range(self.replicas) if d % 2 == c] for c in range(2)]
        return lax.psum(values, "dp", axis_index_groups=groups)


class Gather:
    def __init__(self, links, half_rows, own):
        self.links = links
        self.own = own
        self.by_x = links.across_shard(half_rows, 1)
        self.by_y = links.across_shard(half_rows, 2)

    def jobs(self):
        part = self.links.half // 2
        rest = self.by_x.shape[0] - part
        return [job_copy(self.by_y, 0, part), job_copy(self.by_x, part, rest)]

    def forward(self, results):
        links = self.links
        self.far = (
            links.across_shard(results[0], 1),
            links.across_shard(results[1], 2),
        )
        self.near = (links.swap(self.by_x), links.swap(self.by_y))

    def weights(self):
        links = self.links
        half, rows = links.half, links.rows
        part = half // 2
        far = tuple(links.swap(value) for value in self.far)
        pieces = (self.own, self.by_x, self.by_y, *self.near, *self.far, *far)
        plan = ((0, 0, rows, 0),)
        plan += tuple((n, 0, half, n) for n in range(1, 5))
        plan += tuple((n, 0, part, n) for n in range(5, 9))
        at = lambda bits: jnp.bitwise_xor(links.shard, bits) * rows
        mine = links.core * half
        other = (1 - links.core) * half
        offs = [at(0), at(1) + mine, at(2) + mine, at(1) + other, at(2) + other]
        offs += [at(3) + mine, at(3) + mine + part, at(3) + other, at(3) + other + part]
        return Weights(pieces, plan, jnp.stack(offs).astype(jnp.int32))


LINE, AT_ONCE, EXCHANGE = range(3)


class Reduce:
    def __init__(self, links, way, bits=((1, 2), (2, 1))):
        self.links = links
        self.way = way
        self.bits = bits
        self.stage = 0
        self.groups = []

    def add(self, own, sib):
        shape = (2, self.links.shards, self.links.half, own.shape[2])
        self.groups.append((own.reshape(shape), (self.links.swap(sib).reshape(shape),)))
        return self

    def job(self, steps):
        if self.stage > 2:
            own, received = self.groups[0]
            if self.way == LINE and self.stage == 5:
                return job_pick(own, received, steps)
            return job_add(own, received, steps)
        blocks = self.groups[0][0].shape[1]
        sides = []
        for number in range(2):
            order = self.bits[number % len(self.bits)]
            if blocks == 1:
                sides.append(())
            elif blocks == 2:
                sides.append((1,))
            else:
                sides.append(tuple(block for block in range(blocks) if block & order[0]))
        keep = [[block for block in range(blocks) if block not in gone] for gone in sides]
        send = [list(gone) for gone in sides]
        if len(self.bits) == 1 and blocks > 1:
            send = send[:1]
        return job_sum(self.groups, keep, send, steps)

    def advance(self, results):
        links = self.links
        own = results[0]
        stage = self.stage
        self.stage += 1
        if stage < 2:
            received = tuple(
                links.across_shard(value, order[stage])
                for value, order in zip(results[1:], self.bits)
            )
            self.groups = [(own, received)]
            return
        if stage == 2:
            own = own.reshape(2, own.shape[2], own.shape[3])
        if self.way == AT_ONCE:
            self.own = own
        elif self.way == LINE and stage < 5:
            self.groups = [(own, links.along_dp(own, stage - 2))]
        elif self.way == EXCHANGE and stage < 4:
            self.groups = [(own, links.across_dp(own, 2 * (stage - 1)))]
        else:
            self.grads = (own, links.swap(own))

    def close(self, behind):
        mine, _ = lax.optimization_barrier((self.own, behind))
        self.grads = (mine, self.links.swap(mine))


class Wide:
    def __init__(self, links, joined):
        self.links = links
        self.shape = joined.shape[1:]
        flat = joined.reshape(-1, joined.shape[3])
        self.own = lax.psum_scatter(flat, "shard", scatter_dimension=0, tiled=True)

    def finish(self):
        self.own = self.links.over_dp(self.own).reshape(self.shape)

    def close(self, behind):
        mine, _ = lax.optimization_barrier((self.own, behind))
        self.grads = (mine, self.links.swap(mine))


class Side:
    def __init__(self, links):
        self.links = links
        self.order = ()

    def jobs(self, jobs, steps=1, after=()):
        results = run_side(self.links.core_arr, jobs, after=(*self.order, *after), steps=steps)
        self.order = (results[0][0],)
        return [result[0] for result in results]

    def reduce(self, reduces, jobs=(), steps=2):
        work = [item.job(steps) for item in reduces] + list(jobs)
        results = run_side(self.links.core_arr, work, after=self.order, steps=steps)
        for item, result in zip(reduces, results):
            item.advance(result)
        self.order = (results[0][0],)
        return [result[0] for result in results[len(reduces) :]]

    def then(self, results):
        self.order = (results[0],)
        return results


def small_parts(small, width, hidden):
    bounds = [width] * 3 + [hidden] + [width] * 5
    parts = []
    start = 0
    for size in bounds:
        parts.append(small[:, start : start + size])
        start += size
    return parts


def body(sizes, *args):
    tokens, cotangent, lengths = args[:3]
    attn_state, mlp_state, small_state = args[3:6], args[6:9], args[9:12]
    rows, width = tokens.shape
    links = Links(sizes, attn_state[0].shape[0])
    half = links.half
    hidden = mlp_state[0].shape[1] // 2
    pairs = width // LANES
    pad = 16
    core_arr = links.core_arr
    around = links.turned_offsets(links.fast)
    side = Side(links)

    ends = jnp.cumsum(lengths[0], dtype=jnp.int32)
    small_own = small_state[0][None]
    small_size = small_own.shape[1]
    (
        BIAS_Q,
        BIAS_V,
        BIAS_O,
        BIAS_UP,
    ) = range(4)
    BIAS_DN, GAIN_ONE, SHIFT_ONE, GAIN_TWO, SHIFT_TWO = range(
        BIAS_UP + hidden // width, BIAS_UP + hidden // width + 5
    )

    def first_job():
        ins = [
            (attn_state[0], (half, 4 * width), lambda i, c: (c[0], 0)),
            (small_own, (1, small_size), lambda i, c: (0, 0)),
        ]
        outs = [((half + pad, 4 * width), BF16, (half + pad, 4 * width), lambda i, c: (0, 0))]

        def job(have, give):
            give[0][:half] = have[0][...].astype(BF16)
            row = have[1][...].astype(BF16)
            give[0][half:, :small_size] = jnp.broadcast_to(row, (pad, small_size))

        return ins, outs, job

    block = hidden // 2
    groups = [[(mlp_state[0], number, block) for number in pair] for pair in ((0, 2), (1, 3))]
    (first_half,) = side.jobs([first_job()])
    if links.fast:
        attn_gather = Gather(links, first_half, None)
    else:
        attn_weights = links.gathered(links.gather(first_half))
    dy, dyt, grad_bias_dn = side.then(run_cot(half, around, ends, cotangent, after=side.order))
    (more_half,) = side.jobs([job_cast(half, groups[1], 1, 4)], steps=4)
    if links.fast:
        (attn_gather.own,) = side.jobs(
            [job_cast(links.rows, [(attn_state[0], 0, 4 * width)], 0, 4)], steps=4
        )
        *copied, feed_half = side.jobs([*attn_gather.jobs(), job_cast(half, groups[0], 1, 1)])
        attn_gather.forward(copied)
    else:
        (feed_half,) = side.jobs([job_cast(half, groups[0], 1, 1)])
    wide = links.gather(feed_half)
    more_wide = links.gather(more_half)
    if links.fast:
        attn_weights = attn_gather.weights()
        rows_of = [
            (small_own, 0),
            (attn_gather.by_x, half),
            (attn_gather.by_y, half),
            (attn_gather.far[1], half // 2),
        ]
        (small,) = side.jobs([job_params(rows_of, links.shards, small_size)])
    else:
        small = attn_weights.pieces[0].reshape(links.shards, half + pad, 4 * width)
        small = small[:, half, :small_size].astype(F32).reshape(1, -1)

    qkv, turned_one = side.then(
        run_qkv(
            half,
            attn_weights,
            around,
            tokens,
            small,
            (BIAS_Q, BIAS_V, GAIN_ONE, SHIFT_ONE),
            after=side.order,
        )
    )
    mixed, lse = side.then(run_attend(ends, qkv, 0, pairs, after=side.order))
    wide = links.gathered(wide, lse)
    side.order += (wide.pieces[0],)
    after, low_two, turned_two, turned_mixed = side.then(
        run_after(
            half,
            attn_weights.at(3 * width),
            (around, around),
            mixed,
            tokens,
            small,
            (BIAS_O, GAIN_TWO, SHIFT_TWO),
            after=side.order,
        )
    )

    passed, grad_bias_up = [None], []
    blocked = lambda value: value.reshape(2, links.shards, half, value.shape[2])

    def feed(start, up_weights, down_weights):
        act, du, own, sib, gbias = run_feed(
            up_weights,
            down_weights,
            low_two,
            turned_two,
            dy,
            dyt,
            small,
            BIAS_UP * width + start,
            start,
            block,
            passed[-1],
            after=side.order,
        )
        side.order = (own,)
        passed.append((act, du))
        grad_bias_up.append(gbias)
        return own, sib

    def unit(way, own, sib, bits=((1, 2), (2, 1))):
        if links.fast:
            return Reduce(links, way, bits).add(own, sib)
        return Wide(links, side.jobs([join(own, links.swap(sib))], steps=4)[0])

    def join(own, received):
        return job_join(blocked(own), blocked(received), 4, links.fast)

    def reduce(units, jobs=(), steps=2):
        if links.fast:
            return side.reduce(units, jobs, steps)
        return side.jobs(jobs, steps) if jobs else None

    group_a = feed(0, wide, wide.at(block))
    more_wide = links.gathered(more_wide, grad_bias_up[0])
    unit_a = unit(LINE, *group_a)
    reduce([unit_a], steps=4)
    unit_b = unit(AT_ONCE, *feed(block, more_wide, more_wide.at(block)))
    reduce([unit_a], steps=4)
    (
        grad_after,
        dmix,
        own_out,
        sib_out,
        grad_bias_o,
        grad_gain_two,
        grad_shift_two,
    ) = side.then(
        run_middle(
            [(block, wide), (block, more_wide)],
            attn_weights.at(3 * width),
            passed[-1][1],
            after,
            dy,
            small,
            GAIN_TWO,
            turned_mixed,
            after=side.order,
        )
    )
    received_out = links.swap(sib_out)
    reduce([unit_a, unit_b], steps=4)
    grads, biases = [], []

    def attend_back(first):
        dq, dk, dv, gq, gv = side.then(
            run_attend_back(ends, qkv, mixed, dmix, lse, first, pairs // 2, after=side.order)
        )
        grads.append((dq, dk, dv))
        biases.append((gq, gv))

    def project(group):
        return side.then(run_project(turned_one, *grads[group], after=side.order))

    attend_back(0)
    (joined,) = reduce([unit_a, unit_b], [join(own_out, received_out)], steps=4)
    unit_e = Wide(links, joined)
    unit_c = unit(EXCHANGE, *project(0), ((1, 2),))
    attend_back(pairs // 2)
    reduce([unit_a, unit_b, unit_c], steps=4)
    if links.fast:
        unit_b.own, unit_e.own = links.over_dp((unit_b.own, unit_e.own.reshape(unit_e.shape)))
    unit_d = unit(EXCHANGE, *project(1), ((1, 2),))
    grad_input, grad_gain_one, grad_shift_one = side.then(
        run_input(attn_weights, grads, tokens, grad_after, small, GAIN_ONE, after=side.order)
    )
    small_grads = [biases[0][0], biases[1][0], biases[0][1], biases[1][1], grad_bias_o]
    small_grads += grad_bias_up
    small_grads += [grad_bias_dn, grad_gain_one, grad_shift_one, grad_gain_two, grad_shift_two]
    (grad_small,) = reduce([unit_a, unit_c, unit_d], [job_lay(small_grads)])

    def pick_feed(number, arrays):
        return [arrays[0][number]]

    def adam_mlp(number, item, earlier):
        return side.then(
            run_adam(
                core_arr,
                mlp_state,
                [item.grads],
                block,
                [number, 2 + number],
                pick_feed,
                earlier,
                after=side.order,
            )
        )

    out_block = width // 2

    def pick_heads(number, arrays):
        left, right = arrays[0][0], arrays[0][1]
        split = out_block // 2
        if number > 2:
            return [arrays[1][number - 3]]
        return (
            [left[:, :out_block]],
            [left[:, out_block:], right[:, :split]],
            [right[:, split:]],
        )[number]

    def adam_attn(items, places, earlier):
        return side.then(
            run_adam(
                core_arr,
                attn_state,
                [item.grads for item in items],
                out_block,
                places,
                pick_heads,
                earlier,
                after=side.order,
            )
        )

    def output_now():
        out = run_output(
            [(block, wide.at(block)), (block, more_wide.at(block))],
            passed[-1][0],
            after,
            small,
            BIAS_DN,
            after=side.order,
        )
        side.then([out])
        return out

    if links.fast:
        shard_move = lambda bit: functools.partial(links.across_shard, bit=bit)
        dp_move = lambda bit: functools.partial(links.across_dp, bit=bit)
        moved = links.across_shard(grad_small, 1)

        def step(units, move):
            (total,) = reduce(units, [job_add(grad_small, moved, 2)])
            return total, move(total) if move else None

        mlp_new = adam_mlp(0, unit_a, None)
        grad_small, moved = step([unit_c, unit_d], shard_move(2))
        output = output_now()
        grad_small, moved = step([unit_c, unit_d], links.swap)
        unit_b.close(grad_small)
        unit_e.close(grad_small)
        mlp_new = adam_mlp(1, unit_b, mlp_new)
        grad_small, moved = step([unit_c, unit_d], dp_move(2))
        attn_new = adam_attn([unit_c], [0, 2, 4], None)
        grad_small, moved = step([unit_d], dp_move(4))
        attn_new = adam_attn([unit_d, unit_e], [1, 3, 5, 6, 7], attn_new)
        grad_small, _ = step([], None)
    else:
        for item in (unit_a, unit_b, unit_c, unit_d, unit_e):
            item.finish()
            item.close(grad_input)
        grad_small = lax.psum(grad_small, ("dp", "shard"))
        output = output_now()
        mlp_new = adam_mlp(1, unit_b, adam_mlp(0, unit_a, None))
        attn_new = adam_attn([unit_c], [0, 2, 4], None)
        attn_new = adam_attn([unit_d, unit_e], [1, 3, 5, 6, 7], attn_new)
    grad_small = lax.dynamic_slice_in_dim(grad_small, links.shard * small_size, small_size, 1)[0]
    small_new = adamw(*small_state, grad_small, 0.4, 0.0)
    return (output, grad_input, *attn_new, *mlp_new, *small_new)


def solution(mesh):
    tokens = P(("dp", "shard"), None)
    state = P("shard", None)
    vector = P("shard")
    return jax.shard_map(
        functools.partial(body, (mesh.shape["dp"], mesh.shape["shard"])),
        mesh=mesh,
        in_specs=(tokens,) * 3 + (state,) * 6 + (vector,) * 3,
        out_specs=(tokens,) * 2 + (state,) * 6 + (vector,) * 3,
        check_vma=False,
    )
```

```python
import functools

import jax
import jax.numpy as jnp
from jax import lax
from jax.experimental import pallas as pl
from jax.experimental.pallas import tpu as pltpu
from jax.sharding import PartitionSpec as P

HD = 64
STEP = 10
LANES = 128
MASKED = -1e30
SAFE = 60.0
GELU_IN = 0.7978845608028654
GELU_CUBE = 0.044715

beta_one = 0.9
beta_two = 0.95
adam_eps = 1e-08
norm_eps = 1e-05

F32 = jnp.float32
BF16 = jnp.bfloat16
MIB = 1024 * 1024
VMEM_MIB = 64

ANY = pl.BlockSpec(memory_space=pl.ANY)
SMEM = pl.BlockSpec(memory_space=pltpu.SMEM)


def dot_nn(left, right):
    return lax.dot_general(left, right, (((1,), (0,)), ((), ())), preferred_element_type=F32)


def dot_nt(left, right):
    return lax.dot_general(left, right, (((1,), (1,)), ((), ())), preferred_element_type=F32)


def dot_tn(left, right):
    return lax.dot_general(left, right, (((0,), (0,)), ((), ())), preferred_element_type=F32)


def whole(shape):
    return pl.BlockSpec(shape, lambda *_: (0,) * len(shape))


def call(kernel, grid, ins, outs, after=(), reuse=(), prefetch=(), scratch=(), cost=None, name=None):
    known = len(prefetch) + len(ins)
    idle = [*after, *(array for array, _ in reuse)]

    def run(*refs):
        kernel(*refs[:known], *refs[known + len(idle) :])

    def placed(array, spec):
        if spec is SMEM:
            return array
        return pltpu.with_memory_space_constraint(array, pltpu.HBM)

    return pl.pallas_call(
        run,
        grid_spec=pltpu.PrefetchScalarGridSpec(
            num_scalar_prefetch=len(prefetch),
            grid=grid,
            in_specs=[spec for _, spec in ins] + [ANY] * len(idle),
            out_specs=[spec for _, _, spec in outs],
            scratch_shapes=list(scratch),
        ),
        out_shape=[pltpu.HBM(shape, dtype) for shape, dtype, _ in outs],
        input_output_aliases={
            known + len(after) + number: output for number, (_, output) in enumerate(reuse)
        },
        compiler_params=pltpu.CompilerParams(vmem_limit_bytes=VMEM_MIB * MIB),
        cost_estimate=cost,
        name=name,
    )(*prefetch, *(placed(*item) for item in ins), *(placed(array, ANY) for array in idle))


def param(small, number, width):
    return (small, pl.BlockSpec((1, width), lambda *_: (0, number)))


def cost(flops, moved, exps=0):
    return pl.CostEstimate(flops=int(flops), bytes_accessed=int(moved), transcendentals=int(exps))


def store_turned(turned_ref, toff, block, half, value, columns):
    turned = value.astype(BF16).T
    for part in range(LANES // half):
        offset = pl.multiple_of(toff[block * (LANES // half) + part], half)
        turned_ref[pl.ds(offset, half), columns] = turned[part * half : (part + 1) * half]


def norm_stats(values):
    center = values - jnp.mean(values, axis=-1, keepdims=True)
    spread = jnp.mean(center * center, axis=-1, keepdims=True)
    scale = lax.rsqrt(spread + norm_eps)
    return center * scale, scale


def norm_back(hat, scale, grad_hat):
    mean = jnp.mean(grad_hat, axis=-1, keepdims=True)
    along = jnp.mean(grad_hat * hat, axis=-1, keepdims=True)
    return scale * (grad_hat - mean - hat * along)


def accumulate(ref, value, first):
    @pl.when(first)
    def _():
        ref[...] = value

    @pl.when(jnp.logical_not(first))
    def _():
        ref[...] += value


class Weights:
    def __init__(self, pieces, plan, offs, first=0):
        self.pieces, self.plan, self.offs, self.first = pieces, plan, offs, first

    def at(self, first):
        return Weights(self.pieces, self.plan, self.offs, self.first + first)

    def inputs(self):
        return [(self.offs, SMEM)] + [(piece, ANY) for piece in self.pieces]

    def sems(self):
        return pltpu.SemaphoreType.DMA((len(self.plan),))

    def rest(self, refs):
        return refs[1 + len(self.pieces) :]

    def copies(self, refs, size, target, sems, start=None):
        offs, refs = refs[0], refs[1:]
        columns = slice(self.first, self.first + size)
        if start is not None:
            columns = pl.ds(pl.multiple_of(self.first + start, LANES), size)
        made = []
        for number, (piece, first, rows, index) in enumerate(self.plan):
            offset = pl.multiple_of(offs[index], rows)
            made.append(
                pltpu.make_async_copy(
                    refs[piece].at[pl.ds(first, rows), columns],
                    target(offset, rows),
                    sems.at[number],
                )
            )
        return made, refs[len(self.pieces) :]


def start_all(copies):
    @pl.when(pl.program_id(0) == 0)
    def _():
        for copy in copies:
            copy.start()


def wait_all(copies):
    @pl.when(pl.program_id(0) == 0)
    def _():
        for copy in copies:
            copy.wait()


def cot_kernel(half, toff, ends, cot_ref, dy_ref, turned_ref, bias_ref):
    rows = cot_ref.shape[0]
    place = lax.broadcasted_iota(jnp.int32, (rows, LANES), 0)
    live = (place < ends[ends.shape[0] - 1]).astype(F32)
    for block in range(cot_ref.shape[1] // LANES):
        columns = slice(block * LANES, (block + 1) * LANES)
        value = cot_ref[:, columns].astype(F32) * live
        dy_ref[:, columns] = value.astype(BF16)
        bias_ref[:, columns] = jnp.sum(value, axis=0, keepdims=True)
        store_turned(turned_ref, toff, block, half, value, slice(None))


def run_cot(half, toff, ends, cot, after=()):
    rows, width = cot.shape
    return call(
        functools.partial(cot_kernel, half),
        (1,),
        [(toff, SMEM), (ends, SMEM), (cot, whole(cot.shape))],
        [
            ((rows, width), BF16, whole((rows, width))),
            ((width, rows), BF16, whole((width, rows))),
            ((1, width), F32, whole((1, width))),
        ],
        after=after,
        cost=cost(0, 6 * rows * width),
        name="cotangent",
    )


def run_qkv(half, weights, toff, x, small, numbers, after=()):
    rows, width = x.shape
    span = 256

    def kernel(*refs):
        weight, sems = refs[-2:]
        copies, refs = weights.copies(
            refs, 3 * width, lambda at, size: weight.at[pl.ds(at, size), :], sems
        )
        toff_ref, x_ref, bias_q, bias_v, gain_ref, shift_ref, qkv_ref, turned_ref = refs[:8]
        start_all(copies)
        hat, _ = norm_stats(x_ref[...].astype(F32))
        normed = hat * gain_ref[...] + shift_ref[...]
        for block in range(width // LANES):
            columns = slice(block * LANES, (block + 1) * LANES)
            store_turned(turned_ref, toff_ref, block, half, normed[:, columns], slice(None))
        wait_all(copies)
        low = normed.astype(BF16)
        for part in range(3):
            columns = slice(part * width, (part + 1) * width)
            value = dot_nn(low, weight[:, columns])
            if part == 2:
                value += bias_v[...]
            if part == 0:
                value = (value + bias_q[...]).astype(BF16).astype(F32) * HD ** (-0.5)
            qkv_ref[:, columns] = value.astype(BF16)

    return call(
        kernel,
        (rows // span,),
        weights.inputs()
        + [
            (toff, SMEM),
            (x, pl.BlockSpec((span, width), lambda i: (i, 0))),
        ]
        + [param(small, number, width) for number in numbers],
        [
            ((rows, 3 * width), BF16, pl.BlockSpec((span, 3 * width), lambda i: (i, 0))),
            ((width, rows), BF16, pl.BlockSpec((width, span), lambda i: (0, i))),
        ],
        after=after,
        scratch=[pltpu.VMEM((width, 3 * width), BF16), weights.sems()],
        cost=cost(6 * rows * width * width, 16 * rows * width),
        name="qkv",
    )


def first_of_row(ends, place):
    first = jnp.zeros_like(place)
    for number in range(ends.shape[0]):
        first = jnp.where(place >= ends[number], ends[number], first)
    return first


def attend_kernel(ends, q_ref, k_ref, v_ref, o_ref, lse_ref, allow):
    rows = q_ref.shape[0]
    span = min(256, rows)

    @pl.when(pl.program_id(0) == 0)
    def _():
        for start in range(0, rows, span):
            keys = start + span
            place = lax.broadcasted_iota(jnp.int32, (span, 1), 0) + start
            first = first_of_row(ends, place)
            key = lax.broadcasted_iota(jnp.int32, (span, keys), 1)
            allow[start:keys, :keys] = jnp.where((key <= place) & (key >= first), 0.0, MASKED)

    lane = lax.broadcasted_iota(jnp.int32, (1, LANES), 1)
    low_lane = lane < HD
    one = low_lane.astype(BF16)
    masks = (one, 1 - one)

    same = (lax.broadcasted_iota(jnp.int32, (LANES, LANES), 0) < HD) == (
        lax.broadcasted_iota(jnp.int32, (LANES, LANES), 1) < HD
    )
    same = same.astype(F32).astype(BF16)
    longest = [
        jnp.max(dot_nn(ref[...] * ref[...], same), axis=0, keepdims=True) for ref in (q_ref, k_ref)
    ]
    bounded = jnp.max(longest[0] * longest[1]) < SAFE * SAFE

    def attend(shift):
        mixed = [v_ref[...] * mask + (1 - mask) for mask in masks]
        for start in range(0, rows, span):
            keys = start + span
            sums = []
            tops = []
            for head in range(2):
                query = q_ref[start:keys, :] * masks[head]
                scores = dot_nt(query, k_ref[:keys, :]) + allow[start:keys, :keys]
                if shift:
                    top = jnp.max(scores, axis=1, keepdims=True)
                    tops.append(top)
                    scores = scores - top
                probs = jnp.exp(scores).astype(BF16)
                sums.append(dot_nn(probs, mixed[head][:keys]))
            total = pltpu.roll(jnp.where(low_lane, sums[1], sums[0]), HD, 1)
            out = jnp.where(low_lane, sums[0], sums[1]) / total
            o_ref[start:keys, :] = out.astype(BF16)
            lse = jnp.log(total)
            if shift:
                lse += jnp.where(low_lane, tops[0], tops[1])
            lse = lse.T
            lse_ref[0, 0:1, start:keys] = lse[0:1]
            lse_ref[0, 1:2, start:keys] = lse[HD : HD + 1]

    @pl.when(bounded)
    def _():
        attend(False)

    @pl.when(jnp.logical_not(bounded))
    def _():
        attend(True)


def run_attend(ends, qkv, first, count, earlier=None, after=()):
    rows = qkv.shape[0]
    width = qkv.shape[1] // 3
    pairs = width // LANES
    column = lambda shift: pl.BlockSpec((rows, LANES), lambda i: (0, i + shift))
    return call(
        attend_kernel,
        (count,),
        [(ends, SMEM)] + [(qkv, column(first + part * pairs)) for part in range(3)],
        [
            ((rows, width), BF16, column(first)),
            ((pairs, 2, rows), F32, pl.BlockSpec((1, 2, rows), lambda i: (i + first, 0, 0))),
        ],
        after=after,
        reuse=[] if earlier is None else [(earlier[0], 0), (earlier[1], 1)],
        scratch=[pltpu.VMEM((rows, rows), F32)],
        cost=cost(8 * rows * rows * LANES * count, 8 * rows * LANES * count, 2 * rows * rows * count),
        name="attend",
    )


def run_after(half, weights, toffs, mixed, x, small, numbers, after=()):
    rows, width = x.shape
    span = 256

    def kernel(*refs):
        weight, sems = refs[-2:]
        copies, refs = weights.copies(
            refs, width, lambda at, size: weight.at[pl.ds(at, size), :], sems
        )
        mixed_toff, low_toff, mixed_ref, x_ref, bias_ref, gain_ref, shift_ref = refs[:7]
        after_ref, low_ref, turned_ref, mixed_turned_ref = refs[7:11]
        start_all(copies)
        for block in range(width // LANES):
            columns = slice(block * LANES, (block + 1) * LANES)
            store_turned(mixed_turned_ref, mixed_toff, block, half, mixed_ref[:, columns], slice(None))
        wait_all(copies)
        value = x_ref[...].astype(F32) + dot_nn(mixed_ref[...], weight[...]) + bias_ref[...]
        after_ref[...] = value
        hat, _ = norm_stats(value)
        normed = hat * gain_ref[...] + shift_ref[...]
        low_ref[...] = normed.astype(BF16)
        for block in range(width // LANES):
            columns = slice(block * LANES, (block + 1) * LANES)
            store_turned(turned_ref, low_toff, block, half, normed[:, columns], slice(None))

    by_row = pl.BlockSpec((span, width), lambda i: (i, 0))
    by_column = pl.BlockSpec((width, span), lambda i: (0, i))
    return call(
        kernel,
        (rows // span,),
        weights.inputs()
        + [(toff, SMEM) for toff in toffs]
        + [(mixed, by_row), (x, by_row)]
        + [param(small, number, width) for number in numbers],
        [
            ((rows, width), F32, by_row),
            ((rows, width), BF16, by_row),
            ((width, rows), BF16, by_column),
            ((width, rows), BF16, by_column),
        ],
        after=after,
        scratch=[pltpu.VMEM((width, width), BF16), weights.sems()],
        cost=cost(2 * rows * width * width, 14 * rows * width),
        name="after",
    )


def run_feed(up_weights, down_weights, low, turned, dy, dyt, small, first, begin, block, earlier, after=()):
    rows, width = low.shape
    hidden = earlier[0].shape[1] if earlier is not None else block_total(small, width)
    span = 256
    mid = width // 2
    count = block // span
    by_column = lambda size: pl.BlockSpec((size, span), lambda i: (0, i))
    shifted = pl.BlockSpec((rows, span), lambda i: (0, begin // span + i))
    grad = ((2, mid, block), BF16, pl.BlockSpec((2, mid, span), lambda i: (0, 0, i)))

    def kernel(*refs):
        up, down, up_sems, down_sems = refs[-4:]
        step = pl.program_id(0)

        def copies(number):
            columns = pl.ds(pl.multiple_of(number * span, span), span)
            made, rest = up_weights.copies(
                refs,
                span,
                lambda at, size: up.at[pl.ds(at, size), columns],
                up_sems.at[number],
                number * span,
            )
            more, _ = down_weights.copies(
                rest,
                span,
                lambda at, size: down.at[pl.ds(at, size), columns],
                down_sems.at[number],
                number * span,
            )
            return made + more

        @pl.when(step == 0)
        def _():
            for copy in copies(0):
                copy.start()

        @pl.when(step + 1 < count)
        def _():
            for copy in copies(step + 1):
                copy.start()

        for copy in copies(step):
            copy.wait()
        low_ref, turned_ref, dy_ref, dyt_ref, bias_ref, act_ref, du_ref, own_ref, sib_ref, gbias_ref = (
            down_weights.rest(up_weights.rest(refs))[:10]
        )
        columns = pl.ds(pl.multiple_of(step * span, span), span)
        upper = dot_nn(low_ref[...], up[:, columns]) + bias_ref[...]
        grad_act = dot_nn(dy_ref[...], down[:, columns])
        square = (GELU_IN * GELU_CUBE) * (upper * upper)
        tanh = jnp.tanh(upper * (GELU_IN + square))
        share = 0.5 + 0.5 * tanh
        act = upper * share
        slope = share + act * (1.0 - tanh) * (GELU_IN + 3.0 * square)
        act = act.astype(BF16)
        du = (grad_act * slope).astype(BF16)
        act_ref[...] = act
        du_ref[...] = du
        gbias_ref[...] = jnp.sum(du.astype(F32), axis=0, keepdims=True)
        grad_up = dot_nn(turned_ref[...], du).astype(BF16)
        own_ref[0] = grad_up[:mid]
        sib_ref[0] = grad_up[mid:]
        grad_dn = dot_nn(dyt_ref[...], act).astype(BF16)
        own_ref[1] = grad_dn[:mid]
        sib_ref[1] = grad_dn[mid:]

    return call(
        kernel,
        (count,),
        up_weights.inputs()
        + down_weights.inputs()
        + [
            (low, whole((rows, width))),
            (turned, whole((width, rows))),
            (dy, whole((rows, width))),
            (dyt, whole((width, rows))),
            (small, pl.BlockSpec((1, span), lambda i: (0, first // span + i))),
        ],
        [
            ((rows, hidden), BF16, shifted),
            ((rows, hidden), BF16, shifted),
            grad,
            grad,
            ((1, block), F32, by_column(1)),
        ],
        after=after,
        reuse=[] if earlier is None else [(earlier[0], 0), (earlier[1], 1)],
        scratch=[
            pltpu.VMEM((width, block), BF16),
            pltpu.VMEM((width, block), BF16),
            pltpu.SemaphoreType.DMA((count, len(up_weights.plan))),
            pltpu.SemaphoreType.DMA((count, len(down_weights.plan))),
        ],
        cost=cost(8 * rows * width * block, 24 * width * block, rows * block),
        name="feed",
    )


def block_total(small, width):
    return small.shape[1] - 8 * width


class Stream:
    def __init__(self):
        self.parts = []

    def add(self, copies):
        self.parts.append(copies)

    def start(self):
        for copies in self.parts:
            for copy in copies:
                copy.start()

    def wait(self, number):
        for copy in self.parts[number]:
            copy.wait()


def run_output(weights, acts, after_value, small, number, after=()):
    rows, width = after_value.shape
    hidden = acts.shape[1]
    span = 256
    bounds = [0]
    for size, _ in weights:
        bounds.append(bounds[-1] + size)
    by_row = lambda size: pl.BlockSpec((span, size), lambda i: (i, 0))

    def kernel(*refs):
        down = refs[-1 - len(weights)]
        sems = refs[-len(weights) :]
        stream = []
        for index, (size, item) in enumerate(weights):
            columns = slice(bounds[index], bounds[index + 1])
            copies, refs = item.copies(
                refs,
                size,
                lambda at, lines, columns=columns: down.at[pl.ds(at, lines), columns],
                sems[index],
            )
            stream.append(copies)
        act_ref, after_ref, bias_ref, out_ref = refs[:4]
        for copies in stream:
            start_all(copies)
        total = after_ref[...] + bias_ref[...]
        for index, copies in enumerate(stream):
            wait_all(copies)
            columns = slice(bounds[index], bounds[index + 1])
            total += dot_nt(act_ref[:, columns], down[:, columns])
        out_ref[...] = total.astype(BF16)

    (out,) = call(
        kernel,
        (rows // span,),
        [item for _, weight in weights for item in weight.inputs()]
        + [(acts, by_row(hidden)), (after_value, by_row(width)), param(small, number, width)],
        [((rows, width), BF16, by_row(width))],
        after=after,
        scratch=[pltpu.VMEM((width, hidden), BF16)] + [weight.sems() for _, weight in weights],
        cost=cost(rows * width * hidden // 5, 2 * rows * width),
        name="output",
    )
    return out


def run_middle(weights, out_weights, dus, after_value, dy, small, number, turned, after=()):
    rows, width = after_value.shape
    hidden = dus.shape[1]
    part = width
    parts = hidden // part
    span = 256
    mid = width // 2
    places = [
        (item.at(start)) for size, item in weights for start in range(0, size, part)
    ]
    most = max(len(item.plan) for item in places)

    def kernel(*refs):
        du, up, value_in, dy_in, turned_in, out_weight, branch, sems, out_sems, own_sems = refs[-10:]
        stream = Stream()
        for index, item in enumerate(places):
            columns = slice(index * part, (index + 1) * part)
            copies, refs = item.copies(
                refs,
                part,
                lambda at, size, columns=columns: up.at[pl.ds(at, size), columns],
                sems.at[index],
            )
            stream.add(copies)
        more, refs = out_weights.copies(
            refs, width, lambda at, size: out_weight.at[pl.ds(at, size), :], out_sems
        )
        du_ref, after_ref, dy_ref, gain_ref, turned_ref = refs[:5]
        grad_ref, dmix_ref, own_ref, sib_ref, gbias_ref, ggain_ref, gshift_ref = refs[5:12]
        for index in range(parts):
            columns = slice(index * part, (index + 1) * part)
            stream.parts[index].append(
                pltpu.make_async_copy(du_ref.at[:, columns], du.at[:, columns], own_sems.at[index])
            )
        stream.add(
            [
                pltpu.make_async_copy(after_ref, value_in, own_sems.at[parts]),
                pltpu.make_async_copy(dy_ref, dy_in, own_sems.at[parts + 1]),
            ]
        )
        stream.add([pltpu.make_async_copy(turned_ref, turned_in, own_sems.at[parts + 2]), *more])
        stream.start()
        total = None
        for index in range(parts):
            columns = slice(index * part, (index + 1) * part)
            stream.wait(index)
            value = dot_nt(du[:, columns], up[:, columns])
            total = value if total is None else total + value
        stream.wait(parts)
        gain = gain_ref[...]
        sums = [jnp.zeros((1, width), F32)] * 3
        for start in range(0, rows, span):
            lines = slice(start, start + span)
            grad = total[lines]
            hat, scale = norm_stats(value_in[lines, :])
            full = dy_in[lines, :].astype(F32) + norm_back(hat, scale, grad * gain)
            grad_ref[lines, :] = full
            low = full.astype(BF16)
            branch[lines, :] = low
            for index, value in enumerate((low.astype(F32), grad * hat, grad)):
                sums[index] = sums[index] + jnp.sum(value, axis=0, keepdims=True)
        gbias_ref[...], ggain_ref[...], gshift_ref[...] = sums
        stream.wait(parts + 1)
        dmix_ref[...] = dot_nt(branch[...], out_weight[...]).astype(BF16)
        for side in range(2):
            columns = slice(side * (width // 2), (side + 1) * (width // 2))
            value = dot_nn(turned_in[...], branch[:, columns]).astype(BF16)
            own_ref[side] = value[:mid]
            sib_ref[side] = value[mid:]

    grads = ((2, mid, width // 2), BF16, whole((2, mid, width // 2)))
    vector = ((1, width), F32, whole((1, width)))
    full = whole((rows, width))
    return call(
        kernel,
        (1,),
        [item for place in places for item in place.inputs()]
        + out_weights.inputs()
        + [(dus, ANY), (after_value, ANY), (dy, ANY), param(small, number, width), (turned, ANY)],
        [((rows, width), F32, full), ((rows, width), BF16, full), grads, grads] + [vector] * 3,
        after=after,
        scratch=[
            pltpu.VMEM((rows, hidden), BF16),
            pltpu.VMEM((width, hidden), BF16),
            pltpu.VMEM((rows, width), F32),
            pltpu.VMEM((rows, width), BF16),
            pltpu.VMEM((width, rows), BF16),
            pltpu.VMEM((width, width), BF16),
            pltpu.VMEM((rows, width), BF16),
            pltpu.SemaphoreType.DMA((parts, most)),
            out_weights.sems(),
            pltpu.SemaphoreType.DMA((parts + 3,)),
        ],
        cost=cost(8 * rows * width * (hidden + 2 * width), 120 * rows * width),
        name="middle",
    )


def attend_back_kernel(
    ends,
    q_ref,
    k_ref,
    v_ref,
    o_ref,
    do_ref,
    lse_ref,
    dq_ref,
    dk_ref,
    dv_ref,
    gq_ref,
    gv_ref,
    allow,
    total,
):
    rows = q_ref.shape[0]
    span = min(256, rows)

    @pl.when(pl.program_id(0) == 0)
    def _():
        for start in range(0, rows, span):
            query = lax.broadcasted_iota(jnp.int32, (1, rows - start), 1) + start
            first = first_of_row(ends, query)
            key = lax.broadcasted_iota(jnp.int32, (span, rows - start), 0) + start
            allow[start : start + span, start:] = jnp.where(
                (key <= query) & (key >= first), 0.0, MASKED
            )

    lane = lax.broadcasted_iota(jnp.int32, (1, LANES), 1)
    low_lane = lane < HD
    one = low_lane.astype(BF16)
    masks = (one, 1 - one)
    product = (o_ref[...].astype(F32) * do_ref[...].astype(F32)).T
    inner = (
        jnp.sum(product[:HD], axis=0, keepdims=True),
        jnp.sum(product[HD:], axis=0, keepdims=True),
    )
    for start in range(0, rows, span):
        stop = start + span
        grads = []
        for head in range(2):
            keys = k_ref[start:stop, :] * masks[head]
            vals = v_ref[start:stop, :] * masks[head]
            scores = dot_nt(keys, q_ref[start:, :]) + allow[start:stop, start:]
            probs = jnp.exp(scores - lse_ref[0, head : head + 1, start:])
            grad_probs = dot_nt(vals, do_ref[start:, :])
            grad_scores = (probs * (grad_probs - inner[head][:, start:])).astype(BF16)
            grad_vals = dot_nn(probs.astype(BF16), do_ref[start:, :])
            grad_keys = dot_nn(grad_scores, q_ref[start:, :])
            grads.append((grad_keys, grad_vals))
            update = dot_tn(grad_scores, keys)
            if start == 0 and head == 0:
                total[...] = update
            else:
                total[start:, :] += update
        dk_ref[start:stop, :] = jnp.where(low_lane, grads[0][0], grads[1][0]).astype(BF16)
        dv_ref[start:stop, :] = jnp.where(low_lane, grads[0][1], grads[1][1]).astype(BF16)
    grad_query = (total[...] * HD ** (-0.5)).astype(BF16)
    dq_ref[...] = grad_query
    gq_ref[...] = jnp.sum(grad_query.astype(F32), axis=0, keepdims=True)
    gv_ref[...] = jnp.sum(dv_ref[...].astype(F32), axis=0, keepdims=True)


def run_attend_back(ends, qkv, mixed, dmix, lse, first, count, after=()):
    rows, width = mixed.shape
    pairs = width // LANES
    column = lambda shift: pl.BlockSpec((rows, LANES), lambda i: (0, i + shift))
    return call(
        attend_back_kernel,
        (count,),
        [(ends, SMEM)]
        + [(qkv, column(first + part * pairs)) for part in range(3)]
        + [
            (mixed, column(first)),
            (dmix, column(first)),
            (lse, pl.BlockSpec((1, 2, rows), lambda i: (i + first, 0, 0))),
        ],
        [((rows, LANES * count), BF16, column(0))] * 3
        + [((1, LANES * count), F32, pl.BlockSpec((1, LANES), lambda i: (0, i)))] * 2,
        after=after,
        scratch=[pltpu.VMEM((rows, rows), F32), pltpu.VMEM((rows, LANES), F32)],
        cost=cost(
            80 * rows * rows * LANES * count, rows * LANES * count
        ),
        name="attend_back",
    )


def project_kernel(turned_ref, dq_ref, dk_ref, dv_ref, own_ref, sib_ref):
    mid = own_ref.shape[1]
    size = dq_ref.shape[1]
    left = jnp.concatenate([dq_ref[...], dk_ref[:, : size // 2]], axis=1)
    right = jnp.concatenate([dk_ref[:, size // 2 :], dv_ref[...]], axis=1)
    for side, columns in enumerate((left, right)):
        own_ref[side] = dot_nn(turned_ref[:mid], columns).astype(BF16)
        sib_ref[side] = dot_nn(turned_ref[mid:], columns).astype(BF16)


def run_project(turned, dq, dk, dv, after=()):
    width, rows = turned.shape
    size = dq.shape[1]
    mid = width // 2
    grad = ((2, mid, 3 * size // 2), BF16, whole((2, mid, 3 * size // 2)))
    return call(
        project_kernel,
        (1,),
        [(turned, whole((width, rows)))] + [(value, whole((rows, size))) for value in (dq, dk, dv)],
        [grad, grad],
        after=after,
        cost=cost(6 * rows * width * size, 14 * rows * size),
        name="project",
    )


def run_input(weights, grads, x, grad_after, small, number, after=()):
    rows, width = x.shape
    span = 256
    size = grads[0][0].shape[1]
    flat = [value for group in grads for value in group]
    count = len(flat)
    by_row = lambda size: pl.BlockSpec((span, size), lambda i: (i, 0))

    def kernel(*refs):
        weight, sems = refs[-2:]
        stream = []
        for part in range(3):
            columns = slice(part * width, (part + 1) * width)
            copies, rest = weights.at(part * width).copies(
                refs,
                width,
                lambda at, lines, columns=columns: weight.at[pl.ds(at, lines), columns],
                sems.at[part],
            )
            stream.append(copies)
        refs = rest
        for copies in stream:
            start_all(copies)
        x_ref, grad_ref, gain_ref, out_ref, ggain_ref, gshift_ref = refs[count : count + 6]
        step = pl.program_id(0)
        total = None
        for part in range(3):
            wait_all(stream[part])
            for group in range(len(grads)):
                begin = part * width + group * size
                value = dot_nt(refs[3 * group + part][...], weight[:, begin : begin + size])
                total = value if total is None else total + value
        hat, scale = norm_stats(x_ref[...].astype(F32))
        accumulate(gshift_ref, jnp.sum(total, axis=0, keepdims=True), step == 0)
        accumulate(ggain_ref, jnp.sum(total * hat, axis=0, keepdims=True), step == 0)
        out_ref[...] = grad_ref[...] + norm_back(hat, scale, total * gain_ref[...])

    vector = ((1, width), F32, whole((1, width)))
    return call(
        kernel,
        (rows // span,),
        weights.inputs()
        + [(value, by_row(size)) for value in flat]
        + [(x, by_row(width)), (grad_after, by_row(width)), param(small, number, width)],
        [((rows, width), F32, by_row(width)), vector, vector],
        after=after,
        scratch=[
            pltpu.VMEM((width, 3 * width), BF16),
            pltpu.SemaphoreType.DMA((3, len(weights.plan))),
        ],
        cost=cost(24 * rows * width * width, 88 * rows * width),
        name="grad_input",
    )


def adamw(weight, first, second, grad, rate, decay):
    first_new = beta_one * first + (1.0 - beta_one) * grad
    second_new = beta_two * second + (1.0 - beta_two) * grad * grad
    first_hat = first_new / (1.0 - beta_one**STEP)
    second_hat = second_new / (1.0 - beta_two**STEP)
    weight_new = weight - rate * (first_hat / (jnp.sqrt(second_hat) + adam_eps) + decay * weight)
    return (weight_new, first_new, second_new)


def run_adam(core, state, groups, span, places, pick, earlier, after=()):
    half = groups[0][0].shape[-2]
    count = len(places)
    table = jnp.array(places, jnp.int32)
    place = pl.BlockSpec((half, span), lambda p, h, c, t: (jnp.bitwise_xor(h, c[0]), t[p]))
    flat = [value for group in groups for value in group]

    def kernel(core_ref, table_ref, w_ref, m_ref, v_ref, *refs):
        w_out, m_out, v_out, grad_ref = refs[-4:]
        for side in range(2):
            mine = refs[side : 2 * len(groups) : 2]
            for block in range(count):

                @pl.when((pl.program_id(1) == side) & (pl.program_id(0) == block))
                def _(mine=mine, block=block):
                    start = 0
                    for value in pick(block, mine):
                        grad_ref[:, start : start + value.shape[1]] = value
                        start += value.shape[1]

        w_out[...], m_out[...], v_out[...] = adamw(
            w_ref[...], m_ref[...], v_ref[...], grad_ref[...].astype(F32), 0.05, 0.1
        )

    moved = 2 * half * count * span
    return call(
        kernel,
        (count, 2),
        [(value, place) for value in state] + [(value, whole(value.shape)) for value in flat],
        [(state[0].shape, F32, place)] * 3,
        after=after,
        reuse=[] if earlier is None else [(value, n) for n, value in enumerate(earlier)],
        prefetch=(core, table),
        scratch=[pltpu.VMEM((half, span), BF16)],
        cost=cost(2 * moved, 2 * moved),
        name="adam",
    )


def run_side(core, jobs, after=(), steps=4):
    counts = [(len(job[0]), len(job[1])) for job in jobs]
    total_in = sum(count[0] for count in counts)

    def kernel(core_ref, *refs):
        ins = refs[:total_in]
        outs = refs[total_in:]
        for job, (have, give) in zip(jobs, counts):
            more = (core_ref,) if "places" in job[2].__code__.co_varnames else ()
            job[2](ins[:have], outs[:give], *more)
            ins = ins[have:]
            outs = outs[give:]

    def spec(block, index):
        return pl.BlockSpec(block, lambda i, c: index(i, c))

    moved = sum(array.size * 2 for job in jobs for array, _, _ in job[0])
    results = call(
        kernel,
        (steps,),
        [(array, spec(block, index)) for job in jobs for array, block, index in job[0]],
        [(shape, dtype, spec(block, index)) for job in jobs for shape, dtype, block, index in job[1]],
        after=after,
        prefetch=(core,),
        cost=cost(0, 2 * moved),
        name="side",
    )
    split = []
    for _, give in counts:
        split.append(results[:give])
        results = results[give:]
    return split


def job_cast(rows, columns, by_core, steps):
    span = rows // steps
    total = sum(size for _, _, size in columns)
    ins = []
    for state, number, size in columns:
        index = lambda i, c, number=number: (c[0] * steps * by_core + i, number)
        ins.append((state, (span, size), index))
    outs = [((rows, total), BF16, (span, total), lambda i, c: (i, 0))]

    def run(have, give):
        start = 0
        for ref, (_, _, size) in zip(have, columns):
            give[0][:, start : start + size] = ref[...].astype(BF16)
            start += size

    return ins, outs, run


def job_join(left, right, steps, around):
    _, blocks, rows, size = left.shape
    span = rows // steps
    four = lambda i, c: (0, 0, i, 0)
    ins = [(value, (2, blocks, span, size), four) for value in (left, right)]
    outs = [((blocks, 2, rows, size), BF16, (blocks, 2, span, size), four)]

    def run(have, give, places):
        for side in range(2):
            for block in range(blocks):
                owner = jnp.bitwise_xor(places[1], block) if around else block
                give[0][owner, side] = have[0][side, block] + have[1][side, block]

    return ins, outs, run


def job_copy(value, first, rows):
    size = value.shape[1]
    ins = [(value, value.shape, lambda i, c: (0, 0))]
    outs = [((rows, size), value.dtype, (rows, size), lambda i, c: (0, 0))]

    def run(have, give):
        give[0][...] = have[0][first : first + rows, :]

    return ins, outs, run


def job_add(left, right, steps):
    at = left.ndim - 2
    if left.shape[at] == 1:
        same = lambda i, c: (0,) * left.ndim

        def run_whole(have, give):
            give[0][...] = have[0][...] + have[1][...]

        return (
            [(left, left.shape, same), (right, right.shape, same)],
            [(left.shape, left.dtype, left.shape, same)],
            run_whole,
        )
    block = tuple(size // steps if axis == at else size for axis, size in enumerate(left.shape))
    index = lambda i, c: (0,) * at + (i, 0)

    def run(have, give):
        give[0][...] = have[0][...] + have[1][...]

    return [(left, block, index), (right, block, index)], [(left.shape, left.dtype, block, index)], run


def job_pick(own, received, steps):
    at = own.ndim - 2
    block = tuple(size // steps if axis == at else size for axis, size in enumerate(own.shape))
    index = lambda i, c: (0,) * at + (i, 0)

    def run(have, give, places):
        give[0][...] = jnp.where(places[2] == 1, have[0][...], have[1][...])

    return [(own, block, index), (received, block, index)], [(own.shape, own.dtype, block, index)], run


def job_sum(groups, keep, send, steps):
    _, blocks, rows, _ = groups[0][0].shape
    span = rows // steps
    total = sum(own.shape[3] for own, _ in groups)
    four = lambda i, c: (0, 0, i, 0)
    three = lambda i, c: (0, i, 0)
    ins = []
    for own, received in groups:
        size = own.shape[3]
        ins.append((own, (2, blocks, span, size), four))
        if len(received) == 1:
            ins.append((received[0], (2, blocks, span, size), four))
        else:
            ins += [(value, (blocks, span, size), three) for value in received]
    kept = len(keep[0])
    outs = [((2, kept, rows, total), BF16, (2, kept, span, total), four)]
    if len(send) == 1:
        gone = len(send[0])
        outs.append(((2, gone, rows, total), BF16, (2, gone, span, total), four))
    else:
        for side in range(2):
            if send[side]:
                gone = len(send[side])
                outs.append(((gone, rows, total), BF16, (gone, span, total), three))

    def run(have, give):
        start = 0
        for own, received in groups:
            size = own.shape[3]
            columns = slice(start, start + size)
            start += size
            for side in range(2):
                for block in range(blocks):
                    other = have[1][side, block] if len(received) == 1 else have[1 + side][block]
                    value = have[0][side, block] + other
                    if block in keep[side]:
                        give[0][side, keep[side].index(block), :, columns] = value
                    elif len(send) == 1:
                        give[1][side, send[0].index(block), :, columns] = value
                    else:
                        give[1 + side][send[side].index(block), :, columns] = value
            have = have[1 + len(received) :]

    return ins, outs, run


def job_params(rows, shards, small_size):
    ins = []
    for array, row in rows:
        if array.shape[0] == 1:
            ins.append((array, array.shape, lambda i, c: (0, 0)))
        else:
            size = array.shape[1]
            ins.append((array, (16, size), lambda i, c, row=row: (row // 16, 0)))
    shape = (1, shards * small_size)
    outs = [(shape, F32, shape, lambda i, c: (0, 0))]

    def run(have, give, places):
        for number, ref in enumerate(have):
            owner = jnp.bitwise_xor(places[1], number)
            start = pl.multiple_of(owner * small_size, LANES)
            value = ref[0:1, :small_size].astype(BF16).astype(F32)
            give[0][:, pl.ds(start, small_size)] = value

    return ins, outs, run


def job_lay(values):
    total = sum(value.shape[1] for value in values)
    same = lambda i, c: (0, 0)
    ins = [(value, value.shape, same) for value in values]

    def run(have, give):
        start = 0
        for ref in have:
            give[0][:, start : start + ref.shape[1]] = ref[...]
            start += ref.shape[1]

    return ins, [((1, total), F32, (1, total), same)], run


class Links:
    def __init__(self, sizes, shard_rows):
        self.replicas, self.shards = sizes
        dp = lax.axis_index("dp")
        self.shard = lax.axis_index("shard")
        self.core = lax.rem(dp, 2)
        place = dp // 2
        self.inner = (place > 0) & (place < sizes[0] // 2 - 1)
        self.core_arr = jnp.stack([self.core, self.shard, self.inner]).astype(jnp.int32)
        self.rows = shard_rows
        self.half = shard_rows // 2
        self.fast = sizes == (8, 4)

    def swap(self, value):
        return self.across_dp(value, 1)

    def across_dp(self, value, bit):
        return lax.ppermute(value, "dp", [(d, d ^ bit) for d in range(self.replicas)])

    def along_dp(self, value, step):
        hops = ([(0, 1), (3, 2)], [(1, 2), (2, 1)], [(1, 0), (2, 3)])[step]
        pairs = [(2 * a + core, 2 * b + core) for a, b in hops for core in range(2)]
        return lax.ppermute(value, "dp", pairs)

    def across_shard(self, value, bit):
        return lax.ppermute(value, "shard", [(s, s ^ bit) for s in range(self.shards)])

    def turned_offsets(self, around):
        blocks = jnp.arange(2 * self.shards, dtype=jnp.int32)
        owner = blocks // 2
        if around:
            owner = jnp.bitwise_xor(owner, self.shard)
        away = jnp.bitwise_xor(lax.rem(blocks, 2), self.core)
        return away * (self.shards * self.half) + owner * self.half

    def gather(self, half_rows):
        return lax.all_gather(half_rows, "shard", axis=0, tiled=True)

    def gathered(self, mine, behind=None):
        if behind is not None:
            mine, _ = lax.optimization_barrier((mine, behind))
        first = jnp.arange(self.shards, dtype=jnp.int32) * self.rows
        offs = jnp.concatenate([first + self.core * self.half, first + (1 - self.core) * self.half])
        stride = mine.shape[0] // self.shards
        plan = tuple((0, t * stride, self.half, t) for t in range(self.shards)) + tuple(
            (1, t * stride, self.half, self.shards + t) for t in range(self.shards)
        )
        return Weights((mine, self.swap(mine)), plan, offs.astype(jnp.int32))

    def over_dp(self, values):
        groups = [[d for d in range(self.replicas) if d % 2 == c] for c in range(2)]
        return lax.psum(values, "dp", axis_index_groups=groups)


class Gather:
    def __init__(self, links, half_rows, own):
        self.links = links
        self.own = own
        self.by_x = links.across_shard(half_rows, 1)
        self.by_y = links.across_shard(half_rows, 2)

    def jobs(self):
        part = self.links.half // 2
        rest = self.by_x.shape[0] - part
        return [job_copy(self.by_y, 0, part), job_copy(self.by_x, part, rest)]

    def forward(self, results):
        links = self.links
        self.far = (
            links.across_shard(results[0], 1),
            links.across_shard(results[1], 2),
        )
        self.near = (links.swap(self.by_x), links.swap(self.by_y))

    def weights(self):
        links = self.links
        half, rows = links.half, links.rows
        part = half // 2
        far = tuple(links.swap(value) for value in self.far)
        pieces = (self.own, self.by_x, self.by_y, *self.near, *self.far, *far)
        plan = ((0, 0, rows, 0),)
        plan += tuple((n, 0, half, n) for n in range(1, 5))
        plan += tuple((n, 0, part, n) for n in range(5, 9))
        at = lambda bits: jnp.bitwise_xor(links.shard, bits) * rows
        mine = links.core * half
        other = (1 - links.core) * half
        offs = [at(0), at(1) + mine, at(2) + mine, at(1) + other, at(2) + other]
        offs += [at(3) + mine, at(3) + mine + part, at(3) + other, at(3) + other + part]
        return Weights(pieces, plan, jnp.stack(offs).astype(jnp.int32))


LINE, AT_ONCE, EXCHANGE = range(3)


class Reduce:
    def __init__(self, links, way, bits=((1, 2), (2, 1))):
        self.links = links
        self.way = way
        self.bits = bits
        self.stage = 0
        self.groups = []

    def add(self, own, sib):
        shape = (2, self.links.shards, self.links.half, own.shape[2])
        self.groups.append((own.reshape(shape), (self.links.swap(sib).reshape(shape),)))
        return self

    def job(self, steps):
        if self.stage > 2:
            own, received = self.groups[0]
            if self.way == LINE and self.stage == 5:
                return job_pick(own, received, steps)
            return job_add(own, received, steps)
        blocks = self.groups[0][0].shape[1]
        sides = []
        for number in range(2):
            order = self.bits[number % len(self.bits)]
            if blocks == 1:
                sides.append(())
            elif blocks == 2:
                sides.append((1,))
            else:
                sides.append(tuple(block for block in range(blocks) if block & order[0]))
        keep = [[block for block in range(blocks) if block not in gone] for gone in sides]
        send = [list(gone) for gone in sides]
        if len(self.bits) == 1 and blocks > 1:
            send = send[:1]
        return job_sum(self.groups, keep, send, steps)

    def advance(self, results):
        links = self.links
        own = results[0]
        stage = self.stage
        self.stage += 1
        if stage < 2:
            received = tuple(
                links.across_shard(value, order[stage])
                for value, order in zip(results[1:], self.bits)
            )
            self.groups = [(own, received)]
            return
        if stage == 2:
            own = own.reshape(2, own.shape[2], own.shape[3])
        if self.way == AT_ONCE:
            self.own = own
        elif self.way == LINE and stage < 5:
            self.groups = [(own, links.along_dp(own, stage - 2))]
        elif self.way == EXCHANGE and stage < 4:
            self.groups = [(own, links.across_dp(own, 2 * (stage - 1)))]
        else:
            self.grads = (own, links.swap(own))

    def close(self, behind):
        mine, _ = lax.optimization_barrier((self.own, behind))
        self.grads = (mine, self.links.swap(mine))


class Wide:
    def __init__(self, links, joined):
        self.links = links
        self.shape = joined.shape[1:]
        flat = joined.reshape(-1, joined.shape[3])
        self.own = lax.psum_scatter(flat, "shard", scatter_dimension=0, tiled=True)

    def finish(self):
        self.own = self.links.over_dp(self.own).reshape(self.shape)

    def close(self, behind):
        mine, _ = lax.optimization_barrier((self.own, behind))
        self.grads = (mine, self.links.swap(mine))


class Side:
    def __init__(self, links):
        self.links = links
        self.order = ()

    def jobs(self, jobs, steps=1, after=()):
        results = run_side(self.links.core_arr, jobs, after=(*self.order, *after), steps=steps)
        self.order = (results[0][0],)
        return [result[0] for result in results]

    def reduce(self, reduces, jobs=(), steps=2):
        work = [item.job(steps) for item in reduces] + list(jobs)
        results = run_side(self.links.core_arr, work, after=self.order, steps=steps)
        for item, result in zip(reduces, results):
            item.advance(result)
        self.order = (results[0][0],)
        return [result[0] for result in results[len(reduces) :]]

    def then(self, results):
        self.order = (results[0],)
        return results


def small_parts(small, width, hidden):
    bounds = [width] * 3 + [hidden] + [width] * 5
    parts = []
    start = 0
    for size in bounds:
        parts.append(small[:, start : start + size])
        start += size
    return parts


def body(sizes, *args):
    tokens, cotangent, lengths = args[:3]
    attn_state, mlp_state, small_state = args[3:6], args[6:9], args[9:12]
    rows, width = tokens.shape
    links = Links(sizes, attn_state[0].shape[0])
    half = links.half
    hidden = mlp_state[0].shape[1] // 2
    pairs = width // LANES
    pad = 16
    core_arr = links.core_arr
    around = links.turned_offsets(links.fast)
    side = Side(links)

    ends = jnp.cumsum(lengths[0], dtype=jnp.int32)
    small_own = small_state[0][None]
    small_size = small_own.shape[1]
    (
        BIAS_Q,
        BIAS_V,
        BIAS_O,
        BIAS_UP,
    ) = range(4)
    BIAS_DN, GAIN_ONE, SHIFT_ONE, GAIN_TWO, SHIFT_TWO = range(
        BIAS_UP + hidden // width, BIAS_UP + hidden // width + 5
    )

    def first_job():
        ins = [
            (attn_state[0], (half, 4 * width), lambda i, c: (c[0], 0)),
            (small_own, (1, small_size), lambda i, c: (0, 0)),
        ]
        outs = [((half + pad, 4 * width), BF16, (half + pad, 4 * width), lambda i, c: (0, 0))]

        def job(have, give):
            give[0][:half] = have[0][...].astype(BF16)
            row = have[1][...].astype(BF16)
            give[0][half:, :small_size] = jnp.broadcast_to(row, (pad, small_size))

        return ins, outs, job

    block = hidden // 2
    groups = [[(mlp_state[0], number, block) for number in pair] for pair in ((0, 2), (1, 3))]
    (first_half,) = side.jobs([first_job()])
    if links.fast:
        attn_gather = Gather(links, first_half, None)
    else:
        attn_weights = links.gathered(links.gather(first_half))
    dy, dyt, grad_bias_dn = side.then(run_cot(half, around, ends, cotangent, after=side.order))
    (more_half,) = side.jobs([job_cast(half, groups[1], 1, 4)], steps=4)
    if links.fast:
        (attn_gather.own,) = side.jobs(
            [job_cast(links.rows, [(attn_state[0], 0, 4 * width)], 0, 4)], steps=4
        )
        *copied, feed_half = side.jobs([*attn_gather.jobs(), job_cast(half, groups[0], 1, 1)])
        attn_gather.forward(copied)
    else:
        (feed_half,) = side.jobs([job_cast(half, groups[0], 1, 1)])
    wide = links.gather(feed_half)
    more_wide = links.gather(more_half)
    if links.fast:
        attn_weights = attn_gather.weights()
        rows_of = [
            (small_own, 0),
            (attn_gather.by_x, half),
            (attn_gather.by_y, half),
            (attn_gather.far[1], half // 2),
        ]
        (small,) = side.jobs([job_params(rows_of, links.shards, small_size)])
    else:
        small = attn_weights.pieces[0].reshape(links.shards, half + pad, 4 * width)
        small = small[:, half, :small_size].astype(F32).reshape(1, -1)

    qkv, turned_one = side.then(
        run_qkv(
            half,
            attn_weights,
            around,
            tokens,
            small,
            (BIAS_Q, BIAS_V, GAIN_ONE, SHIFT_ONE),
            after=side.order,
        )
    )
    mixed, lse = side.then(run_attend(ends, qkv, 0, pairs, after=side.order))
    wide = links.gathered(wide, lse)
    side.order += (wide.pieces[0],)
    after, low_two, turned_two, turned_mixed = side.then(
        run_after(
            half,
            attn_weights.at(3 * width),
            (around, around),
            mixed,
            tokens,
            small,
            (BIAS_O, GAIN_TWO, SHIFT_TWO),
            after=side.order,
        )
    )

    passed, grad_bias_up = [None], []
    blocked = lambda value: value.reshape(2, links.shards, half, value.shape[2])

    def feed(start, up_weights, down_weights):
        act, du, own, sib, gbias = run_feed(
            up_weights,
            down_weights,
            low_two,
            turned_two,
            dy,
            dyt,
            small,
            BIAS_UP * width + start,
            start,
            block,
            passed[-1],
            after=side.order,
        )
        side.order = (own,)
        passed.append((act, du))
        grad_bias_up.append(gbias)
        return own, sib

    def unit(way, own, sib, bits=((1, 2), (2, 1))):
        if links.fast:
            return Reduce(links, way, bits).add(own, sib)
        return Wide(links, side.jobs([join(own, links.swap(sib))], steps=4)[0])

    def join(own, received):
        return job_join(blocked(own), blocked(received), 4, links.fast)

    def reduce(units, jobs=(), steps=2):
        if links.fast:
            return side.reduce(units, jobs, steps)
        return side.jobs(jobs, steps) if jobs else None

    group_a = feed(0, wide, wide.at(block))
    more_wide = links.gathered(more_wide, grad_bias_up[0])
    unit_a = unit(LINE, *group_a)
    reduce([unit_a], steps=4)
    unit_b = unit(AT_ONCE, *feed(block, more_wide, more_wide.at(block)))
    reduce([unit_a], steps=4)
    (
        grad_after,
        dmix,
        own_out,
        sib_out,
        grad_bias_o,
        grad_gain_two,
        grad_shift_two,
    ) = side.then(
        run_middle(
            [(block, wide), (block, more_wide)],
            attn_weights.at(3 * width),
            passed[-1][1],
            after,
            dy,
            small,
            GAIN_TWO,
            turned_mixed,
            after=side.order,
        )
    )
    received_out = links.swap(sib_out)
    reduce([unit_a, unit_b], steps=4)
    grads, biases = [], []

    def attend_back(first):
        dq, dk, dv, gq, gv = side.then(
            run_attend_back(ends, qkv, mixed, dmix, lse, first, pairs // 2, after=side.order)
        )
        grads.append((dq, dk, dv))
        biases.append((gq, gv))

    def project(group):
        return side.then(run_project(turned_one, *grads[group], after=side.order))

    attend_back(0)
    (joined,) = reduce([unit_a, unit_b], [join(own_out, received_out)], steps=4)
    unit_e = Wide(links, joined)
    unit_c = unit(EXCHANGE, *project(0), ((1, 2),))
    attend_back(pairs // 2)
    reduce([unit_a, unit_b, unit_c], steps=4)
    if links.fast:
        unit_b.own, unit_e.own = links.over_dp((unit_b.own, unit_e.own.reshape(unit_e.shape)))
    unit_d = unit(EXCHANGE, *project(1), ((1, 2),))
    grad_input, grad_gain_one, grad_shift_one = side.then(
        run_input(attn_weights, grads, tokens, grad_after, small, GAIN_ONE, after=side.order)
    )
    small_grads = [biases[0][0], biases[1][0], biases[0][1], biases[1][1], grad_bias_o]
    small_grads += grad_bias_up
    small_grads += [grad_bias_dn, grad_gain_one, grad_shift_one, grad_gain_two, grad_shift_two]
    (grad_small,) = reduce([unit_a, unit_c, unit_d], [job_lay(small_grads)])

    def pick_feed(number, arrays):
        return [arrays[0][number]]

    def adam_mlp(number, item, earlier):
        return side.then(
            run_adam(
                core_arr,
                mlp_state,
                [item.grads],
                block,
                [number, 2 + number],
                pick_feed,
                earlier,
                after=side.order,
            )
        )

    out_block = width // 2

    def pick_heads(number, arrays):
        left, right = arrays[0][0], arrays[0][1]
        split = out_block // 2
        if number > 2:
            return [arrays[1][number - 3]]
        return (
            [left[:, :out_block]],
            [left[:, out_block:], right[:, :split]],
            [right[:, split:]],
        )[number]

    def adam_attn(items, places, earlier):
        return side.then(
            run_adam(
                core_arr,
                attn_state,
                [item.grads for item in items],
                out_block,
                places,
                pick_heads,
                earlier,
                after=side.order,
            )
        )

    def output_now():
        out = run_output(
            [(block, wide.at(block)), (block, more_wide.at(block))],
            passed[-1][0],
            after,
            small,
            BIAS_DN,
            after=side.order,
        )
        side.then([out])
        return out

    if links.fast:
        shard_move = lambda bit: functools.partial(links.across_shard, bit=bit)
        dp_move = lambda bit: functools.partial(links.across_dp, bit=bit)
        moved = links.swap(grad_small)

        def step(units, move):
            (total,) = reduce(units, [job_add(grad_small, moved, 2)])
            return total, move(total) if move else None

        mlp_new = adam_mlp(0, unit_a, None)
        grad_small, moved = step([unit_c, unit_d], shard_move(1))
        output = output_now()
        grad_small, moved = step([unit_c, unit_d], shard_move(2))
        unit_b.close(grad_small)
        unit_e.close(grad_small)
        mlp_new = adam_mlp(1, unit_b, mlp_new)
        grad_small, moved = step([unit_c, unit_d], dp_move(2))
        attn_new = adam_attn([unit_c], [0, 2, 4], None)
        grad_small, moved = step([unit_d], dp_move(4))
        attn_new = adam_attn([unit_d, unit_e], [1, 3, 5, 6, 7], attn_new)
        grad_small, _ = step([], None)
    else:
        for item in (unit_a, unit_b, unit_c, unit_d, unit_e):
            item.finish()
            item.close(grad_input)
        grad_small = lax.psum(grad_small, ("dp", "shard"))
        output = output_now()
        mlp_new = adam_mlp(1, unit_b, adam_mlp(0, unit_a, None))
        attn_new = adam_attn([unit_c], [0, 2, 4], None)
        attn_new = adam_attn([unit_d, unit_e], [1, 3, 5, 6, 7], attn_new)
    grad_small = lax.dynamic_slice_in_dim(grad_small, links.shard * small_size, small_size, 1)[0]
    small_new = adamw(*small_state, grad_small, 0.4, 0.0)
    return (output, grad_input, *attn_new, *mlp_new, *small_new)


def solution(mesh):
    tokens = P(("dp", "shard"), None)
    state = P("shard", None)
    vector = P("shard")
    return jax.shard_map(
        functools.partial(body, (mesh.shape["dp"], mesh.shape["shard"])),
        mesh=mesh,
        in_specs=(tokens,) * 3 + (state,) * 6 + (vector,) * 3,
        out_specs=(tokens,) * 2 + (state,) * 6 + (vector,) * 3,
        check_vma=False,
    )
```
